32 devices in a mesh: gx: 8 (over y, x, core), gy: 4 (over z).
Axes of the slice: x: 2, y: 2, z: 4, core: 2. Of those that a mesh axis runs over, the one named last changes fastest.
Arguments:
- diag_blocks: float32 [9, 512, 512], P(None, 'gx', 'gy'), may hold values from 0 to 36, as said below
- edge_blocks: float32 [4, 9, 512, 512], P(None, None, 'gx', 'gy'), may hold values from -0.3 to 0.3
- edge_mask: int32 [4, 512, 512], P(None, 'gx', 'gy'), may hold values 0 or 1
- src_values: float32 [3, 32768], P(None, ('gx', 'gy')), may hold values from -48 to 48
- src_owner: int32 [32768, 1], P(('gx', 'gy')), may hold values from 0 to 7; in each aligned block of 1024 rows (0 to 1023, 1024 to 2047, ...) at most 256 rows name the same one
- src_node: int32 [32768], P(('gx', 'gy')), may hold values from 0 to 8191
- src_count: int32 [32], P(('gx', 'gy')), may hold values from 256 to 1024, as said below
- surf_node: int32 [65536], P(('gx', 'gy')), may hold values from 0 to 8191
- surf_param: float32 [3, 65536], P(None, ('gx', 'gy')), may hold values from 0 to 1
- tile_box: int32 [512], P(('gx', 'gy')), may hold values from 0 to 31
Outputs:
- adjoint_field: float32 [3, 512, 512], P(None, 'gx', 'gy')
- box_gradient: float32 [32, 192], P(('gx', 'gy'))
The draws below stay inside these ranges and needn't reach their ends.
Inputs may be any that keep to these rules, and one draw needn't show every extreme that they name: `src_owner`: each device's rows name every gx index at most 256 times. `src_count`: some device has all 1024 rows live. `diag_blocks`: entries 0, 4 and 8 lie between 6 and 36; the other entries between 0 and 1.
All inputs are finite; a program needn't handle non-finite values. No bound on the sum of `edge_mask` on one device may be relied on, other than what follows from the above.
Results may differ from the reference program's by a relative error of at most 0.0015.
Values sent between devices are 32-bit elements; how exact they have to be, the bound alone decides.
No kernel may reach another device: no remote copies, remote signals or barrier semaphores. Data moves between devices by JAX's collectives and lax.ppermute only.
A program may use at most 64 MiB of HBM per device.

```python
import math
import jax
import jax.numpy as jnp
import numpy as np
from jax import lax

CX = 64
CY = 128
ITERS = 2
SRC_DEV = 1024
SURF_TILES = 16
TILE_POINTS = 128
BOXES = 32
CAP = 256
NX = 512
NY = 512
SRC_TOTAL = 32768
TILE_COUNT = 512
SURF_TOTAL = 65536
N_GX = 8
N_GY = 4


def draw_src_count(key, part):
    base = jax.random.randint(key, (BOXES,), SRC_DEV // 4, SRC_DEV + 1)
    chosen = jax.random.randint(jax.random.fold_in(key, 7), (), 0, BOXES)
    return jnp.where(jnp.arange(BOXES) == chosen, SRC_DEV, base).astype(jnp.int32)


def node_blocks():
    block_x = jnp.arange(NX, dtype=jnp.int32) // CX
    block_y = jnp.arange(NY, dtype=jnp.int32) // CY
    return (block_x, block_y)


def draw_diag_blocks(key, part):
    first, second = jax.random.split(key)
    block_x, block_y = node_blocks()
    row_part = jax.random.uniform(jax.random.fold_in(key, 11), (NX // CX,), minval=0.0, maxval=1.0)
    col_part = jax.random.uniform(jax.random.fold_in(key, 12), (NY // CY,), minval=0.0, maxval=1.0)
    coupling_level = 0.1 + 0.4 * row_part[block_x][:, None] + 0.4 * col_part[block_y][None, :]
    coords = jnp.arange(NX, dtype=jnp.float32)[None, :, None]
    rising = 1.0 + 2.0 * coords / NX
    main = jax.random.uniform(first, (9, NX, NY), minval=6.0, maxval=10.0)
    side = coupling_level[None, :, :] + jax.random.uniform(second, (9, NX, NY), minval=-0.05, maxval=0.05)
    onmain = (jnp.arange(9) % 4 == 0)[:, None, None]
    return jnp.where(onmain, main * rising, side).astype(jnp.float32)


def draw_edge_blocks(key, part):
    block_x, block_y = node_blocks()
    sign_table = 2.0 * jax.random.randint(jax.random.fold_in(key, 21), (NX // CX, NY // CY), 0, 2).astype(jnp.float32) - 1.0
    sign_field = sign_table[block_x[:, None], block_y[None, :]]
    jitter = jax.random.uniform(key, (4, 9, NX, NY), minval=-0.05, maxval=0.05)
    result = 0.25 * sign_field[None, None, :, :] + jitter
    return result.astype(jnp.float32)


def draw_src_values(key, part):
    first, second = jax.random.split(key)
    sign_row = 2.0 * jax.random.randint(second, (1, SRC_TOTAL), 0, 2).astype(jnp.float32) - 1.0
    magnitude = jnp.minimum(8.0 * jnp.abs(jax.random.normal(first, (3, SRC_TOTAL))), 48.0)
    return (magnitude * sign_row).astype(jnp.float32)


def place_ends(drawn, rng, low, top_value):
    index_at = [jax.random.randint(jax.random.fold_in(rng, axis), (), 0, length) for axis, length in enumerate(drawn.shape)]
    main_axis = drawn.shape.index(max(drawn.shape))
    neighbour = index_at[:main_axis] + [(index_at[main_axis] + 1) % drawn.shape[main_axis]] + index_at[main_axis + 1:]
    return drawn.at[tuple(index_at)].set(low).at[tuple(neighbour)].set(top_value)


def block_scale(own_key, shape, cuts, smallest, largest):
    loudness, own = 1.0, jax.random.fold_in(own_key, 6)
    for dim, parts in cuts:
        heights = jnp.exp(jax.random.uniform(jax.random.fold_in(own, dim), (parts,), jnp.float32, smallest / len(cuts), largest / len(cuts)))
        loudness = loudness * jnp.repeat(heights, shape[dim] // parts).reshape([-1 if axis == dim else 1 for axis in range(len(shape))])
    return loudness


def deal_out(key, own, number, rows, amount, top, limit, slope):
    order = jax.random.permutation(key, amount)
    heavy_load, common = shares(amount, rows * top, limit, slope, True), shares(amount, rows * top, limit, slope, False)
    places = jnp.arange(amount)

    def named(sizes, rotation):
        used = int((sizes > 0).sum())
        fixed = max(1, used // 4)
        passed = fixed + (places - fixed + rotation * (used - fixed)) % max(1, amount - fixed)
        return jnp.zeros((amount,), jnp.int32).at[order[jnp.where(places < fixed, places, passed)]].set(jnp.asarray(sizes, jnp.int32))

    sizes = jnp.where(number % 4 == 0, named(heavy_load, number // 4), named(common, number - number // 4 - 1))
    mixed = jax.random.permutation(jax.random.fold_in(own, 3), amount)
    giver, sink = mixed[0:amount // 2 * 2:2], mixed[1:amount // 2 * 2:2]
    margin = jnp.minimum(sizes[giver] - 1, limit - sizes[sink]) // 2
    margin = jnp.where((giver == order[0]) | (sink == order[0]) | (sizes[sink] == 0), 0, jnp.maximum(margin, 0))
    passed = jax.random.randint(jax.random.fold_in(own, 4), (amount // 2,), 0, 1 << 20) % (margin + 1)
    sizes = sizes.at[giver].add(-passed).at[sink].add(passed)
    members = jnp.searchsorted(jnp.cumsum(sizes), jnp.arange(rows * top), side="right").astype(jnp.int32)
    listing = members.reshape(top, rows).T
    listing = listing[jax.random.permutation(jax.random.fold_in(own, 1), rows)]
    rotation = jax.random.randint(jax.random.fold_in(own, 2), (rows, 1), 0, top)
    return jnp.take_along_axis(listing, (jnp.arange(top)[None, :] + rotation) % top, axis=1)


def shares(number_of, total, reach, slope, full):
    loads = [(1 << 20) // math.isqrt(grade ** slope) + 1 for grade in range(1, number_of + 1)]
    largest = reach if full else min(reach, max(-(-total // number_of), total * loads[0] // sum(loads)))
    least = 1 if total - largest >= number_of - 1 else 0
    holding, spare = [largest] + [least] * (number_of - 1), total - largest - least * (number_of - 1)
    while spare > 0:
        movable = [i for i in range(1, number_of) if holding[i] < largest] or [i for i in range(1, number_of) if holding[i] < reach]
        pool, left = sum([loads[i] for i in movable]), spare
        for i in movable:
            extra = min(reach - holding[i], max(1, left * loads[i] // pool), spare)
            holding[i] = holding[i] + extra
            spare = spare - extra
    return np.array(holding)


def setup_inputs(seed: int = 0) -> dict:
    seeds = jax.random.split(jax.random.key(seed), 11)
    diag_blocks = draw_diag_blocks(jax.random.fold_in(seeds[10], 71), 0)
    edge_blocks = draw_edge_blocks(jax.random.fold_in(seeds[10], 71), 0)
    edge_mask = place_ends((jax.random.randint(seeds[2], (4, NX, NY), 0, 4) < 3).astype(jnp.int32), jax.random.fold_in(seeds[2], 1), 0, 1)
    src_values = draw_src_values(jax.random.fold_in(seeds[10], 71), 0)
    src_owner_keys = jax.random.split(jax.random.fold_in(seeds[4], 1), SRC_TOTAL // SRC_DEV)
    src_owner_turns = jax.random.permutation(jax.random.fold_in(seeds[4], 3), SRC_TOTAL // SRC_DEV)
    src_owner = jax.vmap(lambda own, number: deal_out(jax.random.fold_in(seeds[4], 2), own, number, SRC_DEV, N_GX, 1, CAP, 2))(src_owner_keys, src_owner_turns).reshape((SRC_TOTAL, 1))
    src_node = place_ends(jax.random.randint(seeds[5], (SRC_TOTAL,), 0, CX * CY), jax.random.fold_in(seeds[5], 1), 0, (CX * CY) - 1).astype(jnp.int32)
    src_count = draw_src_count(jax.random.fold_in(seeds[10], 71), 0)
    surf_node = place_ends(jax.random.randint(seeds[7], (SURF_TOTAL,), 0, CX * CY), jax.random.fold_in(seeds[7], 1), 0, (CX * CY) - 1).astype(jnp.int32)
    surf_param = jnp.clip(1.0 * jax.random.uniform(seeds[8], (3, SURF_TOTAL), jnp.float32) ** block_scale(seeds[8], (3, SURF_TOTAL), ((1, 32),), -0.2, 0.2), 0.0, 1.0)
    tile_box = place_ends(jax.random.randint(seeds[9], (TILE_COUNT,), 0, BOXES), jax.random.fold_in(seeds[9], 1), 0, BOXES - 1).astype(jnp.int32)
    return {"diag_blocks": diag_blocks, "edge_blocks": edge_blocks, "edge_mask": edge_mask, "src_values": src_values, "src_owner": src_owner, "src_node": src_node, "src_count": src_count, "surf_node": surf_node, "surf_param": surf_param, "tile_box": tile_box}


def block_product(blocks, field):
    return jnp.stack([blocks[row] * field[0] + blocks[3 + row] * field[1] + blocks[6 + row] * field[2] for row in range(3)])


def apply_transposed_operator(field, diag_blocks, masked):
    result = block_product(diag_blocks, field)
    upper_x = jnp.pad(block_product(masked[0], field), ((0, 0), (1, 0), (0, 0)))[:, :-1, :]
    lower_x = jnp.pad(block_product(masked[1], field), ((0, 0), (0, 1), (0, 0)))[:, 1:, :]
    upper_y = jnp.pad(block_product(masked[2], field), ((0, 0), (0, 0), (1, 0)))[:, :, :-1]
    lower_y = jnp.pad(block_product(masked[3], field), ((0, 0), (0, 0), (0, 1)))[:, :, 1:]
    return result + upper_x + lower_x + upper_y + lower_y


def bernstein(coord):
    other = 1.0 - coord
    return jnp.stack([other * other * other, 3.0 * coord * other * other, 3.0 * coord * coord * other, coord * coord * coord])


def tile_weights(params):
    first = bernstein(params[0])
    second = bernstein(params[1])
    third = bernstein(params[2])
    table = first[:, None, None, :] * second[None, :, None, :] * third[None, None, :, :]
    return table.reshape(64, -1)


def reference(diag_blocks, edge_blocks, edge_mask, src_values, src_owner, src_node, src_count, surf_node, surf_param, tile_box):
    masked = edge_blocks * edge_mask.astype(jnp.float32)[:, None]
    total_rows = src_node.shape[0]
    rows = jnp.arange(total_rows, dtype=jnp.int32)
    sender = rows // SRC_DEV
    live = (rows % SRC_DEV) < src_count[sender]
    column = sender % N_GY
    xs = src_owner[:, 0] * CX + src_node // CY
    ys = column * CY + src_node % CY
    load = jnp.zeros((3, NX, NY), jnp.float32).at[:, xs, ys].add(src_values * live.astype(jnp.float32))
    scale = jnp.stack([diag_blocks[0], diag_blocks[4], diag_blocks[8]])
    solution = jnp.zeros_like(load)
    residual = load
    precond = residual / scale
    search = precond
    norm_now = jnp.sum(residual * precond)
    for sweep in range(ITERS):
        image = apply_transposed_operator(search, diag_blocks, masked)
        step_size = norm_now / jnp.sum(search * image)
        solution = solution + step_size * search
        residual = residual - step_size * image
        if sweep + 1 < ITERS:
            precond = residual / scale
            norm_next = jnp.sum(residual * precond)
            search = precond + (norm_next / norm_now) * search
            norm_now = norm_next
    points = surf_node.shape[0]
    holder = jnp.arange(points, dtype=jnp.int32) // (SURF_TILES * TILE_POINTS)
    node_x = (holder // N_GY) * CX + surf_node // CY
    node_y = (holder % N_GY) * CY + surf_node % CY
    design_sensitivity = solution[:, node_x, node_y]
    tile_weight_values = tile_weights(surf_param)
    surface_tiles = tile_box.shape[0]
    series_terms = jnp.einsum('bqe,iqe->qib', tile_weight_values.reshape(64, surface_tiles, TILE_POINTS), design_sensitivity.reshape(3, surface_tiles, TILE_POINTS), precision=lax.Precision.HIGHEST).reshape(surface_tiles, 192)
    boxed = jax.ops.segment_sum(series_terms, tile_box, num_segments=BOXES)
    return solution, boxed
```

```python
import functools

import jax
import jax.numpy as jnp
from jax import lax
from jax.experimental import pallas as pl
from jax.experimental.pallas import tpu as pltpu
from jax.sharding import PartitionSpec as P

F32 = jnp.float32
BF16 = jnp.bfloat16
PAD = 16
NOWHERE = -4096.0
LANES = 128
CHUNK = 256
PARAMS = pltpu.CompilerParams(vmem_limit_bytes=24 * 1024 * 1024)

VMEM = pl.BlockSpec(memory_space=pltpu.VMEM)
SMEM = pl.BlockSpec(memory_space=pltpu.SMEM)


def iota(shape, dim):
    return lax.broadcasted_iota(jnp.int32, shape, dim)


def float_iota(shape, dim):
    return iota(shape, dim).astype(F32)


def two_parts(value):
    high = value.astype(BF16).astype(F32)
    return high, value - high


def product(block, field):
    return [
        block(row) * field[0] + block(3 + row) * field[1] + block(6 + row) * field[2]
        for row in range(3)
    ]


def off_diagonal(block, field):
    return [
        sum(block(3 * i + row) * field[i] for i in range(3) if i != row) for row in range(3)
    ]


def masked_product(edge_ref, mask_ref, direction, field):
    mask = mask_ref[direction].astype(F32)
    return [mask * part for part in product(lambda k: edge_ref[direction, k], field)]


def rows_moved(field, edge_row, step):
    size = field.shape[0]
    at = iota(field.shape, 0)
    moved = pltpu.roll(field, step % size, 0)
    return jnp.where(at == (0 if step == 1 else size - 1), edge_row, moved)


def lanes_moved(field, edge_column, step):
    size = field.shape[1]
    at = iota(field.shape, 1)
    moved = pltpu.roll(field, step % size, 1)
    return jnp.where(at == (0 if step == 1 else size - 1), edge_column, moved)


def pack_kernel(
    count_ref, values_ref, owner_ref, node_ref,
    diag_low, diag_high, edge_low, edge_high, mask_low, mask_high,
    rows_ref, up_ref, down_ref, *, cells_x,
):
    targets = rows_ref.shape[0]
    groups = owner_ref.shape[0]
    order = iota((groups, LANES), 0) * LANES + iota((groups, LANES), 1)
    node = node_ref[...]
    row = owner_ref[...] * cells_x + lax.shift_right_logical(node, 7)
    row = jnp.where(order < count_ref[0], row.astype(F32), NOWHERE)
    column = (node & (LANES - 1)).astype(F32)
    for comp in range(3):
        for group in range(groups):
            piece = values_ref[comp : comp + 1, group * LANES : (group + 1) * LANES]
            for target in range(targets):
                rows_ref[target, comp * groups + group : comp * groups + group + 1, :] = piece
    for target in range(targets):
        rows_ref[target, 3 * groups : 4 * groups, :] = row - float(target * cells_x - PAD)
        rows_ref[target, 4 * groups : 5 * groups, :] = column

    def side(out_ref, diag, edge, mask, toward, near, far):
        for k in range(9):
            out_ref[k : k + 1, :] = diag[k, near : near + 1, :]
        for slot, (direction, at) in enumerate(
            ((toward, near), (2, near), (3, near), (toward, far))
        ):
            present = mask[direction, at : at + 1, :].astype(F32)
            for k in range(9):
                first = 9 + 9 * slot + k
                out_ref[first : first + 1, :] = edge[direction, k, at : at + 1, :] * present
        for k in range(3):
            out_ref[45 + k : 46 + k, :] = diag[4 * k, far : far + 1, :]

    side(up_ref, diag_high, edge_high, mask_high, 0, 7, 6)
    side(down_ref, diag_low, edge_low, mask_low, 1, 0, 1)


def halo_row(static_ref, near, far, entering):
    def entry(first):
        return lambda k: static_ref[first + k : first + k + 1, :]

    diag = entry(0)
    field, inverse, far_field = [], [], []
    for comp in range(3):
        scale = diag(4 * comp)
        there = scale > 0.0
        scale = jnp.where(there, scale, 1.0)
        field.append(near[comp] / scale)
        inverse.append(jnp.where(there, 1.0 / scale, 0.0))
        far_scale = entry(45)(comp)
        far_field.append(far[comp] / jnp.where(far_scale > 0.0, far_scale, 1.0))
    into = product(entry(9), field)
    up_y = product(entry(18), field)
    low_y = product(entry(27), field)
    from_far = product(entry(36), far_field)
    within = off_diagonal(diag, field)
    part = [
        (
            within[c]
            + from_far[c]
            + entering[c]
            + lanes_moved(up_y[c], 0.0, 1)
            + lanes_moved(low_y[c], 0.0, -1)
        )
        * inverse[c]
        for c in range(3)
    ]
    return field, into, part, inverse, up_y, low_y


def field_kernel(
    rows_ref, before_ref, after_ref, diag_ref, edge_ref, mask_ref,
    field_ref, part_ref, halo_ref, up_ref, down_ref, load_ref,
):
    senders = rows_ref.shape[0]
    groups = rows_ref.shape[1] // 5
    cells_x = field_ref.shape[1]
    half = (cells_x + 2 * PAD) // 2
    own = cells_x // 2

    load_ref[...] = jnp.zeros_like(load_ref)

    def add_rows(sender, carry):
        row = rows_ref[sender, 3 * groups : 4 * groups, :]
        column = rows_ref[sender, 4 * groups : 5 * groups, :]
        lower = row >= float(half)
        place = jnp.where(lower, row - float(half), row)
        column = jnp.where(lower, column + float(LANES), column)
        at_row = float_iota((half, LANES), 0)
        at_column = float_iota((2 * LANES, LANES), 0)
        parts = [
            two_parts(rows_ref[sender, c * groups : (c + 1) * groups, :]) for c in range(3)
        ]
        lefts, rights = [], []
        for group in range(groups):
            line = slice(group, group + 1)
            here = at_row == place[line]
            lefts.append(
                jnp.concatenate(
                    [
                        jnp.where(here, parts[c][which][line], 0.0)
                        for which in range(2)
                        for c in range(3)
                    ],
                    axis=0,
                ).astype(BF16)
            )
            rights.append(jnp.where(at_column == column[line], 1.0, 0.0).astype(BF16))
        load_ref[...] += lax.dot_general(
            jnp.concatenate(lefts, axis=1),
            jnp.concatenate(rights, axis=1),
            (((1,), (1,)), ((), ())),
            preferred_element_type=F32,
        )
        return carry

    lax.fori_loop(0, senders, add_rows, 0)

    def load_rows(comp, first, last, second_half):
        lanes = slice(LANES, 2 * LANES) if second_half else slice(0, LANES)
        return (
            load_ref[comp * half + first : comp * half + last, lanes]
            + load_ref[(3 + comp) * half + first : (3 + comp) * half + last, lanes]
        )

    field = []
    for comp in range(3):
        load = jnp.concatenate(
            [load_rows(comp, PAD, half, False), load_rows(comp, 0, half - PAD, True)], axis=0
        )
        field.append(load / diag_ref[4 * comp])
        field_ref[comp] = field[comp]
    beyond = half - PAD
    near_before = [load_rows(c, PAD - 1, PAD, False) for c in range(3)]
    far_before = [load_rows(c, PAD - 2, PAD - 1, False) for c in range(3)]
    near_after = [load_rows(c, beyond, beyond + 1, True) for c in range(3)]
    far_after = [load_rows(c, beyond + 1, beyond + 2, True) for c in range(3)]

    up_x = masked_product(edge_ref, mask_ref, 0, field)
    low_x = masked_product(edge_ref, mask_ref, 1, field)
    before = halo_row(before_ref, near_before, far_before, [p[:1] for p in low_x])
    after = halo_row(after_ref, near_after, far_after, [p[-1:] for p in up_x])
    total = off_diagonal(lambda k: diag_ref[k], field)
    total = [total[c] + rows_moved(up_x[c], before[1][c], 1) for c in range(3)]
    total = [total[c] + rows_moved(low_x[c], after[1][c], -1) for c in range(3)]
    up_y = masked_product(edge_ref, mask_ref, 2, field)
    low_y = masked_product(edge_ref, mask_ref, 3, field)
    total = [
        total[c] + lanes_moved(up_y[c], 0.0, 1) + lanes_moved(low_y[c], 0.0, -1)
        for c in range(3)
    ]
    inverse = [1.0 / diag_ref[4 * c] for c in range(3)]
    part = [total[c] * inverse[c] for c in range(3)]
    for comp in range(3):
        part_ref[comp] = part[comp]
    for side, group in enumerate((before, after)):
        for slot, which in enumerate((0, 2, 3)):
            for comp in range(3):
                at = 9 * side + 3 * slot + comp
                halo_ref[at : at + 1, :] = group[which][comp]

    def columns(out_ref, lane, along_y, halo_slot):
        ahead = cells_x
        packed = jnp.zeros((cells_x, LANES), F32)
        extra = jnp.zeros((8, LANES), F32)
        at = iota((cells_x, LANES), 1)
        at_extra = iota((8, LANES), 1)
        which_row = iota((8, LANES), 0)
        for slot, fields in enumerate((field, along_y, part, inverse)):
            for comp in range(3):
                column = fields[comp][:, lane : lane + 1]
                packed = jnp.where(at == 3 * slot + comp, column, packed)
        for comp in range(3):
            first = before[halo_slot][comp][:, lane : lane + 1]
            second = after[halo_slot][comp][:, lane : lane + 1]
            both = jnp.where(which_row == 0, first, second)
            extra = jnp.where((at_extra == 3 + comp) & (which_row < 2), both, extra)
        rest = jnp.zeros((LANES - ahead - 8, LANES), F32)
        whole = jnp.concatenate([packed, extra, rest], axis=0)
        out_ref[...] = whole.T[: out_ref.shape[0]]

    columns(up_ref, LANES - 1, up_y, 4)
    columns(down_ref, 0, low_y, 5)


def bernstein(coord):
    other = 1.0 - coord
    return [
        other * other * other,
        3.0 * coord * other * other,
        3.0 * coord * coord * other,
        coord * coord * coord,
    ]


def weight_table(u, v, w):
    first, second, third = bernstein(u), bernstein(v), bernstein(w)
    line = iota((8, u.shape[1]), 0)
    inner = line & 3
    along = jnp.where(
        inner == 0,
        third[0],
        jnp.where(inner == 1, third[1], jnp.where(inner == 2, third[2], third[3])),
    )
    pair = jnp.concatenate(
        [
            jnp.where(line < 4, second[0], second[1]) * along,
            jnp.where(line < 4, second[2], second[3]) * along,
        ],
        axis=0,
    )
    return jnp.concatenate([pair * first[i] for i in range(4)], axis=0)


def sums_kernel(
    tile_ref, from_low_ref, from_high_ref, field_ref, part_ref, halo_ref,
    diag_ref, edge_ref, mask_ref, node_ref, param_ref,
    quotient_ref, out_ref, boxes_ref, *, tile_points,
):
    cells_x = field_ref.shape[1]
    own = cells_x // 2
    targets = out_ref.shape[0]
    padded_boxes = boxes_ref.shape[1]

    def arrived(ref):
        rest = jnp.zeros((LANES - ref.shape[0], LANES), F32)
        return jnp.concatenate([ref[...], rest], axis=0).T

    low, high = arrived(from_low_ref), arrived(from_high_ref)
    lane = iota((cells_x, LANES), 1)

    def column(source, slot, comp):
        return source[:cells_x, 3 * slot + comp : 3 * slot + comp + 1]

    field = [field_ref[c] for c in range(3)]
    scale = [diag_ref[4 * c] for c in range(3)]
    toward_high = masked_product(edge_ref, mask_ref, 2, field)
    toward_low = masked_product(edge_ref, mask_ref, 3, field)
    quotient, low_edge, high_edge = [], [], []
    for c in range(3):
        entering = jnp.where(
            lane == 0,
            column(low, 1, c),
            jnp.where(lane == LANES - 1, column(high, 1, c), 0.0),
        )
        quotient.append(part_ref[c] + entering / scale[c])
        low_edge.append(column(low, 2, c) + column(low, 3, c) * toward_low[c][:, :1])
        high_edge.append(column(high, 2, c) + column(high, 3, c) * toward_high[c][:, -1:])
    for c in range(3):
        quotient_ref[c] = quotient[c]
    lane_row = iota((1, LANES), 1)
    beyond = []
    for side in range(2):
        fields, quotients = [], []
        for c in range(3):
            at = 9 * side + c
            line = cells_x + side
            entering = jnp.where(
                lane_row == 0,
                low[line : line + 1, 3 + c : 4 + c],
                jnp.where(
                    lane_row == LANES - 1, high[line : line + 1, 3 + c : 4 + c], 0.0
                ),
            )
            fields.append(halo_ref[at : at + 1, :])
            quotients.append(
                halo_ref[at + 3 : at + 4, :] + entering * halo_ref[at + 6 : at + 7, :]
            )
        beyond.append((fields, quotients))

    first_sum = sum(field[c] * scale[c] * field[c] for c in range(3))
    second_sum = sum(field[c] * scale[c] * quotient[c] for c in range(3))
    third_sum = sum(quotient[c] * scale[c] * quotient[c] for c in range(3))
    within = off_diagonal(lambda k: diag_ref[k], quotient)
    fourth_sum = sum(within[c] * field[c] for c in range(3))
    fifth_sum = sum(within[c] * quotient[c] for c in range(3))
    for direction in range(4):
        moving = masked_product(edge_ref, mask_ref, direction, quotient)
        for c in range(3):
            if direction == 0:
                a = rows_moved(field[c], beyond[1][0][c], -1)
                b = rows_moved(quotient[c], beyond[1][1][c], -1)
            elif direction == 1:
                a = rows_moved(field[c], beyond[0][0][c], 1)
                b = rows_moved(quotient[c], beyond[0][1][c], 1)
            elif direction == 2:
                a = lanes_moved(field[c], column(high, 0, c), -1)
                b = lanes_moved(quotient[c], high_edge[c], -1)
            else:
                a = lanes_moved(field[c], column(low, 0, c), 1)
                b = lanes_moved(quotient[c], low_edge[c], 1)
            fourth_sum = fourth_sum + moving[c] * a
            fifth_sum = fifth_sum + moving[c] * b
    sums = jnp.zeros((1, LANES), F32)
    for k, value in enumerate((first_sum, second_sum, third_sum, fourth_sum, fifth_sum)):
        sums = jnp.where(lane_row == k, jnp.sum(value), sums)

    order = [field[0], field[1], quotient[0], quotient[1], field[2], quotient[2]]
    folded = [two_parts(jnp.concatenate([f[:own], f[own:]], axis=1)) for f in order]
    table = jnp.concatenate(
        [folded[f][which] for which in range(2) for f in range(6)], axis=0
    ).astype(BF16)
    points = param_ref.shape[1]
    boxes_ref[...] = jnp.zeros_like(boxes_ref)
    pieces = CHUNK // LANES
    for chunk in range(points // CHUNK):
        node = jnp.concatenate(
            [node_ref[chunk * pieces + k : chunk * pieces + k + 1, :] for k in range(pieces)],
            axis=1,
        )
        row = lax.shift_right_logical(node, 7)
        place = (node & (LANES - 1)) + jnp.where(row >= own, LANES, 0)
        row = jnp.where(row >= own, row - own, row)
        pick = jnp.where(iota((2 * LANES, CHUNK), 0) == place, 1.0, 0.0).astype(BF16)
        read = jnp.dot(table, pick, preferred_element_type=F32)
        read = read[: 6 * own] + read[6 * own :]
        here = iota((own, CHUNK), 0) == row
        lanes = slice(chunk * CHUNK, (chunk + 1) * CHUNK)
        weights = weight_table(
            param_ref[0:1, lanes], param_ref[1:2, lanes], param_ref[2:3, lanes]
        )
        highs, lows = [], []
        for f in range(6):
            values = jnp.where(here, read[f * own : (f + 1) * own], 0.0)
            values = jnp.sum(values, axis=0, keepdims=True)
            one, two = two_parts(weights * values)
            highs.append(one)
            lows.append(two)
        left = jnp.concatenate(
            [jnp.concatenate(highs, axis=0), jnp.concatenate(lows, axis=0)], axis=1
        ).astype(BF16)
        tiles = [
            jnp.where(
                iota((padded_boxes, tile_points), 0)
                == tile_ref[chunk * (CHUNK // tile_points) + k],
                1.0,
                0.0,
            ).astype(BF16)
            for k in range(CHUNK // tile_points)
        ]
        boxes_ref[...] += lax.dot_general(
            left,
            jnp.concatenate(tiles + tiles, axis=1),
            (((1,), (1,)), ((), ())),
            preferred_element_type=F32,
        )
    for pair in range(3):
        for block in range(padded_boxes // LANES):
            turned = boxes_ref[
                pair * LANES : (pair + 1) * LANES, block * LANES : (block + 1) * LANES
            ].T
            for box in range(min(LANES, targets - block * LANES)):
                out_ref[block * LANES + box, pair : pair + 1, :] = turned[box : box + 1]
    for box in range(targets):
        out_ref[box, 3:4, :] = sums


def result_kernel(got_ref, field_ref, quotient_ref, solution_ref, gradient_ref):
    total = jnp.sum(got_ref[...], axis=0)
    rho, a, b, t, u = [total[3:4, k : k + 1] for k in range(5)]
    ratio = a / rho
    norm = rho + a
    step = rho / norm
    rest = jnp.maximum(b - a * ratio, 0.0)
    beta = step * step * rest / rho
    rest_image = (b + u) - ratio * (a + b + a + t) + ratio * ratio * norm
    cross = (a + t) - ratio * norm
    curve = step * step * rest_image - step * beta * (rest + cross) + beta * beta * norm
    second = jnp.where(
        curve > 0.0, step * step * rest / jnp.where(curve > 0.0, curve, 1.0), 0.0
    )
    of_field = step + second * (beta + step * ratio)
    of_quotient = -(step * second)
    for c in range(3):
        solution_ref[c] = of_field * field_ref[c] + of_quotient * quotient_ref[c]
    gradient_ref[:, :LANES] = of_field * total[0:1] + of_quotient * total[1:2]
    gradient_ref[:, LANES:] = (
        of_field * total[2:3, : LANES // 2] + of_quotient * total[2:3, LANES // 2 :]
    )


def per_device(
    diag_blocks, edge_blocks, edge_mask, src_values, src_owner, src_node, src_count,
    surf_node, surf_param, tile_box,
):
    cells_x, cells_y = diag_blocks.shape[1:]
    width_gx, width_gy = lax.axis_size("gx"), lax.axis_size("gy")
    devices = width_gx * width_gy
    groups = src_node.shape[0] // LANES
    whole = functools.partial(jax.ShapeDtypeStruct, dtype=F32)

    def window(shape, at):
        return pl.BlockSpec(shape, lambda i: at)

    last = cells_x // 8 - 1
    rows, static_up, static_down = pl.pallas_call(
        functools.partial(pack_kernel, cells_x=cells_x),
        grid=(1,),
        in_specs=[
            SMEM,
            window(src_values.shape, (0, 0)),
            window((groups, LANES), (0, 0)),
            window((groups, LANES), (0, 0)),
            window((9, 8, cells_y), (0, 0, 0)),
            window((9, 8, cells_y), (0, last, 0)),
            window((4, 9, 8, cells_y), (0, 0, 0, 0)),
            window((4, 9, 8, cells_y), (0, 0, last, 0)),
            window((4, 8, cells_y), (0, 0, 0)),
            window((4, 8, cells_y), (0, last, 0)),
        ],
        out_specs=[
            window((width_gx, 5 * groups, LANES), (0, 0, 0)),
            window((48, cells_y), (0, 0)),
            window((48, cells_y), (0, 0)),
        ],
        out_shape=[
            whole((width_gx, 5 * groups, LANES)),
            whole((48, cells_y)),
            whole((48, cells_y)),
        ],
        compiler_params=PARAMS,
        name="pack_rows_and_edges",
    )(
        src_count, src_values,
        src_owner.reshape(groups, LANES), src_node.reshape(groups, LANES),
        diag_blocks, diag_blocks, edge_blocks, edge_blocks, edge_mask, edge_mask,
    )

    forward_x = [(i, i + 1) for i in range(width_gx - 1)]
    backward_x = [(i + 1, i) for i in range(width_gx - 1)]
    forward_y = [(i, i + 1) for i in range(width_gy - 1)]
    backward_y = [(i + 1, i) for i in range(width_gy - 1)]
    before = lax.ppermute(static_up, "gx", forward_x)
    after = lax.ppermute(static_down, "gx", backward_x)
    rows = lax.all_to_all(rows, "gx", split_axis=0, concat_axis=0, tiled=True)

    nodes = (3, cells_x, cells_y)
    frame = cells_x + 2 * PAD
    field, part, halo, up, down = pl.pallas_call(
        field_kernel,
        in_specs=[VMEM] * 6,
        out_specs=[VMEM] * 5,
        out_shape=[
            whole(nodes), whole(nodes), whole((24, cells_y)), whole((16, LANES)),
            whole((16, LANES)),
        ],
        scratch_shapes=[pltpu.VMEM((3 * frame, 2 * LANES), F32)],
        compiler_params=PARAMS,
        name="load_and_first_product",
    )(rows, before, after, diag_blocks, edge_blocks, edge_mask)

    from_low = lax.ppermute(up, "gy", forward_y)
    from_high = lax.ppermute(down, "gy", backward_y)

    points = surf_node.shape[0]
    padded = -(-devices // LANES) * LANES
    quotient, partial = pl.pallas_call(
        functools.partial(sums_kernel, tile_points=points // tile_box.shape[0]),
        in_specs=[SMEM] + [VMEM] * 10,
        out_specs=[VMEM] * 2,
        out_shape=[whole(nodes), whole((devices, 4, LANES))],
        scratch_shapes=[pltpu.VMEM((6 * 64, padded), F32)],
        compiler_params=PARAMS,
        name="sums_and_box_parts",
    )(
        tile_box, from_low, from_high, field, part, halo, diag_blocks, edge_blocks,
        edge_mask, surf_node.reshape(points // LANES, LANES), surf_param,
    )
    got = lax.all_to_all(partial, ("gx", "gy"), split_axis=0, concat_axis=0, tiled=True)
    return pl.pallas_call(
        result_kernel,
        in_specs=[VMEM] * 3,
        out_specs=[VMEM] * 2,
        out_shape=[whole(nodes), whole((1, 192))],
        compiler_params=PARAMS,
        name="steps_and_outputs",
    )(got, field, quotient)


def solution(mesh):
    return jax.shard_map(
        per_device,
        mesh=mesh,
        in_specs=(
            P(None, "gx", "gy"),
            P(None, None, "gx", "gy"),
            P(None, "gx", "gy"),
            P(None, ("gx", "gy")),
            P(("gx", "gy"), None),
            P(("gx", "gy")),
            P(("gx", "gy")),
            P(("gx", "gy")),
            P(None, ("gx", "gy")),
            P(("gx", "gy")),
        ),
        out_specs=(P(None, "gx", "gy"), P(("gx", "gy"), None)),
        check_vma=False,
    )
```

```python
import functools

import jax
import jax.numpy as jnp
from jax import lax
from jax.experimental import pallas as pl
from jax.experimental.pallas import tpu as pltpu
from jax.sharding import PartitionSpec as P

F32 = jnp.float32
BF16 = jnp.bfloat16
PAD = 16
NOWHERE = -4096.0
LANES = 128
STATIC = 48
CHUNK = 256
PACK_VMEM = 60 * 1000 * 1000
PARAMS = pltpu.CompilerParams(vmem_limit_bytes=24 * 1024 * 1024)

VMEM = pl.BlockSpec(memory_space=pltpu.VMEM)
SMEM = pl.BlockSpec(memory_space=pltpu.SMEM)
HBM = pl.BlockSpec(memory_space=pltpu.HBM)


def iota(shape, dim):
    return lax.broadcasted_iota(jnp.int32, shape, dim)


def float_iota(shape, dim):
    return iota(shape, dim).astype(F32)


def two_parts(value):
    high = value.astype(BF16).astype(F32)
    return high, value - high


def product(block, field):
    return [
        block(row) * field[0] + block(3 + row) * field[1] + block(6 + row) * field[2]
        for row in range(3)
    ]


def off_diagonal(block, field):
    return [
        sum(block(3 * i + row) * field[i] for i in range(3) if i != row) for row in range(3)
    ]


def masked_product(edge_ref, mask_ref, direction, field):
    mask = mask_ref[direction].astype(F32)
    return [mask * part for part in product(lambda k: edge_ref[direction, k], field)]


def rows_moved(field, edge_row, step):
    size = field.shape[0]
    at = iota(field.shape, 0)
    moved = pltpu.roll(field, step % size, 0)
    return jnp.where(at == (0 if step == 1 else size - 1), edge_row, moved)


def lanes_moved(field, edge_column, step):
    size = field.shape[1]
    at = iota(field.shape, 1)
    moved = pltpu.roll(field, step % size, 1)
    return jnp.where(at == (0 if step == 1 else size - 1), edge_column, moved)


def pack_kernel(
    count_in, values_in, owner_in, node_in, diag_in, edge_in, mask_in, rows_ref,
    count_ref, values_ref, owner_ref, node_ref, diag_low, diag_high, edge_low, edge_high,
    mask_low, mask_high, arrived,
):
    targets = rows_ref.shape[0]
    groups = owner_ref.shape[0]
    cells_x = diag_in.shape[1]
    top = pl.ds(cells_x - 8, 8)
    copies = [
        pltpu.make_async_copy(source, target, arrived.at[k])
        for k, (source, target) in enumerate(
            (
                (edge_in.at[:, :, 0:8], edge_low),
                (edge_in.at[:, :, top], edge_high),
                (diag_in.at[:, 0:8], diag_low),
                (diag_in.at[:, top], diag_high),
                (mask_in.at[:, 0:8], mask_low),
                (mask_in.at[:, top], mask_high),
                (values_in, values_ref),
                (owner_in, owner_ref),
                (node_in, node_ref),
                (count_in, count_ref),
            )
        )
    ]
    for copy in copies:
        copy.start()
    statics = 5 * groups
    for target in range(targets):
        rows_ref[target, statics:, :] = jnp.zeros((STATIC, LANES), F32)
    for copy in copies:
        copy.wait()
    order = iota((groups, LANES), 0) * LANES + iota((groups, LANES), 1)
    node = node_ref[...]
    row = owner_ref[...] * cells_x + lax.shift_right_logical(node, 7)
    row = jnp.where(order < count_ref[0], row.astype(F32), NOWHERE)
    column = (node & (LANES - 1)).astype(F32)
    for comp in range(3):
        for group in range(groups):
            piece = values_ref[comp : comp + 1, group * LANES : (group + 1) * LANES]
            for target in range(targets):
                rows_ref[target, comp * groups + group : comp * groups + group + 1, :] = piece
    for target in range(targets):
        rows_ref[target, 3 * groups : 4 * groups, :] = row - float(target * cells_x - PAD)
        rows_ref[target, 4 * groups : 5 * groups, :] = column

    def side(target, diag, edge, mask, toward, near, far):
        def put(slot, value):
            rows_ref[target, statics + slot : statics + slot + 1, :] = value

        for k in range(9):
            put(k, diag[k, near : near + 1, :])
        for slot, (direction, at) in enumerate(
            ((toward, near), (2, near), (3, near), (toward, far))
        ):
            present = mask[direction, at : at + 1, :].astype(F32)
            for k in range(9):
                put(9 + 9 * slot + k, edge[direction, k, at : at + 1, :] * present)
        for k in range(3):
            put(45 + k, diag[4 * k, far : far + 1, :])

    here = lax.axis_index("gx")

    @pl.when(here < targets - 1)
    def _():
        side(here + 1, diag_high, edge_high, mask_high, 0, 7, 6)

    @pl.when(here > 0)
    def _():
        side(here - 1, diag_low, edge_low, mask_low, 1, 0, 1)


def halo_row(rows_ref, sender, near, far, entering):
    base = rows_ref.shape[1] - STATIC

    def entry(first):
        return lambda k: rows_ref[sender, base + first + k : base + first + k + 1, :]

    diag = entry(0)
    field, inverse, far_field = [], [], []
    for comp in range(3):
        scale = diag(4 * comp)
        there = scale > 0.0
        scale = jnp.where(there, scale, 1.0)
        field.append(near[comp] / scale)
        inverse.append(jnp.where(there, 1.0 / scale, 0.0))
        far_scale = entry(45)(comp)
        far_field.append(far[comp] / jnp.where(far_scale > 0.0, far_scale, 1.0))
    into = product(entry(9), field)
    up_y = product(entry(18), field)
    low_y = product(entry(27), field)
    from_far = product(entry(36), far_field)
    within = off_diagonal(diag, field)
    part = [
        (
            within[c]
            + from_far[c]
            + entering[c]
            + lanes_moved(up_y[c], 0.0, 1)
            + lanes_moved(low_y[c], 0.0, -1)
        )
        * inverse[c]
        for c in range(3)
    ]
    return field, into, part, inverse, up_y, low_y


def field_kernel(
    rows_ref, diag_ref, edge_ref, mask_ref,
    field_ref, part_ref, halo_ref, edges_ref, load_ref,
):
    senders = rows_ref.shape[0]
    groups = (rows_ref.shape[1] - STATIC) // 5
    cells_x = field_ref.shape[1]
    half = (cells_x + 2 * PAD) // 2
    own = cells_x // 2

    load_ref[...] = jnp.zeros_like(load_ref)

    def add_rows(sender, carry):
        row = rows_ref[sender, 3 * groups : 4 * groups, :]
        column = rows_ref[sender, 4 * groups : 5 * groups, :]
        lower = row >= float(half)
        place = jnp.where(lower, row - float(half), row)
        column = jnp.where(lower, column + float(LANES), column)
        at_row = float_iota((half, LANES), 0)
        at_column = float_iota((2 * LANES, LANES), 0)
        parts = [
            two_parts(rows_ref[sender, c * groups : (c + 1) * groups, :]) for c in range(3)
        ]
        lefts, rights = [], []
        for group in range(groups):
            line = slice(group, group + 1)
            here = at_row == place[line]
            lefts.append(
                jnp.concatenate(
                    [
                        jnp.where(here, parts[c][which][line], 0.0)
                        for which in range(2)
                        for c in range(3)
                    ],
                    axis=0,
                ).astype(BF16)
            )
            rights.append(jnp.where(at_column == column[line], 1.0, 0.0).astype(BF16))
        load_ref[...] += lax.dot_general(
            jnp.concatenate(lefts, axis=1),
            jnp.concatenate(rights, axis=1),
            (((1,), (1,)), ((), ())),
            preferred_element_type=F32,
        )
        return carry

    lax.fori_loop(0, senders, add_rows, 0, unroll=2)

    def load_rows(comp, first, last, second_half):
        lanes = slice(LANES, 2 * LANES) if second_half else slice(0, LANES)
        return (
            load_ref[comp * half + first : comp * half + last, lanes]
            + load_ref[(3 + comp) * half + first : (3 + comp) * half + last, lanes]
        )

    field = []
    for comp in range(3):
        load = jnp.concatenate(
            [load_rows(comp, PAD, half, False), load_rows(comp, 0, half - PAD, True)], axis=0
        )
        field.append(load / diag_ref[4 * comp])
        field_ref[comp] = field[comp]
    beyond = half - PAD
    near_before = [load_rows(c, PAD - 1, PAD, False) for c in range(3)]
    far_before = [load_rows(c, PAD - 2, PAD - 1, False) for c in range(3)]
    near_after = [load_rows(c, beyond, beyond + 1, True) for c in range(3)]
    far_after = [load_rows(c, beyond + 1, beyond + 2, True) for c in range(3)]

    up_x = masked_product(edge_ref, mask_ref, 0, field)
    low_x = masked_product(edge_ref, mask_ref, 1, field)
    here = lax.axis_index("gx")
    lower, upper = jnp.maximum(here - 1, 0), jnp.minimum(here + 1, senders - 1)
    before = halo_row(rows_ref, lower, near_before, far_before, [p[:1] for p in low_x])
    after = halo_row(rows_ref, upper, near_after, far_after, [p[-1:] for p in up_x])
    total = off_diagonal(lambda k: diag_ref[k], field)
    total = [total[c] + rows_moved(up_x[c], before[1][c], 1) for c in range(3)]
    total = [total[c] + rows_moved(low_x[c], after[1][c], -1) for c in range(3)]
    up_y = masked_product(edge_ref, mask_ref, 2, field)
    low_y = masked_product(edge_ref, mask_ref, 3, field)
    total = [
        total[c] + lanes_moved(up_y[c], 0.0, 1) + lanes_moved(low_y[c], 0.0, -1)
        for c in range(3)
    ]
    inverse = [1.0 / diag_ref[4 * c] for c in range(3)]
    part = [total[c] * inverse[c] for c in range(3)]
    for comp in range(3):
        part_ref[comp] = part[comp]
    for side, group in enumerate((before, after)):
        for slot, which in enumerate((0, 2, 3)):
            for comp in range(3):
                at = 9 * side + 3 * slot + comp
                halo_ref[at : at + 1, :] = group[which][comp]

    def columns(target, lane, along_y, halo_slot):
        ahead = cells_x
        packed = jnp.zeros((cells_x, LANES), F32)
        extra = jnp.zeros((8, LANES), F32)
        at = iota((cells_x, LANES), 1)
        at_extra = iota((8, LANES), 1)
        which_row = iota((8, LANES), 0)
        for slot, fields in enumerate((field, along_y, part, inverse)):
            for comp in range(3):
                column = fields[comp][:, lane : lane + 1]
                packed = jnp.where(at == 3 * slot + comp, column, packed)
        for comp in range(3):
            first = before[halo_slot][comp][:, lane : lane + 1]
            second = after[halo_slot][comp][:, lane : lane + 1]
            both = jnp.where(which_row == 0, first, second)
            extra = jnp.where((at_extra == 3 + comp) & (which_row < 2), both, extra)
        rest = jnp.zeros((LANES - ahead - 8, LANES), F32)
        whole = jnp.concatenate([packed, extra, rest], axis=0)
        edges_ref[target] = whole.T[:16]

    edges_ref[...] = jnp.zeros_like(edges_ref)
    across = lax.axis_index("gy")

    @pl.when(across < edges_ref.shape[0] - 1)
    def _():
        columns(across + 1, LANES - 1, up_y, 4)

    @pl.when(across > 0)
    def _():
        columns(across - 1, 0, low_y, 5)


def bernstein(coord):
    other = 1.0 - coord
    return [
        other * other * other,
        3.0 * coord * other * other,
        3.0 * coord * coord * other,
        coord * coord * coord,
    ]


def weight_table(u, v, w):
    first, second, third = bernstein(u), bernstein(v), bernstein(w)
    line = iota((8, u.shape[1]), 0)
    inner = line & 3
    along = jnp.where(
        inner == 0,
        third[0],
        jnp.where(inner == 1, third[1], jnp.where(inner == 2, third[2], third[3])),
    )
    pair = jnp.concatenate(
        [
            jnp.where(line < 4, second[0], second[1]) * along,
            jnp.where(line < 4, second[2], second[3]) * along,
        ],
        axis=0,
    )
    return jnp.concatenate([pair * first[i] for i in range(4)], axis=0)


def sums_kernel(
    tile_ref, edges_ref, field_ref, part_ref, halo_ref,
    diag_ref, edge_ref, mask_ref, node_ref, param_ref,
    quotient_ref, out_ref, boxes_ref, *, tile_points,
):
    cells_x = field_ref.shape[1]
    own = cells_x // 2
    targets = out_ref.shape[0]
    padded_boxes = boxes_ref.shape[1]

    def arrived(sender):
        rest = jnp.zeros((LANES - 16, LANES), F32)
        return jnp.concatenate([edges_ref[sender], rest], axis=0).T

    across = lax.axis_index("gy")
    low = arrived(jnp.maximum(across - 1, 0))
    high = arrived(jnp.minimum(across + 1, edges_ref.shape[0] - 1))
    lane = iota((cells_x, LANES), 1)

    def column(source, slot, comp):
        return source[:cells_x, 3 * slot + comp : 3 * slot + comp + 1]

    field = [field_ref[c] for c in range(3)]
    scale = [diag_ref[4 * c] for c in range(3)]
    toward_high = masked_product(edge_ref, mask_ref, 2, field)
    toward_low = masked_product(edge_ref, mask_ref, 3, field)
    quotient, low_edge, high_edge = [], [], []
    for c in range(3):
        entering = jnp.where(
            lane == 0,
            column(low, 1, c),
            jnp.where(lane == LANES - 1, column(high, 1, c), 0.0),
        )
        quotient.append(part_ref[c] + entering / scale[c])
        low_edge.append(column(low, 2, c) + column(low, 3, c) * toward_low[c][:, :1])
        high_edge.append(column(high, 2, c) + column(high, 3, c) * toward_high[c][:, -1:])
    for c in range(3):
        quotient_ref[c] = quotient[c]
    lane_row = iota((1, LANES), 1)
    beyond = []
    for side in range(2):
        fields, quotients = [], []
        for c in range(3):
            at = 9 * side + c
            line = cells_x + side
            entering = jnp.where(
                lane_row == 0,
                low[line : line + 1, 3 + c : 4 + c],
                jnp.where(
                    lane_row == LANES - 1, high[line : line + 1, 3 + c : 4 + c], 0.0
                ),
            )
            fields.append(halo_ref[at : at + 1, :])
            quotients.append(
                halo_ref[at + 3 : at + 4, :] + entering * halo_ref[at + 6 : at + 7, :]
            )
        beyond.append((fields, quotients))

    first_sum = sum(field[c] * scale[c] * field[c] for c in range(3))
    second_sum = sum(field[c] * scale[c] * quotient[c] for c in range(3))
    third_sum = sum(quotient[c] * scale[c] * quotient[c] for c in range(3))
    within = off_diagonal(lambda k: diag_ref[k], quotient)
    fourth_sum = sum(within[c] * field[c] for c in range(3))
    fifth_sum = sum(within[c] * quotient[c] for c in range(3))
    for direction in range(4):
        moving = masked_product(edge_ref, mask_ref, direction, quotient)
        for c in range(3):
            if direction == 0:
                a = rows_moved(field[c], beyond[1][0][c], -1)
                b = rows_moved(quotient[c], beyond[1][1][c], -1)
            elif direction == 1:
                a = rows_moved(field[c], beyond[0][0][c], 1)
                b = rows_moved(quotient[c], beyond[0][1][c], 1)
            elif direction == 2:
                a = lanes_moved(field[c], column(high, 0, c), -1)
                b = lanes_moved(quotient[c], high_edge[c], -1)
            else:
                a = lanes_moved(field[c], column(low, 0, c), 1)
                b = lanes_moved(quotient[c], low_edge[c], 1)
            fourth_sum = fourth_sum + moving[c] * a
            fifth_sum = fifth_sum + moving[c] * b
    sums = jnp.zeros((1, LANES), F32)
    for k, value in enumerate((first_sum, second_sum, third_sum, fourth_sum, fifth_sum)):
        sums = jnp.where(lane_row == k, jnp.sum(value), sums)

    order = [field[0], field[1], quotient[0], quotient[1], field[2], quotient[2]]
    folded = [two_parts(jnp.concatenate([f[:own], f[own:]], axis=1)) for f in order]
    table = jnp.concatenate(
        [folded[f][which] for which in range(2) for f in range(6)], axis=0
    ).astype(BF16)
    points = param_ref.shape[1]
    boxes_ref[...] = jnp.zeros_like(boxes_ref)
    pieces = CHUNK // LANES
    for chunk in range(points // CHUNK):
        node = jnp.concatenate(
            [node_ref[chunk * pieces + k : chunk * pieces + k + 1, :] for k in range(pieces)],
            axis=1,
        )
        row = lax.shift_right_logical(node, 7)
        place = (node & (LANES - 1)) + jnp.where(row >= own, LANES, 0)
        row = jnp.where(row >= own, row - own, row)
        pick = jnp.where(iota((2 * LANES, CHUNK), 0) == place, 1.0, 0.0).astype(BF16)
        read = jnp.dot(table, pick, preferred_element_type=F32)
        read = read[: 6 * own] + read[6 * own :]
        here = iota((own, CHUNK), 0) == row
        lanes = slice(chunk * CHUNK, (chunk + 1) * CHUNK)
        weights = weight_table(
            param_ref[0:1, lanes], param_ref[1:2, lanes], param_ref[2:3, lanes]
        )
        highs, lows = [], []
        for f in range(6):
            values = jnp.where(here, read[f * own : (f + 1) * own], 0.0)
            values = jnp.sum(values, axis=0, keepdims=True)
            one, two = two_parts(weights * values)
            highs.append(one)
            lows.append(two)
        left = jnp.concatenate(
            [jnp.concatenate(highs, axis=0), jnp.concatenate(lows, axis=0)], axis=1
        ).astype(BF16)
        tiles = [
            jnp.where(
                iota((padded_boxes, tile_points), 0)
                == tile_ref[chunk * (CHUNK // tile_points) + k],
                1.0,
                0.0,
            ).astype(BF16)
            for k in range(CHUNK // tile_points)
        ]
        boxes_ref[...] += lax.dot_general(
            left,
            jnp.concatenate(tiles + tiles, axis=1),
            (((1,), (1,)), ((), ())),
            preferred_element_type=F32,
        )
    for pair in range(3):
        for block in range(padded_boxes // LANES):
            turned = boxes_ref[
                pair * LANES : (pair + 1) * LANES, block * LANES : (block + 1) * LANES
            ].T
            for box in range(min(LANES, targets - block * LANES)):
                out_ref[block * LANES + box, pair : pair + 1, :] = turned[box : box + 1]
    for box in range(targets):
        out_ref[box, 3:4, :] = sums


def result_kernel(got_ref, field_ref, quotient_ref, solution_ref, gradient_ref):
    total = jnp.sum(got_ref[...], axis=0)
    rho, a, b, t, u = [total[3:4, k : k + 1] for k in range(5)]
    ratio = a / rho
    norm = rho + a
    step = rho / norm
    rest = jnp.maximum(b - a * ratio, 0.0)
    beta = step * step * rest / rho
    rest_image = (b + u) - ratio * (a + b + a + t) + ratio * ratio * norm
    cross = (a + t) - ratio * norm
    curve = step * step * rest_image - step * beta * (rest + cross) + beta * beta * norm
    second = jnp.where(
        curve > 0.0, step * step * rest / jnp.where(curve > 0.0, curve, 1.0), 0.0
    )
    of_field = step + second * (beta + step * ratio)
    of_quotient = -(step * second)
    for c in range(3):
        solution_ref[c] = of_field * field_ref[c] + of_quotient * quotient_ref[c]
    gradient_ref[:, :LANES] = of_field * total[0:1] + of_quotient * total[1:2]
    gradient_ref[:, LANES:] = (
        of_field * total[2:3, : LANES // 2] + of_quotient * total[2:3, LANES // 2 :]
    )


def per_device(
    diag_blocks, edge_blocks, edge_mask, src_values, src_owner, src_node, src_count,
    surf_node, surf_param, tile_box,
):
    cells_x, cells_y = diag_blocks.shape[1:]
    width_gx, width_gy = lax.axis_size("gx"), lax.axis_size("gy")
    devices = width_gx * width_gy
    groups = src_node.shape[0] // LANES
    whole = functools.partial(jax.ShapeDtypeStruct, dtype=F32)

    cells = 5 * groups + STATIC
    i32 = jnp.int32
    rows = pl.pallas_call(
        pack_kernel,
        in_specs=[HBM] * 7,
        out_specs=VMEM,
        out_shape=whole((width_gx, cells, LANES)),
        scratch_shapes=[
            pltpu.SMEM((1,), i32),
            pltpu.VMEM(src_values.shape, F32),
            pltpu.VMEM((groups, LANES), i32),
            pltpu.VMEM((groups, LANES), i32),
            pltpu.VMEM((9, 8, cells_y), F32),
            pltpu.VMEM((9, 8, cells_y), F32),
            pltpu.VMEM((4, 9, 8, cells_y), F32),
            pltpu.VMEM((4, 9, 8, cells_y), F32),
            pltpu.VMEM((4, 8, cells_y), i32),
            pltpu.VMEM((4, 8, cells_y), i32),
            pltpu.SemaphoreType.DMA((10,)),
        ],
        compiler_params=pltpu.CompilerParams(vmem_limit_bytes=PACK_VMEM),
        name="pack_rows_and_edges",
    )(
        src_count, src_values,
        src_owner.reshape(groups, LANES), src_node.reshape(groups, LANES),
        diag_blocks, edge_blocks, edge_mask,
    )
    rows = lax.all_to_all(rows, "gx", split_axis=0, concat_axis=0, tiled=True)

    nodes = (3, cells_x, cells_y)
    frame = cells_x + 2 * PAD
    field, part, halo, edges = pl.pallas_call(
        field_kernel,
        in_specs=[VMEM] * 4,
        out_specs=[VMEM] * 4,
        out_shape=[
            whole(nodes), whole(nodes), whole((24, cells_y)), whole((width_gy, 16, LANES)),
        ],
        scratch_shapes=[pltpu.VMEM((3 * frame, 2 * LANES), F32)],
        compiler_params=PARAMS,
        name="load_and_first_product",
    )(rows, diag_blocks, edge_blocks, edge_mask)
    edges = lax.all_to_all(edges, "gy", split_axis=0, concat_axis=0, tiled=True)

    points = surf_node.shape[0]
    padded = -(-devices // LANES) * LANES
    quotient, partial = pl.pallas_call(
        functools.partial(sums_kernel, tile_points=points // tile_box.shape[0]),
        in_specs=[SMEM] + [VMEM] * 9,
        out_specs=[VMEM] * 2,
        out_shape=[whole(nodes), whole((devices, 4, LANES))],
        scratch_shapes=[pltpu.VMEM((6 * 64, padded), F32)],
        compiler_params=PARAMS,
        name="sums_and_box_parts",
    )(
        tile_box, edges, field, part, halo, diag_blocks, edge_blocks, edge_mask,
        surf_node.reshape(points // LANES, LANES), surf_param,
    )
    got = lax.all_to_all(partial, ("gx", "gy"), split_axis=0, concat_axis=0, tiled=True)
    return pl.pallas_call(
        result_kernel,
        in_specs=[VMEM] * 3,
        out_specs=[VMEM] * 2,
        out_shape=[whole(nodes), whole((1, 192))],
        compiler_params=PARAMS,
        name="steps_and_outputs",
    )(got, field, quotient)


def solution(mesh):
    return jax.shard_map(
        per_device,
        mesh=mesh,
        in_specs=(
            P(None, "gx", "gy"),
            P(None, None, "gx", "gy"),
            P(None, "gx", "gy"),
            P(None, ("gx", "gy")),
            P(("gx", "gy"), None),
            P(("gx", "gy")),
            P(("gx", "gy")),
            P(("gx", "gy")),
            P(None, ("gx", "gy")),
            P(("gx", "gy")),
        ),
        out_specs=(P(None, "gx", "gy"), P(("gx", "gy"), None)),
        check_vma=False,
    )
```

```python
import functools

import jax
import jax.numpy as jnp
from jax import lax
from jax.experimental import pallas as pl
from jax.experimental.pallas import tpu as pltpu
from jax.sharding import PartitionSpec as P

F32 = jnp.float32
BF16 = jnp.bfloat16
PAD = 16
NOWHERE = -4096.0
LANES = 128
STATIC = 48
CHUNK = 256
PACK_VMEM = 60 * 1000 * 1000
PARAMS = pltpu.CompilerParams(vmem_limit_bytes=24 * 1024 * 1024)

VMEM = pl.BlockSpec(memory_space=pltpu.VMEM)
SMEM = pl.BlockSpec(memory_space=pltpu.SMEM)
HBM = pl.BlockSpec(memory_space=pltpu.HBM)


def iota(shape, dim):
    return lax.broadcasted_iota(jnp.int32, shape, dim)


def float_iota(shape, dim):
    return iota(shape, dim).astype(F32)


def two_parts(value):
    high = value.astype(BF16).astype(F32)
    return high, value - high


def product(block, field):
    return [
        block(row) * field[0] + block(3 + row) * field[1] + block(6 + row) * field[2]
        for row in range(3)
    ]


def off_diagonal(block, field):
    return [
        sum(block(3 * i + row) * field[i] for i in range(3) if i != row) for row in range(3)
    ]


def masked_product(edge_ref, mask_ref, direction, field):
    mask = mask_ref[direction].astype(F32)
    return [mask * part for part in product(lambda k: edge_ref[direction, k], field)]


def rows_moved(field, edge_row, step):
    size = field.shape[0]
    at = iota(field.shape, 0)
    moved = pltpu.roll(field, step % size, 0)
    return jnp.where(at == (0 if step == 1 else size - 1), edge_row, moved)


def lanes_moved(field, edge_column, step):
    size = field.shape[1]
    at = iota(field.shape, 1)
    moved = pltpu.roll(field, step % size, 1)
    return jnp.where(at == (0 if step == 1 else size - 1), edge_column, moved)


def pack_kernel(
    count_in, values_in, owner_in, node_in, diag_in, edge_in, mask_in, rows_ref,
    count_ref, values_ref, owner_ref, node_ref, diag_low, diag_high, edge_low, edge_high,
    mask_low, mask_high, arrived,
):
    groups = owner_ref.shape[0]
    cells_x = diag_in.shape[1]
    top = pl.ds(cells_x - 8, 8)
    copies = [
        pltpu.make_async_copy(source, target, arrived.at[k])
        for k, (source, target) in enumerate(
            (
                (edge_in.at[:, :, 0:8], edge_low),
                (edge_in.at[:, :, top], edge_high),
                (diag_in.at[:, 0:8], diag_low),
                (diag_in.at[:, top], diag_high),
                (mask_in.at[:, 0:8], mask_low),
                (mask_in.at[:, top], mask_high),
                (values_in, values_ref),
                (owner_in, owner_ref),
                (node_in, node_ref),
                (count_in, count_ref),
            )
        )
    ]
    for copy in copies:
        copy.start()
    statics = 5 * groups
    for copy in copies:
        copy.wait()
    order = iota((groups, LANES), 0) * LANES + iota((groups, LANES), 1)
    node = node_ref[...]
    row = owner_ref[...] * cells_x + lax.shift_right_logical(node, 7)
    row = jnp.where(order < count_ref[0], row.astype(F32), NOWHERE)
    column = (node & (LANES - 1)).astype(F32)
    for comp in range(3):
        for group in range(groups):
            rows_ref[comp * groups + group : comp * groups + group + 1, :] = values_ref[
                comp : comp + 1, group * LANES : (group + 1) * LANES
            ]
    rows_ref[3 * groups : 4 * groups, :] = row
    rows_ref[4 * groups : 5 * groups, :] = column

    def side(first, diag, edge, mask, toward, near, far):
        def put(slot, value):
            rows_ref[first + slot : first + slot + 1, :] = value

        for k in range(9):
            put(k, diag[k, near : near + 1, :])
        for slot, (direction, at) in enumerate(
            ((toward, near), (2, near), (3, near), (toward, far))
        ):
            present = mask[direction, at : at + 1, :].astype(F32)
            for k in range(9):
                put(9 + 9 * slot + k, edge[direction, k, at : at + 1, :] * present)
        for k in range(3):
            put(45 + k, diag[4 * k, far : far + 1, :])

    side(statics, diag_high, edge_high, mask_high, 0, 7, 6)
    side(statics + STATIC, diag_low, edge_low, mask_low, 1, 0, 1)


def halo_row(rows_ref, sender, base, there, near, far, entering):
    def entry(first):
        return lambda k: jnp.where(
            there, rows_ref[sender, base + first + k : base + first + k + 1, :], 0.0
        )

    diag = entry(0)
    field, inverse, far_field = [], [], []
    for comp in range(3):
        scale = diag(4 * comp)
        present = scale > 0.0
        scale = jnp.where(present, scale, 1.0)
        field.append(near[comp] / scale)
        inverse.append(jnp.where(present, 1.0 / scale, 0.0))
        far_scale = entry(45)(comp)
        far_field.append(far[comp] / jnp.where(far_scale > 0.0, far_scale, 1.0))
    into = product(entry(9), field)
    up_y = product(entry(18), field)
    low_y = product(entry(27), field)
    from_far = product(entry(36), far_field)
    within = off_diagonal(diag, field)
    part = [
        (
            within[c]
            + from_far[c]
            + entering[c]
            + lanes_moved(up_y[c], 0.0, 1)
            + lanes_moved(low_y[c], 0.0, -1)
        )
        * inverse[c]
        for c in range(3)
    ]
    return field, into, part, inverse, up_y, low_y


def field_kernel(
    rows_ref, diag_ref, edge_ref, mask_ref,
    field_ref, part_ref, halo_ref, edges_ref, load_ref,
):
    senders = rows_ref.shape[0]
    groups = (rows_ref.shape[1] - 2 * STATIC) // 5
    cells_x = field_ref.shape[1]
    half = (cells_x + 2 * PAD) // 2
    own = cells_x // 2

    load_ref[...] = jnp.zeros_like(load_ref)
    here = lax.axis_index("gx")
    first_row = (here * cells_x - PAD).astype(F32)

    def add_rows(sender, carry):
        row = rows_ref[sender, 3 * groups : 4 * groups, :] - first_row
        column = rows_ref[sender, 4 * groups : 5 * groups, :]
        lower = row >= float(half)
        place = jnp.where(lower, row - float(half), row)
        column = jnp.where(lower, column + float(LANES), column)
        at_row = float_iota((half, LANES), 0)
        at_column = float_iota((2 * LANES, LANES), 0)
        parts = [
            two_parts(rows_ref[sender, c * groups : (c + 1) * groups, :]) for c in range(3)
        ]
        lefts, rights = [], []
        for group in range(groups):
            line = slice(group, group + 1)
            here = at_row == place[line]
            lefts.append(
                jnp.concatenate(
                    [
                        jnp.where(here, parts[c][which][line], 0.0)
                        for which in range(2)
                        for c in range(3)
                    ],
                    axis=0,
                ).astype(BF16)
            )
            rights.append(jnp.where(at_column == column[line], 1.0, 0.0).astype(BF16))
        load_ref[...] += lax.dot_general(
            jnp.concatenate(lefts, axis=1),
            jnp.concatenate(rights, axis=1),
            (((1,), (1,)), ((), ())),
            preferred_element_type=F32,
        )
        return carry

    lax.fori_loop(0, senders, add_rows, 0, unroll=2)

    def load_rows(comp, first, last, second_half):
        lanes = slice(LANES, 2 * LANES) if second_half else slice(0, LANES)
        return (
            load_ref[comp * half + first : comp * half + last, lanes]
            + load_ref[(3 + comp) * half + first : (3 + comp) * half + last, lanes]
        )

    field = []
    for comp in range(3):
        load = jnp.concatenate(
            [load_rows(comp, PAD, half, False), load_rows(comp, 0, half - PAD, True)], axis=0
        )
        field.append(load / diag_ref[4 * comp])
        field_ref[comp] = field[comp]
    beyond = half - PAD
    near_before = [load_rows(c, PAD - 1, PAD, False) for c in range(3)]
    far_before = [load_rows(c, PAD - 2, PAD - 1, False) for c in range(3)]
    near_after = [load_rows(c, beyond, beyond + 1, True) for c in range(3)]
    far_after = [load_rows(c, beyond + 1, beyond + 2, True) for c in range(3)]

    up_x = masked_product(edge_ref, mask_ref, 0, field)
    low_x = masked_product(edge_ref, mask_ref, 1, field)
    lower, upper = jnp.maximum(here - 1, 0), jnp.minimum(here + 1, senders - 1)
    base = 5 * groups
    before = halo_row(
        rows_ref, lower, base, here > 0, near_before, far_before, [p[:1] for p in low_x]
    )
    after = halo_row(
        rows_ref, upper, base + STATIC, here < senders - 1, near_after, far_after,
        [p[-1:] for p in up_x],
    )
    total = off_diagonal(lambda k: diag_ref[k], field)
    total = [total[c] + rows_moved(up_x[c], before[1][c], 1) for c in range(3)]
    total = [total[c] + rows_moved(low_x[c], after[1][c], -1) for c in range(3)]
    up_y = masked_product(edge_ref, mask_ref, 2, field)
    low_y = masked_product(edge_ref, mask_ref, 3, field)
    total = [
        total[c] + lanes_moved(up_y[c], 0.0, 1) + lanes_moved(low_y[c], 0.0, -1)
        for c in range(3)
    ]
    inverse = [1.0 / diag_ref[4 * c] for c in range(3)]
    part = [total[c] * inverse[c] for c in range(3)]
    for comp in range(3):
        part_ref[comp] = part[comp]
    for side, group in enumerate((before, after)):
        for slot, which in enumerate((0, 2, 3)):
            for comp in range(3):
                at = 9 * side + 3 * slot + comp
                halo_ref[at : at + 1, :] = group[which][comp]

    def columns(target, lane, along_y, halo_slot):
        ahead = cells_x
        packed = jnp.zeros((cells_x, LANES), F32)
        extra = jnp.zeros((8, LANES), F32)
        at = iota((cells_x, LANES), 1)
        at_extra = iota((8, LANES), 1)
        which_row = iota((8, LANES), 0)
        for slot, fields in enumerate((field, along_y, part, inverse)):
            for comp in range(3):
                column = fields[comp][:, lane : lane + 1]
                packed = jnp.where(at == 3 * slot + comp, column, packed)
        for comp in range(3):
            first = before[halo_slot][comp][:, lane : lane + 1]
            second = after[halo_slot][comp][:, lane : lane + 1]
            both = jnp.where(which_row == 0, first, second)
            extra = jnp.where((at_extra == 3 + comp) & (which_row < 2), both, extra)
        rest = jnp.zeros((LANES - ahead - 8, LANES), F32)
        whole = jnp.concatenate([packed, extra, rest], axis=0)
        edges_ref[target] = whole.T[:16]

    edges_ref[...] = jnp.zeros_like(edges_ref)
    across = lax.axis_index("gy")

    @pl.when(across < edges_ref.shape[0] - 1)
    def _():
        columns(across + 1, LANES - 1, up_y, 4)

    @pl.when(across > 0)
    def _():
        columns(across - 1, 0, low_y, 5)


def bernstein(coord):
    other = 1.0 - coord
    return [
        other * other * other,
        3.0 * coord * other * other,
        3.0 * coord * coord * other,
        coord * coord * coord,
    ]


def weight_table(u, v, w):
    first, second, third = bernstein(u), bernstein(v), bernstein(w)
    line = iota((8, u.shape[1]), 0)
    inner = line & 3
    along = jnp.where(
        inner == 0,
        third[0],
        jnp.where(inner == 1, third[1], jnp.where(inner == 2, third[2], third[3])),
    )
    pair = jnp.concatenate(
        [
            jnp.where(line < 4, second[0], second[1]) * along,
            jnp.where(line < 4, second[2], second[3]) * along,
        ],
        axis=0,
    )
    return jnp.concatenate([pair * first[i] for i in range(4)], axis=0)


def sums_kernel(
    tile_ref, edges_ref, field_ref, part_ref, halo_ref,
    diag_ref, edge_ref, mask_ref, node_ref, param_ref,
    quotient_ref, out_ref, boxes_ref, *, tile_points,
):
    cells_x = field_ref.shape[1]
    own = cells_x // 2
    targets = out_ref.shape[0]
    padded_boxes = boxes_ref.shape[1]

    def arrived(sender):
        rest = jnp.zeros((LANES - 16, LANES), F32)
        return jnp.concatenate([edges_ref[sender], rest], axis=0).T

    across = lax.axis_index("gy")
    low = arrived(jnp.maximum(across - 1, 0))
    high = arrived(jnp.minimum(across + 1, edges_ref.shape[0] - 1))
    lane = iota((cells_x, LANES), 1)

    def column(source, slot, comp):
        return source[:cells_x, 3 * slot + comp : 3 * slot + comp + 1]

    field = [field_ref[c] for c in range(3)]
    scale = [diag_ref[4 * c] for c in range(3)]
    toward_high = masked_product(edge_ref, mask_ref, 2, field)
    toward_low = masked_product(edge_ref, mask_ref, 3, field)
    quotient, low_edge, high_edge = [], [], []
    for c in range(3):
        entering = jnp.where(
            lane == 0,
            column(low, 1, c),
            jnp.where(lane == LANES - 1, column(high, 1, c), 0.0),
        )
        quotient.append(part_ref[c] + entering / scale[c])
        low_edge.append(column(low, 2, c) + column(low, 3, c) * toward_low[c][:, :1])
        high_edge.append(column(high, 2, c) + column(high, 3, c) * toward_high[c][:, -1:])
    for c in range(3):
        quotient_ref[c] = quotient[c]
    lane_row = iota((1, LANES), 1)
    beyond = []
    for side in range(2):
        fields, quotients = [], []
        for c in range(3):
            at = 9 * side + c
            line = cells_x + side
            entering = jnp.where(
                lane_row == 0,
                low[line : line + 1, 3 + c : 4 + c],
                jnp.where(
                    lane_row == LANES - 1, high[line : line + 1, 3 + c : 4 + c], 0.0
                ),
            )
            fields.append(halo_ref[at : at + 1, :])
            quotients.append(
                halo_ref[at + 3 : at + 4, :] + entering * halo_ref[at + 6 : at + 7, :]
            )
        beyond.append((fields, quotients))

    first_sum = sum(field[c] * scale[c] * field[c] for c in range(3))
    second_sum = sum(field[c] * scale[c] * quotient[c] for c in range(3))
    third_sum = sum(quotient[c] * scale[c] * quotient[c] for c in range(3))
    within = off_diagonal(lambda k: diag_ref[k], quotient)
    fourth_sum = sum(within[c] * field[c] for c in range(3))
    fifth_sum = sum(within[c] * quotient[c] for c in range(3))
    for direction in range(4):
        moving = masked_product(edge_ref, mask_ref, direction, quotient)
        for c in range(3):
            if direction == 0:
                a = rows_moved(field[c], beyond[1][0][c], -1)
                b = rows_moved(quotient[c], beyond[1][1][c], -1)
            elif direction == 1:
                a = rows_moved(field[c], beyond[0][0][c], 1)
                b = rows_moved(quotient[c], beyond[0][1][c], 1)
            elif direction == 2:
                a = lanes_moved(field[c], column(high, 0, c), -1)
                b = lanes_moved(quotient[c], high_edge[c], -1)
            else:
                a = lanes_moved(field[c], column(low, 0, c), 1)
                b = lanes_moved(quotient[c], low_edge[c], 1)
            fourth_sum = fourth_sum + moving[c] * a
            fifth_sum = fifth_sum + moving[c] * b
    sums = jnp.zeros((1, LANES), F32)
    for k, value in enumerate((first_sum, second_sum, third_sum, fourth_sum, fifth_sum)):
        sums = jnp.where(lane_row == k, jnp.sum(value), sums)

    order = [field[0], field[1], quotient[0], quotient[1], field[2], quotient[2]]
    folded = [two_parts(jnp.concatenate([f[:own], f[own:]], axis=1)) for f in order]
    table = jnp.concatenate(
        [folded[f][which] for which in range(2) for f in range(6)], axis=0
    ).astype(BF16)
    points = param_ref.shape[1]
    boxes_ref[...] = jnp.zeros_like(boxes_ref)
    pieces = CHUNK // LANES
    for chunk in range(points // CHUNK):
        node = jnp.concatenate(
            [node_ref[chunk * pieces + k : chunk * pieces + k + 1, :] for k in range(pieces)],
            axis=1,
        )
        row = lax.shift_right_logical(node, 7)
        place = (node & (LANES - 1)) + jnp.where(row >= own, LANES, 0)
        row = jnp.where(row >= own, row - own, row)
        pick = jnp.where(iota((2 * LANES, CHUNK), 0) == place, 1.0, 0.0).astype(BF16)
        read = jnp.dot(table, pick, preferred_element_type=F32)
        read = read[: 6 * own] + read[6 * own :]
        here = iota((own, CHUNK), 0) == row
        lanes = slice(chunk * CHUNK, (chunk + 1) * CHUNK)
        weights = weight_table(
            param_ref[0:1, lanes], param_ref[1:2, lanes], param_ref[2:3, lanes]
        )
        highs, lows = [], []
        for f in range(6):
            values = jnp.where(here, read[f * own : (f + 1) * own], 0.0)
            values = jnp.sum(values, axis=0, keepdims=True)
            one, two = two_parts(weights * values)
            highs.append(one)
            lows.append(two)
        left = jnp.concatenate(
            [jnp.concatenate(highs, axis=0), jnp.concatenate(lows, axis=0)], axis=1
        ).astype(BF16)
        tiles = [
            jnp.where(
                iota((padded_boxes, tile_points), 0)
                == tile_ref[chunk * (CHUNK // tile_points) + k],
                1.0,
                0.0,
            ).astype(BF16)
            for k in range(CHUNK // tile_points)
        ]
        boxes_ref[...] += lax.dot_general(
            left,
            jnp.concatenate(tiles + tiles, axis=1),
            (((1,), (1,)), ((), ())),
            preferred_element_type=F32,
        )
    for pair in range(3):
        for block in range(padded_boxes // LANES):
            turned = boxes_ref[
                pair * LANES : (pair + 1) * LANES, block * LANES : (block + 1) * LANES
            ].T
            for box in range(min(LANES, targets - block * LANES)):
                out_ref[block * LANES + box, pair : pair + 1, :] = turned[box : box + 1]
    for box in range(targets):
        out_ref[box, 3:4, :] = sums


def result_kernel(got_ref, field_ref, quotient_ref, solution_ref, gradient_ref):
    total = jnp.sum(got_ref[...], axis=0)
    rho, a, b, t, u = [total[3:4, k : k + 1] for k in range(5)]
    ratio = a / rho
    norm = rho + a
    step = rho / norm
    rest = jnp.maximum(b - a * ratio, 0.0)
    beta = step * step * rest / rho
    rest_image = (b + u) - ratio * (a + b + a + t) + ratio * ratio * norm
    cross = (a + t) - ratio * norm
    curve = step * step * rest_image - step * beta * (rest + cross) + beta * beta * norm
    second = jnp.where(
        curve > 0.0, step * step * rest / jnp.where(curve > 0.0, curve, 1.0), 0.0
    )
    of_field = step + second * (beta + step * ratio)
    of_quotient = -(step * second)
    for c in range(3):
        solution_ref[c] = of_field * field_ref[c] + of_quotient * quotient_ref[c]
    gradient_ref[:, :LANES] = of_field * total[0:1] + of_quotient * total[1:2]
    gradient_ref[:, LANES:] = (
        of_field * total[2:3, : LANES // 2] + of_quotient * total[2:3, LANES // 2 :]
    )


def per_device(
    diag_blocks, edge_blocks, edge_mask, src_values, src_owner, src_node, src_count,
    surf_node, surf_param, tile_box,
):
    cells_x, cells_y = diag_blocks.shape[1:]
    width_gx, width_gy = lax.axis_size("gx"), lax.axis_size("gy")
    devices = width_gx * width_gy
    groups = src_node.shape[0] // LANES
    whole = functools.partial(jax.ShapeDtypeStruct, dtype=F32)

    cells = 5 * groups + 2 * STATIC
    i32 = jnp.int32
    rows = pl.pallas_call(
        pack_kernel,
        in_specs=[HBM] * 7,
        out_specs=VMEM,
        out_shape=whole((cells, LANES)),
        scratch_shapes=[
            pltpu.SMEM((1,), i32),
            pltpu.VMEM(src_values.shape, F32),
            pltpu.VMEM((groups, LANES), i32),
            pltpu.VMEM((groups, LANES), i32),
            pltpu.VMEM((9, 8, cells_y), F32),
            pltpu.VMEM((9, 8, cells_y), F32),
            pltpu.VMEM((4, 9, 8, cells_y), F32),
            pltpu.VMEM((4, 9, 8, cells_y), F32),
            pltpu.VMEM((4, 8, cells_y), i32),
            pltpu.VMEM((4, 8, cells_y), i32),
            pltpu.SemaphoreType.DMA((10,)),
        ],
        compiler_params=pltpu.CompilerParams(vmem_limit_bytes=PACK_VMEM),
        name="pack_rows_and_edges",
    )(
        src_count, src_values,
        src_owner.reshape(groups, LANES), src_node.reshape(groups, LANES),
        diag_blocks, edge_blocks, edge_mask,
    )
    rows = lax.all_gather(rows, "gx")

    nodes = (3, cells_x, cells_y)
    frame = cells_x + 2 * PAD
    field, part, halo, edges = pl.pallas_call(
        field_kernel,
        in_specs=[VMEM] * 4,
        out_specs=[VMEM] * 4,
        out_shape=[
            whole(nodes), whole(nodes), whole((24, cells_y)), whole((width_gy, 16, LANES)),
        ],
        scratch_shapes=[pltpu.VMEM((3 * frame, 2 * LANES), F32)],
        compiler_params=PARAMS,
        name="load_and_first_product",
    )(rows, diag_blocks, edge_blocks, edge_mask)
    edges = lax.all_to_all(edges, "gy", split_axis=0, concat_axis=0, tiled=True)

    points = surf_node.shape[0]
    padded = -(-devices // LANES) * LANES
    quotient, partial = pl.pallas_call(
        functools.partial(sums_kernel, tile_points=points // tile_box.shape[0]),
        in_specs=[SMEM] + [VMEM] * 9,
        out_specs=[VMEM] * 2,
        out_shape=[whole(nodes), whole((devices, 4, LANES))],
        scratch_shapes=[pltpu.VMEM((6 * 64, padded), F32)],
        compiler_params=PARAMS,
        name="sums_and_box_parts",
    )(
        tile_box, edges, field, part, halo, diag_blocks, edge_blocks, edge_mask,
        surf_node.reshape(points // LANES, LANES), surf_param,
    )
    got = lax.all_to_all(partial, ("gx", "gy"), split_axis=0, concat_axis=0, tiled=True)
    return pl.pallas_call(
        result_kernel,
        in_specs=[VMEM] * 3,
        out_specs=[VMEM] * 2,
        out_shape=[whole(nodes), whole((1, 192))],
        compiler_params=PARAMS,
        name="steps_and_outputs",
    )(got, field, quotient)


def solution(mesh):
    return jax.shard_map(
        per_device,
        mesh=mesh,
        in_specs=(
            P(None, "gx", "gy"),
            P(None, None, "gx", "gy"),
            P(None, "gx", "gy"),
            P(None, ("gx", "gy")),
            P(("gx", "gy"), None),
            P(("gx", "gy")),
            P(("gx", "gy")),
            P(("gx", "gy")),
            P(None, ("gx", "gy")),
            P(("gx", "gy")),
        ),
        out_specs=(P(None, "gx", "gy"), P(("gx", "gy"), None)),
        check_vma=False,
    )
```

```python
import functools

import jax
import jax.numpy as jnp
from jax import lax
from jax.experimental import pallas as pl
from jax.experimental.pallas import tpu as pltpu
from jax.sharding import PartitionSpec as P

F32 = jnp.float32
BF16 = jnp.bfloat16
PAD = 16
NOWHERE = -4096.0
LANES = 128
LOWER = 48
STRIPS = 64
CHUNK = 256
PACK_VMEM = 60 * 1000 * 1000
PARAMS = pltpu.CompilerParams(vmem_limit_bytes=24 * 1024 * 1024)

VMEM = pl.BlockSpec(memory_space=pltpu.VMEM)
SMEM = pl.BlockSpec(memory_space=pltpu.SMEM)
HBM = pl.BlockSpec(memory_space=pltpu.HBM)


def iota(shape, dim):
    return lax.broadcasted_iota(jnp.int32, shape, dim)


def float_iota(shape, dim):
    return iota(shape, dim).astype(F32)


def two_parts(value):
    high = value.astype(BF16).astype(F32)
    return high, value - high


def product(block, field):
    return [
        block(row) * field[0] + block(3 + row) * field[1] + block(6 + row) * field[2]
        for row in range(3)
    ]


def off_diagonal(block, field):
    return [
        sum(block(3 * i + row) * field[i] for i in range(3) if i != row) for row in range(3)
    ]


def masked_product(edge_ref, mask_ref, direction, field):
    mask = mask_ref[direction].astype(F32)
    return [mask * part for part in product(lambda k: edge_ref[direction, k], field)]


def rows_moved(field, edge_row, step):
    size = field.shape[0]
    at = iota(field.shape, 0)
    moved = pltpu.roll(field, step % size, 0)
    return jnp.where(at == (0 if step == 1 else size - 1), edge_row, moved)


def lanes_moved(field, edge_column, step):
    size = field.shape[1]
    at = iota(field.shape, 1)
    moved = pltpu.roll(field, step % size, 1)
    return jnp.where(at == (0 if step == 1 else size - 1), edge_column, moved)


def pack_kernel(
    count_in, values_in, owner_in, node_in, diag_in, edge_in, mask_in, rows_ref,
    count_ref, values_ref, owner_ref, node_ref, diag_low, diag_high, edge_low, edge_high,
    mask_low, mask_high, arrived,
):
    groups = owner_ref.shape[0]
    cells_x = diag_in.shape[1]
    top = pl.ds(cells_x - 8, 8)
    copies = [
        pltpu.make_async_copy(source, target, arrived.at[k])
        for k, (source, target) in enumerate(
            (
                (edge_in.at[1, :, 0:8], edge_low),
                (edge_in.at[:, :, top], edge_high),
                (diag_in.at[:, 0:8], diag_low),
                (diag_in.at[:, top], diag_high),
                (mask_in.at[1, 0:8], mask_low),
                (mask_in.at[:, top], mask_high),
                (values_in, values_ref),
                (owner_in, owner_ref),
                (node_in, node_ref),
                (count_in, count_ref),
            )
        )
    ]
    for copy in copies:
        copy.start()
    statics = 5 * groups
    for copy in copies:
        copy.wait()
    order = iota((groups, LANES), 0) * LANES + iota((groups, LANES), 1)
    node = node_ref[...]
    row = owner_ref[...] * cells_x + lax.shift_right_logical(node, 7)
    row = jnp.where(order < count_ref[0], row.astype(F32), NOWHERE)
    column = (node & (LANES - 1)).astype(F32)
    for comp in range(3):
        for group in range(groups):
            rows_ref[comp * groups + group : comp * groups + group + 1, :] = values_ref[
                comp : comp + 1, group * LANES : (group + 1) * LANES
            ]
    rows_ref[3 * groups : 4 * groups, :] = row
    rows_ref[4 * groups : 5 * groups, :] = column

    def put(slot, value):
        rows_ref[statics + slot : statics + slot + 1, :] = value

    for k in range(9):
        put(k, diag_high[k, 7:8, :])
    for slot, (direction, at) in enumerate(((0, 7), (2, 7), (3, 7), (0, 6))):
        present = mask_high[direction, at : at + 1, :].astype(F32)
        for k in range(9):
            put(9 + 9 * slot + k, edge_high[direction, k, at : at + 1, :] * present)
    for k in range(3):
        put(45 + k, diag_high[4 * k, 6:7, :])
    for k in range(3):
        put(LOWER + k, diag_low[4 * k, 0:1, :])
    present = mask_low[0:1, :].astype(F32)
    for k in range(9):
        put(LOWER + 3 + k, edge_low[k, 0:1, :] * present)
    rows_ref[statics + LOWER + 12 :, :] = jnp.zeros((STRIPS - LOWER - 12, LANES), F32)


def stretched(row, count):
    tile = jnp.broadcast_to(row, (16, row.shape[1])).astype(BF16)
    return jnp.concatenate([tile] * (count // 16), axis=0)


def strip(rows_ref, sender, base, there):
    return lambda first: lambda k: jnp.where(
        there, rows_ref[sender, base + first + k : base + first + k + 1, :], 0.0
    )


def ratio(value, scale):
    return jnp.where(scale > 0.0, value / jnp.where(scale > 0.0, scale, 1.0), 0.0)


def row_before(entry, near, far, entering):
    diag, toward = entry(0), entry(9)
    field = [ratio(near[c], diag(4 * c)) for c in range(3)]
    inverse = [ratio(1.0, diag(4 * c)) for c in range(3)]
    far_field = [ratio(far[c], entry(45)(c)) for c in range(3)]
    into = product(toward, field)
    up_y = product(entry(18), field)
    low_y = product(entry(27), field)
    from_far = product(entry(36), far_field)
    within = off_diagonal(diag, field)
    part = [
        (
            within[c]
            + from_far[c]
            + entering[c]
            + lanes_moved(up_y[c], 0.0, 1)
            + lanes_moved(low_y[c], 0.0, -1)
        )
        * inverse[c]
        for c in range(3)
    ]
    return field, into, part, inverse, up_y, low_y, [toward(k) for k in range(9)]


def field_kernel(
    rows_ref, diag_ref, edge_ref, mask_ref,
    field_ref, part_ref, halo_ref, edges_ref, load_ref,
):
    senders = rows_ref.shape[0]
    groups = (rows_ref.shape[1] - STRIPS) // 5
    cells_x = field_ref.shape[1]
    half = (cells_x + 2 * PAD) // 2
    own = cells_x // 2

    load_ref[...] = jnp.zeros_like(load_ref)
    here = lax.axis_index("gx")
    first_row = (here * cells_x - PAD).astype(F32)

    def add_rows(sender, carry):
        row = rows_ref[sender, 3 * groups : 4 * groups, :] - first_row
        column = rows_ref[sender, 4 * groups : 5 * groups, :]
        lower = row >= float(half)
        place = jnp.where(lower, row - float(half), row)
        column = jnp.where(lower, column + float(LANES), column)
        at_row = float_iota((half, LANES), 0).astype(BF16)
        at_column = float_iota((2 * LANES, LANES), 0).astype(BF16)
        parts = [
            two_parts(rows_ref[sender, c * groups : (c + 1) * groups, :]) for c in range(3)
        ]
        zero, one = jnp.zeros((), BF16), jnp.ones((), BF16)
        lefts, rights = [], []
        for group in range(groups):
            line = slice(group, group + 1)
            match = at_row == stretched(place[line], half)
            lefts.append(
                jnp.concatenate(
                    [
                        jnp.where(match, stretched(parts[c][which][line], half), zero)
                        for which in range(2)
                        for c in range(3)
                    ],
                    axis=0,
                )
            )
            rights.append(
                jnp.where(at_column == stretched(column[line], 2 * LANES), one, zero)
            )
        load_ref[...] += lax.dot_general(
            jnp.concatenate(lefts, axis=1),
            jnp.concatenate(rights, axis=1),
            (((1,), (1,)), ((), ())),
            preferred_element_type=F32,
        )
        return carry

    lax.fori_loop(0, senders, add_rows, 0, unroll=2)

    def load_rows(comp, first, last, second_half):
        lanes = slice(LANES, 2 * LANES) if second_half else slice(0, LANES)
        return (
            load_ref[comp * half + first : comp * half + last, lanes]
            + load_ref[(3 + comp) * half + first : (3 + comp) * half + last, lanes]
        )

    field = []
    for comp in range(3):
        load = jnp.concatenate(
            [load_rows(comp, PAD, half, False), load_rows(comp, 0, half - PAD, True)], axis=0
        )
        field.append(load / diag_ref[4 * comp])
        field_ref[comp] = field[comp]
    beyond = half - PAD
    near_before = [load_rows(c, PAD - 1, PAD, False) for c in range(3)]
    far_before = [load_rows(c, PAD - 2, PAD - 1, False) for c in range(3)]
    near_after = [load_rows(c, beyond, beyond + 1, True) for c in range(3)]

    up_x = masked_product(edge_ref, mask_ref, 0, field)
    low_x = masked_product(edge_ref, mask_ref, 1, field)
    base = 5 * groups
    before = row_before(
        strip(rows_ref, jnp.maximum(here - 1, 0), base, here > 0),
        near_before, far_before, [p[:1] for p in low_x],
    )
    after = strip(
        rows_ref, jnp.minimum(here + 1, senders - 1), base + LOWER, here < senders - 1
    )
    after = product(after(3), [ratio(near_after[c], after(0)(c)) for c in range(3)])
    total = off_diagonal(lambda k: diag_ref[k], field)
    total = [total[c] + rows_moved(up_x[c], before[1][c], 1) for c in range(3)]
    total = [total[c] + rows_moved(low_x[c], after[c], -1) for c in range(3)]
    up_y = masked_product(edge_ref, mask_ref, 2, field)
    low_y = masked_product(edge_ref, mask_ref, 3, field)
    total = [
        total[c] + lanes_moved(up_y[c], 0.0, 1) + lanes_moved(low_y[c], 0.0, -1)
        for c in range(3)
    ]
    inverse = [1.0 / diag_ref[4 * c] for c in range(3)]
    part = [total[c] * inverse[c] for c in range(3)]
    for comp in range(3):
        part_ref[comp] = part[comp]
    for slot, which in enumerate((0, 2, 3)):
        for comp in range(3):
            at = 3 * slot + comp
            halo_ref[at : at + 1, :] = before[which][comp]
    for k in range(9):
        halo_ref[9 + k : 10 + k, :] = before[6][k]
    halo_ref[18:, :] = jnp.zeros((6, LANES), F32)

    def columns(target, lane, along_y, halo_slot):
        ahead = cells_x
        packed = jnp.zeros((cells_x, LANES), F32)
        extra = jnp.zeros((8, LANES), F32)
        at = iota((cells_x, LANES), 1)
        at_extra = iota((8, LANES), 1)
        which_row = iota((8, LANES), 0)
        for slot, fields in enumerate((field, along_y, part, inverse)):
            for comp in range(3):
                column = fields[comp][:, lane : lane + 1]
                packed = jnp.where(at == 3 * slot + comp, column, packed)
        for comp in range(3):
            first = before[halo_slot][comp][:, lane : lane + 1]
            extra = jnp.where((at_extra == 3 + comp) & (which_row == 0), first, extra)
        rest = jnp.zeros((LANES - ahead - 8, LANES), F32)
        whole = jnp.concatenate([packed, extra, rest], axis=0)
        edges_ref[target] = whole.T[:16]

    edges_ref[...] = jnp.zeros_like(edges_ref)
    across = lax.axis_index("gy")

    @pl.when(across < edges_ref.shape[0] - 1)
    def _():
        columns(across + 1, LANES - 1, up_y, 4)

    @pl.when(across > 0)
    def _():
        columns(across - 1, 0, low_y, 5)


def bernstein(coord):
    other = 1.0 - coord
    return [
        other * other * other,
        3.0 * coord * other * other,
        3.0 * coord * coord * other,
        coord * coord * coord,
    ]


def weight_table(u, v, w):
    first, second, third = bernstein(u), bernstein(v), bernstein(w)
    line = iota((8, u.shape[1]), 0)
    inner = line & 3
    along = jnp.where(
        inner == 0,
        third[0],
        jnp.where(inner == 1, third[1], jnp.where(inner == 2, third[2], third[3])),
    )
    pair = jnp.concatenate(
        [
            jnp.where(line < 4, second[0], second[1]) * along,
            jnp.where(line < 4, second[2], second[3]) * along,
        ],
        axis=0,
    )
    return jnp.concatenate([pair * first[i] for i in range(4)], axis=0)


def sums_kernel(
    tile_ref, edges_ref, field_ref, part_ref, halo_ref,
    diag_ref, edge_ref, mask_ref, node_ref, param_ref,
    quotient_ref, out_ref, *, tile_points,
):
    cells_x = field_ref.shape[1]
    own = cells_x // 2
    targets = out_ref.shape[0]

    def arrived(sender):
        rest = jnp.zeros((LANES - 16, LANES), F32)
        return jnp.concatenate([edges_ref[sender], rest], axis=0).T

    across = lax.axis_index("gy")
    low = arrived(jnp.maximum(across - 1, 0))
    high = arrived(jnp.minimum(across + 1, edges_ref.shape[0] - 1))
    lane = iota((cells_x, LANES), 1)

    def column(source, slot, comp):
        return source[:cells_x, 3 * slot + comp : 3 * slot + comp + 1]

    field = [field_ref[c] for c in range(3)]
    scale = [diag_ref[4 * c] for c in range(3)]
    toward_high = masked_product(edge_ref, mask_ref, 2, field)
    toward_low = masked_product(edge_ref, mask_ref, 3, field)
    quotient, low_edge, high_edge = [], [], []
    for c in range(3):
        entering = jnp.where(
            lane == 0,
            column(low, 1, c),
            jnp.where(lane == LANES - 1, column(high, 1, c), 0.0),
        )
        quotient.append(part_ref[c] + entering / scale[c])
        low_edge.append(column(low, 2, c) + column(low, 3, c) * toward_low[c][:, :1])
        high_edge.append(column(high, 2, c) + column(high, 3, c) * toward_high[c][:, -1:])
    for c in range(3):
        quotient_ref[c] = quotient[c]
    lane_row = iota((1, LANES), 1)
    before, before_quotient = [], []
    for c in range(3):
        entering = jnp.where(
            lane_row == 0,
            low[cells_x : cells_x + 1, 3 + c : 4 + c],
            jnp.where(lane_row == LANES - 1, high[cells_x : cells_x + 1, 3 + c : 4 + c], 0.0),
        )
        before.append(halo_ref[c : c + 1, :])
        before_quotient.append(
            halo_ref[3 + c : 4 + c, :] + entering * halo_ref[6 + c : 7 + c, :]
        )

    first_sum = sum(field[c] * scale[c] * field[c] for c in range(3))
    second_sum = sum(field[c] * scale[c] * quotient[c] for c in range(3))
    third_sum = sum(quotient[c] * scale[c] * quotient[c] for c in range(3))
    within = off_diagonal(lambda k: diag_ref[k], quotient)
    fourth_sum = sum(within[c] * field[c] for c in range(3))
    fifth_sum = sum(within[c] * quotient[c] for c in range(3))
    for direction in range(4):
        moving = masked_product(edge_ref, mask_ref, direction, quotient)
        for c in range(3):
            if direction == 0:
                a = rows_moved(field[c], 0.0, -1)
                b = rows_moved(quotient[c], 0.0, -1)
            elif direction == 1:
                a = rows_moved(field[c], before[c], 1)
                b = rows_moved(quotient[c], before_quotient[c], 1)
            elif direction == 2:
                a = lanes_moved(field[c], column(high, 0, c), -1)
                b = lanes_moved(quotient[c], high_edge[c], -1)
            else:
                a = lanes_moved(field[c], column(low, 0, c), 1)
                b = lanes_moved(quotient[c], low_edge[c], 1)
            fourth_sum = fourth_sum + moving[c] * a
            fifth_sum = fifth_sum + moving[c] * b
    incoming = product(lambda k: halo_ref[9 + k : 10 + k, :], before_quotient)
    extra = [0.0, 0.0, 0.0]
    extra.append(sum(incoming[c] * field[c][:1] for c in range(3)))
    extra.append(sum(incoming[c] * quotient[c][:1] for c in range(3)))
    sums = jnp.zeros((1, LANES), F32)
    for k, value in enumerate((first_sum, second_sum, third_sum, fourth_sum, fifth_sum)):
        line = jnp.sum(value, axis=0, keepdims=True) + extra[k]
        sums = jnp.where(lane_row == k, jnp.sum(line, axis=1, keepdims=True), sums)

    order = [field[0], quotient[0], field[2], field[1], quotient[1], quotient[2]]
    folded = [two_parts(jnp.concatenate([f[:own], f[own:]], axis=1)) for f in order]
    table = jnp.concatenate(
        [folded[f][which] for which in range(2) for f in range(6)], axis=0
    ).astype(BF16)
    points = param_ref.shape[1]
    out_ref[...] = jnp.zeros_like(out_ref)
    pieces = CHUNK // LANES
    zero, one = jnp.zeros((), BF16), jnp.ones((), BF16)
    at_node = float_iota((2 * LANES, CHUNK), 0).astype(BF16)
    nothing = jnp.zeros((1, CHUNK), F32)
    first_half = iota((4, LANES), 1) < LANES // 2
    for chunk in range(points // CHUNK):
        node = jnp.concatenate(
            [node_ref[chunk * pieces + k : chunk * pieces + k + 1, :] for k in range(pieces)],
            axis=1,
        )
        row = lax.shift_right_logical(node, 7)
        place = (node & (LANES - 1)) + jnp.where(row >= own, LANES, 0)
        row = jnp.where(row >= own, row - own, row)
        pick = jnp.where(at_node == stretched(place.astype(F32), 2 * LANES), one, zero)
        read = jnp.dot(table, pick, preferred_element_type=F32)
        read = read[: 6 * own] + read[6 * own :]
        here = iota((own, CHUNK), 0) == row
        values = [
            jnp.sum(
                jnp.where(here, read[f * own : (f + 1) * own], 0.0), axis=0, keepdims=True
            )
            for f in range(6)
        ]
        values = two_parts(
            jnp.concatenate(values[:3] + [nothing] + values[3:] + [nothing], axis=0)
        )
        lanes = slice(chunk * CHUNK, (chunk + 1) * CHUNK)
        weights = two_parts(
            weight_table(param_ref[0:1, lanes], param_ref[1:2, lanes], param_ref[2:3, lanes])
        )
        for k in range(CHUNK // tile_points):
            tile = slice(k * tile_points, (k + 1) * tile_points)
            high, low = values[0][:, tile], values[1][:, tile]
            left = jnp.concatenate(
                [
                    jnp.concatenate([high, high], axis=1),
                    jnp.concatenate([low, jnp.zeros_like(low)], axis=1),
                ],
                axis=0,
            ).astype(BF16)
            right = jnp.concatenate([weights[0][:, tile], weights[1][:, tile]], axis=1)
            right = right.astype(BF16)
            term = lax.dot_general(
                left,
                jnp.concatenate([right, right], axis=0),
                (((1,), (1,)), ((), ())),
                preferred_element_type=F32,
            )
            term = term[:8] + term[8:]
            box = tile_ref[chunk * (CHUNK // tile_points) + k]
            out_ref[box] += jnp.where(first_half, term[:4], term[4:])
    for box in range(targets):
        out_ref[box, 3:4, :] = sums


def result_kernel(got_ref, field_ref, quotient_ref, solution_ref, gradient_ref):
    total = jnp.sum(got_ref[...], axis=0)
    rho, a, b, t, u = [total[3:4, k : k + 1] for k in range(5)]
    ratio = a / rho
    norm = rho + a
    step = rho / norm
    rest = jnp.maximum(b - a * ratio, 0.0)
    beta = step * step * rest / rho
    rest_image = (b + u) - ratio * (a + b + a + t) + ratio * ratio * norm
    cross = (a + t) - ratio * norm
    curve = step * step * rest_image - step * beta * (rest + cross) + beta * beta * norm
    second = jnp.where(
        curve > 0.0, step * step * rest / jnp.where(curve > 0.0, curve, 1.0), 0.0
    )
    of_field = step + second * (beta + step * ratio)
    of_quotient = -(step * second)
    for c in range(3):
        solution_ref[c] = of_field * field_ref[c] + of_quotient * quotient_ref[c]
    gradient_ref[:, :LANES] = of_field * total[0:1] + of_quotient * total[1:2]
    gradient_ref[:, LANES:] = (
        of_field * total[2:3, : LANES // 2] + of_quotient * total[2:3, LANES // 2 :]
    )


def per_device(
    diag_blocks, edge_blocks, edge_mask, src_values, src_owner, src_node, src_count,
    surf_node, surf_param, tile_box,
):
    cells_x, cells_y = diag_blocks.shape[1:]
    width_gx, width_gy = lax.axis_size("gx"), lax.axis_size("gy")
    devices = width_gx * width_gy
    groups = src_node.shape[0] // LANES
    whole = functools.partial(jax.ShapeDtypeStruct, dtype=F32)

    cells = 5 * groups + STRIPS
    i32 = jnp.int32
    rows = pl.pallas_call(
        pack_kernel,
        in_specs=[HBM] * 7,
        out_specs=VMEM,
        out_shape=whole((cells, LANES)),
        scratch_shapes=[
            pltpu.SMEM((1,), i32),
            pltpu.VMEM(src_values.shape, F32),
            pltpu.VMEM((groups, LANES), i32),
            pltpu.VMEM((groups, LANES), i32),
            pltpu.VMEM((9, 8, cells_y), F32),
            pltpu.VMEM((9, 8, cells_y), F32),
            pltpu.VMEM((9, 8, cells_y), F32),
            pltpu.VMEM((4, 9, 8, cells_y), F32),
            pltpu.VMEM((8, cells_y), i32),
            pltpu.VMEM((4, 8, cells_y), i32),
            pltpu.SemaphoreType.DMA((10,)),
        ],
        compiler_params=pltpu.CompilerParams(vmem_limit_bytes=PACK_VMEM),
        name="pack_rows_and_edges",
    )(
        src_count, src_values,
        src_owner.reshape(groups, LANES), src_node.reshape(groups, LANES),
        diag_blocks, edge_blocks, edge_mask,
    )
    rows = lax.all_gather(rows, "gx")

    nodes = (3, cells_x, cells_y)
    frame = cells_x + 2 * PAD
    field, part, halo, edges = pl.pallas_call(
        field_kernel,
        in_specs=[VMEM] * 4,
        out_specs=[VMEM] * 4,
        out_shape=[
            whole(nodes), whole(nodes), whole((24, cells_y)), whole((width_gy, 16, LANES)),
        ],
        scratch_shapes=[pltpu.VMEM((3 * frame, 2 * LANES), F32)],
        compiler_params=PARAMS,
        name="load_and_first_product",
    )(rows, diag_blocks, edge_blocks, edge_mask)
    edges = lax.all_to_all(edges, "gy", split_axis=0, concat_axis=0, tiled=True)

    points = surf_node.shape[0]
    quotient, partial = pl.pallas_call(
        functools.partial(sums_kernel, tile_points=points // tile_box.shape[0]),
        in_specs=[SMEM] + [VMEM] * 9,
        out_specs=[VMEM] * 2,
        out_shape=[whole(nodes), whole((devices, 4, LANES))],
        compiler_params=PARAMS,
        name="sums_and_box_parts",
    )(
        tile_box, edges, field, part, halo, diag_blocks, edge_blocks, edge_mask,
        surf_node.reshape(points // LANES, LANES), surf_param,
    )
    got = lax.all_to_all(partial, ("gx", "gy"), split_axis=0, concat_axis=0, tiled=True)
    return pl.pallas_call(
        result_kernel,
        in_specs=[VMEM] * 3,
        out_specs=[VMEM] * 2,
        out_shape=[whole(nodes), whole((1, 192))],
        compiler_params=PARAMS,
        name="steps_and_outputs",
    )(got, field, quotient)


def solution(mesh):
    return jax.shard_map(
        per_device,
        mesh=mesh,
        in_specs=(
            P(None, "gx", "gy"),
            P(None, None, "gx", "gy"),
            P(None, "gx", "gy"),
            P(None, ("gx", "gy")),
            P(("gx", "gy"), None),
            P(("gx", "gy")),
            P(("gx", "gy")),
            P(("gx", "gy")),
            P(None, ("gx", "gy")),
            P(("gx", "gy")),
        ),
        out_specs=(P(None, "gx", "gy"), P(("gx", "gy"), None)),
        check_vma=False,
    )
```

```python
import functools

import jax
import jax.numpy as jnp
from jax import lax
from jax.experimental import pallas as pl
from jax.experimental.pallas import tpu as pltpu
from jax.sharding import PartitionSpec as P

F32 = jnp.float32
BF16 = jnp.bfloat16
PAD = 16
NOWHERE = -4096.0
LANES = 128
LOWER = 48
STRIPS = 64
CHUNK = 256
PACK_VMEM = 60 * 1000 * 1000
PARAMS = pltpu.CompilerParams(vmem_limit_bytes=24 * 1024 * 1024)

VMEM = pl.BlockSpec(memory_space=pltpu.VMEM)
SMEM = pl.BlockSpec(memory_space=pltpu.SMEM)
HBM = pl.BlockSpec(memory_space=pltpu.HBM)


def iota(shape, dim):
    return lax.broadcasted_iota(jnp.int32, shape, dim)


def float_iota(shape, dim):
    return iota(shape, dim).astype(F32)


def two_parts(value):
    high = value.astype(BF16).astype(F32)
    return high, value - high


def product(block, field):
    return [
        block(row) * field[0] + block(3 + row) * field[1] + block(6 + row) * field[2]
        for row in range(3)
    ]


def off_diagonal(block, field):
    return [
        sum(block(3 * i + row) * field[i] for i in range(3) if i != row) for row in range(3)
    ]


def masked_product(edge_ref, mask_ref, direction, field):
    mask = mask_ref[direction].astype(F32)
    return [mask * part for part in product(lambda k: edge_ref[direction, k], field)]


def rows_moved(field, edge_row, step):
    size = field.shape[0]
    at = iota(field.shape, 0)
    moved = pltpu.roll(field, step % size, 0)
    return jnp.where(at == (0 if step == 1 else size - 1), edge_row, moved)


def lanes_moved(field, edge_column, step):
    size = field.shape[1]
    at = iota(field.shape, 1)
    moved = pltpu.roll(field, step % size, 1)
    return jnp.where(at == (0 if step == 1 else size - 1), edge_column, moved)


def pack_kernel(
    count_in, values_in, owner_in, node_in, diag_in, edge_in, mask_in, rows_ref,
    count_ref, values_ref, owner_ref, node_ref, diag_low, diag_high, edge_low, edge_high,
    mask_low, mask_high, arrived,
):
    groups = owner_ref.shape[0]
    cells_x = diag_in.shape[1]
    top = pl.ds(cells_x - 8, 8)
    copies = [
        pltpu.make_async_copy(source, target, arrived.at[k])
        for k, (source, target) in enumerate(
            (
                (edge_in.at[1, :, 0:8], edge_low),
                (edge_in.at[:, :, top], edge_high),
                (diag_in.at[:, 0:8], diag_low),
                (diag_in.at[:, top], diag_high),
                (mask_in.at[1, 0:8], mask_low),
                (mask_in.at[:, top], mask_high),
                (values_in, values_ref),
                (owner_in, owner_ref),
                (node_in, node_ref),
                (count_in, count_ref),
            )
        )
    ]
    for copy in copies:
        copy.start()
    statics = 5 * groups
    for copy in copies:
        copy.wait()
    order = iota((groups, LANES), 0) * LANES + iota((groups, LANES), 1)
    node = node_ref[...]
    row = owner_ref[...] * cells_x + lax.shift_right_logical(node, 7)
    row = jnp.where(order < count_ref[0], row.astype(F32), NOWHERE)
    column = (node & (LANES - 1)).astype(F32)
    for comp in range(3):
        for group in range(groups):
            rows_ref[comp * groups + group : comp * groups + group + 1, :] = values_ref[
                comp : comp + 1, group * LANES : (group + 1) * LANES
            ]
    rows_ref[3 * groups : 4 * groups, :] = row
    rows_ref[4 * groups : 5 * groups, :] = column

    def put(slot, value):
        rows_ref[statics + slot : statics + slot + 1, :] = value

    for k in range(9):
        put(k, diag_high[k, 7:8, :])
    for slot, (direction, at) in enumerate(((0, 7), (2, 7), (3, 7), (0, 6))):
        present = mask_high[direction, at : at + 1, :].astype(F32)
        for k in range(9):
            put(9 + 9 * slot + k, edge_high[direction, k, at : at + 1, :] * present)
    for k in range(3):
        put(45 + k, diag_high[4 * k, 6:7, :])
    for k in range(3):
        put(LOWER + k, diag_low[4 * k, 0:1, :])
    present = mask_low[0:1, :].astype(F32)
    for k in range(9):
        put(LOWER + 3 + k, edge_low[k, 0:1, :] * present)
    rows_ref[statics + LOWER + 12 :, :] = jnp.zeros((STRIPS - LOWER - 12, LANES), F32)


def stretched(row, count):
    tile = jnp.broadcast_to(row, (16, row.shape[1])).astype(BF16)
    return jnp.concatenate([tile] * (count // 16), axis=0)


def strip(rows_ref, sender, base, there):
    return lambda first: lambda k: jnp.where(
        there, rows_ref[sender, base + first + k : base + first + k + 1, :], 0.0
    )


def ratio(value, scale):
    return jnp.where(scale > 0.0, value / jnp.where(scale > 0.0, scale, 1.0), 0.0)


def row_before(entry, near, far, entering):
    diag, toward = entry(0), entry(9)
    field = [ratio(near[c], diag(4 * c)) for c in range(3)]
    inverse = [ratio(1.0, diag(4 * c)) for c in range(3)]
    far_field = [ratio(far[c], entry(45)(c)) for c in range(3)]
    into = product(toward, field)
    up_y = product(entry(18), field)
    low_y = product(entry(27), field)
    from_far = product(entry(36), far_field)
    within = off_diagonal(diag, field)
    part = [
        (
            within[c]
            + from_far[c]
            + entering[c]
            + lanes_moved(up_y[c], 0.0, 1)
            + lanes_moved(low_y[c], 0.0, -1)
        )
        * inverse[c]
        for c in range(3)
    ]
    return field, into, part, inverse, up_y, low_y, [toward(k) for k in range(9)]


def field_kernel(
    rows_ref, diag_ref, edge_ref, mask_ref,
    field_ref, part_ref, halo_ref, edges_ref, own_ref, load_ref,
):
    senders = rows_ref.shape[0]
    groups = (rows_ref.shape[1] - STRIPS) // 5
    cells_x = field_ref.shape[1]
    half = (cells_x + 2 * PAD) // 2
    own = cells_x // 2

    load_ref[...] = jnp.zeros_like(load_ref)
    here = lax.axis_index("gx")
    first_row = (here * cells_x - PAD).astype(F32)

    def add_rows(sender, carry):
        row = rows_ref[sender, 3 * groups : 4 * groups, :] - first_row
        column = rows_ref[sender, 4 * groups : 5 * groups, :]
        lower = row >= float(half)
        place = jnp.where(lower, row - float(half), row)
        column = jnp.where(lower, column + float(LANES), column)
        at_row = float_iota((half, LANES), 0).astype(BF16)
        at_column = float_iota((2 * LANES, LANES), 0).astype(BF16)
        parts = [
            two_parts(rows_ref[sender, c * groups : (c + 1) * groups, :]) for c in range(3)
        ]
        zero, one = jnp.zeros((), BF16), jnp.ones((), BF16)
        lefts, rights = [], []
        for group in range(groups):
            line = slice(group, group + 1)
            match = at_row == stretched(place[line], half)
            lefts.append(
                jnp.concatenate(
                    [
                        jnp.where(match, stretched(parts[c][which][line], half), zero)
                        for which in range(2)
                        for c in range(3)
                    ],
                    axis=0,
                )
            )
            rights.append(
                jnp.where(at_column == stretched(column[line], 2 * LANES), one, zero)
            )
        load_ref[...] += lax.dot_general(
            jnp.concatenate(lefts, axis=1),
            jnp.concatenate(rights, axis=1),
            (((1,), (1,)), ((), ())),
            preferred_element_type=F32,
        )
        return carry

    lax.fori_loop(0, senders, add_rows, 0, unroll=min(senders, 8))

    def load_rows(comp, first, last, second_half):
        lanes = slice(LANES, 2 * LANES) if second_half else slice(0, LANES)
        return (
            load_ref[comp * half + first : comp * half + last, lanes]
            + load_ref[(3 + comp) * half + first : (3 + comp) * half + last, lanes]
        )

    field = []
    for comp in range(3):
        load = jnp.concatenate(
            [load_rows(comp, PAD, half, False), load_rows(comp, 0, half - PAD, True)], axis=0
        )
        field.append(load / diag_ref[4 * comp])
        field_ref[comp] = field[comp]
    beyond = half - PAD
    near_before = [load_rows(c, PAD - 1, PAD, False) for c in range(3)]
    far_before = [load_rows(c, PAD - 2, PAD - 1, False) for c in range(3)]
    near_after = [load_rows(c, beyond, beyond + 1, True) for c in range(3)]

    up_x = masked_product(edge_ref, mask_ref, 0, field)
    low_x = masked_product(edge_ref, mask_ref, 1, field)
    base = 5 * groups
    before = row_before(
        strip(rows_ref, jnp.maximum(here - 1, 0), base, here > 0),
        near_before, far_before, [p[:1] for p in low_x],
    )
    after = strip(
        rows_ref, jnp.minimum(here + 1, senders - 1), base + LOWER, here < senders - 1
    )
    after = product(after(3), [ratio(near_after[c], after(0)(c)) for c in range(3)])
    total = off_diagonal(lambda k: diag_ref[k], field)
    total = [total[c] + rows_moved(up_x[c], before[1][c], 1) for c in range(3)]
    total = [total[c] + rows_moved(low_x[c], after[c], -1) for c in range(3)]
    up_y = masked_product(edge_ref, mask_ref, 2, field)
    low_y = masked_product(edge_ref, mask_ref, 3, field)
    total = [
        total[c] + lanes_moved(up_y[c], 0.0, 1) + lanes_moved(low_y[c], 0.0, -1)
        for c in range(3)
    ]
    inverse = [1.0 / diag_ref[4 * c] for c in range(3)]
    part = [total[c] * inverse[c] for c in range(3)]
    for comp in range(3):
        part_ref[comp] = part[comp]
    for slot, which in enumerate((0, 2, 3)):
        for comp in range(3):
            at = 3 * slot + comp
            halo_ref[at : at + 1, :] = before[which][comp]
    for k in range(9):
        halo_ref[9 + k : 10 + k, :] = before[6][k]
    halo_ref[18:, :] = jnp.zeros((6, LANES), F32)

    def columns(lane, along_y, halo_slot):
        ahead = cells_x
        packed = jnp.zeros((cells_x, LANES), F32)
        extra = jnp.zeros((8, LANES), F32)
        at = iota((cells_x, LANES), 1)
        at_extra = iota((8, LANES), 1)
        which_row = iota((8, LANES), 0)
        for slot, fields in enumerate((field, along_y, part, inverse)):
            for comp in range(3):
                column = fields[comp][:, lane : lane + 1]
                packed = jnp.where(at == 3 * slot + comp, column, packed)
        for comp in range(3):
            first = before[halo_slot][comp][:, lane : lane + 1]
            extra = jnp.where((at_extra == 3 + comp) & (which_row == 0), first, extra)
        rest = jnp.zeros((LANES - ahead - 8, LANES), F32)
        whole = jnp.concatenate([packed, extra, rest], axis=0)
        return whole.T[:16]

    first_column = columns(0, low_y, 5)
    last_column = columns(LANES - 1, up_y, 4)
    own_ref[0] = first_column
    own_ref[1] = last_column
    edges_ref[...] = jnp.zeros_like(edges_ref)
    across = lax.axis_index("gy")

    @pl.when(across < edges_ref.shape[0] - 1)
    def _():
        edges_ref[across + 1] = last_column

    @pl.when(across > 0)
    def _():
        edges_ref[across - 1] = first_column


def bernstein(coord):
    other = 1.0 - coord
    return [
        other * other * other,
        3.0 * coord * other * other,
        3.0 * coord * coord * other,
        coord * coord * coord,
    ]


def weight_table(u, v, w):
    first, second, third = bernstein(u), bernstein(v), bernstein(w)
    line = iota((8, u.shape[1]), 0)
    inner = line & 3
    along = jnp.where(
        inner == 0,
        third[0],
        jnp.where(inner == 1, third[1], jnp.where(inner == 2, third[2], third[3])),
    )
    pair = jnp.concatenate(
        [
            jnp.where(line < 4, second[0], second[1]) * along,
            jnp.where(line < 4, second[2], second[3]) * along,
        ],
        axis=0,
    )
    return jnp.concatenate([pair * first[i] for i in range(4)], axis=0)


def add_tiles(out_ref, tile_ref, high, low, weights):
    first_half = iota((4, LANES), 1) < LANES // 2
    tiles = tile_ref.shape[0]
    points = high.shape[1] // tiles
    for tile in range(tiles):
        lanes = slice(tile * points, (tile + 1) * points)
        one, two = high[:, lanes], low[:, lanes]
        left = jnp.concatenate(
            [
                jnp.concatenate([one, one], axis=1),
                jnp.concatenate([two, jnp.zeros_like(two)], axis=1),
            ],
            axis=0,
        ).astype(BF16)
        right = weights(tile)
        term = lax.dot_general(
            left,
            jnp.concatenate([right, right], axis=0),
            (((1,), (1,)), ((), ())),
            preferred_element_type=F32,
        )
        term = term[:8] + term[8:]
        out_ref[tile_ref[tile]] += jnp.where(first_half, term[:4], term[4:])


def box_kernel(
    tile_ref, field_ref, part_ref, node_ref, param_ref,
    box_ref, weights_ref, columns_ref, *, tile_points,
):
    cells_x = field_ref.shape[1]
    own = cells_x // 2
    field = [field_ref[c] for c in range(3)]
    part = [part_ref[c] for c in range(3)]
    order = [field[0], part[0], field[2], field[1], part[1], part[2]]
    folded = [two_parts(jnp.concatenate([f[:own], f[own:]], axis=1)) for f in order]
    table = jnp.concatenate(
        [folded[f][which] for which in range(2) for f in range(6)], axis=0
    ).astype(BF16)
    points = param_ref.shape[1]
    pieces = CHUNK // LANES
    zero, one = jnp.zeros((), BF16), jnp.ones((), BF16)
    at_node = float_iota((2 * LANES, CHUNK), 0).astype(BF16)
    nothing = jnp.zeros((1, CHUNK), F32)
    highs, lows = [], []
    for chunk in range(points // CHUNK):
        node = jnp.concatenate(
            [node_ref[chunk * pieces + k : chunk * pieces + k + 1, :] for k in range(pieces)],
            axis=1,
        )
        row = lax.shift_right_logical(node, 7)
        column = node & (LANES - 1)
        lanes = slice(chunk * CHUNK, (chunk + 1) * CHUNK)
        at_edge = jnp.where(
            column == 0, row, jnp.where(column == LANES - 1, row + cells_x, -1)
        ).astype(F32)
        columns_ref[:, lanes] = jnp.where(
            at_node[: 2 * cells_x] == stretched(at_edge, 2 * cells_x), one, zero
        )
        place = column + jnp.where(row >= own, LANES, 0)
        row = jnp.where(row >= own, row - own, row)
        pick = jnp.where(at_node == stretched(place.astype(F32), 2 * LANES), one, zero)
        read = jnp.dot(table, pick, preferred_element_type=F32)
        read = read[: 6 * own] + read[6 * own :]
        here = iota((own, CHUNK), 0) == row
        values = [
            jnp.sum(
                jnp.where(here, read[f * own : (f + 1) * own], 0.0), axis=0, keepdims=True
            )
            for f in range(6)
        ]
        high, low = two_parts(
            jnp.concatenate(values[:3] + [nothing] + values[3:] + [nothing], axis=0)
        )
        highs.append(high)
        lows.append(low)
        weights = two_parts(
            weight_table(param_ref[0:1, lanes], param_ref[1:2, lanes], param_ref[2:3, lanes])
        )
        for k in range(CHUNK // tile_points):
            tile = slice(k * tile_points, (k + 1) * tile_points)
            weights_ref[chunk * (CHUNK // tile_points) + k] = jnp.concatenate(
                [weights[0][:, tile], weights[1][:, tile]], axis=1
            ).astype(BF16)
    box_ref[...] = jnp.zeros_like(box_ref)
    add_tiles(
        box_ref,
        tile_ref,
        jnp.concatenate(highs, axis=1),
        jnp.concatenate(lows, axis=1),
        lambda tile: weights_ref[tile],
    )


def sums_kernel(
    tile_ref, edges_ref, own_ref, field_ref, part_ref, halo_ref,
    diag_ref, edge_ref, mask_ref, box_ref, weights_ref, columns_ref,
    quotient_ref, out_ref,
):
    cells_x = field_ref.shape[1]
    targets = out_ref.shape[0]

    def arrived(sender):
        rest = jnp.zeros((LANES - 16, LANES), F32)
        return jnp.concatenate([edges_ref[sender], rest], axis=0).T

    across = lax.axis_index("gy")
    low = arrived(jnp.maximum(across - 1, 0))
    high = arrived(jnp.minimum(across + 1, edges_ref.shape[0] - 1))
    lane = iota((cells_x, LANES), 1)

    def column(source, slot, comp):
        return source[:cells_x, 3 * slot + comp : 3 * slot + comp + 1]

    field = [field_ref[c] for c in range(3)]
    scale = [diag_ref[4 * c] for c in range(3)]
    toward_high = masked_product(edge_ref, mask_ref, 2, field)
    toward_low = masked_product(edge_ref, mask_ref, 3, field)
    quotient, low_edge, high_edge = [], [], []
    for c in range(3):
        entering = jnp.where(
            lane == 0,
            column(low, 1, c),
            jnp.where(lane == LANES - 1, column(high, 1, c), 0.0),
        )
        quotient.append(part_ref[c] + entering / scale[c])
        low_edge.append(column(low, 2, c) + column(low, 3, c) * toward_low[c][:, :1])
        high_edge.append(column(high, 2, c) + column(high, 3, c) * toward_high[c][:, -1:])
    for c in range(3):
        quotient_ref[c] = quotient[c]
    lane_row = iota((1, LANES), 1)
    before, before_quotient = [], []
    for c in range(3):
        entering = jnp.where(
            lane_row == 0,
            low[cells_x : cells_x + 1, 3 + c : 4 + c],
            jnp.where(lane_row == LANES - 1, high[cells_x : cells_x + 1, 3 + c : 4 + c], 0.0),
        )
        before.append(halo_ref[c : c + 1, :])
        before_quotient.append(
            halo_ref[3 + c : 4 + c, :] + entering * halo_ref[6 + c : 7 + c, :]
        )

    first_sum = sum(field[c] * scale[c] * field[c] for c in range(3))
    second_sum = sum(field[c] * scale[c] * quotient[c] for c in range(3))
    third_sum = sum(quotient[c] * scale[c] * quotient[c] for c in range(3))
    within = off_diagonal(lambda k: diag_ref[k], quotient)
    fourth_sum = sum(within[c] * field[c] for c in range(3))
    fifth_sum = sum(within[c] * quotient[c] for c in range(3))
    for direction in range(4):
        moving = masked_product(edge_ref, mask_ref, direction, quotient)
        for c in range(3):
            if direction == 0:
                a = rows_moved(field[c], 0.0, -1)
                b = rows_moved(quotient[c], 0.0, -1)
            elif direction == 1:
                a = rows_moved(field[c], before[c], 1)
                b = rows_moved(quotient[c], before_quotient[c], 1)
            elif direction == 2:
                a = lanes_moved(field[c], column(high, 0, c), -1)
                b = lanes_moved(quotient[c], high_edge[c], -1)
            else:
                a = lanes_moved(field[c], column(low, 0, c), 1)
                b = lanes_moved(quotient[c], low_edge[c], 1)
            fourth_sum = fourth_sum + moving[c] * a
            fifth_sum = fifth_sum + moving[c] * b
    incoming = product(lambda k: halo_ref[9 + k : 10 + k, :], before_quotient)
    extra = [0.0, 0.0, 0.0]
    extra.append(sum(incoming[c] * field[c][:1] for c in range(3)))
    extra.append(sum(incoming[c] * quotient[c][:1] for c in range(3)))
    sums = jnp.zeros((1, LANES), F32)
    for k, value in enumerate((first_sum, second_sum, third_sum, fourth_sum, fifth_sum)):
        line = jnp.sum(value, axis=0, keepdims=True) + extra[k]
        sums = jnp.where(lane_row == k, jnp.sum(line, axis=1, keepdims=True), sums)

    across_low = edges_ref[jnp.maximum(across - 1, 0)]
    across_high = edges_ref[jnp.minimum(across + 1, edges_ref.shape[0] - 1)]
    added = []
    for c in range(3):
        first = across_low[3 + c : 4 + c] * own_ref[0, 9 + c : 10 + c, :]
        second = across_high[3 + c : 4 + c] * own_ref[1, 9 + c : 10 + c, :]
        added.append(
            jnp.where(lane_row < cells_x, first, pltpu.roll(second, cells_x, 1))
        )
    none = jnp.zeros((1, LANES), F32)
    added = jnp.concatenate(
        [none, added[0], none, none, none, added[1], added[2], none], axis=0
    )
    added = jnp.concatenate(two_parts(added), axis=0).astype(BF16)
    read = jnp.dot(added, columns_ref[...], preferred_element_type=F32)
    high, low = two_parts(read[:8] + read[8:])
    out_ref[...] = box_ref[...]
    add_tiles(out_ref, tile_ref, high, low, lambda tile: weights_ref[tile])
    for box in range(targets):
        out_ref[box, 3:4, :] = sums


def result_kernel(got_ref, field_ref, quotient_ref, solution_ref, gradient_ref):
    total = jnp.sum(got_ref[...], axis=0)
    rho, a, b, t, u = [total[3:4, k : k + 1] for k in range(5)]
    ratio = a / rho
    norm = rho + a
    step = rho / norm
    rest = jnp.maximum(b - a * ratio, 0.0)
    beta = step * step * rest / rho
    rest_image = (b + u) - ratio * (a + b + a + t) + ratio * ratio * norm
    cross = (a + t) - ratio * norm
    curve = step * step * rest_image - step * beta * (rest + cross) + beta * beta * norm
    second = jnp.where(
        curve > 0.0, step * step * rest / jnp.where(curve > 0.0, curve, 1.0), 0.0
    )
    of_field = step + second * (beta + step * ratio)
    of_quotient = -(step * second)
    for c in range(3):
        solution_ref[c] = of_field * field_ref[c] + of_quotient * quotient_ref[c]
    gradient_ref[:, :LANES] = of_field * total[0:1] + of_quotient * total[1:2]
    gradient_ref[:, LANES:] = (
        of_field * total[2:3, : LANES // 2] + of_quotient * total[2:3, LANES // 2 :]
    )


def per_device(
    diag_blocks, edge_blocks, edge_mask, src_values, src_owner, src_node, src_count,
    surf_node, surf_param, tile_box,
):
    cells_x, cells_y = diag_blocks.shape[1:]
    width_gx, width_gy = lax.axis_size("gx"), lax.axis_size("gy")
    devices = width_gx * width_gy
    groups = src_node.shape[0] // LANES
    whole = functools.partial(jax.ShapeDtypeStruct, dtype=F32)

    cells = 5 * groups + STRIPS
    i32 = jnp.int32
    rows = pl.pallas_call(
        pack_kernel,
        in_specs=[HBM] * 7,
        out_specs=VMEM,
        out_shape=whole((cells, LANES)),
        scratch_shapes=[
            pltpu.SMEM((1,), i32),
            pltpu.VMEM(src_values.shape, F32),
            pltpu.VMEM((groups, LANES), i32),
            pltpu.VMEM((groups, LANES), i32),
            pltpu.VMEM((9, 8, cells_y), F32),
            pltpu.VMEM((9, 8, cells_y), F32),
            pltpu.VMEM((9, 8, cells_y), F32),
            pltpu.VMEM((4, 9, 8, cells_y), F32),
            pltpu.VMEM((8, cells_y), i32),
            pltpu.VMEM((4, 8, cells_y), i32),
            pltpu.SemaphoreType.DMA((10,)),
        ],
        compiler_params=pltpu.CompilerParams(vmem_limit_bytes=PACK_VMEM),
        name="pack_rows_and_edges",
    )(
        src_count, src_values,
        src_owner.reshape(groups, LANES), src_node.reshape(groups, LANES),
        diag_blocks, edge_blocks, edge_mask,
    )
    rows = lax.all_gather(rows, "gx")

    nodes = (3, cells_x, cells_y)
    frame = cells_x + 2 * PAD
    field, part, halo, edges, own = pl.pallas_call(
        field_kernel,
        in_specs=[VMEM] * 4,
        out_specs=[VMEM] * 5,
        out_shape=[
            whole(nodes), whole(nodes), whole((24, cells_y)), whole((width_gy, 16, LANES)),
            whole((2, 16, LANES)),
        ],
        scratch_shapes=[pltpu.VMEM((3 * frame, 2 * LANES), F32)],
        compiler_params=PARAMS,
        name="load_and_first_product",
    )(rows, diag_blocks, edge_blocks, edge_mask)
    edges = lax.all_to_all(edges, "gy", split_axis=0, concat_axis=0, tiled=True)

    points, tiles = surf_node.shape[0], tile_box.shape[0]
    boxes = (devices, 4, LANES)
    box_part, weights, columns = pl.pallas_call(
        functools.partial(box_kernel, tile_points=points // tiles),
        in_specs=[SMEM] + [VMEM] * 4,
        out_specs=[VMEM] * 3,
        out_shape=[
            whole(boxes),
            jax.ShapeDtypeStruct((tiles, 64, 2 * points // tiles), BF16),
            jax.ShapeDtypeStruct((2 * cells_x, points), BF16),
        ],
        compiler_params=PARAMS,
        cost_estimate=pl.CostEstimate(
            flops=10**9, bytes_accessed=4 * 10**6, transcendentals=0
        ),
        name="box_parts",
    )(tile_box, field, part, surf_node.reshape(points // LANES, LANES), surf_param)

    quotient, partial = pl.pallas_call(
        sums_kernel,
        in_specs=[SMEM] + [VMEM] * 11,
        out_specs=[VMEM] * 2,
        out_shape=[whole(nodes), whole(boxes)],
        compiler_params=PARAMS,
        name="sums_and_halo_parts",
    )(
        tile_box, edges, own, field, part, halo, diag_blocks, edge_blocks, edge_mask,
        box_part, weights, columns,
    )
    got = lax.all_to_all(partial, ("gx", "gy"), split_axis=0, concat_axis=0, tiled=True)
    return pl.pallas_call(
        result_kernel,
        in_specs=[VMEM] * 3,
        out_specs=[VMEM] * 2,
        out_shape=[whole(nodes), whole((1, 192))],
        compiler_params=PARAMS,
        name="steps_and_outputs",
    )(got, field, quotient)


def solution(mesh):
    return jax.shard_map(
        per_device,
        mesh=mesh,
        in_specs=(
            P(None, "gx", "gy"),
            P(None, None, "gx", "gy"),
            P(None, "gx", "gy"),
            P(None, ("gx", "gy")),
            P(("gx", "gy"), None),
            P(("gx", "gy")),
            P(("gx", "gy")),
            P(("gx", "gy")),
            P(None, ("gx", "gy")),
            P(("gx", "gy")),
        ),
        out_specs=(P(None, "gx", "gy"), P(("gx", "gy"), None)),
        check_vma=False,
    )
```

```python
import functools

import jax
import jax.numpy as jnp
from jax import lax
from jax.experimental import pallas as pl
from jax.experimental.pallas import tpu as pltpu
from jax.sharding import PartitionSpec as P

F32 = jnp.float32
BF16 = jnp.bfloat16
PAD = 16
NOWHERE = -(1 << 20)
LANES = 128
NEAR = 16
STRIP = 40
CHUNK = 256
PACK_VMEM = 60 * 1000 * 1000
PARAMS = pltpu.CompilerParams(vmem_limit_bytes=24 * 1024 * 1024)

VMEM = pl.BlockSpec(memory_space=pltpu.VMEM)
SMEM = pl.BlockSpec(memory_space=pltpu.SMEM)
HBM = pl.BlockSpec(memory_space=pltpu.HBM)


def iota(shape, dim):
    return lax.broadcasted_iota(jnp.int32, shape, dim)


def float_iota(shape, dim):
    return iota(shape, dim).astype(F32)


def two_parts(value):
    high = value.astype(BF16).astype(F32)
    return high, value - high


def product(block, field):
    return [
        block(row) * field[0] + block(3 + row) * field[1] + block(6 + row) * field[2]
        for row in range(3)
    ]


def off_diagonal(block, field):
    return [
        sum(block(3 * i + row) * field[i] for i in range(3) if i != row) for row in range(3)
    ]


def masked_product(edge_ref, mask_ref, direction, field):
    mask = mask_ref[direction].astype(F32)
    return [mask * part for part in product(lambda k: edge_ref[direction, k], field)]


def rows_moved(field, edge_row, step):
    size = field.shape[0]
    at = iota(field.shape, 0)
    moved = pltpu.roll(field, step % size, 0)
    return jnp.where(at == (0 if step == 1 else size - 1), edge_row, moved)


def lanes_moved(field, edge_column, step):
    size = field.shape[1]
    at = iota(field.shape, 1)
    moved = pltpu.roll(field, step % size, 1)
    return jnp.where(at == (0 if step == 1 else size - 1), edge_column, moved)


def pack_kernel(
    count_in, values_in, owner_in, node_in, diag_in, edge_in, mask_in, rows_ref, strip_ref,
    count_ref, values_ref, owner_ref, node_ref, diag_low, diag_high, edge_low, edge_high,
    mask_low, mask_high, arrived,
):
    targets = rows_ref.shape[0]
    groups = owner_ref.shape[0]
    cells_x = diag_in.shape[1]
    top = pl.ds(cells_x - 8, 8)
    copies = [
        pltpu.make_async_copy(source, target, arrived.at[k])
        for k, (source, target) in enumerate(
            (
                (edge_in.at[1, :, 0:8], edge_low),
                (edge_in.at[:, :, top], edge_high),
                (diag_in.at[:, 0:8], diag_low),
                (diag_in.at[:, top], diag_high),
                (mask_in.at[1, 0:8], mask_low),
                (mask_in.at[:, top], mask_high),
                (values_in, values_ref),
                (owner_in, owner_ref),
                (node_in, node_ref),
                (count_in, count_ref),
            )
        )
    ]
    for copy in copies:
        copy.start()
    near = 4 * groups
    for target in range(targets):
        rows_ref[target, near:, :] = jnp.zeros((NEAR, LANES), F32)
    for copy in copies:
        copy.wait()
    order = iota((groups, LANES), 0) * LANES + iota((groups, LANES), 1)
    node = node_ref[...]
    frame = cells_x + 2 * PAD
    row = owner_ref[...] * cells_x + lax.shift_right_logical(node, 7)
    row = jnp.where(order < count_ref[0], row, NOWHERE)
    column = node & (LANES - 1)
    for comp in range(3):
        for group in range(groups):
            piece = values_ref[comp : comp + 1, group * LANES : (group + 1) * LANES]
            for target in range(targets):
                rows_ref[target, comp * groups + group : comp * groups + group + 1, :] = piece
    for target in range(targets):
        line = row - (target * cells_x - PAD)
        inside = (line >= 0) & (line < frame)
        index = jnp.where(inside, line * LANES + column, -1)
        rows_ref[target, 3 * groups : 4 * groups, :] = index.astype(F32)

    def block(edge, mask, direction, at):
        present = mask[direction, at : at + 1, :].astype(F32)
        return [edge[direction, k, at : at + 1, :] * present for k in range(9)]

    up_y, low_y = block(edge_high, mask_high, 2, 7), block(edge_high, mask_high, 3, 7)
    later = [diag_high[k, 7:8, :] for k in range(9) if k % 4]
    later += up_y + low_y + block(edge_high, mask_high, 0, 6)
    later += [diag_high[4 * k, 6:7, :] for k in range(3)]
    for k, value in enumerate(later):
        strip_ref[k : k + 1, :] = value
    strip_ref[len(later) :, :] = jnp.zeros((STRIP - len(later), LANES), F32)

    here = lax.axis_index("gx")

    @pl.when(here < targets - 1)
    def _():
        def put(slot, value):
            rows_ref[here + 1, near + slot : near + slot + 1, :] = value

        for k in range(3):
            put(k, diag_high[4 * k, 7:8, :])
        for k, value in enumerate(block(edge_high, mask_high, 0, 7)):
            put(3 + k, value)
        corners = jnp.zeros((1, LANES), F32)
        lane = iota((1, LANES), 1)
        for k in range(9):
            corners = jnp.where(lane == k, up_y[k][:, LANES - 1 :], corners)
            corners = jnp.where(lane == 9 + k, low_y[k][:, :1], corners)
        put(12, corners)

    @pl.when(here > 0)
    def _():
        def put(slot, value):
            rows_ref[here - 1, near + slot : near + slot + 1, :] = value

        for k in range(3):
            put(k, diag_low[4 * k, 0:1, :])
        present = mask_low[0:1, :].astype(F32)
        for k in range(9):
            put(3 + k, edge_low[k, 0:1, :] * present)


def stretched(row, count):
    tile = jnp.broadcast_to(row, (16, row.shape[1])).astype(BF16)
    return jnp.concatenate([tile] * (count // 16), axis=0)


def ratio(value, scale):
    return jnp.where(scale > 0.0, value / jnp.where(scale > 0.0, scale, 1.0), 0.0)


def field_kernel(
    rows_ref, diag_ref, edge_ref, mask_ref,
    field_ref, part_ref, halo_ref, edges_ref, own_ref, load_ref,
):
    senders = rows_ref.shape[0]
    groups = (rows_ref.shape[1] - NEAR) // 4
    cells_x = field_ref.shape[1]
    half = (cells_x + 2 * PAD) // 2
    own = cells_x // 2

    load_ref[...] = jnp.zeros_like(load_ref)
    here = lax.axis_index("gx")

    def add_rows(sender, carry):
        index = rows_ref[sender, 3 * groups : 4 * groups, :]
        split = float(half * LANES)
        index, shift = (
            jnp.where(index >= split, index - split, index),
            jnp.where(index >= split, float(LANES), 0.0),
        )
        place = jnp.floor(index * (1.0 / LANES))
        column = index - place * float(LANES) + shift
        at_row = float_iota((half, LANES), 0).astype(BF16)
        at_column = float_iota((2 * LANES, LANES), 0).astype(BF16)
        parts = [
            two_parts(rows_ref[sender, c * groups : (c + 1) * groups, :]) for c in range(3)
        ]
        zero, one = jnp.zeros((), BF16), jnp.ones((), BF16)
        lefts, rights = [], []
        for group in range(groups):
            line = slice(group, group + 1)
            match = at_row == stretched(place[line], half)
            lefts.append(
                jnp.concatenate(
                    [
                        jnp.where(match, stretched(parts[c][which][line], half), zero)
                        for which in range(2)
                        for c in range(3)
                    ],
                    axis=0,
                )
            )
            rights.append(
                jnp.where(at_column == stretched(column[line], 2 * LANES), one, zero)
            )
        load_ref[...] += lax.dot_general(
            jnp.concatenate(lefts, axis=1),
            jnp.concatenate(rights, axis=1),
            (((1,), (1,)), ((), ())),
            preferred_element_type=F32,
        )
        return carry

    lax.fori_loop(0, senders, add_rows, 0, unroll=min(senders, 8))

    def load_rows(comp, first, last, second_half):
        lanes = slice(LANES, 2 * LANES) if second_half else slice(0, LANES)
        return (
            load_ref[comp * half + first : comp * half + last, lanes]
            + load_ref[(3 + comp) * half + first : (3 + comp) * half + last, lanes]
        )

    field = []
    for comp in range(3):
        load = jnp.concatenate(
            [load_rows(comp, PAD, half, False), load_rows(comp, 0, half - PAD, True)], axis=0
        )
        field.append(load / diag_ref[4 * comp])
        field_ref[comp] = field[comp]
    beyond = half - PAD
    near_before = [load_rows(c, PAD - 1, PAD, False) for c in range(3)]
    far_before = [load_rows(c, PAD - 2, PAD - 1, False) for c in range(3)]
    near_after = [load_rows(c, beyond, beyond + 1, True) for c in range(3)]

    up_x = masked_product(edge_ref, mask_ref, 0, field)
    low_x = masked_product(edge_ref, mask_ref, 1, field)
    base = 4 * groups

    def neighbour(sender, load):
        def entry(k):
            return rows_ref[sender, base + k : base + k + 1, :]

        scale, toward = [entry(k) for k in range(3)], [entry(3 + k) for k in range(9)]
        beside = [ratio(load[c], scale[c]) for c in range(3)]
        return scale, toward, beside, product(lambda k: toward[k], beside)

    lower = jnp.maximum(here - 1, 0)
    before = neighbour(lower, near_before)
    after = neighbour(jnp.minimum(here + 1, senders - 1), near_after)
    rows = before[2] + [ratio(1.0, scale) for scale in before[0]]
    rows += [p[:1] for p in low_x] + before[1] + far_before
    for k, value in enumerate(rows):
        halo_ref[k : k + 1, :] = value
    halo_ref[len(rows) :, :] = jnp.zeros((halo_ref.shape[0] - len(rows), LANES), F32)
    lane_row = iota((1, LANES), 1)
    ends = jnp.zeros((1, LANES), F32)
    for i in range(3):
        for a in range(3):
            ends = jnp.where(lane_row == 3 * i + a, before[2][i][:, LANES - 1 :], ends)
            ends = jnp.where(lane_row == 9 + 3 * i + a, before[2][i][:, :1], ends)
    ends = ends * rows_ref[lower, base + 12 : base + 13, :]
    ends = ends + pltpu.roll(ends, LANES - 3, 1) + pltpu.roll(ends, LANES - 6, 1)

    total = off_diagonal(lambda k: diag_ref[k], field)
    total = [total[c] + rows_moved(up_x[c], before[3][c], 1) for c in range(3)]
    total = [total[c] + rows_moved(low_x[c], after[3][c], -1) for c in range(3)]
    up_y = masked_product(edge_ref, mask_ref, 2, field)
    low_y = masked_product(edge_ref, mask_ref, 3, field)
    total = [
        total[c] + lanes_moved(up_y[c], 0.0, 1) + lanes_moved(low_y[c], 0.0, -1)
        for c in range(3)
    ]
    inverse = [1.0 / diag_ref[4 * c] for c in range(3)]
    part = [total[c] * inverse[c] for c in range(3)]
    for comp in range(3):
        part_ref[comp] = part[comp]
    def columns(lane, along_y, end):
        packed = jnp.zeros((cells_x, LANES), F32)
        at = iota((cells_x, LANES), 1)
        for slot, fields in enumerate((field, along_y, part, inverse)):
            for comp in range(3):
                column = fields[comp][:, lane : lane + 1]
                packed = jnp.where(at == 3 * slot + comp, column, packed)
        rest = jnp.zeros((LANES - cells_x, LANES), F32)
        turned = jnp.concatenate([packed, rest], axis=0).T[:16]
        at = iota((16, LANES), 1)
        line = iota((16, LANES), 0)
        for comp in range(3):
            turned = jnp.where(
                (line == 3 + comp) & (at == cells_x),
                ends[:, end + comp : end + comp + 1],
                turned,
            )
        return turned

    first_column = columns(0, low_y, 9)
    last_column = columns(LANES - 1, up_y, 0)
    own_ref[0] = first_column
    own_ref[1] = last_column
    edges_ref[...] = jnp.zeros_like(edges_ref)
    across = lax.axis_index("gy")

    @pl.when(across < edges_ref.shape[0] - 1)
    def _():
        edges_ref[across + 1] = last_column

    @pl.when(across > 0)
    def _():
        edges_ref[across - 1] = first_column


def bernstein(coord):
    other = 1.0 - coord
    return [
        other * other * other,
        3.0 * coord * other * other,
        3.0 * coord * coord * other,
        coord * coord * coord,
    ]


def weight_table(u, v, w):
    first, second, third = bernstein(u), bernstein(v), bernstein(w)
    line = iota((8, u.shape[1]), 0)
    inner = line & 3
    along = jnp.where(
        inner == 0,
        third[0],
        jnp.where(inner == 1, third[1], jnp.where(inner == 2, third[2], third[3])),
    )
    pair = jnp.concatenate(
        [
            jnp.where(line < 4, second[0], second[1]) * along,
            jnp.where(line < 4, second[2], second[3]) * along,
        ],
        axis=0,
    )
    return jnp.concatenate([pair * first[i] for i in range(4)], axis=0)


def add_tiles(out_ref, tile_ref, high, low, weights):
    first_half = iota((4, LANES), 1) < LANES // 2
    tiles = tile_ref.shape[0]
    points = high.shape[1] // tiles
    for tile in range(tiles):
        lanes = slice(tile * points, (tile + 1) * points)
        one, two = high[:, lanes], low[:, lanes]
        left = jnp.concatenate(
            [
                jnp.concatenate([one, one], axis=1),
                jnp.concatenate([two, jnp.zeros_like(two)], axis=1),
            ],
            axis=0,
        ).astype(BF16)
        right = weights(tile)
        term = lax.dot_general(
            left,
            jnp.concatenate([right, right], axis=0),
            (((1,), (1,)), ((), ())),
            preferred_element_type=F32,
        )
        term = term[:8] + term[8:]
        out_ref[tile_ref[tile]] += jnp.where(first_half, term[:4], term[4:])


def quotient_before(halo_ref, strip_ref, before_ref):
    def rows(ref, first, count):
        return [ref[first + k : first + k + 1, :] for k in range(count)]

    beside, inverse, entering = rows(halo_ref, 0, 3), rows(halo_ref, 3, 3), rows(halo_ref, 6, 3)
    far_load, within = rows(halo_ref, 18, 3), rows(strip_ref, 0, 6)
    far_scale = rows(strip_ref, 33, 3)
    far = [ratio(far_load[c], far_scale[c]) for c in range(3)]
    whole_block = [None, *within[:3], None, *within[3:], None]
    total = off_diagonal(lambda k: whole_block[k], beside)
    from_far = product(lambda k: strip_ref[24 + k : 25 + k, :], far)
    up_y = product(lambda k: strip_ref[6 + k : 7 + k, :], beside)
    low_y = product(lambda k: strip_ref[15 + k : 16 + k, :], beside)
    for c in range(3):
        before_ref[c : c + 1, :] = inverse[c] * (
            total[c]
            + from_far[c]
            + entering[c]
            + lanes_moved(up_y[c], 0.0, 1)
            + lanes_moved(low_y[c], 0.0, -1)
        )
    before_ref[3:, :] = jnp.zeros((before_ref.shape[0] - 3, LANES), F32)


def box_kernel(
    tile_ref, field_ref, part_ref, node_ref, param_ref, halo_ref, strip_ref,
    box_ref, weights_ref, columns_ref, before_ref, *, tile_points,
):
    cells_x = field_ref.shape[1]
    own = cells_x // 2
    quotient_before(halo_ref, strip_ref, before_ref)
    field = [field_ref[c] for c in range(3)]
    part = [part_ref[c] for c in range(3)]
    order = [field[0], part[0], field[2], field[1], part[1], part[2]]
    folded = [two_parts(jnp.concatenate([f[:own], f[own:]], axis=1)) for f in order]
    table = jnp.concatenate(
        [folded[f][which] for which in range(2) for f in range(6)], axis=0
    ).astype(BF16)
    points = param_ref.shape[1]
    pieces = CHUNK // LANES
    zero, one = jnp.zeros((), BF16), jnp.ones((), BF16)
    at_node = float_iota((2 * LANES, CHUNK), 0).astype(BF16)
    nothing = jnp.zeros((1, CHUNK), F32)
    highs, lows = [], []
    for chunk in range(points // CHUNK):
        node = jnp.concatenate(
            [node_ref[chunk * pieces + k : chunk * pieces + k + 1, :] for k in range(pieces)],
            axis=1,
        )
        row = lax.shift_right_logical(node, 7)
        column = node & (LANES - 1)
        lanes = slice(chunk * CHUNK, (chunk + 1) * CHUNK)
        at_edge = jnp.where(
            column == 0, row, jnp.where(column == LANES - 1, row + cells_x, -1)
        ).astype(F32)
        columns_ref[:, lanes] = jnp.where(
            at_node[: 2 * cells_x] == stretched(at_edge, 2 * cells_x), one, zero
        )
        place = column + jnp.where(row >= own, LANES, 0)
        row = jnp.where(row >= own, row - own, row)
        pick = jnp.where(at_node == stretched(place.astype(F32), 2 * LANES), one, zero)
        read = jnp.dot(table, pick, preferred_element_type=F32)
        read = read[: 6 * own] + read[6 * own :]
        here = iota((own, CHUNK), 0) == row
        values = [
            jnp.sum(
                jnp.where(here, read[f * own : (f + 1) * own], 0.0), axis=0, keepdims=True
            )
            for f in range(6)
        ]
        high, low = two_parts(
            jnp.concatenate(values[:3] + [nothing] + values[3:] + [nothing], axis=0)
        )
        highs.append(high)
        lows.append(low)
        weights = two_parts(
            weight_table(param_ref[0:1, lanes], param_ref[1:2, lanes], param_ref[2:3, lanes])
        )
        for k in range(CHUNK // tile_points):
            tile = slice(k * tile_points, (k + 1) * tile_points)
            weights_ref[chunk * (CHUNK // tile_points) + k] = jnp.concatenate(
                [weights[0][:, tile], weights[1][:, tile]], axis=1
            ).astype(BF16)
    box_ref[...] = jnp.zeros_like(box_ref)
    add_tiles(
        box_ref,
        tile_ref,
        jnp.concatenate(highs, axis=1),
        jnp.concatenate(lows, axis=1),
        lambda tile: weights_ref[tile],
    )


def sums_kernel(
    tile_ref, edges_ref, own_ref, field_ref, part_ref, halo_ref,
    diag_ref, edge_ref, mask_ref, box_ref, weights_ref, columns_ref, before_ref,
    quotient_ref, out_ref,
):
    cells_x = field_ref.shape[1]
    targets = out_ref.shape[0]

    def arrived(sender):
        rest = jnp.zeros((LANES - 16, LANES), F32)
        return jnp.concatenate([edges_ref[sender], rest], axis=0).T

    across = lax.axis_index("gy")
    low = arrived(jnp.maximum(across - 1, 0))
    high = arrived(jnp.minimum(across + 1, edges_ref.shape[0] - 1))
    lane = iota((cells_x, LANES), 1)

    def column(source, slot, comp):
        return source[:cells_x, 3 * slot + comp : 3 * slot + comp + 1]

    field = [field_ref[c] for c in range(3)]
    scale = [diag_ref[4 * c] for c in range(3)]
    toward_high = masked_product(edge_ref, mask_ref, 2, field)
    toward_low = masked_product(edge_ref, mask_ref, 3, field)
    quotient, low_edge, high_edge = [], [], []
    for c in range(3):
        entering = jnp.where(
            lane == 0,
            column(low, 1, c),
            jnp.where(lane == LANES - 1, column(high, 1, c), 0.0),
        )
        quotient.append(part_ref[c] + entering / scale[c])
        low_edge.append(column(low, 2, c) + column(low, 3, c) * toward_low[c][:, :1])
        high_edge.append(column(high, 2, c) + column(high, 3, c) * toward_high[c][:, -1:])
    for c in range(3):
        quotient_ref[c] = quotient[c]
    lane_row = iota((1, LANES), 1)
    before, before_quotient = [], []
    for c in range(3):
        entering = jnp.where(
            lane_row == 0,
            low[cells_x : cells_x + 1, 3 + c : 4 + c],
            jnp.where(lane_row == LANES - 1, high[cells_x : cells_x + 1, 3 + c : 4 + c], 0.0),
        )
        before.append(halo_ref[c : c + 1, :])
        before_quotient.append(
            before_ref[c : c + 1, :] + entering * halo_ref[3 + c : 4 + c, :]
        )

    first_sum = sum(field[c] * scale[c] * field[c] for c in range(3))
    second_sum = sum(field[c] * scale[c] * quotient[c] for c in range(3))
    third_sum = sum(quotient[c] * scale[c] * quotient[c] for c in range(3))
    within = off_diagonal(lambda k: diag_ref[k], quotient)
    fourth_sum = sum(within[c] * field[c] for c in range(3))
    fifth_sum = sum(within[c] * quotient[c] for c in range(3))
    for direction in range(4):
        moving = masked_product(edge_ref, mask_ref, direction, quotient)
        for c in range(3):
            if direction == 0:
                a = rows_moved(field[c], 0.0, -1)
                b = rows_moved(quotient[c], 0.0, -1)
            elif direction == 1:
                a = rows_moved(field[c], before[c], 1)
                b = rows_moved(quotient[c], before_quotient[c], 1)
            elif direction == 2:
                a = lanes_moved(field[c], column(high, 0, c), -1)
                b = lanes_moved(quotient[c], high_edge[c], -1)
            else:
                a = lanes_moved(field[c], column(low, 0, c), 1)
                b = lanes_moved(quotient[c], low_edge[c], 1)
            fourth_sum = fourth_sum + moving[c] * a
            fifth_sum = fifth_sum + moving[c] * b
    incoming = product(lambda k: halo_ref[9 + k : 10 + k, :], before_quotient)
    extra = [0.0, 0.0, 0.0]
    extra.append(sum(incoming[c] * field[c][:1] for c in range(3)))
    extra.append(sum(incoming[c] * quotient[c][:1] for c in range(3)))
    sums = jnp.zeros((1, LANES), F32)
    for k, value in enumerate((first_sum, second_sum, third_sum, fourth_sum, fifth_sum)):
        line = jnp.sum(value, axis=0, keepdims=True) + extra[k]
        sums = jnp.where(lane_row == k, jnp.sum(line, axis=1, keepdims=True), sums)

    across_low = edges_ref[jnp.maximum(across - 1, 0)]
    across_high = edges_ref[jnp.minimum(across + 1, edges_ref.shape[0] - 1)]
    added = []
    for c in range(3):
        first = across_low[3 + c : 4 + c] * own_ref[0, 9 + c : 10 + c, :]
        second = across_high[3 + c : 4 + c] * own_ref[1, 9 + c : 10 + c, :]
        added.append(
            jnp.where(lane_row < cells_x, first, pltpu.roll(second, cells_x, 1))
        )
    none = jnp.zeros((1, LANES), F32)
    added = jnp.concatenate(
        [none, added[0], none, none, none, added[1], added[2], none], axis=0
    )
    added = jnp.concatenate(two_parts(added), axis=0).astype(BF16)
    read = jnp.dot(added, columns_ref[...], preferred_element_type=F32)
    high, low = two_parts(read[:8] + read[8:])
    out_ref[...] = box_ref[...]
    add_tiles(out_ref, tile_ref, high, low, lambda tile: weights_ref[tile])
    for box in range(targets):
        out_ref[box, 3:4, :] = sums


def result_kernel(got_ref, field_ref, quotient_ref, solution_ref, gradient_ref):
    total = jnp.sum(got_ref[...], axis=0)
    rho, a, b, t, u = [total[3:4, k : k + 1] for k in range(5)]
    ratio = a / rho
    norm = rho + a
    step = rho / norm
    rest = jnp.maximum(b - a * ratio, 0.0)
    beta = step * step * rest / rho
    rest_image = (b + u) - ratio * (a + b + a + t) + ratio * ratio * norm
    cross = (a + t) - ratio * norm
    curve = step * step * rest_image - step * beta * (rest + cross) + beta * beta * norm
    second = jnp.where(
        curve > 0.0, step * step * rest / jnp.where(curve > 0.0, curve, 1.0), 0.0
    )
    of_field = step + second * (beta + step * ratio)
    of_quotient = -(step * second)
    for c in range(3):
        solution_ref[c] = of_field * field_ref[c] + of_quotient * quotient_ref[c]
    gradient_ref[:, :LANES] = of_field * total[0:1] + of_quotient * total[1:2]
    gradient_ref[:, LANES:] = (
        of_field * total[2:3, : LANES // 2] + of_quotient * total[2:3, LANES // 2 :]
    )


def per_device(
    diag_blocks, edge_blocks, edge_mask, src_values, src_owner, src_node, src_count,
    surf_node, surf_param, tile_box,
):
    cells_x, cells_y = diag_blocks.shape[1:]
    width_gx, width_gy = lax.axis_size("gx"), lax.axis_size("gy")
    devices = width_gx * width_gy
    groups = src_node.shape[0] // LANES
    whole = functools.partial(jax.ShapeDtypeStruct, dtype=F32)

    cells = 4 * groups + NEAR
    i32 = jnp.int32
    rows, strip = pl.pallas_call(
        pack_kernel,
        in_specs=[HBM] * 7,
        out_specs=[VMEM] * 2,
        out_shape=[whole((width_gx, cells, LANES)), whole((STRIP, LANES))],
        scratch_shapes=[
            pltpu.SMEM((1,), i32),
            pltpu.VMEM(src_values.shape, F32),
            pltpu.VMEM((groups, LANES), i32),
            pltpu.VMEM((groups, LANES), i32),
            pltpu.VMEM((9, 8, cells_y), F32),
            pltpu.VMEM((9, 8, cells_y), F32),
            pltpu.VMEM((9, 8, cells_y), F32),
            pltpu.VMEM((4, 9, 8, cells_y), F32),
            pltpu.VMEM((8, cells_y), i32),
            pltpu.VMEM((4, 8, cells_y), i32),
            pltpu.SemaphoreType.DMA((10,)),
        ],
        compiler_params=pltpu.CompilerParams(vmem_limit_bytes=PACK_VMEM),
        name="pack_rows_and_edges",
    )(
        src_count, src_values,
        src_owner.reshape(groups, LANES), src_node.reshape(groups, LANES),
        diag_blocks, edge_blocks, edge_mask,
    )
    rows = lax.all_to_all(rows, "gx", split_axis=0, concat_axis=0, tiled=True)
    strip = lax.ppermute(strip, "gx", [(i, i + 1) for i in range(width_gx - 1)])

    nodes = (3, cells_x, cells_y)
    frame = cells_x + 2 * PAD
    field, part, halo, edges, own = pl.pallas_call(
        field_kernel,
        in_specs=[VMEM] * 4,
        out_specs=[VMEM] * 5,
        out_shape=[
            whole(nodes), whole(nodes), whole((24, cells_y)), whole((width_gy, 16, LANES)),
            whole((2, 16, LANES)),
        ],
        scratch_shapes=[pltpu.VMEM((3 * frame, 2 * LANES), F32)],
        compiler_params=PARAMS,
        name="load_and_first_product",
    )(rows, diag_blocks, edge_blocks, edge_mask)
    edges = lax.all_to_all(edges, "gy", split_axis=0, concat_axis=0, tiled=True)

    points, tiles = surf_node.shape[0], tile_box.shape[0]
    boxes = (devices, 4, LANES)
    box_part, weights, columns, before = pl.pallas_call(
        functools.partial(box_kernel, tile_points=points // tiles),
        in_specs=[SMEM] + [VMEM] * 6,
        out_specs=[VMEM] * 4,
        out_shape=[
            whole(boxes),
            jax.ShapeDtypeStruct((tiles, 64, 2 * points // tiles), BF16),
            jax.ShapeDtypeStruct((2 * cells_x, points), BF16),
            whole((8, LANES)),
        ],
        compiler_params=PARAMS,
        cost_estimate=pl.CostEstimate(
            flops=10**9, bytes_accessed=4 * 10**6, transcendentals=0
        ),
        name="box_parts",
    )(
        tile_box, field, part, surf_node.reshape(points // LANES, LANES), surf_param, halo,
        strip,
    )

    quotient, partial = pl.pallas_call(
        sums_kernel,
        in_specs=[SMEM] + [VMEM] * 12,
        out_specs=[VMEM] * 2,
        out_shape=[whole(nodes), whole(boxes)],
        compiler_params=PARAMS,
        name="sums_and_halo_parts",
    )(
        tile_box, edges, own, field, part, halo, diag_blocks, edge_blocks, edge_mask,
        box_part, weights, columns, before,
    )
    got = lax.all_to_all(partial, ("gx", "gy"), split_axis=0, concat_axis=0, tiled=True)
    return pl.pallas_call(
        result_kernel,
        in_specs=[VMEM] * 3,
        out_specs=[VMEM] * 2,
        out_shape=[whole(nodes), whole((1, 192))],
        compiler_params=PARAMS,
        name="steps_and_outputs",
    )(got, field, quotient)


def solution(mesh):
    return jax.shard_map(
        per_device,
        mesh=mesh,
        in_specs=(
            P(None, "gx", "gy"),
            P(None, None, "gx", "gy"),
            P(None, "gx", "gy"),
            P(None, ("gx", "gy")),
            P(("gx", "gy"), None),
            P(("gx", "gy")),
            P(("gx", "gy")),
            P(("gx", "gy")),
            P(None, ("gx", "gy")),
            P(("gx", "gy")),
        ),
        out_specs=(P(None, "gx", "gy"), P(("gx", "gy"), None)),
        check_vma=False,
    )
```

```python
import functools

import jax
import jax.numpy as jnp
from jax import lax
from jax.experimental import pallas as pl
from jax.experimental.pallas import tpu as pltpu
from jax.sharding import PartitionSpec as P

F32 = jnp.float32
BF16 = jnp.bfloat16
PAD = 16
NOWHERE = -(1 << 20)
LANES = 128
NEAR = 16
STRIP = 40
CHUNK = 256
PARAMS = pltpu.CompilerParams(vmem_limit_bytes=24 * 1024 * 1024)

VMEM = pl.BlockSpec(memory_space=pltpu.VMEM)
SMEM = pl.BlockSpec(memory_space=pltpu.SMEM)
HBM = pl.BlockSpec(memory_space=pltpu.HBM)


def iota(shape, dim):
    return lax.broadcasted_iota(jnp.int32, shape, dim)


def float_iota(shape, dim):
    return iota(shape, dim).astype(F32)


def two_parts(value):
    high = value.astype(BF16).astype(F32)
    return high, value - high


def product(block, field):
    return [
        block(row) * field[0] + block(3 + row) * field[1] + block(6 + row) * field[2]
        for row in range(3)
    ]


def off_diagonal(block, field):
    return [
        sum(block(3 * i + row) * field[i] for i in range(3) if i != row) for row in range(3)
    ]


def masked_product(edge_ref, mask_ref, direction, field):
    mask = mask_ref[direction].astype(F32)
    return [mask * part for part in product(lambda k: edge_ref[direction, k], field)]


def rows_moved(field, edge_row, step):
    size = field.shape[0]
    at = iota(field.shape, 0)
    moved = pltpu.roll(field, step % size, 0)
    return jnp.where(at == (0 if step == 1 else size - 1), edge_row, moved)


def lanes_moved(field, edge_column, step):
    size = field.shape[1]
    at = iota(field.shape, 1)
    moved = pltpu.roll(field, step % size, 1)
    return jnp.where(at == (0 if step == 1 else size - 1), edge_column, moved)


def pack_kernel(
    count_in, values_in, owner_in, node_in, diag_in, edge_in, mask_in, rows_ref, strip_ref,
    count_ref, values_ref, owner_ref, node_ref, diag_low, diag_high, edge_low, edge_high,
    mask_low, mask_high, arrived,
):
    targets = rows_ref.shape[0]
    groups = owner_ref.shape[0]
    cells_x = diag_in.shape[1]
    top = pl.ds(cells_x - 8, 8)
    copies = [
        pltpu.make_async_copy(source, target, arrived.at[k])
        for k, (source, target) in enumerate(
            (
                (edge_in.at[1, :, 0:8], edge_low),
                (edge_in.at[:, :, top], edge_high),
                (diag_in.at[:, 0:8], diag_low),
                (diag_in.at[:, top], diag_high),
                (mask_in.at[1, 0:8], mask_low),
                (mask_in.at[:, top], mask_high),
                (values_in, values_ref),
                (owner_in, owner_ref),
                (node_in, node_ref),
                (count_in, count_ref),
            )
        )
    ]
    for copy in copies:
        copy.start()
    near = 4 * groups
    for target in range(targets):
        rows_ref[target, near:, :] = jnp.zeros((NEAR, LANES), F32)
    for copy in copies:
        copy.wait()
    order = iota((groups, LANES), 0) * LANES + iota((groups, LANES), 1)
    node = node_ref[...]
    frame = cells_x + 2 * PAD
    row = owner_ref[...] * cells_x + lax.shift_right_logical(node, 7)
    row = jnp.where(order < count_ref[0], row, NOWHERE)
    column = node & (LANES - 1)
    for comp in range(3):
        for group in range(groups):
            piece = values_ref[comp : comp + 1, group * LANES : (group + 1) * LANES]
            for target in range(targets):
                rows_ref[target, comp * groups + group : comp * groups + group + 1, :] = piece
    for target in range(targets):
        line = row - (target * cells_x - PAD)
        inside = (line >= 0) & (line < frame)
        index = jnp.where(inside, line * LANES + column, -1)
        rows_ref[target, 3 * groups : 4 * groups, :] = index.astype(F32)

    def block(edge, mask, direction, at):
        present = mask[direction, at : at + 1, :].astype(F32)
        return [edge[direction, k, at : at + 1, :] * present for k in range(9)]

    up_y, low_y = block(edge_high, mask_high, 2, 7), block(edge_high, mask_high, 3, 7)
    later = [diag_high[k, 7:8, :] for k in range(9) if k % 4]
    later += up_y + low_y + block(edge_high, mask_high, 0, 6)
    later += [diag_high[4 * k, 6:7, :] for k in range(3)]
    for k, value in enumerate(later):
        strip_ref[k : k + 1, :] = value
    strip_ref[len(later) :, :] = jnp.zeros((STRIP - len(later), LANES), F32)

    here = lax.axis_index("gx")

    @pl.when(here < targets - 1)
    def _():
        def put(slot, value):
            rows_ref[here + 1, near + slot : near + slot + 1, :] = value

        for k in range(3):
            put(k, diag_high[4 * k, 7:8, :])
        for k, value in enumerate(block(edge_high, mask_high, 0, 7)):
            put(3 + k, value)
        corners = jnp.zeros((1, LANES), F32)
        lane = iota((1, LANES), 1)
        for k in range(9):
            corners = jnp.where(lane == k, up_y[k][:, LANES - 1 :], corners)
            corners = jnp.where(lane == 9 + k, low_y[k][:, :1], corners)
        put(12, corners)

    @pl.when(here > 0)
    def _():
        def put(slot, value):
            rows_ref[here - 1, near + slot : near + slot + 1, :] = value

        for k in range(3):
            put(k, diag_low[4 * k, 0:1, :])
        present = mask_low[0:1, :].astype(F32)
        for k in range(9):
            put(3 + k, edge_low[k, 0:1, :] * present)


def stretched(row, count):
    tile = jnp.broadcast_to(row, (16, row.shape[1])).astype(BF16)
    return jnp.concatenate([tile] * (count // 16), axis=0)


def ratio(value, scale):
    return jnp.where(scale > 0.0, value / jnp.where(scale > 0.0, scale, 1.0), 0.0)


def field_kernel(
    rows_ref, diag_ref, edge_ref, mask_ref,
    field_ref, part_ref, halo_ref, edges_ref, own_ref, load_ref,
):
    senders = rows_ref.shape[0]
    groups = (rows_ref.shape[1] - NEAR) // 4
    cells_x = field_ref.shape[1]
    half = (cells_x + 2 * PAD) // 2
    own = cells_x // 2

    load_ref[...] = jnp.zeros_like(load_ref)
    here = lax.axis_index("gx")

    def add_rows(sender, carry):
        index = rows_ref[sender, 3 * groups : 4 * groups, :]
        split = float(half * LANES)
        index, shift = (
            jnp.where(index >= split, index - split, index),
            jnp.where(index >= split, float(LANES), 0.0),
        )
        place = jnp.floor(index * (1.0 / LANES))
        column = index - place * float(LANES) + shift
        at_row = float_iota((half, LANES), 0).astype(BF16)
        at_column = float_iota((2 * LANES, LANES), 0).astype(BF16)
        parts = [
            two_parts(rows_ref[sender, c * groups : (c + 1) * groups, :]) for c in range(3)
        ]
        zero, one = jnp.zeros((), BF16), jnp.ones((), BF16)
        lefts, rights = [], []
        for group in range(groups):
            line = slice(group, group + 1)
            match = at_row == stretched(place[line], half)
            lefts.append(
                jnp.concatenate(
                    [
                        jnp.where(match, stretched(parts[c][which][line], half), zero)
                        for which in range(2)
                        for c in range(3)
                    ],
                    axis=0,
                )
            )
            rights.append(
                jnp.where(at_column == stretched(column[line], 2 * LANES), one, zero)
            )
        load_ref[...] += lax.dot_general(
            jnp.concatenate(lefts, axis=1),
            jnp.concatenate(rights, axis=1),
            (((1,), (1,)), ((), ())),
            preferred_element_type=F32,
        )
        return carry

    lax.fori_loop(0, senders, add_rows, 0, unroll=min(senders, 8))

    def load_rows(comp, first, last, second_half):
        lanes = slice(LANES, 2 * LANES) if second_half else slice(0, LANES)
        return (
            load_ref[comp * half + first : comp * half + last, lanes]
            + load_ref[(3 + comp) * half + first : (3 + comp) * half + last, lanes]
        )

    field = []
    for comp in range(3):
        load = jnp.concatenate(
            [load_rows(comp, PAD, half, False), load_rows(comp, 0, half - PAD, True)], axis=0
        )
        field.append(load / diag_ref[4 * comp])
        field_ref[comp] = field[comp]
    beyond = half - PAD
    near_before = [load_rows(c, PAD - 1, PAD, False) for c in range(3)]
    far_before = [load_rows(c, PAD - 2, PAD - 1, False) for c in range(3)]
    near_after = [load_rows(c, beyond, beyond + 1, True) for c in range(3)]

    up_x = masked_product(edge_ref, mask_ref, 0, field)
    low_x = masked_product(edge_ref, mask_ref, 1, field)
    base = 4 * groups

    def neighbour(sender, load):
        def entry(k):
            return rows_ref[sender, base + k : base + k + 1, :]

        scale, toward = [entry(k) for k in range(3)], [entry(3 + k) for k in range(9)]
        beside = [ratio(load[c], scale[c]) for c in range(3)]
        return scale, toward, beside, product(lambda k: toward[k], beside)

    lower = jnp.maximum(here - 1, 0)
    before = neighbour(lower, near_before)
    after = neighbour(jnp.minimum(here + 1, senders - 1), near_after)
    rows = before[2] + [ratio(1.0, scale) for scale in before[0]]
    rows += [p[:1] for p in low_x] + before[1] + far_before
    for k, value in enumerate(rows):
        halo_ref[k : k + 1, :] = value
    halo_ref[len(rows) :, :] = jnp.zeros((halo_ref.shape[0] - len(rows), LANES), F32)
    lane_row = iota((1, LANES), 1)
    ends = jnp.zeros((1, LANES), F32)
    for i in range(3):
        for a in range(3):
            ends = jnp.where(lane_row == 3 * i + a, before[2][i][:, LANES - 1 :], ends)
            ends = jnp.where(lane_row == 9 + 3 * i + a, before[2][i][:, :1], ends)
    ends = ends * rows_ref[lower, base + 12 : base + 13, :]
    ends = ends + pltpu.roll(ends, LANES - 3, 1) + pltpu.roll(ends, LANES - 6, 1)

    total = off_diagonal(lambda k: diag_ref[k], field)
    total = [total[c] + rows_moved(up_x[c], before[3][c], 1) for c in range(3)]
    total = [total[c] + rows_moved(low_x[c], after[3][c], -1) for c in range(3)]
    up_y = masked_product(edge_ref, mask_ref, 2, field)
    low_y = masked_product(edge_ref, mask_ref, 3, field)
    total = [
        total[c] + lanes_moved(up_y[c], 0.0, 1) + lanes_moved(low_y[c], 0.0, -1)
        for c in range(3)
    ]
    inverse = [1.0 / diag_ref[4 * c] for c in range(3)]
    part = [total[c] * inverse[c] for c in range(3)]
    for comp in range(3):
        part_ref[comp] = part[comp]
    def columns(lane, along_y, end):
        packed = jnp.zeros((cells_x, LANES), F32)
        at = iota((cells_x, LANES), 1)
        for slot, fields in enumerate((field, along_y, part, inverse)):
            for comp in range(3):
                column = fields[comp][:, lane : lane + 1]
                packed = jnp.where(at == 3 * slot + comp, column, packed)
        rest = jnp.zeros((LANES - cells_x, LANES), F32)
        turned = jnp.concatenate([packed, rest], axis=0).T[:16]
        at = iota((16, LANES), 1)
        line = iota((16, LANES), 0)
        for comp in range(3):
            turned = jnp.where(
                (line == 3 + comp) & (at == cells_x),
                ends[:, end + comp : end + comp + 1],
                turned,
            )
        return turned

    first_column = columns(0, low_y, 9)
    last_column = columns(LANES - 1, up_y, 0)
    own_ref[0] = first_column
    own_ref[1] = last_column
    edges_ref[...] = jnp.zeros_like(edges_ref)
    across = lax.axis_index("gy")

    @pl.when(across < edges_ref.shape[0] - 1)
    def _():
        edges_ref[across + 1] = last_column

    @pl.when(across > 0)
    def _():
        edges_ref[across - 1] = first_column


def bernstein(coord):
    other = 1.0 - coord
    return [
        other * other * other,
        3.0 * coord * other * other,
        3.0 * coord * coord * other,
        coord * coord * coord,
    ]


def weight_table(u, v, w):
    first, second, third = bernstein(u), bernstein(v), bernstein(w)
    line = iota((8, u.shape[1]), 0)
    inner = line & 3
    along = jnp.where(
        inner == 0,
        third[0],
        jnp.where(inner == 1, third[1], jnp.where(inner == 2, third[2], third[3])),
    )
    pair = jnp.concatenate(
        [
            jnp.where(line < 4, second[0], second[1]) * along,
            jnp.where(line < 4, second[2], second[3]) * along,
        ],
        axis=0,
    )
    return jnp.concatenate([pair * first[i] for i in range(4)], axis=0)


def add_tiles(out_ref, tile_ref, high, low, weights):
    first_half = iota((4, LANES), 1) < LANES // 2
    tiles = tile_ref.shape[0]
    points = high.shape[1] // tiles
    both = jnp.concatenate([high, low], axis=0).astype(BF16)
    for tile in range(tiles):
        term = jnp.dot(
            both[:, tile * points : (tile + 1) * points],
            weights(tile),
            preferred_element_type=F32,
        )
        term = term[:8] + term[8:]
        term = term + pltpu.roll(term, LANES // 2, 1)
        out_ref[tile_ref[tile]] += jnp.where(first_half, term[:4], term[4:])


def quotient_before(halo_ref, strip_ref, before_ref):
    def rows(ref, first, count):
        return [ref[first + k : first + k + 1, :] for k in range(count)]

    beside, inverse, entering = rows(halo_ref, 0, 3), rows(halo_ref, 3, 3), rows(halo_ref, 6, 3)
    far_load, within = rows(halo_ref, 18, 3), rows(strip_ref, 0, 6)
    far_scale = rows(strip_ref, 33, 3)
    far = [ratio(far_load[c], far_scale[c]) for c in range(3)]
    whole_block = [None, *within[:3], None, *within[3:], None]
    total = off_diagonal(lambda k: whole_block[k], beside)
    from_far = product(lambda k: strip_ref[24 + k : 25 + k, :], far)
    up_y = product(lambda k: strip_ref[6 + k : 7 + k, :], beside)
    low_y = product(lambda k: strip_ref[15 + k : 16 + k, :], beside)
    for c in range(3):
        before_ref[c : c + 1, :] = inverse[c] * (
            total[c]
            + from_far[c]
            + entering[c]
            + lanes_moved(up_y[c], 0.0, 1)
            + lanes_moved(low_y[c], 0.0, -1)
        )
    before_ref[3:, :] = jnp.zeros((before_ref.shape[0] - 3, LANES), F32)


def box_kernel(
    tile_ref, field_ref, part_ref, node_ref, param_ref, halo_ref, strip_ref,
    box_ref, weights_ref, columns_ref, before_ref, *, tile_points,
):
    cells_x = field_ref.shape[1]
    own = cells_x // 2
    quotient_before(halo_ref, strip_ref, before_ref)
    field = [field_ref[c] for c in range(3)]
    part = [part_ref[c] for c in range(3)]
    order = [field[0], part[0], field[2], field[1], part[1], part[2]]
    folded = [two_parts(jnp.concatenate([f[:own], f[own:]], axis=1)) for f in order]
    table = jnp.concatenate(
        [folded[f][which] for which in range(2) for f in range(6)], axis=0
    ).astype(BF16)
    points = param_ref.shape[1]
    pieces = CHUNK // LANES
    zero, one = jnp.zeros((), BF16), jnp.ones((), BF16)
    at_node = float_iota((2 * LANES, CHUNK), 0).astype(BF16)
    nothing = jnp.zeros((1, CHUNK), F32)
    highs, lows = [], []
    for chunk in range(points // CHUNK):
        node = jnp.concatenate(
            [node_ref[chunk * pieces + k : chunk * pieces + k + 1, :] for k in range(pieces)],
            axis=1,
        )
        row = lax.shift_right_logical(node, 7)
        column = node & (LANES - 1)
        lanes = slice(chunk * CHUNK, (chunk + 1) * CHUNK)
        at_edge = jnp.where(
            column == 0, row, jnp.where(column == LANES - 1, row + cells_x, -1)
        ).astype(F32)
        columns_ref[:, lanes] = jnp.where(
            at_node[: 2 * cells_x] == stretched(at_edge, 2 * cells_x), one, zero
        )
        place = column + jnp.where(row >= own, LANES, 0)
        row = jnp.where(row >= own, row - own, row)
        pick = jnp.where(at_node == stretched(place.astype(F32), 2 * LANES), one, zero)
        read = jnp.dot(table, pick, preferred_element_type=F32)
        read = read[: 6 * own] + read[6 * own :]
        here = iota((own, CHUNK), 0) == row
        values = [
            jnp.sum(
                jnp.where(here, read[f * own : (f + 1) * own], 0.0), axis=0, keepdims=True
            )
            for f in range(6)
        ]
        high, low = two_parts(
            jnp.concatenate(values[:3] + [nothing] + values[3:] + [nothing], axis=0)
        )
        highs.append(high)
        lows.append(low)
        weights = two_parts(
            weight_table(param_ref[0:1, lanes], param_ref[1:2, lanes], param_ref[2:3, lanes])
        )
        for k in range(CHUNK // tile_points):
            tile = slice(k * tile_points, (k + 1) * tile_points)
            sides = jnp.concatenate([weights[0][:, tile], weights[1][:, tile]], axis=0)
            weights_ref[chunk * (CHUNK // tile_points) + k] = sides.T.astype(BF16)
    box_ref[...] = jnp.zeros_like(box_ref)
    add_tiles(
        box_ref,
        tile_ref,
        jnp.concatenate(highs, axis=1),
        jnp.concatenate(lows, axis=1),
        lambda tile: weights_ref[tile],
    )


def sums_kernel(
    tile_ref, edges_ref, own_ref, field_ref, part_ref, halo_ref,
    diag_ref, edge_ref, mask_ref, box_ref, weights_ref, columns_ref, before_ref,
    quotient_ref, out_ref,
):
    cells_x = field_ref.shape[1]
    targets = out_ref.shape[0]

    def arrived(sender):
        rest = jnp.zeros((LANES - 16, LANES), F32)
        return jnp.concatenate([edges_ref[sender], rest], axis=0).T

    across = lax.axis_index("gy")
    low = arrived(jnp.maximum(across - 1, 0))
    high = arrived(jnp.minimum(across + 1, edges_ref.shape[0] - 1))
    lane = iota((cells_x, LANES), 1)

    def column(source, slot, comp):
        return source[:cells_x, 3 * slot + comp : 3 * slot + comp + 1]

    field = [field_ref[c] for c in range(3)]
    scale = [diag_ref[4 * c] for c in range(3)]
    toward_high = masked_product(edge_ref, mask_ref, 2, field)
    toward_low = masked_product(edge_ref, mask_ref, 3, field)
    quotient, low_edge, high_edge = [], [], []
    for c in range(3):
        entering = jnp.where(
            lane == 0,
            column(low, 1, c),
            jnp.where(lane == LANES - 1, column(high, 1, c), 0.0),
        )
        quotient.append(part_ref[c] + entering / scale[c])
        low_edge.append(column(low, 2, c) + column(low, 3, c) * toward_low[c][:, :1])
        high_edge.append(column(high, 2, c) + column(high, 3, c) * toward_high[c][:, -1:])
    for c in range(3):
        quotient_ref[c] = quotient[c]
    lane_row = iota((1, LANES), 1)
    before, before_quotient = [], []
    for c in range(3):
        entering = jnp.where(
            lane_row == 0,
            low[cells_x : cells_x + 1, 3 + c : 4 + c],
            jnp.where(lane_row == LANES - 1, high[cells_x : cells_x + 1, 3 + c : 4 + c], 0.0),
        )
        before.append(halo_ref[c : c + 1, :])
        before_quotient.append(
            before_ref[c : c + 1, :] + entering * halo_ref[3 + c : 4 + c, :]
        )

    first_sum = sum(field[c] * scale[c] * field[c] for c in range(3))
    second_sum = sum(field[c] * scale[c] * quotient[c] for c in range(3))
    third_sum = sum(quotient[c] * scale[c] * quotient[c] for c in range(3))
    within = off_diagonal(lambda k: diag_ref[k], quotient)
    fourth_sum = sum(within[c] * field[c] for c in range(3))
    fifth_sum = sum(within[c] * quotient[c] for c in range(3))
    at_row = iota((cells_x, LANES), 0)
    moves = (
        (pltpu.roll, 1, 0, at_row == 0),
        (pltpu.roll, cells_x - 1, 0, at_row == cells_x - 1),
        (pltpu.roll, 1, 1, lane == 0),
        (pltpu.roll, LANES - 1, 1, lane == LANES - 1),
    )
    extra = [0.0, 0.0]
    sides = [0.0, 0.0]
    for direction, (roll, step, dim, edge) in enumerate(moves):
        moving = masked_product(edge_ref, mask_ref, direction, quotient)
        for c in range(3):
            moved = jnp.where(edge, 0.0, roll(moving[c], step, dim))
            fourth_sum = fourth_sum + moved * field[c]
            fifth_sum = fifth_sum + moved * quotient[c]
            if direction == 1:
                extra[0] += moving[c][:1] * before[c]
                extra[1] += moving[c][:1] * before_quotient[c]
            elif direction == 2:
                sides[0] += moving[c][:, LANES - 1 :] * column(high, 0, c)
                sides[1] += moving[c][:, LANES - 1 :] * high_edge[c]
            elif direction == 3:
                sides[0] += moving[c][:, :1] * column(low, 0, c)
                sides[1] += moving[c][:, :1] * low_edge[c]
    incoming = product(lambda k: halo_ref[9 + k : 10 + k, :], before_quotient)
    extra[0] += sum(incoming[c] * field[c][:1] for c in range(3))
    extra[1] += sum(incoming[c] * quotient[c][:1] for c in range(3))
    fourth_sum = fourth_sum + jnp.where(lane == 0, sides[0], 0.0)
    fifth_sum = fifth_sum + jnp.where(lane == 0, sides[1], 0.0)
    extra = [0.0, 0.0, 0.0, extra[0], extra[1]]
    sums = jnp.zeros((1, LANES), F32)
    for k, value in enumerate((first_sum, second_sum, third_sum, fourth_sum, fifth_sum)):
        line = jnp.sum(value, axis=0, keepdims=True) + extra[k]
        sums = jnp.where(lane_row == k, jnp.sum(line, axis=1, keepdims=True), sums)

    across_low = edges_ref[jnp.maximum(across - 1, 0)]
    across_high = edges_ref[jnp.minimum(across + 1, edges_ref.shape[0] - 1)]
    added = []
    for c in range(3):
        first = across_low[3 + c : 4 + c] * own_ref[0, 9 + c : 10 + c, :]
        second = across_high[3 + c : 4 + c] * own_ref[1, 9 + c : 10 + c, :]
        added.append(
            jnp.where(lane_row < cells_x, first, pltpu.roll(second, cells_x, 1))
        )
    none = jnp.zeros((1, LANES), F32)
    added = jnp.concatenate(
        [none, added[0], none, none, none, added[1], added[2], none], axis=0
    )
    added = jnp.concatenate(two_parts(added), axis=0).astype(BF16)
    read = jnp.dot(added, columns_ref[...], preferred_element_type=F32)
    high, low = two_parts(read[:8] + read[8:])
    out_ref[...] = box_ref[...]
    add_tiles(out_ref, tile_ref, high, low, lambda tile: weights_ref[tile])
    for box in range(targets):
        out_ref[box, 3:4, :] = sums


def result_kernel(got_ref, field_ref, quotient_ref, solution_ref, gradient_ref):
    total = jnp.sum(got_ref[...], axis=0)
    rho, a, b, t, u = [total[3:4, k : k + 1] for k in range(5)]
    ratio = a / rho
    norm = rho + a
    step = rho / norm
    rest = jnp.maximum(b - a * ratio, 0.0)
    beta = step * step * rest / rho
    rest_image = (b + u) - ratio * (a + b + a + t) + ratio * ratio * norm
    cross = (a + t) - ratio * norm
    curve = step * step * rest_image - step * beta * (rest + cross) + beta * beta * norm
    second = jnp.where(
        curve > 0.0, step * step * rest / jnp.where(curve > 0.0, curve, 1.0), 0.0
    )
    of_field = step + second * (beta + step * ratio)
    of_quotient = -(step * second)
    for c in range(3):
        solution_ref[c] = of_field * field_ref[c] + of_quotient * quotient_ref[c]
    gradient_ref[:, :LANES] = of_field * total[0:1] + of_quotient * total[1:2]
    gradient_ref[:, LANES:] = (
        of_field * total[2:3, : LANES // 2] + of_quotient * total[2:3, LANES // 2 :]
    )


def per_device(
    diag_blocks, edge_blocks, edge_mask, src_values, src_owner, src_node, src_count,
    surf_node, surf_param, tile_box,
):
    cells_x, cells_y = diag_blocks.shape[1:]
    width_gx, width_gy = lax.axis_size("gx"), lax.axis_size("gy")
    devices = width_gx * width_gy
    groups = src_node.shape[0] // LANES
    whole = functools.partial(jax.ShapeDtypeStruct, dtype=F32)

    cells = 4 * groups + NEAR

    def kept(array):
        return pltpu.with_memory_space_constraint(array, pltpu.HBM)

    i32 = jnp.int32
    rows, strip = pl.pallas_call(
        pack_kernel,
        in_specs=[HBM] * 7,
        out_specs=[VMEM] * 2,
        out_shape=[
            pltpu.VMEM((width_gx, cells, LANES), F32), pltpu.VMEM((STRIP, LANES), F32)
        ],
        scratch_shapes=[
            pltpu.SMEM((1,), i32),
            pltpu.VMEM(src_values.shape, F32),
            pltpu.VMEM((groups, LANES), i32),
            pltpu.VMEM((groups, LANES), i32),
            pltpu.VMEM((9, 8, cells_y), F32),
            pltpu.VMEM((9, 8, cells_y), F32),
            pltpu.VMEM((9, 8, cells_y), F32),
            pltpu.VMEM((4, 9, 8, cells_y), F32),
            pltpu.VMEM((8, cells_y), i32),
            pltpu.VMEM((4, 8, cells_y), i32),
            pltpu.SemaphoreType.DMA((10,)),
        ],
        compiler_params=PARAMS,
        name="pack_rows_and_edges",
    )(
        src_count, kept(src_values),
        kept(src_owner.reshape(groups, LANES)), kept(src_node.reshape(groups, LANES)),
        kept(diag_blocks), kept(edge_blocks), kept(edge_mask),
    )
    rows = lax.all_to_all(rows, "gx", split_axis=0, concat_axis=0, tiled=True)
    strip = lax.ppermute(strip, "gx", [(i, i + 1) for i in range(width_gx - 1)])

    nodes = (3, cells_x, cells_y)
    frame = cells_x + 2 * PAD
    field, part, halo, edges, own = pl.pallas_call(
        field_kernel,
        in_specs=[VMEM] * 4,
        out_specs=[VMEM] * 5,
        out_shape=[
            whole(nodes), whole(nodes), whole((24, cells_y)), whole((width_gy, 16, LANES)),
            whole((2, 16, LANES)),
        ],
        scratch_shapes=[pltpu.VMEM((3 * frame, 2 * LANES), F32)],
        compiler_params=PARAMS,
        name="load_and_first_product",
    )(rows, diag_blocks, edge_blocks, edge_mask)
    edges = lax.all_to_all(edges, "gy", split_axis=0, concat_axis=0, tiled=True)

    points, tiles = surf_node.shape[0], tile_box.shape[0]
    boxes = (devices, 4, LANES)
    box_part, weights, columns, before = pl.pallas_call(
        functools.partial(box_kernel, tile_points=points // tiles),
        in_specs=[SMEM] + [VMEM] * 6,
        out_specs=[VMEM] * 4,
        out_shape=[
            whole(boxes),
            jax.ShapeDtypeStruct((tiles, points // tiles, LANES), BF16),
            jax.ShapeDtypeStruct((2 * cells_x, points), BF16),
            whole((8, LANES)),
        ],
        compiler_params=PARAMS,
        cost_estimate=pl.CostEstimate(
            flops=10**9, bytes_accessed=4 * 10**6, transcendentals=0
        ),
        name="box_parts",
    )(
        tile_box, field, part, surf_node.reshape(points // LANES, LANES), surf_param, halo,
        strip,
    )

    quotient, partial = pl.pallas_call(
        sums_kernel,
        in_specs=[SMEM] + [VMEM] * 12,
        out_specs=[VMEM] * 2,
        out_shape=[whole(nodes), whole(boxes)],
        compiler_params=PARAMS,
        name="sums_and_halo_parts",
    )(
        tile_box, edges, own, field, part, halo, diag_blocks, edge_blocks, edge_mask,
        box_part, weights, columns, before,
    )
    got = lax.all_to_all(partial, ("gx", "gy"), split_axis=0, concat_axis=0, tiled=True)
    return pl.pallas_call(
        result_kernel,
        in_specs=[VMEM] * 3,
        out_specs=[VMEM] * 2,
        out_shape=[whole(nodes), whole((1, 192))],
        compiler_params=PARAMS,
        name="steps_and_outputs",
    )(got, field, quotient)


def solution(mesh):
    return jax.shard_map(
        per_device,
        mesh=mesh,
        in_specs=(
            P(None, "gx", "gy"),
            P(None, None, "gx", "gy"),
            P(None, "gx", "gy"),
            P(None, ("gx", "gy")),
            P(("gx", "gy"), None),
            P(("gx", "gy")),
            P(("gx", "gy")),
            P(("gx", "gy")),
            P(None, ("gx", "gy")),
            P(("gx", "gy")),
        ),
        out_specs=(P(None, "gx", "gy"), P(("gx", "gy"), None)),
        check_vma=False,
    )
```

```python
import functools

import jax
import jax.numpy as jnp
from jax import lax
from jax.experimental import pallas as pl
from jax.experimental.pallas import tpu as pltpu
from jax.sharding import PartitionSpec as P

F32 = jnp.float32
BF16 = jnp.bfloat16
PAD = 16
NOWHERE = -(1 << 20)
LANES = 128
NEAR = 16
STRIP = 40
CHUNK = 256
PARAMS = pltpu.CompilerParams(vmem_limit_bytes=24 * 1024 * 1024)

VMEM = pl.BlockSpec(memory_space=pltpu.VMEM)
SMEM = pl.BlockSpec(memory_space=pltpu.SMEM)
HBM = pl.BlockSpec(memory_space=pltpu.HBM)


def iota(shape, dim):
    return lax.broadcasted_iota(jnp.int32, shape, dim)


def float_iota(shape, dim):
    return iota(shape, dim).astype(F32)


def two_parts(value):
    high = value.astype(BF16).astype(F32)
    return high, value - high


def product(block, field):
    return [
        block(row) * field[0] + block(3 + row) * field[1] + block(6 + row) * field[2]
        for row in range(3)
    ]


def off_diagonal(block, field):
    return [
        sum(block(3 * i + row) * field[i] for i in range(3) if i != row) for row in range(3)
    ]


def masked_product(edge_ref, mask_ref, direction, field):
    mask = mask_ref[direction].astype(F32)
    return [mask * part for part in product(lambda k: edge_ref[direction, k], field)]


def rows_moved(field, edge_row, step):
    size = field.shape[0]
    at = iota(field.shape, 0)
    moved = pltpu.roll(field, step % size, 0)
    return jnp.where(at == (0 if step == 1 else size - 1), edge_row, moved)


def lanes_moved(field, edge_column, step):
    size = field.shape[1]
    at = iota(field.shape, 1)
    moved = pltpu.roll(field, step % size, 1)
    return jnp.where(at == (0 if step == 1 else size - 1), edge_column, moved)


def pack_kernel(
    count_in, values_in, owner_in, node_in, diag_in, edge_in, mask_in, rows_ref, strip_ref,
    count_ref, values_ref, owner_ref, node_ref, diag_low, diag_high, edge_low, edge_high,
    mask_low, mask_high, arrived,
):
    targets = rows_ref.shape[0]
    groups = owner_ref.shape[0]
    cells_x = diag_in.shape[1]
    top = pl.ds(cells_x - 8, 8)
    copies = [
        pltpu.make_async_copy(source, target, arrived.at[k])
        for k, (source, target) in enumerate(
            (
                (owner_in, owner_ref),
                (node_in, node_ref),
                (count_in, count_ref),
                (values_in, values_ref),
                (diag_in.at[:, 0:8], diag_low),
                (diag_in.at[:, top], diag_high),
                (mask_in.at[1, 0:8], mask_low),
                (mask_in.at[:, top], mask_high),
                (edge_in.at[1, :, 0:8], edge_low),
                (edge_in.at[:, :, top], edge_high),
            )
        )
    ]
    for copy in copies:
        copy.start()
    near = 4 * groups
    for target in range(targets):
        rows_ref[target, near:, :] = jnp.zeros((NEAR, LANES), F32)
    for copy in copies[:3]:
        copy.wait()
    order = iota((groups, LANES), 0) * LANES + iota((groups, LANES), 1)
    node = node_ref[...]
    frame = cells_x + 2 * PAD
    row = owner_ref[...] * cells_x + lax.shift_right_logical(node, 7)
    row = jnp.where(order < count_ref[0], row, NOWHERE)
    column = node & (LANES - 1)
    for target in range(targets):
        line = row - (target * cells_x - PAD)
        inside = (line >= 0) & (line < frame)
        index = jnp.where(inside, line * LANES + column, -1)
        rows_ref[target, 3 * groups : 4 * groups, :] = index.astype(F32)

    copies[3].wait()
    for comp in range(3):
        value = jnp.concatenate(
            [
                values_ref[comp : comp + 1, group * LANES : (group + 1) * LANES]
                for group in range(groups)
            ],
            axis=0,
        )
        for target in range(targets):
            rows_ref[target, comp * groups : (comp + 1) * groups, :] = value
    for copy in copies[4:]:
        copy.wait()

    def block(edge, mask, direction, at):
        present = mask[direction, at : at + 1, :].astype(F32)
        return [edge[direction, k, at : at + 1, :] * present for k in range(9)]

    up_y, low_y = block(edge_high, mask_high, 2, 7), block(edge_high, mask_high, 3, 7)
    later = [diag_high[k, 7:8, :] for k in range(9) if k % 4]
    later += up_y + low_y + block(edge_high, mask_high, 0, 6)
    later += [diag_high[4 * k, 6:7, :] for k in range(3)]
    for k, value in enumerate(later):
        strip_ref[k : k + 1, :] = value
    strip_ref[len(later) :, :] = jnp.zeros((STRIP - len(later), LANES), F32)

    here = lax.axis_index("gx")

    @pl.when(here < targets - 1)
    def _():
        def put(slot, value):
            rows_ref[here + 1, near + slot : near + slot + 1, :] = value

        for k in range(3):
            put(k, diag_high[4 * k, 7:8, :])
        for k, value in enumerate(block(edge_high, mask_high, 0, 7)):
            put(3 + k, value)
        corners = jnp.zeros((1, LANES), F32)
        lane = iota((1, LANES), 1)
        for k in range(9):
            corners = jnp.where(lane == k, up_y[k][:, LANES - 1 :], corners)
            corners = jnp.where(lane == 9 + k, low_y[k][:, :1], corners)
        put(12, corners)

    @pl.when(here > 0)
    def _():
        def put(slot, value):
            rows_ref[here - 1, near + slot : near + slot + 1, :] = value

        for k in range(3):
            put(k, diag_low[4 * k, 0:1, :])
        present = mask_low[0:1, :].astype(F32)
        for k in range(9):
            put(3 + k, edge_low[k, 0:1, :] * present)


def stretched(row, count):
    tile = jnp.broadcast_to(row, (16, row.shape[1])).astype(BF16)
    return jnp.concatenate([tile] * (count // 16), axis=0)


def ratio(value, scale):
    return jnp.where(scale > 0.0, value / jnp.where(scale > 0.0, scale, 1.0), 0.0)


def field_kernel(
    rows_ref, diag_ref, edge_ref, mask_ref,
    field_ref, part_ref, halo_ref, edges_ref, own_ref, load_ref,
):
    senders = rows_ref.shape[0]
    groups = (rows_ref.shape[1] - NEAR) // 4
    cells_x = field_ref.shape[1]
    half = (cells_x + 2 * PAD) // 2
    own = cells_x // 2

    load_ref[...] = jnp.zeros_like(load_ref)
    here = lax.axis_index("gx")

    def add_rows(sender, carry):
        index = rows_ref[sender, 3 * groups : 4 * groups, :]
        split = float(half * LANES)
        index, shift = (
            jnp.where(index >= split, index - split, index),
            jnp.where(index >= split, float(LANES), 0.0),
        )
        place = jnp.floor(index * (1.0 / LANES))
        column = index - place * float(LANES) + shift
        at_row = float_iota((half, LANES), 0).astype(BF16)
        at_column = float_iota((2 * LANES, LANES), 0).astype(BF16)
        parts = [
            two_parts(rows_ref[sender, c * groups : (c + 1) * groups, :]) for c in range(3)
        ]
        zero, one = jnp.zeros((), BF16), jnp.ones((), BF16)
        lefts, rights = [], []
        for group in range(groups):
            line = slice(group, group + 1)
            match = at_row == stretched(place[line], half)
            lefts.append(
                jnp.concatenate(
                    [
                        jnp.where(match, stretched(parts[c][which][line], half), zero)
                        for which in range(2)
                        for c in range(3)
                    ],
                    axis=0,
                )
            )
            rights.append(
                jnp.where(at_column == stretched(column[line], 2 * LANES), one, zero)
            )
        load_ref[...] += lax.dot_general(
            jnp.concatenate(lefts, axis=1),
            jnp.concatenate(rights, axis=1),
            (((1,), (1,)), ((), ())),
            preferred_element_type=F32,
        )
        return carry

    lax.fori_loop(0, senders, add_rows, 0, unroll=min(senders, 8))

    def load_rows(comp, first, last, second_half):
        lanes = slice(LANES, 2 * LANES) if second_half else slice(0, LANES)
        return (
            load_ref[comp * half + first : comp * half + last, lanes]
            + load_ref[(3 + comp) * half + first : (3 + comp) * half + last, lanes]
        )

    field = []
    for comp in range(3):
        load = jnp.concatenate(
            [load_rows(comp, PAD, half, False), load_rows(comp, 0, half - PAD, True)], axis=0
        )
        field.append(load / diag_ref[4 * comp])
        field_ref[comp] = field[comp]
    beyond = half - PAD
    near_before = [load_rows(c, PAD - 1, PAD, False) for c in range(3)]
    far_before = [load_rows(c, PAD - 2, PAD - 1, False) for c in range(3)]
    near_after = [load_rows(c, beyond, beyond + 1, True) for c in range(3)]

    up_x = masked_product(edge_ref, mask_ref, 0, field)
    low_x = masked_product(edge_ref, mask_ref, 1, field)
    base = 4 * groups

    def neighbour(sender, load):
        def entry(k):
            return rows_ref[sender, base + k : base + k + 1, :]

        scale, toward = [entry(k) for k in range(3)], [entry(3 + k) for k in range(9)]
        beside = [ratio(load[c], scale[c]) for c in range(3)]
        return scale, toward, beside, product(lambda k: toward[k], beside)

    lower = jnp.maximum(here - 1, 0)
    before = neighbour(lower, near_before)
    after = neighbour(jnp.minimum(here + 1, senders - 1), near_after)
    rows = before[2] + [ratio(1.0, scale) for scale in before[0]]
    rows += [p[:1] for p in low_x] + before[1] + far_before
    for k, value in enumerate(rows):
        halo_ref[k : k + 1, :] = value
    halo_ref[len(rows) :, :] = jnp.zeros((halo_ref.shape[0] - len(rows), LANES), F32)
    lane_row = iota((1, LANES), 1)
    ends = jnp.zeros((1, LANES), F32)
    for i in range(3):
        for a in range(3):
            ends = jnp.where(lane_row == 3 * i + a, before[2][i][:, LANES - 1 :], ends)
            ends = jnp.where(lane_row == 9 + 3 * i + a, before[2][i][:, :1], ends)
    ends = ends * rows_ref[lower, base + 12 : base + 13, :]
    ends = ends + pltpu.roll(ends, LANES - 3, 1) + pltpu.roll(ends, LANES - 6, 1)

    total = off_diagonal(lambda k: diag_ref[k], field)
    total = [total[c] + rows_moved(up_x[c], before[3][c], 1) for c in range(3)]
    total = [total[c] + rows_moved(low_x[c], after[3][c], -1) for c in range(3)]
    up_y = masked_product(edge_ref, mask_ref, 2, field)
    low_y = masked_product(edge_ref, mask_ref, 3, field)
    total = [
        total[c] + lanes_moved(up_y[c], 0.0, 1) + lanes_moved(low_y[c], 0.0, -1)
        for c in range(3)
    ]
    inverse = [1.0 / diag_ref[4 * c] for c in range(3)]
    part = [total[c] * inverse[c] for c in range(3)]
    for comp in range(3):
        part_ref[comp] = part[comp]
    def columns(lane, along_y, end):
        packed = jnp.zeros((cells_x, LANES), F32)
        at = iota((cells_x, LANES), 1)
        for slot, fields in enumerate((field, along_y, part, inverse)):
            for comp in range(3):
                column = fields[comp][:, lane : lane + 1]
                packed = jnp.where(at == 3 * slot + comp, column, packed)
        rest = jnp.zeros((LANES - cells_x, LANES), F32)
        turned = jnp.concatenate([packed, rest], axis=0).T[:16]
        at = iota((16, LANES), 1)
        line = iota((16, LANES), 0)
        for comp in range(3):
            turned = jnp.where(
                (line == 3 + comp) & (at == cells_x),
                ends[:, end + comp : end + comp + 1],
                turned,
            )
        return turned

    first_column = columns(0, low_y, 9)
    last_column = columns(LANES - 1, up_y, 0)
    own_ref[0] = first_column
    own_ref[1] = last_column
    edges_ref[...] = jnp.zeros_like(edges_ref)
    across = lax.axis_index("gy")

    @pl.when(across < edges_ref.shape[0] - 1)
    def _():
        edges_ref[across + 1] = last_column

    @pl.when(across > 0)
    def _():
        edges_ref[across - 1] = first_column


def bernstein(coord):
    other = 1.0 - coord
    return [
        other * other * other,
        3.0 * coord * other * other,
        3.0 * coord * coord * other,
        coord * coord * coord,
    ]


def weight_table(u, v, w):
    first, second, third = bernstein(u), bernstein(v), bernstein(w)
    line = iota((8, u.shape[1]), 0)
    inner = line & 3
    along = jnp.where(
        inner == 0,
        third[0],
        jnp.where(inner == 1, third[1], jnp.where(inner == 2, third[2], third[3])),
    )
    pair = jnp.concatenate(
        [
            jnp.where(line < 4, second[0], second[1]) * along,
            jnp.where(line < 4, second[2], second[3]) * along,
        ],
        axis=0,
    )
    return jnp.concatenate([pair * first[i] for i in range(4)], axis=0)


def add_tiles(out_ref, tile_ref, left, right):
    first_half = iota((4, LANES), 1) < LANES // 2
    for tile in range(tile_ref.shape[0]):
        term = jnp.dot(left(tile), right(tile), preferred_element_type=F32)
        term = term[:8] + term[8:]
        term = term + pltpu.roll(term, LANES // 2, 1)
        out_ref[tile_ref[tile]] += jnp.where(first_half, term[:4], term[4:])


def quotient_before(halo_ref, strip_ref, before_ref):
    def rows(ref, first, count):
        return [ref[first + k : first + k + 1, :] for k in range(count)]

    beside, inverse, entering = rows(halo_ref, 0, 3), rows(halo_ref, 3, 3), rows(halo_ref, 6, 3)
    far_load, within = rows(halo_ref, 18, 3), rows(strip_ref, 0, 6)
    far_scale = rows(strip_ref, 33, 3)
    far = [ratio(far_load[c], far_scale[c]) for c in range(3)]
    whole_block = [None, *within[:3], None, *within[3:], None]
    total = off_diagonal(lambda k: whole_block[k], beside)
    from_far = product(lambda k: strip_ref[24 + k : 25 + k, :], far)
    up_y = product(lambda k: strip_ref[6 + k : 7 + k, :], beside)
    low_y = product(lambda k: strip_ref[15 + k : 16 + k, :], beside)
    for c in range(3):
        before_ref[c : c + 1, :] = inverse[c] * (
            total[c]
            + from_far[c]
            + entering[c]
            + lanes_moved(up_y[c], 0.0, 1)
            + lanes_moved(low_y[c], 0.0, -1)
        )
    before_ref[3:, :] = jnp.zeros((before_ref.shape[0] - 3, LANES), F32)


def box_kernel(
    tile_ref, field_ref, part_ref, node_ref, param_ref, halo_ref, strip_ref,
    box_ref, adjoint_ref, before_ref, weights_ref, columns_ref, *, tile_points,
):
    cells_x = field_ref.shape[1]
    own = cells_x // 2
    quotient_before(halo_ref, strip_ref, before_ref)
    field = [field_ref[c] for c in range(3)]
    part = [part_ref[c] for c in range(3)]
    order = [field[0], part[0], field[2], field[1], part[1], part[2]]
    folded = [two_parts(jnp.concatenate([f[:own], f[own:]], axis=1)) for f in order]
    table = jnp.concatenate(
        [folded[f][which] for which in range(2) for f in range(6)], axis=0
    ).astype(BF16)
    points = param_ref.shape[1]
    pieces = CHUNK // LANES
    zero, one = jnp.zeros((), BF16), jnp.ones((), BF16)
    at_node = float_iota((2 * LANES, CHUNK), 0).astype(BF16)
    nothing = jnp.zeros((1, CHUNK), F32)
    highs, lows = [], []
    for chunk in range(points // CHUNK):
        node = jnp.concatenate(
            [node_ref[chunk * pieces + k : chunk * pieces + k + 1, :] for k in range(pieces)],
            axis=1,
        )
        row = lax.shift_right_logical(node, 7)
        column = node & (LANES - 1)
        lanes = slice(chunk * CHUNK, (chunk + 1) * CHUNK)
        at_edge = jnp.where(
            column == 0, row, jnp.where(column == LANES - 1, row + cells_x, -1)
        ).astype(F32)
        columns_ref[:, lanes] = jnp.where(
            at_node[: 2 * cells_x] == stretched(at_edge, 2 * cells_x), one, zero
        )
        place = column + jnp.where(row >= own, LANES, 0)
        row = jnp.where(row >= own, row - own, row)
        pick = jnp.where(at_node == stretched(place.astype(F32), 2 * LANES), one, zero)
        read = jnp.dot(table, pick, preferred_element_type=F32)
        read = read[: 6 * own] + read[6 * own :]
        here = iota((own, CHUNK), 0) == row
        values = [
            jnp.sum(
                jnp.where(here, read[f * own : (f + 1) * own], 0.0), axis=0, keepdims=True
            )
            for f in range(6)
        ]
        high, low = two_parts(
            jnp.concatenate(values[:3] + [nothing] + values[3:] + [nothing], axis=0)
        )
        highs.append(high)
        lows.append(low)
        weights = two_parts(
            weight_table(param_ref[0:1, lanes], param_ref[1:2, lanes], param_ref[2:3, lanes])
        )
        for k in range(CHUNK // tile_points):
            tile = slice(k * tile_points, (k + 1) * tile_points)
            sides = jnp.concatenate([weights[0][:, tile], weights[1][:, tile]], axis=0)
            weights_ref[chunk * (CHUNK // tile_points) + k] = sides.T.astype(BF16)
    box_ref[...] = jnp.zeros_like(box_ref)
    both = jnp.concatenate(
        [jnp.concatenate(highs, axis=1), jnp.concatenate(lows, axis=1)], axis=0
    ).astype(BF16)
    add_tiles(
        box_ref,
        tile_ref,
        lambda tile: both[:, tile * tile_points : (tile + 1) * tile_points],
        lambda tile: weights_ref[tile],
    )
    low_half = iota((2 * cells_x, LANES), 1) < LANES // 2
    for tile in range(tile_ref.shape[0]):
        lanes = slice(tile * tile_points, (tile + 1) * tile_points)
        term = jnp.dot(
            columns_ref[:, lanes], weights_ref[tile], preferred_element_type=F32
        )
        high, low = two_parts(term + pltpu.roll(term, LANES // 2, 1))
        adjoint_ref[tile] = jnp.where(low_half, high, low).astype(BF16)


def sums_kernel(
    tile_ref, edges_ref, own_ref, field_ref, part_ref, halo_ref,
    diag_ref, edge_ref, mask_ref, box_ref, adjoint_ref, before_ref,
    quotient_ref, out_ref,
):
    cells_x = field_ref.shape[1]
    targets = out_ref.shape[0]

    def arrived(sender):
        rest = jnp.zeros((LANES - 16, LANES), F32)
        return jnp.concatenate([edges_ref[sender], rest], axis=0).T

    across = lax.axis_index("gy")
    low = arrived(jnp.maximum(across - 1, 0))
    high = arrived(jnp.minimum(across + 1, edges_ref.shape[0] - 1))
    lane = iota((cells_x, LANES), 1)

    def column(source, slot, comp):
        return source[:cells_x, 3 * slot + comp : 3 * slot + comp + 1]

    field = [field_ref[c] for c in range(3)]
    scale = [diag_ref[4 * c] for c in range(3)]
    toward_high = masked_product(edge_ref, mask_ref, 2, field)
    toward_low = masked_product(edge_ref, mask_ref, 3, field)
    quotient, low_edge, high_edge = [], [], []
    for c in range(3):
        entering = jnp.where(
            lane == 0,
            column(low, 1, c),
            jnp.where(lane == LANES - 1, column(high, 1, c), 0.0),
        )
        quotient.append(part_ref[c] + entering / scale[c])
        low_edge.append(column(low, 2, c) + column(low, 3, c) * toward_low[c][:, :1])
        high_edge.append(column(high, 2, c) + column(high, 3, c) * toward_high[c][:, -1:])
    for c in range(3):
        quotient_ref[c] = quotient[c]
    lane_row = iota((1, LANES), 1)
    before, before_quotient = [], []
    for c in range(3):
        entering = jnp.where(
            lane_row == 0,
            low[cells_x : cells_x + 1, 3 + c : 4 + c],
            jnp.where(lane_row == LANES - 1, high[cells_x : cells_x + 1, 3 + c : 4 + c], 0.0),
        )
        before.append(halo_ref[c : c + 1, :])
        before_quotient.append(
            before_ref[c : c + 1, :] + entering * halo_ref[3 + c : 4 + c, :]
        )

    first_sum = sum(field[c] * scale[c] * field[c] for c in range(3))
    second_sum = sum(field[c] * scale[c] * quotient[c] for c in range(3))
    third_sum = sum(quotient[c] * scale[c] * quotient[c] for c in range(3))
    within = off_diagonal(lambda k: diag_ref[k], quotient)
    fourth_sum = sum(within[c] * field[c] for c in range(3))
    fifth_sum = sum(within[c] * quotient[c] for c in range(3))
    at_row = iota((cells_x, LANES), 0)
    moves = (
        (pltpu.roll, 1, 0, at_row == 0),
        (pltpu.roll, cells_x - 1, 0, at_row == cells_x - 1),
        (pltpu.roll, 1, 1, lane == 0),
        (pltpu.roll, LANES - 1, 1, lane == LANES - 1),
    )
    extra = [0.0, 0.0]
    sides = [0.0, 0.0]
    for direction, (roll, step, dim, edge) in enumerate(moves):
        moving = masked_product(edge_ref, mask_ref, direction, quotient)
        for c in range(3):
            moved = jnp.where(edge, 0.0, roll(moving[c], step, dim))
            fourth_sum = fourth_sum + moved * field[c]
            fifth_sum = fifth_sum + moved * quotient[c]
            if direction == 1:
                extra[0] += moving[c][:1] * before[c]
                extra[1] += moving[c][:1] * before_quotient[c]
            elif direction == 2:
                sides[0] += moving[c][:, LANES - 1 :] * column(high, 0, c)
                sides[1] += moving[c][:, LANES - 1 :] * high_edge[c]
            elif direction == 3:
                sides[0] += moving[c][:, :1] * column(low, 0, c)
                sides[1] += moving[c][:, :1] * low_edge[c]
    incoming = product(lambda k: halo_ref[9 + k : 10 + k, :], before_quotient)
    extra[0] += sum(incoming[c] * field[c][:1] for c in range(3))
    extra[1] += sum(incoming[c] * quotient[c][:1] for c in range(3))
    fourth_sum = fourth_sum + jnp.where(lane == 0, sides[0], 0.0)
    fifth_sum = fifth_sum + jnp.where(lane == 0, sides[1], 0.0)
    extra = [0.0, 0.0, 0.0, extra[0], extra[1]]
    sums = jnp.zeros((1, LANES), F32)
    for k, value in enumerate((first_sum, second_sum, third_sum, fourth_sum, fifth_sum)):
        line = jnp.sum(value, axis=0, keepdims=True) + extra[k]
        sums = jnp.where(lane_row == k, jnp.sum(line, axis=1, keepdims=True), sums)

    across_low = edges_ref[jnp.maximum(across - 1, 0)]
    across_high = edges_ref[jnp.minimum(across + 1, edges_ref.shape[0] - 1)]
    added = []
    for c in range(3):
        first = across_low[3 + c : 4 + c] * own_ref[0, 9 + c : 10 + c, :]
        second = across_high[3 + c : 4 + c] * own_ref[1, 9 + c : 10 + c, :]
        added.append(
            jnp.where(lane_row < cells_x, first, pltpu.roll(second, cells_x, 1))
        )
    none = jnp.zeros((1, LANES), F32)
    added = jnp.concatenate(
        [none, added[0], none, none, none, added[1], added[2], none], axis=0
    )
    added = jnp.concatenate(two_parts(added), axis=0).astype(BF16)
    out_ref[...] = box_ref[...]
    add_tiles(out_ref, tile_ref, lambda tile: added, lambda tile: adjoint_ref[tile])
    for box in range(targets):
        out_ref[box, 3:4, :] = sums


def result_kernel(got_ref, field_ref, quotient_ref, solution_ref, gradient_ref):
    total = jnp.sum(got_ref[...], axis=0)
    rho, a, b, t, u = [total[3:4, k : k + 1] for k in range(5)]
    ratio = a / rho
    norm = rho + a
    step = rho / norm
    rest = jnp.maximum(b - a * ratio, 0.0)
    beta = step * step * rest / rho
    rest_image = (b + u) - ratio * (a + b + a + t) + ratio * ratio * norm
    cross = (a + t) - ratio * norm
    curve = step * step * rest_image - step * beta * (rest + cross) + beta * beta * norm
    second = jnp.where(
        curve > 0.0, step * step * rest / jnp.where(curve > 0.0, curve, 1.0), 0.0
    )
    of_field = step + second * (beta + step * ratio)
    of_quotient = -(step * second)
    for c in range(3):
        solution_ref[c] = of_field * field_ref[c] + of_quotient * quotient_ref[c]
    gradient_ref[:, :LANES] = of_field * total[0:1] + of_quotient * total[1:2]
    gradient_ref[:, LANES:] = (
        of_field * total[2:3, : LANES // 2] + of_quotient * total[2:3, LANES // 2 :]
    )


def per_device(
    diag_blocks, edge_blocks, edge_mask, src_values, src_owner, src_node, src_count,
    surf_node, surf_param, tile_box,
):
    cells_x, cells_y = diag_blocks.shape[1:]
    width_gx, width_gy = lax.axis_size("gx"), lax.axis_size("gy")
    devices = width_gx * width_gy
    groups = src_node.shape[0] // LANES
    whole = functools.partial(jax.ShapeDtypeStruct, dtype=F32)

    cells = 4 * groups + NEAR

    def kept(array):
        return pltpu.with_memory_space_constraint(array, pltpu.HBM)

    i32 = jnp.int32
    rows, strip = pl.pallas_call(
        pack_kernel,
        in_specs=[HBM] * 7,
        out_specs=[VMEM] * 2,
        out_shape=[
            pltpu.VMEM((width_gx, cells, LANES), F32), pltpu.VMEM((STRIP, LANES), F32)
        ],
        scratch_shapes=[
            pltpu.SMEM((1,), i32),
            pltpu.VMEM(src_values.shape, F32),
            pltpu.VMEM((groups, LANES), i32),
            pltpu.VMEM((groups, LANES), i32),
            pltpu.VMEM((9, 8, cells_y), F32),
            pltpu.VMEM((9, 8, cells_y), F32),
            pltpu.VMEM((9, 8, cells_y), F32),
            pltpu.VMEM((4, 9, 8, cells_y), F32),
            pltpu.VMEM((8, cells_y), i32),
            pltpu.VMEM((4, 8, cells_y), i32),
            pltpu.SemaphoreType.DMA((10,)),
        ],
        compiler_params=PARAMS,
        name="pack_rows_and_edges",
    )(
        src_count, kept(src_values),
        kept(src_owner.reshape(groups, LANES)), kept(src_node.reshape(groups, LANES)),
        kept(diag_blocks), kept(edge_blocks), kept(edge_mask),
    )
    rows = lax.all_to_all(rows, "gx", split_axis=0, concat_axis=0, tiled=True)
    strip = lax.ppermute(strip, "gx", [(i, i + 1) for i in range(width_gx - 1)])

    nodes = (3, cells_x, cells_y)
    frame = cells_x + 2 * PAD
    field, part, halo, edges, own = pl.pallas_call(
        field_kernel,
        in_specs=[VMEM] * 4,
        out_specs=[VMEM] * 5,
        out_shape=[
            whole(nodes), whole(nodes), whole((24, cells_y)), whole((width_gy, 16, LANES)),
            whole((2, 16, LANES)),
        ],
        scratch_shapes=[pltpu.VMEM((3 * frame, 2 * LANES), F32)],
        compiler_params=PARAMS,
        name="load_and_first_product",
    )(rows, diag_blocks, edge_blocks, edge_mask)
    edges = lax.all_to_all(edges, "gy", split_axis=0, concat_axis=0, tiled=True)

    points, tiles = surf_node.shape[0], tile_box.shape[0]
    boxes = (devices, 4, LANES)
    box_part, adjoint, before = pl.pallas_call(
        functools.partial(box_kernel, tile_points=points // tiles),
        in_specs=[SMEM] + [VMEM] * 6,
        out_specs=[VMEM] * 3,
        out_shape=[
            whole(boxes),
            jax.ShapeDtypeStruct((tiles, 2 * cells_x, LANES), BF16),
            whole((8, LANES)),
        ],
        scratch_shapes=[
            pltpu.VMEM((tiles, points // tiles, LANES), BF16),
            pltpu.VMEM((2 * cells_x, points), BF16),
        ],
        compiler_params=PARAMS,
        cost_estimate=pl.CostEstimate(
            flops=10**9, bytes_accessed=4 * 10**6, transcendentals=0
        ),
        name="box_parts",
    )(
        tile_box, field, part, surf_node.reshape(points // LANES, LANES), surf_param, halo,
        strip,
    )

    quotient, partial = pl.pallas_call(
        sums_kernel,
        in_specs=[SMEM] + [VMEM] * 11,
        out_specs=[VMEM] * 2,
        out_shape=[whole(nodes), whole(boxes)],
        compiler_params=PARAMS,
        name="sums_and_halo_parts",
    )(
        tile_box, edges, own, field, part, halo, diag_blocks, edge_blocks, edge_mask,
        box_part, adjoint, before,
    )
    got = lax.all_to_all(partial, ("gx", "gy"), split_axis=0, concat_axis=0, tiled=True)
    return pl.pallas_call(
        result_kernel,
        in_specs=[VMEM] * 3,
        out_specs=[VMEM] * 2,
        out_shape=[whole(nodes), whole((1, 192))],
        compiler_params=PARAMS,
        name="steps_and_outputs",
    )(got, field, quotient)


def solution(mesh):
    return jax.shard_map(
        per_device,
        mesh=mesh,
        in_specs=(
            P(None, "gx", "gy"),
            P(None, None, "gx", "gy"),
            P(None, "gx", "gy"),
            P(None, ("gx", "gy")),
            P(("gx", "gy"), None),
            P(("gx", "gy")),
            P(("gx", "gy")),
            P(("gx", "gy")),
            P(None, ("gx", "gy")),
            P(("gx", "gy")),
        ),
        out_specs=(P(None, "gx", "gy"), P(("gx", "gy"), None)),
        check_vma=False,
    )
```

```python
import functools

import jax
import jax.numpy as jnp
from jax import lax
from jax.experimental import pallas as pl
from jax.experimental.pallas import tpu as pltpu
from jax.sharding import PartitionSpec as P

F32 = jnp.float32
BF16 = jnp.bfloat16
PAD = 16
NOWHERE = -(1 << 20)
LANES = 128
NEAR = 16
STRIP = 40
CHUNK = 256
PARAMS = pltpu.CompilerParams(vmem_limit_bytes=24 * 1024 * 1024)

VMEM = pl.BlockSpec(memory_space=pltpu.VMEM)
SMEM = pl.BlockSpec(memory_space=pltpu.SMEM)
HBM = pl.BlockSpec(memory_space=pltpu.HBM)


def iota(shape, dim):
    return lax.broadcasted_iota(jnp.int32, shape, dim)


def float_iota(shape, dim):
    return iota(shape, dim).astype(F32)


def two_parts(value):
    high = value.astype(BF16).astype(F32)
    return high, value - high


def product(block, field):
    return [
        block(row) * field[0] + block(3 + row) * field[1] + block(6 + row) * field[2]
        for row in range(3)
    ]


def off_diagonal(block, field):
    return [
        sum(block(3 * i + row) * field[i] for i in range(3) if i != row) for row in range(3)
    ]


def masked_product(edge_ref, mask_ref, direction, field):
    mask = mask_ref[direction].astype(F32)
    return [mask * part for part in product(lambda k: edge_ref[direction, k], field)]


def rows_moved(field, edge_row, step):
    size = field.shape[0]
    at = iota(field.shape, 0)
    moved = pltpu.roll(field, step % size, 0)
    return jnp.where(at == (0 if step == 1 else size - 1), edge_row, moved)


def lanes_moved(field, edge_column, step):
    size = field.shape[1]
    at = iota(field.shape, 1)
    moved = pltpu.roll(field, step % size, 1)
    return jnp.where(at == (0 if step == 1 else size - 1), edge_column, moved)


def pack_kernel(
    count_ref, values_in, owner_in, node_in, diag_in, edge_in, mask_in, rows_ref, strip_ref,
    values_ref, owner_ref, node_ref, diag_low, diag_high, edge_low, edge_high,
    mask_low, mask_high, arrived,
):
    targets = rows_ref.shape[0]
    groups = owner_ref.shape[0]
    cells_x = diag_in.shape[1]
    top = pl.ds(cells_x - 8, 8)
    copies = [
        pltpu.make_async_copy(source, target, arrived.at[k])
        for k, (source, target) in enumerate(
            (
                (owner_in, owner_ref),
                (node_in, node_ref),
                (values_in, values_ref),
                (diag_in.at[:, 0:8], diag_low),
                (diag_in.at[:, top], diag_high),
                (mask_in.at[1, 0:8], mask_low),
                (mask_in.at[:, top], mask_high),
                (edge_in.at[1, :, 0:8], edge_low),
                (edge_in.at[:, :, top], edge_high),
            )
        )
    ]
    for copy in copies:
        copy.start()
    near = 4 * groups
    for target in range(targets):
        rows_ref[target, near:, :] = jnp.zeros((NEAR, LANES), F32)
    for copy in copies[:2]:
        copy.wait()
    order = iota((groups, LANES), 0) * LANES + iota((groups, LANES), 1)
    node = node_ref[...]
    frame = cells_x + 2 * PAD
    row = owner_ref[...] * cells_x + lax.shift_right_logical(node, 7)
    row = jnp.where(order < count_ref[0], row, NOWHERE)
    column = node & (LANES - 1)
    for target in range(targets):
        line = row - (target * cells_x - PAD)
        inside = (line >= 0) & (line < frame)
        index = jnp.where(inside, line * LANES + column, -1)
        rows_ref[target, 3 * groups : 4 * groups, :] = index.astype(F32)

    copies[2].wait()
    for comp in range(3):
        value = jnp.concatenate(
            [
                values_ref[comp : comp + 1, group * LANES : (group + 1) * LANES]
                for group in range(groups)
            ],
            axis=0,
        )
        for target in range(targets):
            rows_ref[target, comp * groups : (comp + 1) * groups, :] = value
    for copy in copies[3:]:
        copy.wait()

    def block(edge, mask, direction, at):
        present = mask[direction, at : at + 1, :].astype(F32)
        return [edge[direction, k, at : at + 1, :] * present for k in range(9)]

    up_y, low_y = block(edge_high, mask_high, 2, 7), block(edge_high, mask_high, 3, 7)
    later = [diag_high[k, 7:8, :] for k in range(9) if k % 4]
    later += up_y + low_y + block(edge_high, mask_high, 0, 6)
    later += [diag_high[4 * k, 6:7, :] for k in range(3)]
    for k, value in enumerate(later):
        strip_ref[k : k + 1, :] = value
    strip_ref[len(later) :, :] = jnp.zeros((STRIP - len(later), LANES), F32)

    here = lax.axis_index("gx")

    @pl.when(here < targets - 1)
    def _():
        def put(slot, value):
            rows_ref[here + 1, near + slot : near + slot + 1, :] = value

        for k in range(3):
            put(k, diag_high[4 * k, 7:8, :])
        for k, value in enumerate(block(edge_high, mask_high, 0, 7)):
            put(3 + k, value)
        corners = jnp.zeros((1, LANES), F32)
        lane = iota((1, LANES), 1)
        for k in range(9):
            corners = jnp.where(lane == k, up_y[k][:, LANES - 1 :], corners)
            corners = jnp.where(lane == 9 + k, low_y[k][:, :1], corners)
        put(12, corners)

    @pl.when(here > 0)
    def _():
        def put(slot, value):
            rows_ref[here - 1, near + slot : near + slot + 1, :] = value

        for k in range(3):
            put(k, diag_low[4 * k, 0:1, :])
        present = mask_low[0:1, :].astype(F32)
        for k in range(9):
            put(3 + k, edge_low[k, 0:1, :] * present)


def stretched(row, count):
    tile = jnp.broadcast_to(row, (16, row.shape[1])).astype(BF16)
    return jnp.concatenate([tile] * (count // 16), axis=0)


def ratio(value, scale):
    return jnp.where(scale > 0.0, value / jnp.where(scale > 0.0, scale, 1.0), 0.0)


def field_kernel(
    rows_ref, diag_ref, edge_ref, mask_ref,
    field_ref, part_ref, halo_ref, edges_ref, own_ref, load_ref,
):
    senders = rows_ref.shape[0]
    groups = (rows_ref.shape[1] - NEAR) // 4
    cells_x = field_ref.shape[1]
    half = (cells_x + 2 * PAD) // 2
    own = cells_x // 2

    load_ref[...] = jnp.zeros_like(load_ref)
    here = lax.axis_index("gx")

    def add_rows(sender, carry):
        index = rows_ref[sender, 3 * groups : 4 * groups, :]
        split = float(half * LANES)
        index, shift = (
            jnp.where(index >= split, index - split, index),
            jnp.where(index >= split, float(LANES), 0.0),
        )
        place = jnp.floor(index * (1.0 / LANES))
        column = index - place * float(LANES) + shift
        at_row = float_iota((half, LANES), 0).astype(BF16)
        at_column = float_iota((2 * LANES, LANES), 0).astype(BF16)
        parts = [
            two_parts(rows_ref[sender, c * groups : (c + 1) * groups, :]) for c in range(3)
        ]
        zero, one = jnp.zeros((), BF16), jnp.ones((), BF16)
        lefts, rights = [], []
        for group in range(groups):
            line = slice(group, group + 1)
            match = at_row == stretched(place[line], half)
            lefts.append(
                jnp.concatenate(
                    [
                        jnp.where(match, stretched(parts[c][which][line], half), zero)
                        for which in range(2)
                        for c in range(3)
                    ],
                    axis=0,
                )
            )
            rights.append(
                jnp.where(at_column == stretched(column[line], 2 * LANES), one, zero)
            )
        load_ref[...] += lax.dot_general(
            jnp.concatenate(lefts, axis=1),
            jnp.concatenate(rights, axis=1),
            (((1,), (1,)), ((), ())),
            preferred_element_type=F32,
        )
        return carry

    lax.fori_loop(0, senders, add_rows, 0, unroll=min(senders, 8))

    def load_rows(comp, first, last, second_half):
        lanes = slice(LANES, 2 * LANES) if second_half else slice(0, LANES)
        return (
            load_ref[comp * half + first : comp * half + last, lanes]
            + load_ref[(3 + comp) * half + first : (3 + comp) * half + last, lanes]
        )

    field = []
    for comp in range(3):
        load = jnp.concatenate(
            [load_rows(comp, PAD, half, False), load_rows(comp, 0, half - PAD, True)], axis=0
        )
        field.append(load / diag_ref[4 * comp])
        field_ref[comp] = field[comp]
    beyond = half - PAD
    near_before = [load_rows(c, PAD - 1, PAD, False) for c in range(3)]
    far_before = [load_rows(c, PAD - 2, PAD - 1, False) for c in range(3)]
    near_after = [load_rows(c, beyond, beyond + 1, True) for c in range(3)]

    up_x = masked_product(edge_ref, mask_ref, 0, field)
    low_x = masked_product(edge_ref, mask_ref, 1, field)
    base = 4 * groups

    def neighbour(sender, load):
        def entry(k):
            return rows_ref[sender, base + k : base + k + 1, :]

        scale, toward = [entry(k) for k in range(3)], [entry(3 + k) for k in range(9)]
        beside = [ratio(load[c], scale[c]) for c in range(3)]
        return scale, toward, beside, product(lambda k: toward[k], beside)

    lower = jnp.maximum(here - 1, 0)
    before = neighbour(lower, near_before)
    after = neighbour(jnp.minimum(here + 1, senders - 1), near_after)
    rows = before[2] + [ratio(1.0, scale) for scale in before[0]]
    rows += [p[:1] for p in low_x] + before[1] + far_before
    for k, value in enumerate(rows):
        halo_ref[k : k + 1, :] = value
    halo_ref[len(rows) :, :] = jnp.zeros((halo_ref.shape[0] - len(rows), LANES), F32)
    lane_row = iota((1, LANES), 1)
    ends = jnp.zeros((1, LANES), F32)
    for i in range(3):
        for a in range(3):
            ends = jnp.where(lane_row == 3 * i + a, before[2][i][:, LANES - 1 :], ends)
            ends = jnp.where(lane_row == 9 + 3 * i + a, before[2][i][:, :1], ends)
    ends = ends * rows_ref[lower, base + 12 : base + 13, :]
    ends = ends + pltpu.roll(ends, LANES - 3, 1) + pltpu.roll(ends, LANES - 6, 1)

    total = off_diagonal(lambda k: diag_ref[k], field)
    total = [total[c] + rows_moved(up_x[c], before[3][c], 1) for c in range(3)]
    total = [total[c] + rows_moved(low_x[c], after[3][c], -1) for c in range(3)]
    up_y = masked_product(edge_ref, mask_ref, 2, field)
    low_y = masked_product(edge_ref, mask_ref, 3, field)
    total = [
        total[c] + lanes_moved(up_y[c], 0.0, 1) + lanes_moved(low_y[c], 0.0, -1)
        for c in range(3)
    ]
    inverse = [1.0 / diag_ref[4 * c] for c in range(3)]
    part = [total[c] * inverse[c] for c in range(3)]
    for comp in range(3):
        part_ref[comp] = part[comp]
    def columns(lane, along_y, end):
        packed = jnp.zeros((cells_x, LANES), F32)
        at = iota((cells_x, LANES), 1)
        for slot, fields in enumerate((field, along_y, part, inverse)):
            for comp in range(3):
                column = fields[comp][:, lane : lane + 1]
                packed = jnp.where(at == 3 * slot + comp, column, packed)
        rest = jnp.zeros((LANES - cells_x, LANES), F32)
        turned = jnp.concatenate([packed, rest], axis=0).T[:16]
        at = iota((16, LANES), 1)
        line = iota((16, LANES), 0)
        for comp in range(3):
            turned = jnp.where(
                (line == 3 + comp) & (at == cells_x),
                ends[:, end + comp : end + comp + 1],
                turned,
            )
        return turned

    first_column = columns(0, low_y, 9)
    last_column = columns(LANES - 1, up_y, 0)
    own_ref[0] = first_column
    own_ref[1] = last_column
    edges_ref[...] = jnp.zeros_like(edges_ref)
    across = lax.axis_index("gy")

    @pl.when(across < edges_ref.shape[0] - 1)
    def _():
        edges_ref[across + 1] = last_column

    @pl.when(across > 0)
    def _():
        edges_ref[across - 1] = first_column


def bernstein(coord):
    other = 1.0 - coord
    return [
        other * other * other,
        3.0 * coord * other * other,
        3.0 * coord * coord * other,
        coord * coord * coord,
    ]


def weight_table(u, v, w):
    first, second, third = bernstein(u), bernstein(v), bernstein(w)
    line = iota((8, u.shape[1]), 0)
    inner = line & 3
    along = jnp.where(
        inner == 0,
        third[0],
        jnp.where(inner == 1, third[1], jnp.where(inner == 2, third[2], third[3])),
    )
    pair = jnp.concatenate(
        [
            jnp.where(line < 4, second[0], second[1]) * along,
            jnp.where(line < 4, second[2], second[3]) * along,
        ],
        axis=0,
    )
    return jnp.concatenate([pair * first[i] for i in range(4)], axis=0)


def tile_rows(terms):
    first_half = iota((4, LANES), 1) < LANES // 2
    rows = []
    for term in terms:
        term = term[:8] + term[8:]
        term = term + pltpu.roll(term, LANES // 2, 1)
        rows.append(jnp.where(first_half, term[:4], term[4:]))
    return jnp.concatenate(two_parts(jnp.concatenate(rows, axis=0)), axis=0).astype(BF16)


def box_matrix(tile_row, boxes):
    tiles = tile_row.shape[1]
    shape = (4 * boxes, 8 * tiles)
    column = iota((1, shape[1]), 1)
    box = jnp.zeros((1, shape[1]), jnp.int32)
    for tile in range(tiles):
        mine = lax.rem(lax.shift_right_logical(column, 2), tiles) == tile
        box = jnp.where(mine, tile_row[:, tile : tile + 1], box)
    target = 4 * box + (column & 3)
    return jnp.where(iota(shape, 0) == target, 1.0, 0.0).astype(BF16)


def quotient_before(halo_ref, strip_ref, before_ref):
    def rows(ref, first, count):
        return [ref[first + k : first + k + 1, :] for k in range(count)]

    beside, inverse, entering = rows(halo_ref, 0, 3), rows(halo_ref, 3, 3), rows(halo_ref, 6, 3)
    far_load, within = rows(halo_ref, 18, 3), rows(strip_ref, 0, 6)
    far_scale = rows(strip_ref, 33, 3)
    far = [ratio(far_load[c], far_scale[c]) for c in range(3)]
    whole_block = [None, *within[:3], None, *within[3:], None]
    total = off_diagonal(lambda k: whole_block[k], beside)
    from_far = product(lambda k: strip_ref[24 + k : 25 + k, :], far)
    up_y = product(lambda k: strip_ref[6 + k : 7 + k, :], beside)
    low_y = product(lambda k: strip_ref[15 + k : 16 + k, :], beside)
    for c in range(3):
        before_ref[c : c + 1, :] = inverse[c] * (
            total[c]
            + from_far[c]
            + entering[c]
            + lanes_moved(up_y[c], 0.0, 1)
            + lanes_moved(low_y[c], 0.0, -1)
        )
    before_ref[3:, :] = jnp.zeros((before_ref.shape[0] - 3, LANES), F32)


def box_kernel(
    tile_ref, field_ref, part_ref, node_ref, param_ref, halo_ref, strip_ref,
    box_ref, adjoint_ref, before_ref, matrix_ref, weights_ref, columns_ref, *, tile_points,
):
    cells_x = field_ref.shape[1]
    own = cells_x // 2
    quotient_before(halo_ref, strip_ref, before_ref)
    field = [field_ref[c] for c in range(3)]
    part = [part_ref[c] for c in range(3)]
    order = [field[0], part[0], field[2], field[1], part[1], part[2]]
    folded = [two_parts(jnp.concatenate([f[:own], f[own:]], axis=1)) for f in order]
    table = jnp.concatenate(
        [folded[f][which] for which in range(2) for f in range(6)], axis=0
    ).astype(BF16)
    points = param_ref.shape[1]
    pieces = CHUNK // LANES
    zero, one = jnp.zeros((), BF16), jnp.ones((), BF16)
    at_node = float_iota((2 * LANES, CHUNK), 0).astype(BF16)
    nothing = jnp.zeros((1, CHUNK), F32)
    highs, lows = [], []
    for chunk in range(points // CHUNK):
        node = jnp.concatenate(
            [node_ref[chunk * pieces + k : chunk * pieces + k + 1, :] for k in range(pieces)],
            axis=1,
        )
        row = lax.shift_right_logical(node, 7)
        column = node & (LANES - 1)
        lanes = slice(chunk * CHUNK, (chunk + 1) * CHUNK)
        at_edge = jnp.where(
            column == 0, row, jnp.where(column == LANES - 1, row + cells_x, -1)
        ).astype(F32)
        columns_ref[:, lanes] = jnp.where(
            at_node[: 2 * cells_x] == stretched(at_edge, 2 * cells_x), one, zero
        )
        place = column + jnp.where(row >= own, LANES, 0)
        row = jnp.where(row >= own, row - own, row)
        pick = jnp.where(at_node == stretched(place.astype(F32), 2 * LANES), one, zero)
        read = jnp.dot(table, pick, preferred_element_type=F32)
        read = read[: 6 * own] + read[6 * own :]
        here = iota((own, CHUNK), 0) == row
        values = [
            jnp.sum(
                jnp.where(here, read[f * own : (f + 1) * own], 0.0), axis=0, keepdims=True
            )
            for f in range(6)
        ]
        high, low = two_parts(
            jnp.concatenate(values[:3] + [nothing] + values[3:] + [nothing], axis=0)
        )
        highs.append(high)
        lows.append(low)
        weights = two_parts(
            weight_table(param_ref[0:1, lanes], param_ref[1:2, lanes], param_ref[2:3, lanes])
        )
        for k in range(CHUNK // tile_points):
            tile = slice(k * tile_points, (k + 1) * tile_points)
            sides = jnp.concatenate([weights[0][:, tile], weights[1][:, tile]], axis=0)
            weights_ref[chunk * (CHUNK // tile_points) + k] = sides.T.astype(BF16)
    both = jnp.concatenate(
        [jnp.concatenate(highs, axis=1), jnp.concatenate(lows, axis=1)], axis=0
    ).astype(BF16)
    matrix_ref[...] = box_matrix(tile_ref[...], matrix_ref.shape[0] // 4)
    tiles = tile_ref.shape[1]
    terms = [
        jnp.dot(
            both[:, tile * tile_points : (tile + 1) * tile_points],
            weights_ref[tile],
            preferred_element_type=F32,
        )
        for tile in range(tiles)
    ]
    box_ref[...] = jnp.dot(matrix_ref[...], tile_rows(terms), preferred_element_type=F32)
    low_half = iota((2 * cells_x, LANES), 1) < LANES // 2
    for tile in range(tiles):
        lanes = slice(tile * tile_points, (tile + 1) * tile_points)
        term = jnp.dot(
            columns_ref[:, lanes], weights_ref[tile], preferred_element_type=F32
        )
        high, low = two_parts(term + pltpu.roll(term, LANES // 2, 1))
        adjoint_ref[tile] = jnp.where(low_half, high, low).astype(BF16)


def sums_kernel(
    edges_ref, own_ref, field_ref, part_ref, halo_ref,
    diag_ref, edge_ref, mask_ref, box_ref, adjoint_ref, before_ref, matrix_ref,
    quotient_ref, out_ref,
):
    cells_x = field_ref.shape[1]
    targets = out_ref.shape[0]

    def arrived(sender):
        rest = jnp.zeros((LANES - 16, LANES), F32)
        return jnp.concatenate([edges_ref[sender], rest], axis=0).T

    across = lax.axis_index("gy")
    low = arrived(jnp.maximum(across - 1, 0))
    high = arrived(jnp.minimum(across + 1, edges_ref.shape[0] - 1))
    lane = iota((cells_x, LANES), 1)

    def column(source, slot, comp):
        return source[:cells_x, 3 * slot + comp : 3 * slot + comp + 1]

    field = [field_ref[c] for c in range(3)]
    scale = [diag_ref[4 * c] for c in range(3)]
    toward_high = masked_product(edge_ref, mask_ref, 2, field)
    toward_low = masked_product(edge_ref, mask_ref, 3, field)
    quotient, low_edge, high_edge = [], [], []
    for c in range(3):
        entering = jnp.where(
            lane == 0,
            column(low, 1, c),
            jnp.where(lane == LANES - 1, column(high, 1, c), 0.0),
        )
        quotient.append(part_ref[c] + entering / scale[c])
        low_edge.append(column(low, 2, c) + column(low, 3, c) * toward_low[c][:, :1])
        high_edge.append(column(high, 2, c) + column(high, 3, c) * toward_high[c][:, -1:])
    for c in range(3):
        quotient_ref[c] = quotient[c]
    lane_row = iota((1, LANES), 1)
    before, before_quotient = [], []
    for c in range(3):
        entering = jnp.where(
            lane_row == 0,
            low[cells_x : cells_x + 1, 3 + c : 4 + c],
            jnp.where(lane_row == LANES - 1, high[cells_x : cells_x + 1, 3 + c : 4 + c], 0.0),
        )
        before.append(halo_ref[c : c + 1, :])
        before_quotient.append(
            before_ref[c : c + 1, :] + entering * halo_ref[3 + c : 4 + c, :]
        )

    first_sum = sum(field[c] * scale[c] * field[c] for c in range(3))
    second_sum = sum(field[c] * scale[c] * quotient[c] for c in range(3))
    third_sum = sum(quotient[c] * scale[c] * quotient[c] for c in range(3))
    within = off_diagonal(lambda k: diag_ref[k], quotient)
    fourth_sum = sum(within[c] * field[c] for c in range(3))
    fifth_sum = sum(within[c] * quotient[c] for c in range(3))
    at_row = iota((cells_x, LANES), 0)
    moves = (
        (pltpu.roll, 1, 0, at_row == 0),
        (pltpu.roll, cells_x - 1, 0, at_row == cells_x - 1),
        (pltpu.roll, 1, 1, lane == 0),
        (pltpu.roll, LANES - 1, 1, lane == LANES - 1),
    )
    extra = [0.0, 0.0]
    sides = [0.0, 0.0]
    for direction, (roll, step, dim, edge) in enumerate(moves):
        moving = masked_product(edge_ref, mask_ref, direction, quotient)
        for c in range(3):
            moved = jnp.where(edge, 0.0, roll(moving[c], step, dim))
            fourth_sum = fourth_sum + moved * field[c]
            fifth_sum = fifth_sum + moved * quotient[c]
            if direction == 1:
                extra[0] += moving[c][:1] * before[c]
                extra[1] += moving[c][:1] * before_quotient[c]
            elif direction == 2:
                sides[0] += moving[c][:, LANES - 1 :] * column(high, 0, c)
                sides[1] += moving[c][:, LANES - 1 :] * high_edge[c]
            elif direction == 3:
                sides[0] += moving[c][:, :1] * column(low, 0, c)
                sides[1] += moving[c][:, :1] * low_edge[c]
    incoming = product(lambda k: halo_ref[9 + k : 10 + k, :], before_quotient)
    extra[0] += sum(incoming[c] * field[c][:1] for c in range(3))
    extra[1] += sum(incoming[c] * quotient[c][:1] for c in range(3))
    fourth_sum = fourth_sum + jnp.where(lane == 0, sides[0], 0.0)
    fifth_sum = fifth_sum + jnp.where(lane == 0, sides[1], 0.0)
    extra = [0.0, 0.0, 0.0, extra[0], extra[1]]
    sums = jnp.zeros((1, LANES), F32)
    for k, value in enumerate((first_sum, second_sum, third_sum, fourth_sum, fifth_sum)):
        line = jnp.sum(value, axis=0, keepdims=True) + extra[k]
        sums = jnp.where(lane_row == k, jnp.sum(line, axis=1, keepdims=True), sums)

    across_low = edges_ref[jnp.maximum(across - 1, 0)]
    across_high = edges_ref[jnp.minimum(across + 1, edges_ref.shape[0] - 1)]
    added = []
    for c in range(3):
        first = across_low[3 + c : 4 + c] * own_ref[0, 9 + c : 10 + c, :]
        second = across_high[3 + c : 4 + c] * own_ref[1, 9 + c : 10 + c, :]
        added.append(
            jnp.where(lane_row < cells_x, first, pltpu.roll(second, cells_x, 1))
        )
    none = jnp.zeros((1, LANES), F32)
    added = jnp.concatenate(
        [none, added[0], none, none, none, added[1], added[2], none], axis=0
    )
    added = jnp.concatenate(two_parts(added), axis=0).astype(BF16)
    terms = [
        jnp.dot(added, adjoint_ref[tile], preferred_element_type=F32)
        for tile in range(adjoint_ref.shape[0])
    ]
    total = box_ref[...] + jnp.dot(
        matrix_ref[...], tile_rows(terms), preferred_element_type=F32
    )
    total = jnp.where((iota(total.shape, 0) & 3) == 3, sums, total)
    for box in range(targets):
        out_ref[box] = total[4 * box : 4 * box + 4]


def result_kernel(got_ref, field_ref, quotient_ref, solution_ref, gradient_ref):
    total = jnp.sum(got_ref[...], axis=0)
    rho, a, b, t, u = [total[3:4, k : k + 1] for k in range(5)]
    ratio = a / rho
    norm = rho + a
    step = rho / norm
    rest = jnp.maximum(b - a * ratio, 0.0)
    beta = step * step * rest / rho
    rest_image = (b + u) - ratio * (a + b + a + t) + ratio * ratio * norm
    cross = (a + t) - ratio * norm
    curve = step * step * rest_image - step * beta * (rest + cross) + beta * beta * norm
    second = jnp.where(
        curve > 0.0, step * step * rest / jnp.where(curve > 0.0, curve, 1.0), 0.0
    )
    of_field = step + second * (beta + step * ratio)
    of_quotient = -(step * second)
    for c in range(3):
        solution_ref[c] = of_field * field_ref[c] + of_quotient * quotient_ref[c]
    gradient_ref[:, :LANES] = of_field * total[0:1] + of_quotient * total[1:2]
    gradient_ref[:, LANES:] = (
        of_field * total[2:3, : LANES // 2] + of_quotient * total[2:3, LANES // 2 :]
    )


def per_device(
    diag_blocks, edge_blocks, edge_mask, src_values, src_owner, src_node, src_count,
    surf_node, surf_param, tile_box,
):
    cells_x, cells_y = diag_blocks.shape[1:]
    width_gx, width_gy = lax.axis_size("gx"), lax.axis_size("gy")
    devices = width_gx * width_gy
    groups = src_node.shape[0] // LANES
    whole = functools.partial(jax.ShapeDtypeStruct, dtype=F32)

    cells = 4 * groups + NEAR

    def kept(array):
        return pltpu.with_memory_space_constraint(array, pltpu.HBM)

    i32 = jnp.int32
    rows, strip = pl.pallas_call(
        pack_kernel,
        in_specs=[SMEM] + [HBM] * 6,
        out_specs=[VMEM] * 2,
        out_shape=[
            pltpu.VMEM((width_gx, cells, LANES), F32), pltpu.VMEM((STRIP, LANES), F32)
        ],
        scratch_shapes=[
            pltpu.VMEM(src_values.shape, F32),
            pltpu.VMEM((groups, LANES), i32),
            pltpu.VMEM((groups, LANES), i32),
            pltpu.VMEM((9, 8, cells_y), F32),
            pltpu.VMEM((9, 8, cells_y), F32),
            pltpu.VMEM((9, 8, cells_y), F32),
            pltpu.VMEM((4, 9, 8, cells_y), F32),
            pltpu.VMEM((8, cells_y), i32),
            pltpu.VMEM((4, 8, cells_y), i32),
            pltpu.SemaphoreType.DMA((9,)),
        ],
        compiler_params=PARAMS,
        name="pack_rows_and_edges",
    )(
        src_count, kept(src_values),
        kept(src_owner.reshape(groups, LANES)), kept(src_node.reshape(groups, LANES)),
        kept(diag_blocks), kept(edge_blocks), kept(edge_mask),
    )
    rows = lax.all_to_all(rows, "gx", split_axis=0, concat_axis=0, tiled=True)
    strip = lax.ppermute(strip, "gx", [(i, i + 1) for i in range(width_gx - 1)])

    nodes = (3, cells_x, cells_y)
    frame = cells_x + 2 * PAD
    field, part, halo, edges, own = pl.pallas_call(
        field_kernel,
        in_specs=[VMEM] * 4,
        out_specs=[VMEM] * 5,
        out_shape=[
            whole(nodes), whole(nodes), whole((24, cells_y)), whole((width_gy, 16, LANES)),
            whole((2, 16, LANES)),
        ],
        scratch_shapes=[pltpu.VMEM((3 * frame, 2 * LANES), F32)],
        compiler_params=PARAMS,
        name="load_and_first_product",
    )(rows, diag_blocks, edge_blocks, edge_mask)
    edges = lax.all_to_all(edges, "gy", split_axis=0, concat_axis=0, tiled=True)

    points, tiles = surf_node.shape[0], tile_box.shape[0]
    box_part, adjoint, before, matrix = pl.pallas_call(
        functools.partial(box_kernel, tile_points=points // tiles),
        in_specs=[VMEM] * 7,
        out_specs=[VMEM] * 4,
        out_shape=[
            whole((4 * devices, LANES)),
            jax.ShapeDtypeStruct((tiles, 2 * cells_x, LANES), BF16),
            whole((8, LANES)),
            jax.ShapeDtypeStruct((4 * devices, 8 * tiles), BF16),
        ],
        scratch_shapes=[
            pltpu.VMEM((tiles, points // tiles, LANES), BF16),
            pltpu.VMEM((2 * cells_x, points), BF16),
        ],
        compiler_params=PARAMS,
        cost_estimate=pl.CostEstimate(
            flops=10**9, bytes_accessed=4 * 10**6, transcendentals=0
        ),
        name="box_parts",
    )(
        tile_box.reshape(1, tiles), field, part, surf_node.reshape(points // LANES, LANES),
        surf_param, halo, strip,
    )

    quotient, partial = pl.pallas_call(
        sums_kernel,
        in_specs=[VMEM] * 12,
        out_specs=[VMEM] * 2,
        out_shape=[whole(nodes), whole((devices, 4, LANES))],
        compiler_params=PARAMS,
        name="sums_and_halo_parts",
    )(
        edges, own, field, part, halo, diag_blocks, edge_blocks, edge_mask,
        box_part, adjoint, before, matrix,
    )
    got = lax.all_to_all(partial, ("gx", "gy"), split_axis=0, concat_axis=0, tiled=True)
    return pl.pallas_call(
        result_kernel,
        in_specs=[VMEM] * 3,
        out_specs=[VMEM] * 2,
        out_shape=[whole(nodes), whole((1, 192))],
        compiler_params=PARAMS,
        name="steps_and_outputs",
    )(got, field, quotient)


def solution(mesh):
    return jax.shard_map(
        per_device,
        mesh=mesh,
        in_specs=(
            P(None, "gx", "gy"),
            P(None, None, "gx", "gy"),
            P(None, "gx", "gy"),
            P(None, ("gx", "gy")),
            P(("gx", "gy"), None),
            P(("gx", "gy")),
            P(("gx", "gy")),
            P(("gx", "gy")),
            P(None, ("gx", "gy")),
            P(("gx", "gy")),
        ),
        out_specs=(P(None, "gx", "gy"), P(("gx", "gy"), None)),
        check_vma=False,
    )
```

```python
import functools

import jax
import jax.numpy as jnp
from jax import lax
from jax.experimental import pallas as pl
from jax.experimental.pallas import tpu as pltpu
from jax.sharding import PartitionSpec as P

F32 = jnp.float32
BF16 = jnp.bfloat16
PAD = 16
NOWHERE = -(1 << 20)
LANES = 128
NEAR = 16
STRIP = 40
CHUNK = 256
PARAMS = pltpu.CompilerParams(vmem_limit_bytes=24 * 1024 * 1024)

VMEM = pl.BlockSpec(memory_space=pltpu.VMEM)
SMEM = pl.BlockSpec(memory_space=pltpu.SMEM)
HBM = pl.BlockSpec(memory_space=pltpu.HBM)


def iota(shape, dim):
    return lax.broadcasted_iota(jnp.int32, shape, dim)


def float_iota(shape, dim):
    return iota(shape, dim).astype(F32)


def two_parts(value):
    high = value.astype(BF16).astype(F32)
    return high, value - high


def product(block, field):
    return [
        block(row) * field[0] + block(3 + row) * field[1] + block(6 + row) * field[2]
        for row in range(3)
    ]


def off_diagonal(block, field):
    return [
        sum(block(3 * i + row) * field[i] for i in range(3) if i != row) for row in range(3)
    ]


def masked_product(edge_ref, mask_ref, direction, field):
    mask = mask_ref[direction].astype(F32)
    return [mask * part for part in product(lambda k: edge_ref[direction, k], field)]


def rows_moved(field, edge_row, step):
    size = field.shape[0]
    at = iota(field.shape, 0)
    moved = pltpu.roll(field, step % size, 0)
    return jnp.where(at == (0 if step == 1 else size - 1), edge_row, moved)


def lanes_moved(field, edge_column, step):
    size = field.shape[1]
    at = iota(field.shape, 1)
    moved = pltpu.roll(field, step % size, 1)
    return jnp.where(at == (0 if step == 1 else size - 1), edge_column, moved)


def pack_kernel(
    count_ref, values_in, owner_in, node_in, diag_in, edge_in, mask_in, rows_ref, strip_ref,
    values_ref, owner_ref, node_ref, diag_low, diag_high, edge_low, edge_high,
    mask_low, mask_high, arrived,
):
    targets = rows_ref.shape[0]
    groups = owner_ref.shape[0]
    cells_x = diag_in.shape[1]
    top = pl.ds(cells_x - 8, 8)
    copies = [
        pltpu.make_async_copy(source, target, arrived.at[k])
        for k, (source, target) in enumerate(
            (
                (owner_in, owner_ref),
                (node_in, node_ref),
                (values_in, values_ref),
                (diag_in.at[:, 0:8], diag_low),
                (diag_in.at[:, top], diag_high),
                (mask_in.at[1, 0:8], mask_low),
                (mask_in.at[:, top], mask_high),
                (edge_in.at[1, :, 0:8], edge_low),
                (edge_in.at[:, :, top], edge_high),
            )
        )
    ]
    for copy in copies:
        copy.start()
    near = 4 * groups
    for target in range(targets):
        rows_ref[target, near:, :] = jnp.zeros((NEAR, LANES), F32)
    for copy in copies[:2]:
        copy.wait()
    order = iota((groups, LANES), 0) * LANES + iota((groups, LANES), 1)
    node = node_ref[...]
    frame = cells_x + 2 * PAD
    row = owner_ref[...] * cells_x + lax.shift_right_logical(node, 7)
    row = jnp.where(order < count_ref[0], row, NOWHERE)
    column = node & (LANES - 1)
    for target in range(targets):
        line = row - (target * cells_x - PAD)
        inside = (line >= 0) & (line < frame)
        index = jnp.where(inside, line * LANES + column, -1)
        rows_ref[target, 3 * groups : 4 * groups, :] = index.astype(F32)

    copies[2].wait()
    for comp in range(3):
        value = jnp.concatenate(
            [
                values_ref[comp : comp + 1, group * LANES : (group + 1) * LANES]
                for group in range(groups)
            ],
            axis=0,
        )
        for target in range(targets):
            rows_ref[target, comp * groups : (comp + 1) * groups, :] = value
    for copy in copies[3:]:
        copy.wait()

    def block(edge, mask, direction, at):
        present = mask[direction, at : at + 1, :].astype(F32)
        return [edge[direction, k, at : at + 1, :] * present for k in range(9)]

    up_y, low_y = block(edge_high, mask_high, 2, 7), block(edge_high, mask_high, 3, 7)
    later = [diag_high[k, 7:8, :] for k in range(9) if k % 4]
    later += up_y + low_y + block(edge_high, mask_high, 0, 6)
    later += [diag_high[4 * k, 6:7, :] for k in range(3)]
    for k, value in enumerate(later):
        strip_ref[k : k + 1, :] = value
    strip_ref[len(later) :, :] = jnp.zeros((STRIP - len(later), LANES), F32)

    here = lax.axis_index("gx")

    @pl.when(here < targets - 1)
    def _():
        def put(slot, value):
            rows_ref[here + 1, near + slot : near + slot + 1, :] = value

        for k in range(3):
            put(k, diag_high[4 * k, 7:8, :])
        for k, value in enumerate(block(edge_high, mask_high, 0, 7)):
            put(3 + k, value)
        corners = jnp.zeros((1, LANES), F32)
        lane = iota((1, LANES), 1)
        for k in range(9):
            corners = jnp.where(lane == k, up_y[k][:, LANES - 1 :], corners)
            corners = jnp.where(lane == 9 + k, low_y[k][:, :1], corners)
        put(12, corners)

    @pl.when(here > 0)
    def _():
        def put(slot, value):
            rows_ref[here - 1, near + slot : near + slot + 1, :] = value

        for k in range(3):
            put(k, diag_low[4 * k, 0:1, :])
        present = mask_low[0:1, :].astype(F32)
        for k in range(9):
            put(3 + k, edge_low[k, 0:1, :] * present)


def stretched(row, count):
    tile = jnp.broadcast_to(row, (16, row.shape[1])).astype(BF16)
    return jnp.concatenate([tile] * (count // 16), axis=0)


def ratio(value, scale):
    return jnp.where(scale > 0.0, value / jnp.where(scale > 0.0, scale, 1.0), 0.0)


def field_kernel(
    rows_ref, diag_ref, edge_ref, mask_ref,
    field_ref, part_ref, halo_ref, first_ref, last_ref, load_ref,
):
    senders = rows_ref.shape[0]
    groups = (rows_ref.shape[1] - NEAR) // 4
    cells_x = field_ref.shape[1]
    half = (cells_x + 2 * PAD) // 2
    own = cells_x // 2

    load_ref[...] = jnp.zeros_like(load_ref)
    here = lax.axis_index("gx")

    def add_rows(sender, carry):
        index = rows_ref[sender, 3 * groups : 4 * groups, :]
        split = float(half * LANES)
        index, shift = (
            jnp.where(index >= split, index - split, index),
            jnp.where(index >= split, float(LANES), 0.0),
        )
        place = jnp.floor(index * (1.0 / LANES))
        column = index - place * float(LANES) + shift
        at_row = float_iota((half, LANES), 0).astype(BF16)
        at_column = float_iota((2 * LANES, LANES), 0).astype(BF16)
        parts = [
            two_parts(rows_ref[sender, c * groups : (c + 1) * groups, :]) for c in range(3)
        ]
        zero, one = jnp.zeros((), BF16), jnp.ones((), BF16)
        lefts, rights = [], []
        for group in range(groups):
            line = slice(group, group + 1)
            match = at_row == stretched(place[line], half)
            lefts.append(
                jnp.concatenate(
                    [
                        jnp.where(match, stretched(parts[c][which][line], half), zero)
                        for which in range(2)
                        for c in range(3)
                    ],
                    axis=0,
                )
            )
            rights.append(
                jnp.where(at_column == stretched(column[line], 2 * LANES), one, zero)
            )
        load_ref[...] += lax.dot_general(
            jnp.concatenate(lefts, axis=1),
            jnp.concatenate(rights, axis=1),
            (((1,), (1,)), ((), ())),
            preferred_element_type=F32,
        )
        return carry

    lax.fori_loop(0, senders, add_rows, 0, unroll=min(senders, 8))

    def load_rows(comp, first, last, second_half):
        lanes = slice(LANES, 2 * LANES) if second_half else slice(0, LANES)
        return (
            load_ref[comp * half + first : comp * half + last, lanes]
            + load_ref[(3 + comp) * half + first : (3 + comp) * half + last, lanes]
        )

    field = []
    for comp in range(3):
        load = jnp.concatenate(
            [load_rows(comp, PAD, half, False), load_rows(comp, 0, half - PAD, True)], axis=0
        )
        field.append(load / diag_ref[4 * comp])
        field_ref[comp] = field[comp]
    beyond = half - PAD
    near_before = [load_rows(c, PAD - 1, PAD, False) for c in range(3)]
    far_before = [load_rows(c, PAD - 2, PAD - 1, False) for c in range(3)]
    near_after = [load_rows(c, beyond, beyond + 1, True) for c in range(3)]

    up_x = masked_product(edge_ref, mask_ref, 0, field)
    low_x = masked_product(edge_ref, mask_ref, 1, field)
    base = 4 * groups

    def neighbour(sender, load):
        def entry(k):
            return rows_ref[sender, base + k : base + k + 1, :]

        scale, toward = [entry(k) for k in range(3)], [entry(3 + k) for k in range(9)]
        beside = [ratio(load[c], scale[c]) for c in range(3)]
        return scale, toward, beside, product(lambda k: toward[k], beside)

    lower = jnp.maximum(here - 1, 0)
    before = neighbour(lower, near_before)
    after = neighbour(jnp.minimum(here + 1, senders - 1), near_after)
    rows = before[2] + [ratio(1.0, scale) for scale in before[0]]
    rows += [p[:1] for p in low_x] + before[1] + far_before
    for k, value in enumerate(rows):
        halo_ref[k : k + 1, :] = value
    halo_ref[len(rows) :, :] = jnp.zeros((halo_ref.shape[0] - len(rows), LANES), F32)
    lane_row = iota((1, LANES), 1)
    ends = jnp.zeros((1, LANES), F32)
    for i in range(3):
        for a in range(3):
            ends = jnp.where(lane_row == 3 * i + a, before[2][i][:, LANES - 1 :], ends)
            ends = jnp.where(lane_row == 9 + 3 * i + a, before[2][i][:, :1], ends)
    ends = ends * rows_ref[lower, base + 12 : base + 13, :]
    ends = ends + pltpu.roll(ends, LANES - 3, 1) + pltpu.roll(ends, LANES - 6, 1)

    total = off_diagonal(lambda k: diag_ref[k], field)
    total = [total[c] + rows_moved(up_x[c], before[3][c], 1) for c in range(3)]
    total = [total[c] + rows_moved(low_x[c], after[3][c], -1) for c in range(3)]
    up_y = masked_product(edge_ref, mask_ref, 2, field)
    low_y = masked_product(edge_ref, mask_ref, 3, field)
    total = [
        total[c] + lanes_moved(up_y[c], 0.0, 1) + lanes_moved(low_y[c], 0.0, -1)
        for c in range(3)
    ]
    inverse = [1.0 / diag_ref[4 * c] for c in range(3)]
    part = [total[c] * inverse[c] for c in range(3)]
    for comp in range(3):
        part_ref[comp] = part[comp]
    def columns(lane, along_y, end):
        packed = jnp.zeros((cells_x, LANES), F32)
        at = iota((cells_x, LANES), 1)
        for slot, fields in enumerate((field, along_y, part, inverse)):
            for comp in range(3):
                column = fields[comp][:, lane : lane + 1]
                packed = jnp.where(at == 3 * slot + comp, column, packed)
        rest = jnp.zeros((LANES - cells_x, LANES), F32)
        turned = jnp.concatenate([packed, rest], axis=0).T[:16]
        at = iota((16, LANES), 1)
        line = iota((16, LANES), 0)
        for comp in range(3):
            turned = jnp.where(
                (line == 3 + comp) & (at == cells_x),
                ends[:, end + comp : end + comp + 1],
                turned,
            )
        return turned

    first_ref[...] = columns(0, low_y, 9)
    last_ref[...] = columns(LANES - 1, up_y, 0)


def bernstein(coord):
    other = 1.0 - coord
    return [
        other * other * other,
        3.0 * coord * other * other,
        3.0 * coord * coord * other,
        coord * coord * coord,
    ]


def weight_table(u, v, w):
    first, second, third = bernstein(u), bernstein(v), bernstein(w)
    line = iota((8, u.shape[1]), 0)
    inner = line & 3
    along = jnp.where(
        inner == 0,
        third[0],
        jnp.where(inner == 1, third[1], jnp.where(inner == 2, third[2], third[3])),
    )
    pair = jnp.concatenate(
        [
            jnp.where(line < 4, second[0], second[1]) * along,
            jnp.where(line < 4, second[2], second[3]) * along,
        ],
        axis=0,
    )
    return jnp.concatenate([pair * first[i] for i in range(4)], axis=0)


def tile_rows(terms):
    first_half = iota((4, LANES), 1) < LANES // 2
    rows = []
    for term in terms:
        term = term[:8] + term[8:]
        term = term + pltpu.roll(term, LANES // 2, 1)
        rows.append(jnp.where(first_half, term[:4], term[4:]))
    return jnp.concatenate(two_parts(jnp.concatenate(rows, axis=0)), axis=0).astype(BF16)


def box_matrix(tile_row, boxes):
    tiles = tile_row.shape[1]
    shape = (4 * boxes, 8 * tiles)
    column = iota((1, shape[1]), 1)
    box = jnp.zeros((1, shape[1]), jnp.int32)
    for tile in range(tiles):
        mine = lax.rem(lax.shift_right_logical(column, 2), tiles) == tile
        box = jnp.where(mine, tile_row[:, tile : tile + 1], box)
    target = 4 * box + (column & 3)
    return jnp.where(iota(shape, 0) == target, 1.0, 0.0).astype(BF16)


def quotient_before(halo_ref, strip_ref, before_ref):
    def rows(ref, first, count):
        return [ref[first + k : first + k + 1, :] for k in range(count)]

    beside, inverse, entering = rows(halo_ref, 0, 3), rows(halo_ref, 3, 3), rows(halo_ref, 6, 3)
    far_load, within = rows(halo_ref, 18, 3), rows(strip_ref, 0, 6)
    far_scale = rows(strip_ref, 33, 3)
    far = [ratio(far_load[c], far_scale[c]) for c in range(3)]
    whole_block = [None, *within[:3], None, *within[3:], None]
    total = off_diagonal(lambda k: whole_block[k], beside)
    from_far = product(lambda k: strip_ref[24 + k : 25 + k, :], far)
    up_y = product(lambda k: strip_ref[6 + k : 7 + k, :], beside)
    low_y = product(lambda k: strip_ref[15 + k : 16 + k, :], beside)
    for c in range(3):
        before_ref[c : c + 1, :] = inverse[c] * (
            total[c]
            + from_far[c]
            + entering[c]
            + lanes_moved(up_y[c], 0.0, 1)
            + lanes_moved(low_y[c], 0.0, -1)
        )
    before_ref[3:, :] = jnp.zeros((before_ref.shape[0] - 3, LANES), F32)


def box_kernel(
    tile_ref, field_ref, part_ref, node_ref, param_ref, halo_ref, strip_ref,
    box_ref, adjoint_ref, before_ref, matrix_ref, weights_ref, columns_ref, *, tile_points,
):
    cells_x = field_ref.shape[1]
    own = cells_x // 2
    quotient_before(halo_ref, strip_ref, before_ref)
    field = [field_ref[c] for c in range(3)]
    part = [part_ref[c] for c in range(3)]
    order = [field[0], part[0], field[2], field[1], part[1], part[2]]
    folded = [two_parts(jnp.concatenate([f[:own], f[own:]], axis=1)) for f in order]
    table = jnp.concatenate(
        [folded[f][which] for which in range(2) for f in range(6)], axis=0
    ).astype(BF16)
    points = param_ref.shape[1]
    pieces = CHUNK // LANES
    zero, one = jnp.zeros((), BF16), jnp.ones((), BF16)
    at_node = float_iota((2 * LANES, CHUNK), 0).astype(BF16)
    nothing = jnp.zeros((1, CHUNK), F32)
    highs, lows = [], []
    for chunk in range(points // CHUNK):
        node = jnp.concatenate(
            [node_ref[chunk * pieces + k : chunk * pieces + k + 1, :] for k in range(pieces)],
            axis=1,
        )
        row = lax.shift_right_logical(node, 7)
        column = node & (LANES - 1)
        lanes = slice(chunk * CHUNK, (chunk + 1) * CHUNK)
        at_edge = jnp.where(
            column == 0, row, jnp.where(column == LANES - 1, row + cells_x, -1)
        ).astype(F32)
        columns_ref[:, lanes] = jnp.where(
            at_node[: 2 * cells_x] == stretched(at_edge, 2 * cells_x), one, zero
        )
        place = column + jnp.where(row >= own, LANES, 0)
        row = jnp.where(row >= own, row - own, row)
        pick = jnp.where(at_node == stretched(place.astype(F32), 2 * LANES), one, zero)
        read = jnp.dot(table, pick, preferred_element_type=F32)
        read = read[: 6 * own] + read[6 * own :]
        here = iota((own, CHUNK), 0) == row
        values = [
            jnp.sum(
                jnp.where(here, read[f * own : (f + 1) * own], 0.0), axis=0, keepdims=True
            )
            for f in range(6)
        ]
        high, low = two_parts(
            jnp.concatenate(values[:3] + [nothing] + values[3:] + [nothing], axis=0)
        )
        highs.append(high)
        lows.append(low)
        weights = two_parts(
            weight_table(param_ref[0:1, lanes], param_ref[1:2, lanes], param_ref[2:3, lanes])
        )
        for k in range(CHUNK // tile_points):
            tile = slice(k * tile_points, (k + 1) * tile_points)
            sides = jnp.concatenate([weights[0][:, tile], weights[1][:, tile]], axis=0)
            weights_ref[chunk * (CHUNK // tile_points) + k] = sides.T.astype(BF16)
    both = jnp.concatenate(
        [jnp.concatenate(highs, axis=1), jnp.concatenate(lows, axis=1)], axis=0
    ).astype(BF16)
    matrix_ref[...] = box_matrix(tile_ref[...], matrix_ref.shape[0] // 4)
    tiles = tile_ref.shape[1]
    terms = [
        jnp.dot(
            both[:, tile * tile_points : (tile + 1) * tile_points],
            weights_ref[tile],
            preferred_element_type=F32,
        )
        for tile in range(tiles)
    ]
    box_ref[...] = jnp.dot(matrix_ref[...], tile_rows(terms), preferred_element_type=F32)
    low_half = iota((2 * cells_x, LANES), 1) < LANES // 2
    for tile in range(tiles):
        lanes = slice(tile * tile_points, (tile + 1) * tile_points)
        term = jnp.dot(
            columns_ref[:, lanes], weights_ref[tile], preferred_element_type=F32
        )
        high, low = two_parts(term + pltpu.roll(term, LANES // 2, 1))
        adjoint_ref[tile] = jnp.where(low_half, high, low).astype(BF16)


def sums_kernel(
    from_high_ref, from_low_ref, first_ref, last_ref, field_ref, part_ref, halo_ref,
    diag_ref, edge_ref, mask_ref, box_ref, adjoint_ref, before_ref, matrix_ref,
    quotient_ref, out_ref,
):
    cells_x = field_ref.shape[1]
    targets = out_ref.shape[0]

    def arrived(ref):
        rest = jnp.zeros((LANES - 16, LANES), F32)
        return jnp.concatenate([ref[...], rest], axis=0).T

    low, high = arrived(from_low_ref), arrived(from_high_ref)
    lane = iota((cells_x, LANES), 1)

    def column(source, slot, comp):
        return source[:cells_x, 3 * slot + comp : 3 * slot + comp + 1]

    field = [field_ref[c] for c in range(3)]
    scale = [diag_ref[4 * c] for c in range(3)]
    toward_high = masked_product(edge_ref, mask_ref, 2, field)
    toward_low = masked_product(edge_ref, mask_ref, 3, field)
    quotient, low_edge, high_edge = [], [], []
    for c in range(3):
        entering = jnp.where(
            lane == 0,
            column(low, 1, c),
            jnp.where(lane == LANES - 1, column(high, 1, c), 0.0),
        )
        quotient.append(part_ref[c] + entering / scale[c])
        low_edge.append(column(low, 2, c) + column(low, 3, c) * toward_low[c][:, :1])
        high_edge.append(column(high, 2, c) + column(high, 3, c) * toward_high[c][:, -1:])
    for c in range(3):
        quotient_ref[c] = quotient[c]
    lane_row = iota((1, LANES), 1)
    before, before_quotient = [], []
    for c in range(3):
        entering = jnp.where(
            lane_row == 0,
            low[cells_x : cells_x + 1, 3 + c : 4 + c],
            jnp.where(lane_row == LANES - 1, high[cells_x : cells_x + 1, 3 + c : 4 + c], 0.0),
        )
        before.append(halo_ref[c : c + 1, :])
        before_quotient.append(
            before_ref[c : c + 1, :] + entering * halo_ref[3 + c : 4 + c, :]
        )

    first_sum = sum(field[c] * scale[c] * field[c] for c in range(3))
    second_sum = sum(field[c] * scale[c] * quotient[c] for c in range(3))
    third_sum = sum(quotient[c] * scale[c] * quotient[c] for c in range(3))
    within = off_diagonal(lambda k: diag_ref[k], quotient)
    fourth_sum = sum(within[c] * field[c] for c in range(3))
    fifth_sum = sum(within[c] * quotient[c] for c in range(3))
    at_row = iota((cells_x, LANES), 0)
    moves = (
        (pltpu.roll, 1, 0, at_row == 0),
        (pltpu.roll, cells_x - 1, 0, at_row == cells_x - 1),
        (pltpu.roll, 1, 1, lane == 0),
        (pltpu.roll, LANES - 1, 1, lane == LANES - 1),
    )
    extra = [0.0, 0.0]
    sides = [0.0, 0.0]
    for direction, (roll, step, dim, edge) in enumerate(moves):
        moving = masked_product(edge_ref, mask_ref, direction, quotient)
        for c in range(3):
            moved = jnp.where(edge, 0.0, roll(moving[c], step, dim))
            fourth_sum = fourth_sum + moved * field[c]
            fifth_sum = fifth_sum + moved * quotient[c]
            if direction == 1:
                extra[0] += moving[c][:1] * before[c]
                extra[1] += moving[c][:1] * before_quotient[c]
            elif direction == 2:
                sides[0] += moving[c][:, LANES - 1 :] * column(high, 0, c)
                sides[1] += moving[c][:, LANES - 1 :] * high_edge[c]
            elif direction == 3:
                sides[0] += moving[c][:, :1] * column(low, 0, c)
                sides[1] += moving[c][:, :1] * low_edge[c]
    incoming = product(lambda k: halo_ref[9 + k : 10 + k, :], before_quotient)
    extra[0] += sum(incoming[c] * field[c][:1] for c in range(3))
    extra[1] += sum(incoming[c] * quotient[c][:1] for c in range(3))
    fourth_sum = fourth_sum + jnp.where(lane == 0, sides[0], 0.0)
    fifth_sum = fifth_sum + jnp.where(lane == 0, sides[1], 0.0)
    extra = [0.0, 0.0, 0.0, extra[0], extra[1]]
    sums = jnp.zeros((1, LANES), F32)
    for k, value in enumerate((first_sum, second_sum, third_sum, fourth_sum, fifth_sum)):
        line = jnp.sum(value, axis=0, keepdims=True) + extra[k]
        sums = jnp.where(lane_row == k, jnp.sum(line, axis=1, keepdims=True), sums)

    added = []
    for c in range(3):
        first = from_low_ref[3 + c : 4 + c, :] * first_ref[9 + c : 10 + c, :]
        second = from_high_ref[3 + c : 4 + c, :] * last_ref[9 + c : 10 + c, :]
        added.append(
            jnp.where(lane_row < cells_x, first, pltpu.roll(second, cells_x, 1))
        )
    none = jnp.zeros((1, LANES), F32)
    added = jnp.concatenate(
        [none, added[0], none, none, none, added[1], added[2], none], axis=0
    )
    added = jnp.concatenate(two_parts(added), axis=0).astype(BF16)
    terms = [
        jnp.dot(added, adjoint_ref[tile], preferred_element_type=F32)
        for tile in range(adjoint_ref.shape[0])
    ]
    total = box_ref[...] + jnp.dot(
        matrix_ref[...], tile_rows(terms), preferred_element_type=F32
    )
    total = jnp.where((iota(total.shape, 0) & 3) == 3, sums, total)
    for box in range(targets):
        out_ref[box] = total[4 * box : 4 * box + 4]


def result_kernel(got_ref, field_ref, quotient_ref, solution_ref, gradient_ref):
    total = jnp.sum(got_ref[...], axis=0)
    rho, a, b, t, u = [total[3:4, k : k + 1] for k in range(5)]
    ratio = a / rho
    norm = rho + a
    step = rho / norm
    rest = jnp.maximum(b - a * ratio, 0.0)
    beta = step * step * rest / rho
    rest_image = (b + u) - ratio * (a + b + a + t) + ratio * ratio * norm
    cross = (a + t) - ratio * norm
    curve = step * step * rest_image - step * beta * (rest + cross) + beta * beta * norm
    second = jnp.where(
        curve > 0.0, step * step * rest / jnp.where(curve > 0.0, curve, 1.0), 0.0
    )
    of_field = step + second * (beta + step * ratio)
    of_quotient = -(step * second)
    for c in range(3):
        solution_ref[c] = of_field * field_ref[c] + of_quotient * quotient_ref[c]
    gradient_ref[:, :LANES] = of_field * total[0:1] + of_quotient * total[1:2]
    gradient_ref[:, LANES:] = (
        of_field * total[2:3, : LANES // 2] + of_quotient * total[2:3, LANES // 2 :]
    )


def per_device(
    diag_blocks, edge_blocks, edge_mask, src_values, src_owner, src_node, src_count,
    surf_node, surf_param, tile_box,
):
    cells_x, cells_y = diag_blocks.shape[1:]
    width_gx, width_gy = lax.axis_size("gx"), lax.axis_size("gy")
    devices = width_gx * width_gy
    groups = src_node.shape[0] // LANES
    whole = functools.partial(jax.ShapeDtypeStruct, dtype=F32)

    cells = 4 * groups + NEAR

    def kept(array):
        return pltpu.with_memory_space_constraint(array, pltpu.HBM)

    i32 = jnp.int32
    rows, strip = pl.pallas_call(
        pack_kernel,
        in_specs=[SMEM] + [HBM] * 6,
        out_specs=[VMEM] * 2,
        out_shape=[
            pltpu.VMEM((width_gx, cells, LANES), F32), pltpu.VMEM((STRIP, LANES), F32)
        ],
        scratch_shapes=[
            pltpu.VMEM(src_values.shape, F32),
            pltpu.VMEM((groups, LANES), i32),
            pltpu.VMEM((groups, LANES), i32),
            pltpu.VMEM((9, 8, cells_y), F32),
            pltpu.VMEM((9, 8, cells_y), F32),
            pltpu.VMEM((9, 8, cells_y), F32),
            pltpu.VMEM((4, 9, 8, cells_y), F32),
            pltpu.VMEM((8, cells_y), i32),
            pltpu.VMEM((4, 8, cells_y), i32),
            pltpu.SemaphoreType.DMA((9,)),
        ],
        compiler_params=PARAMS,
        name="pack_rows_and_edges",
    )(
        src_count, kept(src_values),
        kept(src_owner.reshape(groups, LANES)), kept(src_node.reshape(groups, LANES)),
        kept(diag_blocks), kept(edge_blocks), kept(edge_mask),
    )
    rows = lax.all_to_all(rows, "gx", split_axis=0, concat_axis=0, tiled=True)
    strip = lax.ppermute(strip, "gx", [(i, i + 1) for i in range(width_gx - 1)])

    nodes = (3, cells_x, cells_y)
    frame = cells_x + 2 * PAD
    field, part, halo, first, last = pl.pallas_call(
        field_kernel,
        in_specs=[VMEM] * 4,
        out_specs=[VMEM] * 5,
        out_shape=[
            whole(nodes), whole(nodes), whole((24, cells_y)), whole((16, LANES)),
            whole((16, LANES)),
        ],
        scratch_shapes=[pltpu.VMEM((3 * frame, 2 * LANES), F32)],
        compiler_params=PARAMS,
        name="load_and_first_product",
    )(rows, diag_blocks, edge_blocks, edge_mask)
    from_high = lax.ppermute(first, "gy", [(i + 1, i) for i in range(width_gy - 1)])
    from_low = lax.ppermute(last, "gy", [(i, i + 1) for i in range(width_gy - 1)])

    points, tiles = surf_node.shape[0], tile_box.shape[0]
    box_part, adjoint, before, matrix = pl.pallas_call(
        functools.partial(box_kernel, tile_points=points // tiles),
        in_specs=[VMEM] * 7,
        out_specs=[VMEM] * 4,
        out_shape=[
            whole((4 * devices, LANES)),
            jax.ShapeDtypeStruct((tiles, 2 * cells_x, LANES), BF16),
            whole((8, LANES)),
            jax.ShapeDtypeStruct((4 * devices, 8 * tiles), BF16),
        ],
        scratch_shapes=[
            pltpu.VMEM((tiles, points // tiles, LANES), BF16),
            pltpu.VMEM((2 * cells_x, points), BF16),
        ],
        compiler_params=PARAMS,
        cost_estimate=pl.CostEstimate(
            flops=10**9, bytes_accessed=4 * 10**6, transcendentals=0
        ),
        name="box_parts",
    )(
        tile_box.reshape(1, tiles), field, part, surf_node.reshape(points // LANES, LANES),
        surf_param, halo, strip,
    )

    quotient, partial = pl.pallas_call(
        sums_kernel,
        in_specs=[VMEM] * 14,
        out_specs=[VMEM] * 2,
        out_shape=[whole(nodes), whole((devices, 4, LANES))],
        compiler_params=PARAMS,
        name="sums_and_halo_parts",
    )(
        from_high, from_low, first, last, field, part, halo, diag_blocks, edge_blocks, edge_mask,
        box_part, adjoint, before, matrix,
    )
    got = lax.all_to_all(partial, ("gx", "gy"), split_axis=0, concat_axis=0, tiled=True)
    return pl.pallas_call(
        result_kernel,
        in_specs=[VMEM] * 3,
        out_specs=[VMEM] * 2,
        out_shape=[whole(nodes), whole((1, 192))],
        compiler_params=PARAMS,
        name="steps_and_outputs",
    )(got, field, quotient)


def solution(mesh):
    return jax.shard_map(
        per_device,
        mesh=mesh,
        in_specs=(
            P(None, "gx", "gy"),
            P(None, None, "gx", "gy"),
            P(None, "gx", "gy"),
            P(None, ("gx", "gy")),
            P(("gx", "gy"), None),
            P(("gx", "gy")),
            P(("gx", "gy")),
            P(("gx", "gy")),
            P(None, ("gx", "gy")),
            P(("gx", "gy")),
        ),
        out_specs=(P(None, "gx", "gy"), P(("gx", "gy"), None)),
        check_vma=False,
    )
```

```python
import functools

import jax
import jax.numpy as jnp
from jax import lax
from jax.experimental import pallas as pl
from jax.experimental.pallas import tpu as pltpu
from jax.sharding import PartitionSpec as P

F32 = jnp.float32
BF16 = jnp.bfloat16
PAD = 16
NOWHERE = -(1 << 20)
LANES = 128
NEAR = 16
STRIP = 40
CHUNK = 256
PARAMS = pltpu.CompilerParams(vmem_limit_bytes=24 * 1024 * 1024)

VMEM = pl.BlockSpec(memory_space=pltpu.VMEM)
SMEM = pl.BlockSpec(memory_space=pltpu.SMEM)
HBM = pl.BlockSpec(memory_space=pltpu.HBM)


def iota(shape, dim):
    return lax.broadcasted_iota(jnp.int32, shape, dim)


def float_iota(shape, dim):
    return iota(shape, dim).astype(F32)


def two_parts(value):
    high = value.astype(BF16).astype(F32)
    return high, value - high


def product(block, field):
    return [
        block(row) * field[0] + block(3 + row) * field[1] + block(6 + row) * field[2]
        for row in range(3)
    ]


def off_diagonal(block, field):
    return [
        sum(block(3 * i + row) * field[i] for i in range(3) if i != row) for row in range(3)
    ]


def masked_product(edge_ref, mask_ref, direction, field):
    mask = mask_ref[direction].astype(F32)
    return [mask * part for part in product(lambda k: edge_ref[direction, k], field)]


def rows_moved(field, edge_row, step):
    size = field.shape[0]
    at = iota(field.shape, 0)
    moved = pltpu.roll(field, step % size, 0)
    return jnp.where(at == (0 if step == 1 else size - 1), edge_row, moved)


def lanes_moved(field, edge_column, step):
    size = field.shape[1]
    at = iota(field.shape, 1)
    moved = pltpu.roll(field, step % size, 1)
    return jnp.where(at == (0 if step == 1 else size - 1), edge_column, moved)


def pack_kernel(
    count_ref, values_in, owner_in, node_in, diag_in, edge_in, mask_in, rows_ref, strip_ref,
    values_ref, owner_ref, node_ref, diag_low, diag_high, edge_low, edge_high,
    mask_low, mask_high, arrived,
):
    targets = rows_ref.shape[0]
    groups = owner_ref.shape[0]
    cells_x = diag_in.shape[1]
    top = pl.ds(cells_x - 8, 8)
    copies = [
        pltpu.make_async_copy(source, target, arrived.at[k])
        for k, (source, target) in enumerate(
            (
                (owner_in, owner_ref),
                (node_in, node_ref),
                (values_in, values_ref),
                (diag_in.at[:, 0:8], diag_low),
                (diag_in.at[:, top], diag_high),
                (mask_in.at[1, 0:8], mask_low),
                (mask_in.at[:, top], mask_high),
                (edge_in.at[1, :, 0:8], edge_low),
                (edge_in.at[:, :, top], edge_high),
            )
        )
    ]
    for copy in copies:
        copy.start()
    near = 4 * groups
    for target in range(targets):
        rows_ref[target, near:, :] = jnp.zeros((NEAR, LANES), F32)
    for copy in copies[:2]:
        copy.wait()
    order = iota((groups, LANES), 0) * LANES + iota((groups, LANES), 1)
    node = node_ref[...]
    frame = cells_x + 2 * PAD
    row = owner_ref[...] * cells_x + lax.shift_right_logical(node, 7)
    row = jnp.where(order < count_ref[0], row, NOWHERE)
    column = node & (LANES - 1)
    for target in range(targets):
        line = row - (target * cells_x - PAD)
        inside = (line >= 0) & (line < frame)
        index = jnp.where(inside, line * LANES + column, -1)
        rows_ref[target, 3 * groups : 4 * groups, :] = index.astype(F32)

    copies[2].wait()
    for comp in range(3):
        value = jnp.concatenate(
            [
                values_ref[comp : comp + 1, group * LANES : (group + 1) * LANES]
                for group in range(groups)
            ],
            axis=0,
        )
        for target in range(targets):
            rows_ref[target, comp * groups : (comp + 1) * groups, :] = value
    for copy in copies[3:]:
        copy.wait()

    def block(edge, mask, direction, at):
        present = mask[direction, at : at + 1, :].astype(F32)
        return [edge[direction, k, at : at + 1, :] * present for k in range(9)]

    up_y, low_y = block(edge_high, mask_high, 2, 7), block(edge_high, mask_high, 3, 7)
    later = [diag_high[k, 7:8, :] for k in range(9) if k % 4]
    later += up_y + low_y + block(edge_high, mask_high, 0, 6)
    later += [diag_high[4 * k, 6:7, :] for k in range(3)]
    for k, value in enumerate(later):
        strip_ref[k : k + 1, :] = value
    strip_ref[len(later) :, :] = jnp.zeros((STRIP - len(later), LANES), F32)

    here = lax.axis_index("gx")

    @pl.when(here < targets - 1)
    def _():
        def put(slot, value):
            rows_ref[here + 1, near + slot : near + slot + 1, :] = value

        for k in range(3):
            put(k, diag_high[4 * k, 7:8, :])
        for k, value in enumerate(block(edge_high, mask_high, 0, 7)):
            put(3 + k, value)
        corners = jnp.zeros((1, LANES), F32)
        lane = iota((1, LANES), 1)
        for k in range(9):
            corners = jnp.where(lane == k, up_y[k][:, LANES - 1 :], corners)
            corners = jnp.where(lane == 9 + k, low_y[k][:, :1], corners)
        put(12, corners)

    @pl.when(here > 0)
    def _():
        def put(slot, value):
            rows_ref[here - 1, near + slot : near + slot + 1, :] = value

        for k in range(3):
            put(k, diag_low[4 * k, 0:1, :])
        present = mask_low[0:1, :].astype(F32)
        for k in range(9):
            put(3 + k, edge_low[k, 0:1, :] * present)


def stretched(row, count):
    tile = jnp.broadcast_to(row, (16, row.shape[1])).astype(BF16)
    return jnp.concatenate([tile] * (count // 16), axis=0)


def ratio(value, scale):
    return jnp.where(scale > 0.0, value / jnp.where(scale > 0.0, scale, 1.0), 0.0)


def field_kernel(
    rows_ref, diag_ref, edge_ref, mask_ref,
    field_ref, part_ref, halo_ref, inner_ref, outer_ref, load_ref,
):
    senders = rows_ref.shape[0]
    groups = (rows_ref.shape[1] - NEAR) // 4
    cells_x = field_ref.shape[1]
    half = (cells_x + 2 * PAD) // 2
    own = cells_x // 2

    load_ref[...] = jnp.zeros_like(load_ref)
    here = lax.axis_index("gx")

    def add_rows(sender, carry):
        index = rows_ref[sender, 3 * groups : 4 * groups, :]
        split = float(half * LANES)
        index, shift = (
            jnp.where(index >= split, index - split, index),
            jnp.where(index >= split, float(LANES), 0.0),
        )
        place = jnp.floor(index * (1.0 / LANES))
        column = index - place * float(LANES) + shift
        at_row = float_iota((half, LANES), 0).astype(BF16)
        at_column = float_iota((2 * LANES, LANES), 0).astype(BF16)
        parts = [
            two_parts(rows_ref[sender, c * groups : (c + 1) * groups, :]) for c in range(3)
        ]
        zero, one = jnp.zeros((), BF16), jnp.ones((), BF16)
        lefts, rights = [], []
        for group in range(groups):
            line = slice(group, group + 1)
            match = at_row == stretched(place[line], half)
            lefts.append(
                jnp.concatenate(
                    [
                        jnp.where(match, stretched(parts[c][which][line], half), zero)
                        for which in range(2)
                        for c in range(3)
                    ],
                    axis=0,
                )
            )
            rights.append(
                jnp.where(at_column == stretched(column[line], 2 * LANES), one, zero)
            )
        load_ref[...] += lax.dot_general(
            jnp.concatenate(lefts, axis=1),
            jnp.concatenate(rights, axis=1),
            (((1,), (1,)), ((), ())),
            preferred_element_type=F32,
        )
        return carry

    lax.fori_loop(0, senders, add_rows, 0, unroll=min(senders, 8))

    def load_rows(comp, first, last, second_half):
        lanes = slice(LANES, 2 * LANES) if second_half else slice(0, LANES)
        return (
            load_ref[comp * half + first : comp * half + last, lanes]
            + load_ref[(3 + comp) * half + first : (3 + comp) * half + last, lanes]
        )

    field = []
    for comp in range(3):
        load = jnp.concatenate(
            [load_rows(comp, PAD, half, False), load_rows(comp, 0, half - PAD, True)], axis=0
        )
        field.append(load / diag_ref[4 * comp])
        field_ref[comp] = field[comp]
    beyond = half - PAD
    near_before = [load_rows(c, PAD - 1, PAD, False) for c in range(3)]
    far_before = [load_rows(c, PAD - 2, PAD - 1, False) for c in range(3)]
    near_after = [load_rows(c, beyond, beyond + 1, True) for c in range(3)]

    up_x = masked_product(edge_ref, mask_ref, 0, field)
    low_x = masked_product(edge_ref, mask_ref, 1, field)
    base = 4 * groups

    def neighbour(sender, load):
        def entry(k):
            return rows_ref[sender, base + k : base + k + 1, :]

        scale, toward = [entry(k) for k in range(3)], [entry(3 + k) for k in range(9)]
        beside = [ratio(load[c], scale[c]) for c in range(3)]
        return scale, toward, beside, product(lambda k: toward[k], beside)

    lower = jnp.maximum(here - 1, 0)
    before = neighbour(lower, near_before)
    after = neighbour(jnp.minimum(here + 1, senders - 1), near_after)
    rows = before[2] + [ratio(1.0, scale) for scale in before[0]]
    rows += [p[:1] for p in low_x] + before[1] + far_before
    for k, value in enumerate(rows):
        halo_ref[k : k + 1, :] = value
    halo_ref[len(rows) :, :] = jnp.zeros((halo_ref.shape[0] - len(rows), LANES), F32)
    lane_row = iota((1, LANES), 1)
    ends = jnp.zeros((1, LANES), F32)
    for i in range(3):
        for a in range(3):
            ends = jnp.where(lane_row == 3 * i + a, before[2][i][:, LANES - 1 :], ends)
            ends = jnp.where(lane_row == 9 + 3 * i + a, before[2][i][:, :1], ends)
    ends = ends * rows_ref[lower, base + 12 : base + 13, :]
    ends = ends + pltpu.roll(ends, LANES - 3, 1) + pltpu.roll(ends, LANES - 6, 1)

    total = off_diagonal(lambda k: diag_ref[k], field)
    total = [total[c] + rows_moved(up_x[c], before[3][c], 1) for c in range(3)]
    total = [total[c] + rows_moved(low_x[c], after[3][c], -1) for c in range(3)]
    up_y = masked_product(edge_ref, mask_ref, 2, field)
    low_y = masked_product(edge_ref, mask_ref, 3, field)
    total = [
        total[c] + lanes_moved(up_y[c], 0.0, 1) + lanes_moved(low_y[c], 0.0, -1)
        for c in range(3)
    ]
    inverse = [1.0 / diag_ref[4 * c] for c in range(3)]
    part = [total[c] * inverse[c] for c in range(3)]
    for comp in range(3):
        part_ref[comp] = part[comp]
    def columns(lane, along_y, end):
        packed = jnp.zeros((cells_x, LANES), F32)
        at = iota((cells_x, LANES), 1)
        for slot, fields in enumerate((field, along_y, part, inverse)):
            for comp in range(3):
                column = fields[comp][:, lane : lane + 1]
                packed = jnp.where(at == 3 * slot + comp, column, packed)
        rest = jnp.zeros((LANES - cells_x, LANES), F32)
        turned = jnp.concatenate([packed, rest], axis=0).T[:16]
        at = iota((16, LANES), 1)
        line = iota((16, LANES), 0)
        for comp in range(3):
            turned = jnp.where(
                (line == 3 + comp) & (at == cells_x),
                ends[:, end + comp : end + comp + 1],
                turned,
            )
        return turned

    inner_ref[...], outer_ref[...] = by_parity(
        columns(0, low_y, 9), columns(LANES - 1, up_y, 0)
    )


def bernstein(coord):
    other = 1.0 - coord
    return [
        other * other * other,
        3.0 * coord * other * other,
        3.0 * coord * coord * other,
        coord * coord * coord,
    ]


def weight_table(u, v, w):
    first, second, third = bernstein(u), bernstein(v), bernstein(w)
    line = iota((8, u.shape[1]), 0)
    inner = line & 3
    along = jnp.where(
        inner == 0,
        third[0],
        jnp.where(inner == 1, third[1], jnp.where(inner == 2, third[2], third[3])),
    )
    pair = jnp.concatenate(
        [
            jnp.where(line < 4, second[0], second[1]) * along,
            jnp.where(line < 4, second[2], second[3]) * along,
        ],
        axis=0,
    )
    return jnp.concatenate([pair * first[i] for i in range(4)], axis=0)


def tile_rows(terms):
    first_half = iota((4, LANES), 1) < LANES // 2
    rows = []
    for term in terms:
        term = term[:8] + term[8:]
        term = term + pltpu.roll(term, LANES // 2, 1)
        rows.append(jnp.where(first_half, term[:4], term[4:]))
    return jnp.concatenate(two_parts(jnp.concatenate(rows, axis=0)), axis=0).astype(BF16)


def box_matrix(tile_row, boxes):
    tiles = tile_row.shape[1]
    shape = (4 * boxes, 8 * tiles)
    column = iota((1, shape[1]), 1)
    box = jnp.zeros((1, shape[1]), jnp.int32)
    for tile in range(tiles):
        mine = lax.rem(lax.shift_right_logical(column, 2), tiles) == tile
        box = jnp.where(mine, tile_row[:, tile : tile + 1], box)
    target = 4 * box + (column & 3)
    return jnp.where(iota(shape, 0) == target, 1.0, 0.0).astype(BF16)


def by_parity(low, high):
    odd = lax.rem(lax.axis_index("gy"), 2) == 1
    return jnp.where(odd, high, low), jnp.where(odd, low, high)


def quotient_before(halo_ref, strip_ref, before_ref):
    def rows(ref, first, count):
        return [ref[first + k : first + k + 1, :] for k in range(count)]

    beside, inverse, entering = rows(halo_ref, 0, 3), rows(halo_ref, 3, 3), rows(halo_ref, 6, 3)
    far_load, within = rows(halo_ref, 18, 3), rows(strip_ref, 0, 6)
    far_scale = rows(strip_ref, 33, 3)
    far = [ratio(far_load[c], far_scale[c]) for c in range(3)]
    whole_block = [None, *within[:3], None, *within[3:], None]
    total = off_diagonal(lambda k: whole_block[k], beside)
    from_far = product(lambda k: strip_ref[24 + k : 25 + k, :], far)
    up_y = product(lambda k: strip_ref[6 + k : 7 + k, :], beside)
    low_y = product(lambda k: strip_ref[15 + k : 16 + k, :], beside)
    for c in range(3):
        before_ref[c : c + 1, :] = inverse[c] * (
            total[c]
            + from_far[c]
            + entering[c]
            + lanes_moved(up_y[c], 0.0, 1)
            + lanes_moved(low_y[c], 0.0, -1)
        )
    before_ref[3:, :] = jnp.zeros((before_ref.shape[0] - 3, LANES), F32)


def box_kernel(
    tile_ref, field_ref, part_ref, node_ref, param_ref, halo_ref, strip_ref,
    box_ref, adjoint_ref, before_ref, matrix_ref, weights_ref, columns_ref, *, tile_points,
):
    cells_x = field_ref.shape[1]
    own = cells_x // 2
    quotient_before(halo_ref, strip_ref, before_ref)
    field = [field_ref[c] for c in range(3)]
    part = [part_ref[c] for c in range(3)]
    order = [field[0], part[0], field[2], field[1], part[1], part[2]]
    folded = [two_parts(jnp.concatenate([f[:own], f[own:]], axis=1)) for f in order]
    table = jnp.concatenate(
        [folded[f][which] for which in range(2) for f in range(6)], axis=0
    ).astype(BF16)
    points = param_ref.shape[1]
    pieces = CHUNK // LANES
    zero, one = jnp.zeros((), BF16), jnp.ones((), BF16)
    at_node = float_iota((2 * LANES, CHUNK), 0).astype(BF16)
    nothing = jnp.zeros((1, CHUNK), F32)
    highs, lows = [], []
    for chunk in range(points // CHUNK):
        node = jnp.concatenate(
            [node_ref[chunk * pieces + k : chunk * pieces + k + 1, :] for k in range(pieces)],
            axis=1,
        )
        row = lax.shift_right_logical(node, 7)
        column = node & (LANES - 1)
        lanes = slice(chunk * CHUNK, (chunk + 1) * CHUNK)
        at_edge = jnp.where(
            column == 0, row, jnp.where(column == LANES - 1, row + cells_x, -1)
        ).astype(F32)
        columns_ref[:, lanes] = jnp.where(
            at_node[: 2 * cells_x] == stretched(at_edge, 2 * cells_x), one, zero
        )
        place = column + jnp.where(row >= own, LANES, 0)
        row = jnp.where(row >= own, row - own, row)
        pick = jnp.where(at_node == stretched(place.astype(F32), 2 * LANES), one, zero)
        read = jnp.dot(table, pick, preferred_element_type=F32)
        read = read[: 6 * own] + read[6 * own :]
        here = iota((own, CHUNK), 0) == row
        values = [
            jnp.sum(
                jnp.where(here, read[f * own : (f + 1) * own], 0.0), axis=0, keepdims=True
            )
            for f in range(6)
        ]
        high, low = two_parts(
            jnp.concatenate(values[:3] + [nothing] + values[3:] + [nothing], axis=0)
        )
        highs.append(high)
        lows.append(low)
        weights = two_parts(
            weight_table(param_ref[0:1, lanes], param_ref[1:2, lanes], param_ref[2:3, lanes])
        )
        for k in range(CHUNK // tile_points):
            tile = slice(k * tile_points, (k + 1) * tile_points)
            sides = jnp.concatenate([weights[0][:, tile], weights[1][:, tile]], axis=0)
            weights_ref[chunk * (CHUNK // tile_points) + k] = sides.T.astype(BF16)
    both = jnp.concatenate(
        [jnp.concatenate(highs, axis=1), jnp.concatenate(lows, axis=1)], axis=0
    ).astype(BF16)
    matrix_ref[...] = box_matrix(tile_ref[...], matrix_ref.shape[0] // 4)
    tiles = tile_ref.shape[1]
    terms = [
        jnp.dot(
            both[:, tile * tile_points : (tile + 1) * tile_points],
            weights_ref[tile],
            preferred_element_type=F32,
        )
        for tile in range(tiles)
    ]
    box_ref[...] = jnp.dot(matrix_ref[...], tile_rows(terms), preferred_element_type=F32)
    low_half = iota((2 * cells_x, LANES), 1) < LANES // 2
    for tile in range(tiles):
        lanes = slice(tile * tile_points, (tile + 1) * tile_points)
        term = jnp.dot(
            columns_ref[:, lanes], weights_ref[tile], preferred_element_type=F32
        )
        high, low = two_parts(term + pltpu.roll(term, LANES // 2, 1))
        adjoint_ref[tile] = jnp.where(low_half, high, low).astype(BF16)


def sums_kernel(
    from_inner_ref, from_outer_ref, inner_ref, outer_ref, field_ref, part_ref, halo_ref,
    diag_ref, edge_ref, mask_ref, box_ref, adjoint_ref, before_ref, matrix_ref,
    quotient_ref, out_ref,
):
    cells_x = field_ref.shape[1]
    targets = out_ref.shape[0]

    from_low, from_high = by_parity(from_inner_ref[...], from_outer_ref[...])
    first, last = by_parity(inner_ref[...], outer_ref[...])

    def turned(columns):
        rest = jnp.zeros((LANES - 16, LANES), F32)
        return jnp.concatenate([columns, rest], axis=0).T

    low, high = turned(from_low), turned(from_high)
    lane = iota((cells_x, LANES), 1)

    def column(source, slot, comp):
        return source[:cells_x, 3 * slot + comp : 3 * slot + comp + 1]

    field = [field_ref[c] for c in range(3)]
    scale = [diag_ref[4 * c] for c in range(3)]
    toward_high = masked_product(edge_ref, mask_ref, 2, field)
    toward_low = masked_product(edge_ref, mask_ref, 3, field)
    quotient, low_edge, high_edge = [], [], []
    for c in range(3):
        entering = jnp.where(
            lane == 0,
            column(low, 1, c),
            jnp.where(lane == LANES - 1, column(high, 1, c), 0.0),
        )
        quotient.append(part_ref[c] + entering / scale[c])
        low_edge.append(column(low, 2, c) + column(low, 3, c) * toward_low[c][:, :1])
        high_edge.append(column(high, 2, c) + column(high, 3, c) * toward_high[c][:, -1:])
    for c in range(3):
        quotient_ref[c] = quotient[c]
    lane_row = iota((1, LANES), 1)
    before, before_quotient = [], []
    for c in range(3):
        entering = jnp.where(
            lane_row == 0,
            low[cells_x : cells_x + 1, 3 + c : 4 + c],
            jnp.where(lane_row == LANES - 1, high[cells_x : cells_x + 1, 3 + c : 4 + c], 0.0),
        )
        before.append(halo_ref[c : c + 1, :])
        before_quotient.append(
            before_ref[c : c + 1, :] + entering * halo_ref[3 + c : 4 + c, :]
        )

    first_sum = sum(field[c] * scale[c] * field[c] for c in range(3))
    second_sum = sum(field[c] * scale[c] * quotient[c] for c in range(3))
    third_sum = sum(quotient[c] * scale[c] * quotient[c] for c in range(3))
    within = off_diagonal(lambda k: diag_ref[k], quotient)
    fourth_sum = sum(within[c] * field[c] for c in range(3))
    fifth_sum = sum(within[c] * quotient[c] for c in range(3))
    at_row = iota((cells_x, LANES), 0)
    moves = (
        (pltpu.roll, 1, 0, at_row == 0),
        (pltpu.roll, cells_x - 1, 0, at_row == cells_x - 1),
        (pltpu.roll, 1, 1, lane == 0),
        (pltpu.roll, LANES - 1, 1, lane == LANES - 1),
    )
    extra = [0.0, 0.0]
    sides = [0.0, 0.0]
    for direction, (roll, step, dim, edge) in enumerate(moves):
        moving = masked_product(edge_ref, mask_ref, direction, quotient)
        for c in range(3):
            moved = jnp.where(edge, 0.0, roll(moving[c], step, dim))
            fourth_sum = fourth_sum + moved * field[c]
            fifth_sum = fifth_sum + moved * quotient[c]
            if direction == 1:
                extra[0] += moving[c][:1] * before[c]
                extra[1] += moving[c][:1] * before_quotient[c]
            elif direction == 2:
                sides[0] += moving[c][:, LANES - 1 :] * column(high, 0, c)
                sides[1] += moving[c][:, LANES - 1 :] * high_edge[c]
            elif direction == 3:
                sides[0] += moving[c][:, :1] * column(low, 0, c)
                sides[1] += moving[c][:, :1] * low_edge[c]
    incoming = product(lambda k: halo_ref[9 + k : 10 + k, :], before_quotient)
    extra[0] += sum(incoming[c] * field[c][:1] for c in range(3))
    extra[1] += sum(incoming[c] * quotient[c][:1] for c in range(3))
    fourth_sum = fourth_sum + jnp.where(lane == 0, sides[0], 0.0)
    fifth_sum = fifth_sum + jnp.where(lane == 0, sides[1], 0.0)
    extra = [0.0, 0.0, 0.0, extra[0], extra[1]]
    sums = jnp.zeros((1, LANES), F32)
    for k, value in enumerate((first_sum, second_sum, third_sum, fourth_sum, fifth_sum)):
        line = jnp.sum(value, axis=0, keepdims=True) + extra[k]
        sums = jnp.where(lane_row == k, jnp.sum(line, axis=1, keepdims=True), sums)

    added = []
    for c in range(3):
        at_first = from_low[3 + c : 4 + c] * first[9 + c : 10 + c]
        at_last = from_high[3 + c : 4 + c] * last[9 + c : 10 + c]
        added.append(
            jnp.where(lane_row < cells_x, at_first, pltpu.roll(at_last, cells_x, 1))
        )
    none = jnp.zeros((1, LANES), F32)
    added = jnp.concatenate(
        [none, added[0], none, none, none, added[1], added[2], none], axis=0
    )
    added = jnp.concatenate(two_parts(added), axis=0).astype(BF16)
    terms = [
        jnp.dot(added, adjoint_ref[tile], preferred_element_type=F32)
        for tile in range(adjoint_ref.shape[0])
    ]
    total = box_ref[...] + jnp.dot(
        matrix_ref[...], tile_rows(terms), preferred_element_type=F32
    )
    total = jnp.where((iota(total.shape, 0) & 3) == 3, sums, total)
    for box in range(targets):
        out_ref[box] = total[4 * box : 4 * box + 4]


def result_kernel(got_ref, field_ref, quotient_ref, solution_ref, gradient_ref):
    total = jnp.sum(got_ref[...], axis=0)
    rho, a, b, t, u = [total[3:4, k : k + 1] for k in range(5)]
    ratio = a / rho
    norm = rho + a
    step = rho / norm
    rest = jnp.maximum(b - a * ratio, 0.0)
    beta = step * step * rest / rho
    rest_image = (b + u) - ratio * (a + b + a + t) + ratio * ratio * norm
    cross = (a + t) - ratio * norm
    curve = step * step * rest_image - step * beta * (rest + cross) + beta * beta * norm
    second = jnp.where(
        curve > 0.0, step * step * rest / jnp.where(curve > 0.0, curve, 1.0), 0.0
    )
    of_field = step + second * (beta + step * ratio)
    of_quotient = -(step * second)
    for c in range(3):
        solution_ref[c] = of_field * field_ref[c] + of_quotient * quotient_ref[c]
    gradient_ref[:, :LANES] = of_field * total[0:1] + of_quotient * total[1:2]
    gradient_ref[:, LANES:] = (
        of_field * total[2:3, : LANES // 2] + of_quotient * total[2:3, LANES // 2 :]
    )


def per_device(
    diag_blocks, edge_blocks, edge_mask, src_values, src_owner, src_node, src_count,
    surf_node, surf_param, tile_box,
):
    cells_x, cells_y = diag_blocks.shape[1:]
    width_gx, width_gy = lax.axis_size("gx"), lax.axis_size("gy")
    devices = width_gx * width_gy
    groups = src_node.shape[0] // LANES
    whole = functools.partial(jax.ShapeDtypeStruct, dtype=F32)

    cells = 4 * groups + NEAR

    def kept(array):
        return pltpu.with_memory_space_constraint(array, pltpu.HBM)

    i32 = jnp.int32
    rows, strip = pl.pallas_call(
        pack_kernel,
        in_specs=[SMEM] + [HBM] * 6,
        out_specs=[VMEM] * 2,
        out_shape=[
            pltpu.VMEM((width_gx, cells, LANES), F32), pltpu.VMEM((STRIP, LANES), F32)
        ],
        scratch_shapes=[
            pltpu.VMEM(src_values.shape, F32),
            pltpu.VMEM((groups, LANES), i32),
            pltpu.VMEM((groups, LANES), i32),
            pltpu.VMEM((9, 8, cells_y), F32),
            pltpu.VMEM((9, 8, cells_y), F32),
            pltpu.VMEM((9, 8, cells_y), F32),
            pltpu.VMEM((4, 9, 8, cells_y), F32),
            pltpu.VMEM((8, cells_y), i32),
            pltpu.VMEM((4, 8, cells_y), i32),
            pltpu.SemaphoreType.DMA((9,)),
        ],
        compiler_params=PARAMS,
        name="pack_rows_and_edges",
    )(
        src_count, kept(src_values),
        kept(src_owner.reshape(groups, LANES)), kept(src_node.reshape(groups, LANES)),
        kept(diag_blocks), kept(edge_blocks), kept(edge_mask),
    )
    rows = lax.all_to_all(rows, "gx", split_axis=0, concat_axis=0, tiled=True)
    strip = lax.ppermute(strip, "gx", [(i, i + 1) for i in range(width_gx - 1)])

    nodes = (3, cells_x, cells_y)
    frame = cells_x + 2 * PAD
    field, part, halo, inner, outer = pl.pallas_call(
        field_kernel,
        in_specs=[VMEM] * 4,
        out_specs=[VMEM] * 5,
        out_shape=[
            whole(nodes), whole(nodes), whole((24, cells_y)), whole((16, LANES)),
            whole((16, LANES)),
        ],
        scratch_shapes=[pltpu.VMEM((3 * frame, 2 * LANES), F32)],
        compiler_params=PARAMS,
        name="load_and_first_product",
    )(rows, diag_blocks, edge_blocks, edge_mask)
    def swapped(columns, first):
        low = range(first, width_gy - 1, 2)
        pairs = [(i, i + 1) for i in low] + [(i + 1, i) for i in low]
        return lax.ppermute(columns, "gy", pairs)

    from_inner, from_outer = swapped(inner, 1), swapped(outer, 0)
    points, tiles = surf_node.shape[0], tile_box.shape[0]
    box_part, adjoint, before, matrix = pl.pallas_call(
        functools.partial(box_kernel, tile_points=points // tiles),
        in_specs=[VMEM] * 7,
        out_specs=[VMEM] * 4,
        out_shape=[
            whole((4 * devices, LANES)),
            jax.ShapeDtypeStruct((tiles, 2 * cells_x, LANES), BF16),
            whole((8, LANES)),
            jax.ShapeDtypeStruct((4 * devices, 8 * tiles), BF16),
        ],
        scratch_shapes=[
            pltpu.VMEM((tiles, points // tiles, LANES), BF16),
            pltpu.VMEM((2 * cells_x, points), BF16),
        ],
        compiler_params=PARAMS,
        cost_estimate=pl.CostEstimate(
            flops=10**9, bytes_accessed=4 * 10**6, transcendentals=0
        ),
        name="box_parts",
    )(
        tile_box.reshape(1, tiles), field, part, surf_node.reshape(points // LANES, LANES),
        surf_param, halo, strip,
    )

    quotient, partial = pl.pallas_call(
        sums_kernel,
        in_specs=[VMEM] * 14,
        out_specs=[VMEM] * 2,
        out_shape=[whole(nodes), whole((devices, 4, LANES))],
        compiler_params=PARAMS,
        name="sums_and_halo_parts",
    )(
        from_inner, from_outer, inner, outer, field, part, halo, diag_blocks, edge_blocks, edge_mask,
        box_part, adjoint, before, matrix,
    )
    got = lax.all_to_all(partial, ("gx", "gy"), split_axis=0, concat_axis=0, tiled=True)
    return pl.pallas_call(
        result_kernel,
        in_specs=[VMEM] * 3,
        out_specs=[VMEM] * 2,
        out_shape=[whole(nodes), whole((1, 192))],
        compiler_params=PARAMS,
        name="steps_and_outputs",
    )(got, field, quotient)


def solution(mesh):
    return jax.shard_map(
        per_device,
        mesh=mesh,
        in_specs=(
            P(None, "gx", "gy"),
            P(None, None, "gx", "gy"),
            P(None, "gx", "gy"),
            P(None, ("gx", "gy")),
            P(("gx", "gy"), None),
            P(("gx", "gy")),
            P(("gx", "gy")),
            P(("gx", "gy")),
            P(None, ("gx", "gy")),
            P(("gx", "gy")),
        ),
        out_specs=(P(None, "gx", "gy"), P(("gx", "gy"), None)),
        check_vma=False,
    )
```

```python
import functools
import math

import jax
import jax.numpy as jnp
from jax import lax
from jax.experimental import pallas as pl
from jax.experimental.pallas import tpu as pltpu
from jax.sharding import PartitionSpec as P

F32 = jnp.float32
BF16 = jnp.bfloat16
PAD = 16
NOWHERE = -(1 << 20)
LANES = 128
NEAR = 16
STRIP = 40
CHUNK = 256
PARAMS = pltpu.CompilerParams(vmem_limit_bytes=24 * 1024 * 1024)

VMEM = pl.BlockSpec(memory_space=pltpu.VMEM)
SMEM = pl.BlockSpec(memory_space=pltpu.SMEM)
HBM = pl.BlockSpec(memory_space=pltpu.HBM)


def iota(shape, dim):
    return lax.broadcasted_iota(jnp.int32, shape, dim)


def float_iota(shape, dim):
    return iota(shape, dim).astype(F32)


def two_parts(value):
    high = value.astype(BF16).astype(F32)
    return high, value - high


def product(block, field):
    return [
        block(row) * field[0] + block(3 + row) * field[1] + block(6 + row) * field[2]
        for row in range(3)
    ]


def off_diagonal(block, field):
    return [
        sum(block(3 * i + row) * field[i] for i in range(3) if i != row) for row in range(3)
    ]


def masked_product(edge_ref, mask_ref, direction, field):
    mask = mask_ref[direction].astype(F32)
    return [mask * part for part in product(lambda k: edge_ref[direction, k], field)]


def rows_moved(field, edge_row, step):
    size = field.shape[0]
    at = iota(field.shape, 0)
    moved = pltpu.roll(field, step % size, 0)
    return jnp.where(at == (0 if step == 1 else size - 1), edge_row, moved)


def lanes_moved(field, edge_column, step):
    size = field.shape[1]
    at = iota(field.shape, 1)
    moved = pltpu.roll(field, step % size, 1)
    return jnp.where(at == (0 if step == 1 else size - 1), edge_column, moved)


def pack_kernel(
    count_ref, values_in, owner_in, node_in, diag_in, edge_in, mask_in, rows_out, strip_ref,
    values_ref, owner_ref, node_ref, diag_low, diag_high, edge_low, edge_high,
    mask_low, mask_high, rows_ref, arrived, left,
):
    targets = rows_ref.shape[0]
    groups = owner_ref.shape[0]
    cells_x = diag_in.shape[1]
    top = pl.ds(cells_x - 8, 8)
    copies = [
        pltpu.make_async_copy(source, target, arrived.at[k])
        for k, (source, target) in enumerate(
            (
                (owner_in, owner_ref),
                (node_in, node_ref),
                (values_in, values_ref),
                (diag_in.at[:, 0:8], diag_low),
                (diag_in.at[:, top], diag_high),
                (mask_in.at[1, 0:8], mask_low),
                (mask_in.at[:, top], mask_high),
                (edge_in.at[1, :, 0:8], edge_low),
                (edge_in.at[:, :, top], edge_high),
            )
        )
    ]
    for copy in copies:
        copy.start()
    base = 4 * groups
    for target in range(targets):
        rows_ref[target, base:, :] = jnp.zeros((NEAR, LANES), F32)
    for copy in copies[:2]:
        copy.wait()
    order = iota((groups, LANES), 0) * LANES + iota((groups, LANES), 1)
    node = node_ref[...]
    frame = cells_x + 2 * PAD
    row = owner_ref[...] * cells_x + lax.shift_right_logical(node, 7)
    row = jnp.where(order < count_ref[0], row, NOWHERE)
    column = node & (LANES - 1)
    for target in range(targets):
        line = row - (target * cells_x - PAD)
        inside = (line >= 0) & (line < frame)
        index = jnp.where(inside, line * LANES + column, -1)
        rows_ref[target, 3 * groups : 4 * groups, :] = index.astype(F32)

    copies[2].wait()
    for comp in range(3):
        value = jnp.concatenate(
            [
                values_ref[comp : comp + 1, group * LANES : (group + 1) * LANES]
                for group in range(groups)
            ],
            axis=0,
        )
        for target in range(targets):
            rows_ref[target, comp * groups : (comp + 1) * groups, :] = value
    near = pl.ds(4 * groups, NEAR)
    leaving = [
        pltpu.make_async_copy(rows_ref.at[:, part], rows_out.at[:, part], left.at[k])
        for k, part in enumerate((pl.ds(0, 4 * groups), near))
    ]
    leaving[0].start()
    for copy in copies[3:]:
        copy.wait()

    def block(edge, mask, direction, at):
        present = mask[direction, at : at + 1, :].astype(F32)
        return [edge[direction, k, at : at + 1, :] * present for k in range(9)]

    up_y, low_y = block(edge_high, mask_high, 2, 7), block(edge_high, mask_high, 3, 7)
    here = lax.axis_index("gx")

    @pl.when(here < targets - 1)
    def _():
        def put(slot, value):
            rows_ref[here + 1, base + slot : base + slot + 1, :] = value

        for k in range(3):
            put(k, diag_high[4 * k, 7:8, :])
        for k, value in enumerate(block(edge_high, mask_high, 0, 7)):
            put(3 + k, value)
        corners = jnp.zeros((1, LANES), F32)
        lane = iota((1, LANES), 1)
        for k in range(9):
            corners = jnp.where(lane == k, up_y[k][:, LANES - 1 :], corners)
            corners = jnp.where(lane == 9 + k, low_y[k][:, :1], corners)
        put(12, corners)

    @pl.when(here > 0)
    def _():
        def put(slot, value):
            rows_ref[here - 1, base + slot : base + slot + 1, :] = value

        for k in range(3):
            put(k, diag_low[4 * k, 0:1, :])
        present = mask_low[0:1, :].astype(F32)
        for k in range(9):
            put(3 + k, edge_low[k, 0:1, :] * present)

    leaving[1].start()
    later = [diag_high[k, 7:8, :] for k in range(9) if k % 4]
    later += up_y + low_y + block(edge_high, mask_high, 0, 6)
    later += [diag_high[4 * k, 6:7, :] for k in range(3)]
    for k, value in enumerate(later):
        strip_ref[k : k + 1, :] = value
    strip_ref[len(later) :, :] = jnp.zeros((STRIP - len(later), LANES), F32)
    for copy in leaving:
        copy.wait()


def stretched(row, count):
    tile = jnp.broadcast_to(row, (16, row.shape[1])).astype(BF16)
    return jnp.concatenate([tile] * (count // 16), axis=0)


def ratio(value, scale):
    return jnp.where(scale > 0.0, value / jnp.where(scale > 0.0, scale, 1.0), 0.0)


def field_kernel(
    rows_ref, diag_ref, edge_ref, mask_ref,
    field_ref, part_ref, halo_ref, inner_ref, outer_ref, load_ref,
):
    senders = rows_ref.shape[0]
    groups = (rows_ref.shape[1] - NEAR) // 4
    cells_x = field_ref.shape[1]
    half = (cells_x + 2 * PAD) // 2
    own = cells_x // 2

    load_ref[...] = jnp.zeros_like(load_ref)
    here = lax.axis_index("gx")

    at_row = float_iota((half, LANES), 0).astype(BF16)
    at_column = float_iota((2 * LANES, LANES), 0).astype(BF16)
    zero, one = jnp.zeros((), BF16), jnp.ones((), BF16)

    def operands(sender):
        index = rows_ref[sender, 3 * groups : 4 * groups, :]
        split = float(half * LANES)
        index, shift = (
            jnp.where(index >= split, index - split, index),
            jnp.where(index >= split, float(LANES), 0.0),
        )
        place = jnp.floor(index * (1.0 / LANES))
        column = index - place * float(LANES) + shift
        parts = [
            two_parts(rows_ref[sender, c * groups : (c + 1) * groups, :]) for c in range(3)
        ]
        lefts, rights = [], []
        for group in range(groups):
            line = slice(group, group + 1)
            match = at_row == stretched(place[line], half)
            lefts.append(
                jnp.concatenate(
                    [
                        jnp.where(match, stretched(parts[c][which][line], half), zero)
                        for which in range(2)
                        for c in range(3)
                    ],
                    axis=0,
                )
            )
            rights.append(
                jnp.where(at_column == stretched(column[line], 2 * LANES), one, zero)
            )
        return lefts, rights

    together = math.gcd(senders, 4)

    def add_rows(step, carry):
        lefts, rights = [], []
        for k in range(together):
            left, right = operands(step * together + k)
            lefts += left
            rights += right
        load_ref[...] += lax.dot_general(
            jnp.concatenate(lefts, axis=1),
            jnp.concatenate(rights, axis=1),
            (((1,), (1,)), ((), ())),
            preferred_element_type=F32,
        )
        return carry

    steps = senders // together
    lax.fori_loop(0, steps, add_rows, 0, unroll=min(steps, 2))

    def load_rows(comp, first, last, second_half):
        lanes = slice(LANES, 2 * LANES) if second_half else slice(0, LANES)
        return (
            load_ref[comp * half + first : comp * half + last, lanes]
            + load_ref[(3 + comp) * half + first : (3 + comp) * half + last, lanes]
        )

    field = []
    for comp in range(3):
        load = jnp.concatenate(
            [load_rows(comp, PAD, half, False), load_rows(comp, 0, half - PAD, True)], axis=0
        )
        field.append(load / diag_ref[4 * comp])
        field_ref[comp] = field[comp]
    beyond = half - PAD
    near_before = [load_rows(c, PAD - 1, PAD, False) for c in range(3)]
    far_before = [load_rows(c, PAD - 2, PAD - 1, False) for c in range(3)]
    near_after = [load_rows(c, beyond, beyond + 1, True) for c in range(3)]

    up_x = masked_product(edge_ref, mask_ref, 0, field)
    low_x = masked_product(edge_ref, mask_ref, 1, field)
    base = 4 * groups

    def neighbour(sender, load):
        def entry(k):
            return rows_ref[sender, base + k : base + k + 1, :]

        scale, toward = [entry(k) for k in range(3)], [entry(3 + k) for k in range(9)]
        beside = [ratio(load[c], scale[c]) for c in range(3)]
        return scale, toward, beside, product(lambda k: toward[k], beside)

    lower = jnp.maximum(here - 1, 0)
    before = neighbour(lower, near_before)
    after = neighbour(jnp.minimum(here + 1, senders - 1), near_after)
    rows = before[2] + [ratio(1.0, scale) for scale in before[0]]
    rows += [p[:1] for p in low_x] + before[1] + far_before
    for k, value in enumerate(rows):
        halo_ref[k : k + 1, :] = value
    halo_ref[len(rows) :, :] = jnp.zeros((halo_ref.shape[0] - len(rows), LANES), F32)
    lane_row = iota((1, LANES), 1)
    ends = jnp.zeros((1, LANES), F32)
    for i in range(3):
        for a in range(3):
            ends = jnp.where(lane_row == 3 * i + a, before[2][i][:, LANES - 1 :], ends)
            ends = jnp.where(lane_row == 9 + 3 * i + a, before[2][i][:, :1], ends)
    ends = ends * rows_ref[lower, base + 12 : base + 13, :]
    ends = ends + pltpu.roll(ends, LANES - 3, 1) + pltpu.roll(ends, LANES - 6, 1)

    total = off_diagonal(lambda k: diag_ref[k], field)
    total = [total[c] + rows_moved(up_x[c], before[3][c], 1) for c in range(3)]
    total = [total[c] + rows_moved(low_x[c], after[3][c], -1) for c in range(3)]
    up_y = masked_product(edge_ref, mask_ref, 2, field)
    low_y = masked_product(edge_ref, mask_ref, 3, field)
    total = [
        total[c] + lanes_moved(up_y[c], 0.0, 1) + lanes_moved(low_y[c], 0.0, -1)
        for c in range(3)
    ]
    inverse = [1.0 / diag_ref[4 * c] for c in range(3)]
    part = [total[c] * inverse[c] for c in range(3)]
    for comp in range(3):
        part_ref[comp] = part[comp]
    def columns(lane, along_y, end):
        packed = jnp.zeros((cells_x, LANES), F32)
        at = iota((cells_x, LANES), 1)
        for slot, fields in enumerate((field, along_y, part, inverse)):
            for comp in range(3):
                column = fields[comp][:, lane : lane + 1]
                packed = jnp.where(at == 3 * slot + comp, column, packed)
        rest = jnp.zeros((LANES - cells_x, LANES), F32)
        turned = jnp.concatenate([packed, rest], axis=0).T[:16]
        at = iota((16, LANES), 1)
        line = iota((16, LANES), 0)
        for comp in range(3):
            turned = jnp.where(
                (line == 3 + comp) & (at == cells_x),
                ends[:, end + comp : end + comp + 1],
                turned,
            )
        return turned

    inner_ref[...], outer_ref[...] = by_parity(
        columns(0, low_y, 9), columns(LANES - 1, up_y, 0)
    )


def bernstein(coord):
    other = 1.0 - coord
    return [
        other * other * other,
        3.0 * coord * other * other,
        3.0 * coord * coord * other,
        coord * coord * coord,
    ]


def weight_table(u, v, w):
    first, second, third = bernstein(u), bernstein(v), bernstein(w)
    line = iota((8, u.shape[1]), 0)
    inner = line & 3
    along = jnp.where(
        inner == 0,
        third[0],
        jnp.where(inner == 1, third[1], jnp.where(inner == 2, third[2], third[3])),
    )
    pair = jnp.concatenate(
        [
            jnp.where(line < 4, second[0], second[1]) * along,
            jnp.where(line < 4, second[2], second[3]) * along,
        ],
        axis=0,
    )
    return jnp.concatenate([pair * first[i] for i in range(4)], axis=0)


def tile_rows(terms):
    first_half = iota((4, LANES), 1) < LANES // 2
    rows = []
    for term in terms:
        term = term[:8] + term[8:]
        term = term + pltpu.roll(term, LANES // 2, 1)
        rows.append(jnp.where(first_half, term[:4], term[4:]))
    return jnp.concatenate(two_parts(jnp.concatenate(rows, axis=0)), axis=0).astype(BF16)


def box_matrix(tile_row, boxes):
    tiles = tile_row.shape[1]
    shape = (4 * boxes, 8 * tiles)
    column = iota((1, shape[1]), 1)
    box = jnp.zeros((1, shape[1]), jnp.int32)
    for tile in range(tiles):
        mine = lax.rem(lax.shift_right_logical(column, 2), tiles) == tile
        box = jnp.where(mine, tile_row[:, tile : tile + 1], box)
    target = 4 * box + (column & 3)
    return jnp.where(iota(shape, 0) == target, 1.0, 0.0).astype(BF16)


def by_parity(low, high):
    odd = lax.rem(lax.axis_index("gy"), 2) == 1
    return jnp.where(odd, high, low), jnp.where(odd, low, high)


def quotient_before(halo_ref, strip_ref, before_ref):
    def rows(ref, first, count):
        return [ref[first + k : first + k + 1, :] for k in range(count)]

    beside, inverse, entering = rows(halo_ref, 0, 3), rows(halo_ref, 3, 3), rows(halo_ref, 6, 3)
    far_load, within = rows(halo_ref, 18, 3), rows(strip_ref, 0, 6)
    far_scale = rows(strip_ref, 33, 3)
    far = [ratio(far_load[c], far_scale[c]) for c in range(3)]
    whole_block = [None, *within[:3], None, *within[3:], None]
    total = off_diagonal(lambda k: whole_block[k], beside)
    from_far = product(lambda k: strip_ref[24 + k : 25 + k, :], far)
    up_y = product(lambda k: strip_ref[6 + k : 7 + k, :], beside)
    low_y = product(lambda k: strip_ref[15 + k : 16 + k, :], beside)
    for c in range(3):
        before_ref[c : c + 1, :] = inverse[c] * (
            total[c]
            + from_far[c]
            + entering[c]
            + lanes_moved(up_y[c], 0.0, 1)
            + lanes_moved(low_y[c], 0.0, -1)
        )
    before_ref[3:, :] = jnp.zeros((before_ref.shape[0] - 3, LANES), F32)


def box_kernel(
    tile_ref, field_ref, part_ref, node_ref, param_ref, halo_ref, strip_ref,
    box_ref, adjoint_ref, before_ref, matrix_ref, weights_ref, columns_ref, *, tile_points,
):
    cells_x = field_ref.shape[1]
    own = cells_x // 2
    quotient_before(halo_ref, strip_ref, before_ref)
    field = [field_ref[c] for c in range(3)]
    part = [part_ref[c] for c in range(3)]
    order = [field[0], part[0], field[2], field[1], part[1], part[2]]
    folded = [two_parts(jnp.concatenate([f[:own], f[own:]], axis=1)) for f in order]
    table = jnp.concatenate(
        [folded[f][which] for which in range(2) for f in range(6)], axis=0
    ).astype(BF16)
    points = param_ref.shape[1]
    pieces = CHUNK // LANES
    zero, one = jnp.zeros((), BF16), jnp.ones((), BF16)
    at_node = float_iota((2 * LANES, CHUNK), 0).astype(BF16)
    nothing = jnp.zeros((1, CHUNK), F32)
    highs, lows = [], []
    for chunk in range(points // CHUNK):
        node = jnp.concatenate(
            [node_ref[chunk * pieces + k : chunk * pieces + k + 1, :] for k in range(pieces)],
            axis=1,
        )
        row = lax.shift_right_logical(node, 7)
        column = node & (LANES - 1)
        lanes = slice(chunk * CHUNK, (chunk + 1) * CHUNK)
        at_edge = jnp.where(
            column == 0, row, jnp.where(column == LANES - 1, row + cells_x, -1)
        ).astype(F32)
        columns_ref[:, lanes] = jnp.where(
            at_node[: 2 * cells_x] == stretched(at_edge, 2 * cells_x), one, zero
        )
        place = column + jnp.where(row >= own, LANES, 0)
        row = jnp.where(row >= own, row - own, row)
        pick = jnp.where(at_node == stretched(place.astype(F32), 2 * LANES), one, zero)
        read = jnp.dot(table, pick, preferred_element_type=F32)
        read = read[: 6 * own] + read[6 * own :]
        here = iota((own, CHUNK), 0) == row
        values = [
            jnp.sum(
                jnp.where(here, read[f * own : (f + 1) * own], 0.0), axis=0, keepdims=True
            )
            for f in range(6)
        ]
        high, low = two_parts(
            jnp.concatenate(values[:3] + [nothing] + values[3:] + [nothing], axis=0)
        )
        highs.append(high)
        lows.append(low)
        weights = two_parts(
            weight_table(param_ref[0:1, lanes], param_ref[1:2, lanes], param_ref[2:3, lanes])
        )
        for k in range(CHUNK // tile_points):
            tile = slice(k * tile_points, (k + 1) * tile_points)
            sides = jnp.concatenate([weights[0][:, tile], weights[1][:, tile]], axis=0)
            weights_ref[chunk * (CHUNK // tile_points) + k] = sides.T.astype(BF16)
    both = jnp.concatenate(
        [jnp.concatenate(highs, axis=1), jnp.concatenate(lows, axis=1)], axis=0
    ).astype(BF16)
    matrix_ref[...] = box_matrix(tile_ref[...], matrix_ref.shape[0] // 4)
    tiles = tile_ref.shape[1]
    terms = [
        jnp.dot(
            both[:, tile * tile_points : (tile + 1) * tile_points],
            weights_ref[tile],
            preferred_element_type=F32,
        )
        for tile in range(tiles)
    ]
    box_ref[...] = jnp.dot(matrix_ref[...], tile_rows(terms), preferred_element_type=F32)
    low_half = iota((2 * cells_x, LANES), 1) < LANES // 2
    for tile in range(tiles):
        lanes = slice(tile * tile_points, (tile + 1) * tile_points)
        term = jnp.dot(
            columns_ref[:, lanes], weights_ref[tile], preferred_element_type=F32
        )
        high, low = two_parts(term + pltpu.roll(term, LANES // 2, 1))
        adjoint_ref[tile] = jnp.where(low_half, high, low).astype(BF16)


def sums_kernel(
    from_inner_ref, from_outer_ref, inner_ref, outer_ref, field_ref, part_ref, halo_ref,
    diag_ref, edge_ref, mask_ref, box_ref, adjoint_ref, before_ref, matrix_ref,
    quotient_ref, out_ref,
):
    cells_x = field_ref.shape[1]
    targets = out_ref.shape[0]

    from_low, from_high = by_parity(from_inner_ref[...], from_outer_ref[...])
    first, last = by_parity(inner_ref[...], outer_ref[...])

    def turned(columns):
        rest = jnp.zeros((LANES - 16, LANES), F32)
        return jnp.concatenate([columns, rest], axis=0).T

    low, high = turned(from_low), turned(from_high)
    lane = iota((cells_x, LANES), 1)

    def column(source, slot, comp):
        return source[:cells_x, 3 * slot + comp : 3 * slot + comp + 1]

    field = [field_ref[c] for c in range(3)]
    scale = [diag_ref[4 * c] for c in range(3)]
    toward_high = masked_product(edge_ref, mask_ref, 2, field)
    toward_low = masked_product(edge_ref, mask_ref, 3, field)
    quotient, low_edge, high_edge = [], [], []
    for c in range(3):
        entering = jnp.where(
            lane == 0,
            column(low, 1, c),
            jnp.where(lane == LANES - 1, column(high, 1, c), 0.0),
        )
        quotient.append(part_ref[c] + entering / scale[c])
        low_edge.append(column(low, 2, c) + column(low, 3, c) * toward_low[c][:, :1])
        high_edge.append(column(high, 2, c) + column(high, 3, c) * toward_high[c][:, -1:])
    for c in range(3):
        quotient_ref[c] = quotient[c]
    lane_row = iota((1, LANES), 1)
    before, before_quotient = [], []
    for c in range(3):
        entering = jnp.where(
            lane_row == 0,
            low[cells_x : cells_x + 1, 3 + c : 4 + c],
            jnp.where(lane_row == LANES - 1, high[cells_x : cells_x + 1, 3 + c : 4 + c], 0.0),
        )
        before.append(halo_ref[c : c + 1, :])
        before_quotient.append(
            before_ref[c : c + 1, :] + entering * halo_ref[3 + c : 4 + c, :]
        )

    first_sum = sum(field[c] * scale[c] * field[c] for c in range(3))
    second_sum = sum(field[c] * scale[c] * quotient[c] for c in range(3))
    third_sum = sum(quotient[c] * scale[c] * quotient[c] for c in range(3))
    within = off_diagonal(lambda k: diag_ref[k], quotient)
    fourth_sum = sum(within[c] * field[c] for c in range(3))
    fifth_sum = sum(within[c] * quotient[c] for c in range(3))
    at_row = iota((cells_x, LANES), 0)
    moves = (
        (pltpu.roll, 1, 0, at_row == 0),
        (pltpu.roll, cells_x - 1, 0, at_row == cells_x - 1),
        (pltpu.roll, 1, 1, lane == 0),
        (pltpu.roll, LANES - 1, 1, lane == LANES - 1),
    )
    extra = [0.0, 0.0]
    sides = [0.0, 0.0]
    for direction, (roll, step, dim, edge) in enumerate(moves):
        moving = masked_product(edge_ref, mask_ref, direction, quotient)
        for c in range(3):
            moved = jnp.where(edge, 0.0, roll(moving[c], step, dim))
            fourth_sum = fourth_sum + moved * field[c]
            fifth_sum = fifth_sum + moved * quotient[c]
            if direction == 1:
                extra[0] += moving[c][:1] * before[c]
                extra[1] += moving[c][:1] * before_quotient[c]
            elif direction == 2:
                sides[0] += moving[c][:, LANES - 1 :] * column(high, 0, c)
                sides[1] += moving[c][:, LANES - 1 :] * high_edge[c]
            elif direction == 3:
                sides[0] += moving[c][:, :1] * column(low, 0, c)
                sides[1] += moving[c][:, :1] * low_edge[c]
    incoming = product(lambda k: halo_ref[9 + k : 10 + k, :], before_quotient)
    extra[0] += sum(incoming[c] * field[c][:1] for c in range(3))
    extra[1] += sum(incoming[c] * quotient[c][:1] for c in range(3))
    fourth_sum = fourth_sum + jnp.where(lane == 0, sides[0], 0.0)
    fifth_sum = fifth_sum + jnp.where(lane == 0, sides[1], 0.0)
    extra = [0.0, 0.0, 0.0, extra[0], extra[1]]
    sums = jnp.zeros((1, LANES), F32)
    for k, value in enumerate((first_sum, second_sum, third_sum, fourth_sum, fifth_sum)):
        line = jnp.sum(value, axis=0, keepdims=True) + extra[k]
        sums = jnp.where(lane_row == k, jnp.sum(line, axis=1, keepdims=True), sums)

    added = []
    for c in range(3):
        at_first = from_low[3 + c : 4 + c] * first[9 + c : 10 + c]
        at_last = from_high[3 + c : 4 + c] * last[9 + c : 10 + c]
        added.append(
            jnp.where(lane_row < cells_x, at_first, pltpu.roll(at_last, cells_x, 1))
        )
    none = jnp.zeros((1, LANES), F32)
    added = jnp.concatenate(
        [none, added[0], none, none, none, added[1], added[2], none], axis=0
    )
    added = jnp.concatenate(two_parts(added), axis=0).astype(BF16)
    terms = [
        jnp.dot(added, adjoint_ref[tile], preferred_element_type=F32)
        for tile in range(adjoint_ref.shape[0])
    ]
    total = box_ref[...] + jnp.dot(
        matrix_ref[...], tile_rows(terms), preferred_element_type=F32
    )
    total = jnp.where((iota(total.shape, 0) & 3) == 3, sums, total)
    for box in range(targets):
        out_ref[box] = total[4 * box : 4 * box + 4]


def result_kernel(got_ref, field_ref, quotient_ref, solution_ref, gradient_ref):
    total = jnp.sum(got_ref[...], axis=0)
    rho, a, b, t, u = [total[3:4, k : k + 1] for k in range(5)]
    ratio = a / rho
    norm = rho + a
    step = rho / norm
    rest = jnp.maximum(b - a * ratio, 0.0)
    beta = step * step * rest / rho
    rest_image = (b + u) - ratio * (a + b + a + t) + ratio * ratio * norm
    cross = (a + t) - ratio * norm
    curve = step * step * rest_image - step * beta * (rest + cross) + beta * beta * norm
    second = jnp.where(
        curve > 0.0, step * step * rest / jnp.where(curve > 0.0, curve, 1.0), 0.0
    )
    of_field = step + second * (beta + step * ratio)
    of_quotient = -(step * second)
    for c in range(3):
        solution_ref[c] = of_field * field_ref[c] + of_quotient * quotient_ref[c]
    gradient_ref[:, :LANES] = of_field * total[0:1] + of_quotient * total[1:2]
    gradient_ref[:, LANES:] = (
        of_field * total[2:3, : LANES // 2] + of_quotient * total[2:3, LANES // 2 :]
    )


def per_device(
    diag_blocks, edge_blocks, edge_mask, src_values, src_owner, src_node, src_count,
    surf_node, surf_param, tile_box,
):
    cells_x, cells_y = diag_blocks.shape[1:]
    width_gx, width_gy = lax.axis_size("gx"), lax.axis_size("gy")
    devices = width_gx * width_gy
    groups = src_node.shape[0] // LANES
    whole = functools.partial(jax.ShapeDtypeStruct, dtype=F32)

    cells = 4 * groups + NEAR

    def kept(array):
        return pltpu.with_memory_space_constraint(array, pltpu.HBM)

    i32 = jnp.int32
    rows, strip = pl.pallas_call(
        pack_kernel,
        in_specs=[SMEM] + [HBM] * 6,
        out_specs=[HBM, VMEM],
        out_shape=[
            pltpu.HBM((width_gx, cells, LANES), F32), pltpu.VMEM((STRIP, LANES), F32)
        ],
        scratch_shapes=[
            pltpu.VMEM(src_values.shape, F32),
            pltpu.VMEM((groups, LANES), i32),
            pltpu.VMEM((groups, LANES), i32),
            pltpu.VMEM((9, 8, cells_y), F32),
            pltpu.VMEM((9, 8, cells_y), F32),
            pltpu.VMEM((9, 8, cells_y), F32),
            pltpu.VMEM((4, 9, 8, cells_y), F32),
            pltpu.VMEM((8, cells_y), i32),
            pltpu.VMEM((4, 8, cells_y), i32),
            pltpu.VMEM((width_gx, cells, LANES), F32),
            pltpu.SemaphoreType.DMA((9,)),
            pltpu.SemaphoreType.DMA((2,)),
        ],
        compiler_params=PARAMS,
        name="pack_rows_and_edges",
    )(
        src_count, kept(src_values),
        kept(src_owner.reshape(groups, LANES)), kept(src_node.reshape(groups, LANES)),
        kept(diag_blocks), kept(edge_blocks), kept(edge_mask),
    )
    rows = lax.all_to_all(rows, "gx", split_axis=0, concat_axis=0, tiled=True)
    strip = lax.ppermute(strip, "gx", [(i, i + 1) for i in range(width_gx - 1)])

    nodes = (3, cells_x, cells_y)
    frame = cells_x + 2 * PAD
    field, part, halo, inner, outer = pl.pallas_call(
        field_kernel,
        in_specs=[VMEM] * 4,
        out_specs=[VMEM] * 5,
        out_shape=[
            whole(nodes), whole(nodes), whole((24, cells_y)), whole((16, LANES)),
            whole((16, LANES)),
        ],
        scratch_shapes=[pltpu.VMEM((3 * frame, 2 * LANES), F32)],
        compiler_params=PARAMS,
        name="load_and_first_product",
    )(rows, diag_blocks, edge_blocks, edge_mask)
    def swapped(columns, first):
        low = range(first, width_gy - 1, 2)
        pairs = [(i, i + 1) for i in low] + [(i + 1, i) for i in low]
        return lax.ppermute(columns, "gy", pairs)

    from_inner, from_outer = swapped(inner, 1), swapped(outer, 0)
    points, tiles = surf_node.shape[0], tile_box.shape[0]
    box_part, adjoint, before, matrix = pl.pallas_call(
        functools.partial(box_kernel, tile_points=points // tiles),
        in_specs=[VMEM] * 7,
        out_specs=[VMEM] * 4,
        out_shape=[
            whole((4 * devices, LANES)),
            jax.ShapeDtypeStruct((tiles, 2 * cells_x, LANES), BF16),
            whole((8, LANES)),
            jax.ShapeDtypeStruct((4 * devices, 8 * tiles), BF16),
        ],
        scratch_shapes=[
            pltpu.VMEM((tiles, points // tiles, LANES), BF16),
            pltpu.VMEM((2 * cells_x, points), BF16),
        ],
        compiler_params=PARAMS,
        cost_estimate=pl.CostEstimate(
            flops=10**9, bytes_accessed=4 * 10**6, transcendentals=0
        ),
        name="box_parts",
    )(
        tile_box.reshape(1, tiles), field, part, surf_node.reshape(points // LANES, LANES),
        surf_param, halo, strip,
    )

    quotient, partial = pl.pallas_call(
        sums_kernel,
        in_specs=[VMEM] * 14,
        out_specs=[VMEM] * 2,
        out_shape=[whole(nodes), whole((devices, 4, LANES))],
        compiler_params=PARAMS,
        name="sums_and_halo_parts",
    )(
        from_inner, from_outer, inner, outer, field, part, halo, diag_blocks, edge_blocks, edge_mask,
        box_part, adjoint, before, matrix,
    )
    got = lax.all_to_all(partial, ("gx", "gy"), split_axis=0, concat_axis=0, tiled=True)
    return pl.pallas_call(
        result_kernel,
        in_specs=[VMEM] * 3,
        out_specs=[VMEM] * 2,
        out_shape=[whole(nodes), whole((1, 192))],
        compiler_params=PARAMS,
        name="steps_and_outputs",
    )(got, field, quotient)


def solution(mesh):
    return jax.shard_map(
        per_device,
        mesh=mesh,
        in_specs=(
            P(None, "gx", "gy"),
            P(None, None, "gx", "gy"),
            P(None, "gx", "gy"),
            P(None, ("gx", "gy")),
            P(("gx", "gy"), None),
            P(("gx", "gy")),
            P(("gx", "gy")),
            P(("gx", "gy")),
            P(None, ("gx", "gy")),
            P(("gx", "gy")),
        ),
        out_specs=(P(None, "gx", "gy"), P(("gx", "gy"), None)),
        check_vma=False,
    )
```

```python
import functools
import math

import jax
import jax.numpy as jnp
from jax import lax
from jax.experimental import pallas as pl
from jax.experimental.pallas import tpu as pltpu
from jax.sharding import PartitionSpec as P

F32 = jnp.float32
BF16 = jnp.bfloat16
PAD = 2
NOWHERE = -(1 << 20)
LANES = 128
NEAR = 16
STRIP = 40
CHUNK = 256
PARAMS = pltpu.CompilerParams(vmem_limit_bytes=24 * 1024 * 1024)

VMEM = pl.BlockSpec(memory_space=pltpu.VMEM)
SMEM = pl.BlockSpec(memory_space=pltpu.SMEM)
HBM = pl.BlockSpec(memory_space=pltpu.HBM)


def iota(shape, dim):
    return lax.broadcasted_iota(jnp.int32, shape, dim)


def float_iota(shape, dim):
    return iota(shape, dim).astype(F32)


def two_parts(value):
    high = value.astype(BF16).astype(F32)
    return high, value - high


def product(block, field):
    return [
        block(row) * field[0] + block(3 + row) * field[1] + block(6 + row) * field[2]
        for row in range(3)
    ]


def off_diagonal(block, field):
    return [
        sum(block(3 * i + row) * field[i] for i in range(3) if i != row) for row in range(3)
    ]


def masked_product(edge_ref, mask_ref, direction, field):
    mask = mask_ref[direction].astype(F32)
    return [mask * part for part in product(lambda k: edge_ref[direction, k], field)]


def rows_moved(field, edge_row, step):
    size = field.shape[0]
    at = iota(field.shape, 0)
    moved = pltpu.roll(field, step % size, 0)
    return jnp.where(at == (0 if step == 1 else size - 1), edge_row, moved)


def lanes_moved(field, edge_column, step):
    size = field.shape[1]
    at = iota(field.shape, 1)
    moved = pltpu.roll(field, step % size, 1)
    return jnp.where(at == (0 if step == 1 else size - 1), edge_column, moved)


def pack_kernel(
    count_ref, values_in, owner_in, node_in, diag_in, edge_in, mask_in, rows_out, strip_ref,
    values_ref, owner_ref, node_ref, diag_low, diag_high, edge_low, edge_high,
    mask_low, mask_high, rows_ref, arrived, left,
):
    targets = rows_ref.shape[0]
    groups = owner_ref.shape[0]
    cells_x = diag_in.shape[1]
    top = pl.ds(cells_x - 8, 8)
    copies = [
        pltpu.make_async_copy(source, target, arrived.at[k])
        for k, (source, target) in enumerate(
            (
                (owner_in, owner_ref),
                (node_in, node_ref),
                (values_in, values_ref),
                (diag_in.at[:, 0:8], diag_low),
                (diag_in.at[:, top], diag_high),
                (mask_in.at[1, 0:8], mask_low),
                (mask_in.at[:, top], mask_high),
                (edge_in.at[1, :, 0:8], edge_low),
                (edge_in.at[:, :, top], edge_high),
            )
        )
    ]
    for copy in copies:
        copy.start()
    base = 4 * groups
    for target in range(targets):
        rows_ref[target, base:, :] = jnp.zeros((NEAR, LANES), F32)
    for copy in copies[:2]:
        copy.wait()
    order = iota((groups, LANES), 0) * LANES + iota((groups, LANES), 1)
    node = node_ref[...]
    frame = cells_x + 2 * PAD
    row = owner_ref[...] * cells_x + lax.shift_right_logical(node, 7)
    row = jnp.where(order < count_ref[0], row, NOWHERE)
    column = node & (LANES - 1)
    for target in range(targets):
        line = row - (target * cells_x - PAD)
        inside = (line >= 0) & (line < frame)
        index = jnp.where(inside, line * LANES + column, -1)
        rows_ref[target, 3 * groups : 4 * groups, :] = index.astype(F32)

    copies[2].wait()
    for comp in range(3):
        value = jnp.concatenate(
            [
                values_ref[comp : comp + 1, group * LANES : (group + 1) * LANES]
                for group in range(groups)
            ],
            axis=0,
        )
        for target in range(targets):
            rows_ref[target, comp * groups : (comp + 1) * groups, :] = value
    near = pl.ds(4 * groups, NEAR)
    leaving = [
        pltpu.make_async_copy(rows_ref.at[:, part], rows_out.at[:, part], left.at[k])
        for k, part in enumerate((pl.ds(0, 4 * groups), near))
    ]
    leaving[0].start()
    for copy in copies[3:]:
        copy.wait()

    def block(edge, mask, direction, at):
        present = mask[direction, at : at + 1, :].astype(F32)
        return [edge[direction, k, at : at + 1, :] * present for k in range(9)]

    up_y, low_y = block(edge_high, mask_high, 2, 7), block(edge_high, mask_high, 3, 7)
    here = lax.axis_index("gx")

    @pl.when(here < targets - 1)
    def _():
        def put(slot, value):
            rows_ref[here + 1, base + slot : base + slot + 1, :] = value

        for k in range(3):
            put(k, diag_high[4 * k, 7:8, :])
        for k, value in enumerate(block(edge_high, mask_high, 0, 7)):
            put(3 + k, value)
        corners = jnp.zeros((1, LANES), F32)
        lane = iota((1, LANES), 1)
        for k in range(9):
            corners = jnp.where(lane == k, up_y[k][:, LANES - 1 :], corners)
            corners = jnp.where(lane == 9 + k, low_y[k][:, :1], corners)
        put(12, corners)

    @pl.when(here > 0)
    def _():
        def put(slot, value):
            rows_ref[here - 1, base + slot : base + slot + 1, :] = value

        for k in range(3):
            put(k, diag_low[4 * k, 0:1, :])
        present = mask_low[0:1, :].astype(F32)
        for k in range(9):
            put(3 + k, edge_low[k, 0:1, :] * present)

    leaving[1].start()
    later = [diag_high[k, 7:8, :] for k in range(9) if k % 4]
    later += up_y + low_y + block(edge_high, mask_high, 0, 6)
    later += [diag_high[4 * k, 6:7, :] for k in range(3)]
    for k, value in enumerate(later):
        strip_ref[k : k + 1, :] = value
    strip_ref[len(later) :, :] = jnp.zeros((STRIP - len(later), LANES), F32)
    for copy in leaving:
        copy.wait()


def stretched(row, count):
    tile = jnp.broadcast_to(row, (16, row.shape[1])).astype(BF16)
    return jnp.concatenate([tile] * (count // 16), axis=0)


def ratio(value, scale):
    return jnp.where(scale > 0.0, value / jnp.where(scale > 0.0, scale, 1.0), 0.0)


def field_kernel(
    rows_ref, diag_ref, edge_ref, mask_ref,
    field_ref, part_ref, halo_ref, inner_ref, outer_ref, load_ref,
):
    senders = rows_ref.shape[0]
    groups = (rows_ref.shape[1] - NEAR) // 4
    cells_x = field_ref.shape[1]
    half = (cells_x + 2 * PAD) // 2
    own = cells_x // 2

    load_ref[...] = jnp.zeros_like(load_ref)
    here = lax.axis_index("gx")

    size = load_ref.shape[0]
    line = iota((size, LANES), 0)
    block = sum(jnp.where(line >= half * k, 1, 0) for k in range(1, 6))
    at_row = jnp.where(line < 6 * half, line - half * block, -5).astype(F32).astype(BF16)
    at_column = float_iota((2 * LANES, LANES), 0).astype(BF16)
    in_tile = float_iota((16, LANES), 0).astype(BF16)
    zero, one = jnp.zeros((), BF16), jnp.ones((), BF16)

    def operands(sender):
        index = rows_ref[sender, 3 * groups : 4 * groups, :]
        split = float(half * LANES)
        index, shift = (
            jnp.where(index >= split, index - split, index),
            jnp.where(index >= split, float(LANES), 0.0),
        )
        place = jnp.floor(index * (1.0 / LANES))
        column = index - place * float(LANES) + shift
        parts = [
            two_parts(rows_ref[sender, c * groups : (c + 1) * groups, :]) for c in range(3)
        ]
        lefts, rights = [], []
        for group in range(groups):
            line = slice(group, group + 1)
            values = [
                stretched(parts[c][which][line], 16) for which in range(2) for c in range(3)
            ]
            tiles = []
            for first in range(0, size, 16):
                low, high = first // half, min((first + 15) // half, 5)
                tiles.append(
                    values[low]
                    if low == high
                    else jnp.where(
                        in_tile < float(half * high - first), values[low], values[high]
                    )
                )
            match = at_row == stretched(place[line], size)
            lefts.append(jnp.where(match, jnp.concatenate(tiles, axis=0), zero))
            rights.append(
                jnp.where(at_column == stretched(column[line], 2 * LANES), one, zero)
            )
        return lefts, rights

    together = math.gcd(senders, 4)

    def add_rows(step, carry):
        lefts, rights = [], []
        for k in range(together):
            left, right = operands(step * together + k)
            lefts += left
            rights += right
        load_ref[...] += lax.dot_general(
            jnp.concatenate(lefts, axis=1),
            jnp.concatenate(rights, axis=1),
            (((1,), (1,)), ((), ())),
            preferred_element_type=F32,
        )
        return carry

    steps = senders // together
    lax.fori_loop(0, steps, add_rows, 0, unroll=min(steps, 2))

    def load_rows(comp, first, last, second_half):
        lanes = slice(LANES, 2 * LANES) if second_half else slice(0, LANES)
        return (
            load_ref[comp * half + first : comp * half + last, lanes]
            + load_ref[(3 + comp) * half + first : (3 + comp) * half + last, lanes]
        )

    field = []
    for comp in range(3):
        load = jnp.concatenate(
            [load_rows(comp, PAD, half, False), load_rows(comp, 0, half - PAD, True)], axis=0
        )
        field.append(load / diag_ref[4 * comp])
        field_ref[comp] = field[comp]
    beyond = half - PAD
    near_before = [load_rows(c, PAD - 1, PAD, False) for c in range(3)]
    far_before = [load_rows(c, PAD - 2, PAD - 1, False) for c in range(3)]
    near_after = [load_rows(c, beyond, beyond + 1, True) for c in range(3)]

    up_x = masked_product(edge_ref, mask_ref, 0, field)
    low_x = masked_product(edge_ref, mask_ref, 1, field)
    base = 4 * groups

    def neighbour(sender, load):
        def entry(k):
            return rows_ref[sender, base + k : base + k + 1, :]

        scale, toward = [entry(k) for k in range(3)], [entry(3 + k) for k in range(9)]
        beside = [ratio(load[c], scale[c]) for c in range(3)]
        return scale, toward, beside, product(lambda k: toward[k], beside)

    lower = jnp.maximum(here - 1, 0)
    before = neighbour(lower, near_before)
    after = neighbour(jnp.minimum(here + 1, senders - 1), near_after)
    rows = before[2] + [ratio(1.0, scale) for scale in before[0]]
    rows += [p[:1] for p in low_x] + before[1] + far_before
    for k, value in enumerate(rows):
        halo_ref[k : k + 1, :] = value
    halo_ref[len(rows) :, :] = jnp.zeros((halo_ref.shape[0] - len(rows), LANES), F32)
    lane_row = iota((1, LANES), 1)
    ends = jnp.zeros((1, LANES), F32)
    for i in range(3):
        for a in range(3):
            ends = jnp.where(lane_row == 3 * i + a, before[2][i][:, LANES - 1 :], ends)
            ends = jnp.where(lane_row == 9 + 3 * i + a, before[2][i][:, :1], ends)
    ends = ends * rows_ref[lower, base + 12 : base + 13, :]
    ends = ends + pltpu.roll(ends, LANES - 3, 1) + pltpu.roll(ends, LANES - 6, 1)

    total = off_diagonal(lambda k: diag_ref[k], field)
    total = [total[c] + rows_moved(up_x[c], before[3][c], 1) for c in range(3)]
    total = [total[c] + rows_moved(low_x[c], after[3][c], -1) for c in range(3)]
    up_y = masked_product(edge_ref, mask_ref, 2, field)
    low_y = masked_product(edge_ref, mask_ref, 3, field)
    total = [
        total[c] + lanes_moved(up_y[c], 0.0, 1) + lanes_moved(low_y[c], 0.0, -1)
        for c in range(3)
    ]
    inverse = [1.0 / diag_ref[4 * c] for c in range(3)]
    part = [total[c] * inverse[c] for c in range(3)]
    for comp in range(3):
        part_ref[comp] = part[comp]
    def columns(lane, along_y, end):
        packed = jnp.zeros((cells_x, LANES), F32)
        at = iota((cells_x, LANES), 1)
        for slot, fields in enumerate((field, along_y, part, inverse)):
            for comp in range(3):
                column = fields[comp][:, lane : lane + 1]
                packed = jnp.where(at == 3 * slot + comp, column, packed)
        rest = jnp.zeros((LANES - cells_x, LANES), F32)
        turned = jnp.concatenate([packed, rest], axis=0).T[:16]
        at = iota((16, LANES), 1)
        line = iota((16, LANES), 0)
        for comp in range(3):
            turned = jnp.where(
                (line == 3 + comp) & (at == cells_x),
                ends[:, end + comp : end + comp + 1],
                turned,
            )
        return turned

    inner_ref[...], outer_ref[...] = by_parity(
        columns(0, low_y, 9), columns(LANES - 1, up_y, 0)
    )


def bernstein(coord):
    other = 1.0 - coord
    return [
        other * other * other,
        3.0 * coord * other * other,
        3.0 * coord * coord * other,
        coord * coord * coord,
    ]


def weight_table(u, v, w):
    first, second, third = bernstein(u), bernstein(v), bernstein(w)
    line = iota((8, u.shape[1]), 0)
    inner = line & 3
    along = jnp.where(
        inner == 0,
        third[0],
        jnp.where(inner == 1, third[1], jnp.where(inner == 2, third[2], third[3])),
    )
    pair = jnp.concatenate(
        [
            jnp.where(line < 4, second[0], second[1]) * along,
            jnp.where(line < 4, second[2], second[3]) * along,
        ],
        axis=0,
    )
    return jnp.concatenate([pair * first[i] for i in range(4)], axis=0)


def tile_rows(terms):
    first_half = iota((4, LANES), 1) < LANES // 2
    rows = []
    for term in terms:
        term = term[:8] + term[8:]
        term = term + pltpu.roll(term, LANES // 2, 1)
        rows.append(jnp.where(first_half, term[:4], term[4:]))
    return jnp.concatenate(two_parts(jnp.concatenate(rows, axis=0)), axis=0).astype(BF16)


def box_matrix(tile_row, boxes):
    tiles = tile_row.shape[1]
    shape = (4 * boxes, 8 * tiles)
    column = iota((1, shape[1]), 1)
    box = jnp.zeros((1, shape[1]), jnp.int32)
    for tile in range(tiles):
        mine = lax.rem(lax.shift_right_logical(column, 2), tiles) == tile
        box = jnp.where(mine, tile_row[:, tile : tile + 1], box)
    target = 4 * box + (column & 3)
    return jnp.where(iota(shape, 0) == target, 1.0, 0.0).astype(BF16)


def by_parity(low, high):
    odd = lax.rem(lax.axis_index("gy"), 2) == 1
    return jnp.where(odd, high, low), jnp.where(odd, low, high)


def quotient_before(halo_ref, strip_ref, before_ref):
    def rows(ref, first, count):
        return [ref[first + k : first + k + 1, :] for k in range(count)]

    beside, inverse, entering = rows(halo_ref, 0, 3), rows(halo_ref, 3, 3), rows(halo_ref, 6, 3)
    far_load, within = rows(halo_ref, 18, 3), rows(strip_ref, 0, 6)
    far_scale = rows(strip_ref, 33, 3)
    far = [ratio(far_load[c], far_scale[c]) for c in range(3)]
    whole_block = [None, *within[:3], None, *within[3:], None]
    total = off_diagonal(lambda k: whole_block[k], beside)
    from_far = product(lambda k: strip_ref[24 + k : 25 + k, :], far)
    up_y = product(lambda k: strip_ref[6 + k : 7 + k, :], beside)
    low_y = product(lambda k: strip_ref[15 + k : 16 + k, :], beside)
    for c in range(3):
        before_ref[c : c + 1, :] = inverse[c] * (
            total[c]
            + from_far[c]
            + entering[c]
            + lanes_moved(up_y[c], 0.0, 1)
            + lanes_moved(low_y[c], 0.0, -1)
        )
    before_ref[3:, :] = jnp.zeros((before_ref.shape[0] - 3, LANES), F32)


def box_kernel(
    tile_ref, field_ref, part_ref, node_ref, param_ref, halo_ref, strip_ref,
    box_ref, adjoint_ref, before_ref, matrix_ref, weights_ref, columns_ref, *, tile_points,
):
    cells_x = field_ref.shape[1]
    own = cells_x // 2
    quotient_before(halo_ref, strip_ref, before_ref)
    field = [field_ref[c] for c in range(3)]
    part = [part_ref[c] for c in range(3)]
    order = [field[0], part[0], field[2], field[1], part[1], part[2]]
    folded = [two_parts(jnp.concatenate([f[:own], f[own:]], axis=1)) for f in order]
    table = jnp.concatenate(
        [folded[f][which] for which in range(2) for f in range(6)], axis=0
    ).astype(BF16)
    points = param_ref.shape[1]
    pieces = CHUNK // LANES
    zero, one = jnp.zeros((), BF16), jnp.ones((), BF16)
    at_node = float_iota((2 * LANES, CHUNK), 0).astype(BF16)
    nothing = jnp.zeros((1, CHUNK), F32)
    highs, lows = [], []
    for chunk in range(points // CHUNK):
        node = jnp.concatenate(
            [node_ref[chunk * pieces + k : chunk * pieces + k + 1, :] for k in range(pieces)],
            axis=1,
        )
        row = lax.shift_right_logical(node, 7)
        column = node & (LANES - 1)
        lanes = slice(chunk * CHUNK, (chunk + 1) * CHUNK)
        at_edge = jnp.where(
            column == 0, row, jnp.where(column == LANES - 1, row + cells_x, -1)
        ).astype(F32)
        columns_ref[:, lanes] = jnp.where(
            at_node[: 2 * cells_x] == stretched(at_edge, 2 * cells_x), one, zero
        )
        place = column + jnp.where(row >= own, LANES, 0)
        row = jnp.where(row >= own, row - own, row)
        pick = jnp.where(at_node == stretched(place.astype(F32), 2 * LANES), one, zero)
        read = jnp.dot(table, pick, preferred_element_type=F32)
        read = read[: 6 * own] + read[6 * own :]
        here = iota((own, CHUNK), 0) == row
        values = [
            jnp.sum(
                jnp.where(here, read[f * own : (f + 1) * own], 0.0), axis=0, keepdims=True
            )
            for f in range(6)
        ]
        high, low = two_parts(
            jnp.concatenate(values[:3] + [nothing] + values[3:] + [nothing], axis=0)
        )
        highs.append(high)
        lows.append(low)
        weights = two_parts(
            weight_table(param_ref[0:1, lanes], param_ref[1:2, lanes], param_ref[2:3, lanes])
        )
        for k in range(CHUNK // tile_points):
            tile = slice(k * tile_points, (k + 1) * tile_points)
            sides = jnp.concatenate([weights[0][:, tile], weights[1][:, tile]], axis=0)
            weights_ref[chunk * (CHUNK // tile_points) + k] = sides.T.astype(BF16)
    both = jnp.concatenate(
        [jnp.concatenate(highs, axis=1), jnp.concatenate(lows, axis=1)], axis=0
    ).astype(BF16)
    matrix_ref[...] = box_matrix(tile_ref[...], matrix_ref.shape[0] // 4)
    tiles = tile_ref.shape[1]
    terms = [
        jnp.dot(
            both[:, tile * tile_points : (tile + 1) * tile_points],
            weights_ref[tile],
            preferred_element_type=F32,
        )
        for tile in range(tiles)
    ]
    box_ref[...] = jnp.dot(matrix_ref[...], tile_rows(terms), preferred_element_type=F32)
    low_half = iota((2 * cells_x, LANES), 1) < LANES // 2
    for tile in range(tiles):
        lanes = slice(tile * tile_points, (tile + 1) * tile_points)
        term = jnp.dot(
            columns_ref[:, lanes], weights_ref[tile], preferred_element_type=F32
        )
        high, low = two_parts(term + pltpu.roll(term, LANES // 2, 1))
        adjoint_ref[tile] = jnp.where(low_half, high, low).astype(BF16)


def sums_kernel(
    from_inner_ref, from_outer_ref, inner_ref, outer_ref, field_ref, part_ref, halo_ref,
    diag_ref, edge_ref, mask_ref, box_ref, adjoint_ref, before_ref, matrix_ref,
    quotient_ref, out_ref,
):
    cells_x = field_ref.shape[1]
    targets = out_ref.shape[0]

    from_low, from_high = by_parity(from_inner_ref[...], from_outer_ref[...])
    first, last = by_parity(inner_ref[...], outer_ref[...])

    def turned(columns):
        rest = jnp.zeros((LANES - 16, LANES), F32)
        return jnp.concatenate([columns, rest], axis=0).T

    low, high = turned(from_low), turned(from_high)
    lane = iota((cells_x, LANES), 1)

    def column(source, slot, comp):
        return source[:cells_x, 3 * slot + comp : 3 * slot + comp + 1]

    field = [field_ref[c] for c in range(3)]
    scale = [diag_ref[4 * c] for c in range(3)]
    toward_high = masked_product(edge_ref, mask_ref, 2, field)
    toward_low = masked_product(edge_ref, mask_ref, 3, field)
    quotient, low_edge, high_edge = [], [], []
    for c in range(3):
        entering = jnp.where(
            lane == 0,
            column(low, 1, c),
            jnp.where(lane == LANES - 1, column(high, 1, c), 0.0),
        )
        quotient.append(part_ref[c] + entering / scale[c])
        low_edge.append(column(low, 2, c) + column(low, 3, c) * toward_low[c][:, :1])
        high_edge.append(column(high, 2, c) + column(high, 3, c) * toward_high[c][:, -1:])
    for c in range(3):
        quotient_ref[c] = quotient[c]
    lane_row = iota((1, LANES), 1)
    before, before_quotient = [], []
    for c in range(3):
        entering = jnp.where(
            lane_row == 0,
            low[cells_x : cells_x + 1, 3 + c : 4 + c],
            jnp.where(lane_row == LANES - 1, high[cells_x : cells_x + 1, 3 + c : 4 + c], 0.0),
        )
        before.append(halo_ref[c : c + 1, :])
        before_quotient.append(
            before_ref[c : c + 1, :] + entering * halo_ref[3 + c : 4 + c, :]
        )

    first_sum = sum(field[c] * scale[c] * field[c] for c in range(3))
    second_sum = sum(field[c] * scale[c] * quotient[c] for c in range(3))
    third_sum = sum(quotient[c] * scale[c] * quotient[c] for c in range(3))
    within = off_diagonal(lambda k: diag_ref[k], quotient)
    fourth_sum = sum(within[c] * field[c] for c in range(3))
    fifth_sum = sum(within[c] * quotient[c] for c in range(3))
    at_row = iota((cells_x, LANES), 0)
    moves = (
        (pltpu.roll, 1, 0, at_row == 0),
        (pltpu.roll, cells_x - 1, 0, at_row == cells_x - 1),
        (pltpu.roll, 1, 1, lane == 0),
        (pltpu.roll, LANES - 1, 1, lane == LANES - 1),
    )
    extra = [0.0, 0.0]
    sides = [0.0, 0.0]
    for direction, (roll, step, dim, edge) in enumerate(moves):
        moving = masked_product(edge_ref, mask_ref, direction, quotient)
        for c in range(3):
            moved = jnp.where(edge, 0.0, roll(moving[c], step, dim))
            fourth_sum = fourth_sum + moved * field[c]
            fifth_sum = fifth_sum + moved * quotient[c]
            if direction == 1:
                extra[0] += moving[c][:1] * before[c]
                extra[1] += moving[c][:1] * before_quotient[c]
            elif direction == 2:
                sides[0] += moving[c][:, LANES - 1 :] * column(high, 0, c)
                sides[1] += moving[c][:, LANES - 1 :] * high_edge[c]
            elif direction == 3:
                sides[0] += moving[c][:, :1] * column(low, 0, c)
                sides[1] += moving[c][:, :1] * low_edge[c]
    incoming = product(lambda k: halo_ref[9 + k : 10 + k, :], before_quotient)
    extra[0] += sum(incoming[c] * field[c][:1] for c in range(3))
    extra[1] += sum(incoming[c] * quotient[c][:1] for c in range(3))
    fourth_sum = fourth_sum + jnp.where(lane == 0, sides[0], 0.0)
    fifth_sum = fifth_sum + jnp.where(lane == 0, sides[1], 0.0)
    extra = [0.0, 0.0, 0.0, extra[0], extra[1]]
    sums = jnp.zeros((1, LANES), F32)
    for k, value in enumerate((first_sum, second_sum, third_sum, fourth_sum, fifth_sum)):
        line = jnp.sum(value, axis=0, keepdims=True) + extra[k]
        sums = jnp.where(lane_row == k, jnp.sum(line, axis=1, keepdims=True), sums)

    added = []
    for c in range(3):
        at_first = from_low[3 + c : 4 + c] * first[9 + c : 10 + c]
        at_last = from_high[3 + c : 4 + c] * last[9 + c : 10 + c]
        added.append(
            jnp.where(lane_row < cells_x, at_first, pltpu.roll(at_last, cells_x, 1))
        )
    none = jnp.zeros((1, LANES), F32)
    added = jnp.concatenate(
        [none, added[0], none, none, none, added[1], added[2], none], axis=0
    )
    added = jnp.concatenate(two_parts(added), axis=0).astype(BF16)
    terms = [
        jnp.dot(added, adjoint_ref[tile], preferred_element_type=F32)
        for tile in range(adjoint_ref.shape[0])
    ]
    total = box_ref[...] + jnp.dot(
        matrix_ref[...], tile_rows(terms), preferred_element_type=F32
    )
    total = jnp.where((iota(total.shape, 0) & 3) == 3, sums, total)
    for box in range(targets):
        out_ref[box] = total[4 * box : 4 * box + 4]


def result_kernel(got_ref, field_ref, quotient_ref, solution_ref, gradient_ref):
    total = jnp.sum(got_ref[...], axis=0)
    rho, a, b, t, u = [total[3:4, k : k + 1] for k in range(5)]
    ratio = a / rho
    norm = rho + a
    step = rho / norm
    rest = jnp.maximum(b - a * ratio, 0.0)
    beta = step * step * rest / rho
    rest_image = (b + u) - ratio * (a + b + a + t) + ratio * ratio * norm
    cross = (a + t) - ratio * norm
    curve = step * step * rest_image - step * beta * (rest + cross) + beta * beta * norm
    second = jnp.where(
        curve > 0.0, step * step * rest / jnp.where(curve > 0.0, curve, 1.0), 0.0
    )
    of_field = step + second * (beta + step * ratio)
    of_quotient = -(step * second)
    for c in range(3):
        solution_ref[c] = of_field * field_ref[c] + of_quotient * quotient_ref[c]
    gradient_ref[:, :LANES] = of_field * total[0:1] + of_quotient * total[1:2]
    gradient_ref[:, LANES:] = (
        of_field * total[2:3, : LANES // 2] + of_quotient * total[2:3, LANES // 2 :]
    )


def per_device(
    diag_blocks, edge_blocks, edge_mask, src_values, src_owner, src_node, src_count,
    surf_node, surf_param, tile_box,
):
    cells_x, cells_y = diag_blocks.shape[1:]
    width_gx, width_gy = lax.axis_size("gx"), lax.axis_size("gy")
    devices = width_gx * width_gy
    groups = src_node.shape[0] // LANES
    whole = functools.partial(jax.ShapeDtypeStruct, dtype=F32)

    cells = 4 * groups + NEAR

    def kept(array):
        return pltpu.with_memory_space_constraint(array, pltpu.HBM)

    i32 = jnp.int32
    rows, strip = pl.pallas_call(
        pack_kernel,
        in_specs=[SMEM] + [HBM] * 6,
        out_specs=[HBM, VMEM],
        out_shape=[
            pltpu.HBM((width_gx, cells, LANES), F32), pltpu.VMEM((STRIP, LANES), F32)
        ],
        scratch_shapes=[
            pltpu.VMEM(src_values.shape, F32),
            pltpu.VMEM((groups, LANES), i32),
            pltpu.VMEM((groups, LANES), i32),
            pltpu.VMEM((9, 8, cells_y), F32),
            pltpu.VMEM((9, 8, cells_y), F32),
            pltpu.VMEM((9, 8, cells_y), F32),
            pltpu.VMEM((4, 9, 8, cells_y), F32),
            pltpu.VMEM((8, cells_y), i32),
            pltpu.VMEM((4, 8, cells_y), i32),
            pltpu.VMEM((width_gx, cells, LANES), F32),
            pltpu.SemaphoreType.DMA((9,)),
            pltpu.SemaphoreType.DMA((2,)),
        ],
        compiler_params=PARAMS,
        name="pack_rows_and_edges",
    )(
        src_count, kept(src_values),
        kept(src_owner.reshape(groups, LANES)), kept(src_node.reshape(groups, LANES)),
        kept(diag_blocks), kept(edge_blocks), kept(edge_mask),
    )
    rows = lax.all_to_all(rows, "gx", split_axis=0, concat_axis=0, tiled=True)
    strip = lax.ppermute(strip, "gx", [(i, i + 1) for i in range(width_gx - 1)])

    nodes = (3, cells_x, cells_y)
    size = -(-3 * (cells_x + 2 * PAD) // 16) * 16
    field, part, halo, inner, outer = pl.pallas_call(
        field_kernel,
        in_specs=[VMEM] * 4,
        out_specs=[VMEM] * 5,
        out_shape=[
            whole(nodes), whole(nodes), whole((24, cells_y)), whole((16, LANES)),
            whole((16, LANES)),
        ],
        scratch_shapes=[pltpu.VMEM((size, 2 * LANES), F32)],
        compiler_params=PARAMS,
        name="load_and_first_product",
    )(rows, diag_blocks, edge_blocks, edge_mask)
    def swapped(columns, first):
        low = range(first, width_gy - 1, 2)
        pairs = [(i, i + 1) for i in low] + [(i + 1, i) for i in low]
        return lax.ppermute(columns, "gy", pairs)

    from_inner, from_outer = swapped(inner, 1), swapped(outer, 0)
    points, tiles = surf_node.shape[0], tile_box.shape[0]
    box_part, adjoint, before, matrix = pl.pallas_call(
        functools.partial(box_kernel, tile_points=points // tiles),
        in_specs=[VMEM] * 7,
        out_specs=[VMEM] * 4,
        out_shape=[
            whole((4 * devices, LANES)),
            jax.ShapeDtypeStruct((tiles, 2 * cells_x, LANES), BF16),
            whole((8, LANES)),
            jax.ShapeDtypeStruct((4 * devices, 8 * tiles), BF16),
        ],
        scratch_shapes=[
            pltpu.VMEM((tiles, points // tiles, LANES), BF16),
            pltpu.VMEM((2 * cells_x, points), BF16),
        ],
        compiler_params=PARAMS,
        cost_estimate=pl.CostEstimate(
            flops=10**9, bytes_accessed=4 * 10**6, transcendentals=0
        ),
        name="box_parts",
    )(
        tile_box.reshape(1, tiles), field, part, surf_node.reshape(points // LANES, LANES),
        surf_param, halo, strip,
    )

    quotient, partial = pl.pallas_call(
        sums_kernel,
        in_specs=[VMEM] * 14,
        out_specs=[VMEM] * 2,
        out_shape=[whole(nodes), whole((devices, 4, LANES))],
        compiler_params=PARAMS,
        name="sums_and_halo_parts",
    )(
        from_inner, from_outer, inner, outer, field, part, halo, diag_blocks, edge_blocks, edge_mask,
        box_part, adjoint, before, matrix,
    )
    got = lax.all_to_all(partial, ("gx", "gy"), split_axis=0, concat_axis=0, tiled=True)
    return pl.pallas_call(
        result_kernel,
        in_specs=[VMEM] * 3,
        out_specs=[VMEM] * 2,
        out_shape=[whole(nodes), whole((1, 192))],
        compiler_params=PARAMS,
        name="steps_and_outputs",
    )(got, field, quotient)


def solution(mesh):
    return jax.shard_map(
        per_device,
        mesh=mesh,
        in_specs=(
            P(None, "gx", "gy"),
            P(None, None, "gx", "gy"),
            P(None, "gx", "gy"),
            P(None, ("gx", "gy")),
            P(("gx", "gy"), None),
            P(("gx", "gy")),
            P(("gx", "gy")),
            P(("gx", "gy")),
            P(None, ("gx", "gy")),
            P(("gx", "gy")),
        ),
        out_specs=(P(None, "gx", "gy"), P(("gx", "gy"), None)),
        check_vma=False,
    )
```

```python
import functools
import math

import jax
import jax.numpy as jnp
from jax import lax
from jax.experimental import pallas as pl
from jax.experimental.pallas import tpu as pltpu
from jax.sharding import PartitionSpec as P

F32 = jnp.float32
BF16 = jnp.bfloat16
PAD = 2
NOWHERE = -(1 << 20)
LANES = 128
NEAR = 16
STRIP = 40
CHUNK = 256
PARAMS = pltpu.CompilerParams(vmem_limit_bytes=24 * 1024 * 1024)

VMEM = pl.BlockSpec(memory_space=pltpu.VMEM)
SMEM = pl.BlockSpec(memory_space=pltpu.SMEM)
HBM = pl.BlockSpec(memory_space=pltpu.HBM)


def iota(shape, dim):
    return lax.broadcasted_iota(jnp.int32, shape, dim)


def float_iota(shape, dim):
    return iota(shape, dim).astype(F32)


def two_parts(value):
    high = value.astype(BF16).astype(F32)
    return high, value - high


def product(block, field):
    return [
        block(row) * field[0] + block(3 + row) * field[1] + block(6 + row) * field[2]
        for row in range(3)
    ]


def off_diagonal(block, field):
    return [
        sum(block(3 * i + row) * field[i] for i in range(3) if i != row) for row in range(3)
    ]


def masked_product(edge_ref, mask_ref, direction, field):
    mask = mask_ref[direction].astype(F32)
    return [mask * part for part in product(lambda k: edge_ref[direction, k], field)]


def rows_moved(field, edge_row, step):
    size = field.shape[0]
    at = iota(field.shape, 0)
    moved = pltpu.roll(field, step % size, 0)
    return jnp.where(at == (0 if step == 1 else size - 1), edge_row, moved)


def lanes_moved(field, edge_column, step):
    size = field.shape[1]
    at = iota(field.shape, 1)
    moved = pltpu.roll(field, step % size, 1)
    return jnp.where(at == (0 if step == 1 else size - 1), edge_column, moved)


def pack_kernel(
    count_ref, values_in, owner_in, node_in, diag_in, edge_in, mask_in, rows_out, strip_ref,
    values_ref, owner_ref, node_ref, diag_low, diag_high, edge_low, edge_high,
    mask_low, mask_high, rows_ref, arrived, left,
):
    targets = rows_ref.shape[0]
    groups = owner_ref.shape[0]
    cells_x = diag_in.shape[1]
    top = pl.ds(cells_x - 8, 8)
    copies = [
        pltpu.make_async_copy(source, target, arrived.at[k])
        for k, (source, target) in enumerate(
            (
                (owner_in, owner_ref),
                (node_in, node_ref),
                (values_in, values_ref),
                (diag_in.at[:, 0:8], diag_low),
                (diag_in.at[:, top], diag_high),
                (mask_in.at[1, 0:8], mask_low),
                (mask_in.at[:, top], mask_high),
                (edge_in.at[1, :, 0:8], edge_low),
                (edge_in.at[:, :, top], edge_high),
            )
        )
    ]
    for copy in copies:
        copy.start()
    base = 4 * groups
    for target in range(targets):
        rows_ref[target, base:, :] = jnp.zeros((NEAR, LANES), F32)
    for copy in copies[:2]:
        copy.wait()
    order = iota((groups, LANES), 0) * LANES + iota((groups, LANES), 1)
    node = node_ref[...]
    frame = cells_x + 2 * PAD
    row = owner_ref[...] * cells_x + lax.shift_right_logical(node, 7)
    row = jnp.where(order < count_ref[0], row, NOWHERE)
    column = node & (LANES - 1)
    for target in range(targets):
        line = row - (target * cells_x - PAD)
        inside = (line >= 0) & (line < frame)
        index = jnp.where(inside, line * LANES + column, -1)
        rows_ref[target, 3 * groups : 4 * groups, :] = index.astype(F32)

    copies[2].wait()
    for comp in range(3):
        value = jnp.concatenate(
            [
                values_ref[comp : comp + 1, group * LANES : (group + 1) * LANES]
                for group in range(groups)
            ],
            axis=0,
        )
        for target in range(targets):
            rows_ref[target, comp * groups : (comp + 1) * groups, :] = value
    near = pl.ds(4 * groups, NEAR)
    leaving = [
        pltpu.make_async_copy(rows_ref.at[:, part], rows_out.at[:, part], left.at[k])
        for k, part in enumerate((pl.ds(0, 4 * groups), near))
    ]
    leaving[0].start()
    for copy in copies[3:]:
        copy.wait()

    def block(edge, mask, direction, at):
        present = mask[direction, at : at + 1, :].astype(F32)
        return [edge[direction, k, at : at + 1, :] * present for k in range(9)]

    up_y, low_y = block(edge_high, mask_high, 2, 7), block(edge_high, mask_high, 3, 7)
    here = lax.axis_index("gx")

    @pl.when(here < targets - 1)
    def _():
        def put(slot, value):
            rows_ref[here + 1, base + slot : base + slot + 1, :] = value

        for k in range(3):
            put(k, diag_high[4 * k, 7:8, :])
        for k, value in enumerate(block(edge_high, mask_high, 0, 7)):
            put(3 + k, value)
        corners = jnp.zeros((1, LANES), F32)
        lane = iota((1, LANES), 1)
        for k in range(9):
            corners = jnp.where(lane == k, up_y[k][:, LANES - 1 :], corners)
            corners = jnp.where(lane == 9 + k, low_y[k][:, :1], corners)
        put(12, corners)

    @pl.when(here > 0)
    def _():
        def put(slot, value):
            rows_ref[here - 1, base + slot : base + slot + 1, :] = value

        for k in range(3):
            put(k, diag_low[4 * k, 0:1, :])
        present = mask_low[0:1, :].astype(F32)
        for k in range(9):
            put(3 + k, edge_low[k, 0:1, :] * present)

    leaving[1].start()
    later = [diag_high[k, 7:8, :] for k in range(9) if k % 4]
    later += up_y + low_y + block(edge_high, mask_high, 0, 6)
    later += [diag_high[4 * k, 6:7, :] for k in range(3)]
    for k, value in enumerate(later):
        strip_ref[k : k + 1, :] = value
    strip_ref[len(later) :, :] = jnp.zeros((STRIP - len(later), LANES), F32)
    for copy in leaving:
        copy.wait()


def stretched(row, count):
    tile = jnp.broadcast_to(row, (16, row.shape[1])).astype(BF16)
    return jnp.concatenate([tile] * (count // 16), axis=0)


def ratio(value, scale):
    return jnp.where(scale > 0.0, value / jnp.where(scale > 0.0, scale, 1.0), 0.0)


def field_kernel(
    rows_ref, diag_ref, edge_ref, mask_ref,
    field_ref, part_ref, halo_ref, inner_ref, outer_ref, load_ref,
):
    senders = rows_ref.shape[0]
    groups = (rows_ref.shape[1] - NEAR) // 4
    cells_x = field_ref.shape[1]
    half = (cells_x + 2 * PAD) // 2
    own = cells_x // 2

    load_ref[...] = jnp.zeros_like(load_ref)
    here = lax.axis_index("gx")

    size = load_ref.shape[0]
    line = iota((size, LANES), 0)
    block = sum(jnp.where(line >= half * k, 1, 0) for k in range(1, 6))
    at_row = jnp.where(line < 6 * half, line - half * block, -5).astype(F32).astype(BF16)
    at_column = float_iota((2 * LANES, LANES), 0).astype(BF16)
    in_tile = float_iota((16, LANES), 0).astype(BF16)
    zero, one = jnp.zeros((), BF16), jnp.ones((), BF16)

    def operands(sender):
        index = rows_ref[sender, 3 * groups : 4 * groups, :]
        split = float(half * LANES)
        index, shift = (
            jnp.where(index >= split, index - split, index),
            jnp.where(index >= split, float(LANES), 0.0),
        )
        place = jnp.floor(index * (1.0 / LANES))
        column = index - place * float(LANES) + shift
        parts = [
            two_parts(rows_ref[sender, c * groups : (c + 1) * groups, :]) for c in range(3)
        ]
        lefts, rights = [], []
        for group in range(groups):
            line = slice(group, group + 1)
            values = [
                stretched(parts[c][which][line], 16) for which in range(2) for c in range(3)
            ]
            tiles = []
            for first in range(0, size, 16):
                low, high = first // half, min((first + 15) // half, 5)
                tiles.append(
                    values[low]
                    if low == high
                    else jnp.where(
                        in_tile < float(half * high - first), values[low], values[high]
                    )
                )
            match = at_row == stretched(place[line], size)
            lefts.append(jnp.where(match, jnp.concatenate(tiles, axis=0), zero))
            rights.append(
                jnp.where(at_column == stretched(column[line], 2 * LANES), one, zero)
            )
        return lefts, rights

    together = math.gcd(senders, 4)

    def add_rows(step, carry):
        lefts, rights = [], []
        for k in range(together):
            left, right = operands(step * together + k)
            lefts += left
            rights += right
        load_ref[...] += lax.dot_general(
            jnp.concatenate(lefts, axis=1),
            jnp.concatenate(rights, axis=1),
            (((1,), (1,)), ((), ())),
            preferred_element_type=F32,
        )
        return carry

    steps = senders // together
    lax.fori_loop(0, steps, add_rows, 0, unroll=min(steps, 2))

    def load_rows(comp, first, last, second_half):
        lanes = slice(LANES, 2 * LANES) if second_half else slice(0, LANES)
        return (
            load_ref[comp * half + first : comp * half + last, lanes]
            + load_ref[(3 + comp) * half + first : (3 + comp) * half + last, lanes]
        )

    field = []
    for comp in range(3):
        load = jnp.concatenate(
            [load_rows(comp, PAD, half, False), load_rows(comp, 0, half - PAD, True)], axis=0
        )
        field.append(load / diag_ref[4 * comp])
        field_ref[comp] = field[comp]
    beyond = half - PAD
    near_before = [load_rows(c, PAD - 1, PAD, False) for c in range(3)]
    far_before = [load_rows(c, PAD - 2, PAD - 1, False) for c in range(3)]
    near_after = [load_rows(c, beyond, beyond + 1, True) for c in range(3)]

    up_x = masked_product(edge_ref, mask_ref, 0, field)
    low_x = masked_product(edge_ref, mask_ref, 1, field)
    base = 4 * groups

    def neighbour(sender, load):
        def entry(k):
            return rows_ref[sender, base + k : base + k + 1, :]

        scale, toward = [entry(k) for k in range(3)], [entry(3 + k) for k in range(9)]
        beside = [ratio(load[c], scale[c]) for c in range(3)]
        return scale, toward, beside, product(lambda k: toward[k], beside)

    lower = jnp.maximum(here - 1, 0)
    before = neighbour(lower, near_before)
    after = neighbour(jnp.minimum(here + 1, senders - 1), near_after)
    rows = before[2] + [ratio(1.0, scale) for scale in before[0]]
    rows += [p[:1] for p in low_x] + before[1] + far_before
    for k, value in enumerate(rows):
        halo_ref[k : k + 1, :] = value
    halo_ref[len(rows) :, :] = jnp.zeros((halo_ref.shape[0] - len(rows), LANES), F32)
    lane_row = iota((1, LANES), 1)
    ends = jnp.zeros((1, LANES), F32)
    for i in range(3):
        for a in range(3):
            ends = jnp.where(lane_row == 3 * i + a, before[2][i][:, LANES - 1 :], ends)
            ends = jnp.where(lane_row == 9 + 3 * i + a, before[2][i][:, :1], ends)
    ends = ends * rows_ref[lower, base + 12 : base + 13, :]
    ends = ends + pltpu.roll(ends, LANES - 3, 1) + pltpu.roll(ends, LANES - 6, 1)

    total = off_diagonal(lambda k: diag_ref[k], field)
    total = [total[c] + rows_moved(up_x[c], before[3][c], 1) for c in range(3)]
    total = [total[c] + rows_moved(low_x[c], after[3][c], -1) for c in range(3)]
    up_y = masked_product(edge_ref, mask_ref, 2, field)
    low_y = masked_product(edge_ref, mask_ref, 3, field)
    total = [
        total[c] + lanes_moved(up_y[c], 0.0, 1) + lanes_moved(low_y[c], 0.0, -1)
        for c in range(3)
    ]
    inverse = [1.0 / diag_ref[4 * c] for c in range(3)]
    part = [total[c] * inverse[c] for c in range(3)]
    for comp in range(3):
        part_ref[comp] = part[comp]
    def columns(lane, along_y, end):
        packed = jnp.zeros((cells_x, LANES), F32)
        at = iota((cells_x, LANES), 1)
        for slot, fields in enumerate((field, along_y, part, inverse)):
            for comp in range(3):
                column = fields[comp][:, lane : lane + 1]
                packed = jnp.where(at == 3 * slot + comp, column, packed)
        rest = jnp.zeros((LANES - cells_x, LANES), F32)
        turned = jnp.concatenate([packed, rest], axis=0).T[:16]
        at = iota((16, LANES), 1)
        line = iota((16, LANES), 0)
        for comp in range(3):
            turned = jnp.where(
                (line == 3 + comp) & (at == cells_x),
                ends[:, end + comp : end + comp + 1],
                turned,
            )
        return turned

    inner_ref[...], outer_ref[...] = by_parity(
        columns(0, low_y, 9), columns(LANES - 1, up_y, 0)
    )


def bernstein(coord):
    other = 1.0 - coord
    return [
        other * other * other,
        3.0 * coord * other * other,
        3.0 * coord * coord * other,
        coord * coord * coord,
    ]


def weight_table(u, v, w):
    first, second, third = bernstein(u), bernstein(v), bernstein(w)
    line = iota((8, u.shape[1]), 0)
    inner = line & 3
    along = jnp.where(
        inner == 0,
        third[0],
        jnp.where(inner == 1, third[1], jnp.where(inner == 2, third[2], third[3])),
    )
    pair = jnp.concatenate(
        [
            jnp.where(line < 4, second[0], second[1]) * along,
            jnp.where(line < 4, second[2], second[3]) * along,
        ],
        axis=0,
    )
    return jnp.concatenate([pair * first[i] for i in range(4)], axis=0)


def tile_rows(terms):
    first_half = iota((4, LANES), 1) < LANES // 2
    rows = []
    for term in terms:
        term = term[:8] + term[8:]
        term = term + pltpu.roll(term, LANES // 2, 1)
        rows.append(jnp.where(first_half, term[:4], term[4:]))
    return jnp.concatenate(two_parts(jnp.concatenate(rows, axis=0)), axis=0).astype(BF16)


def box_matrix(tile_row, boxes):
    tiles = tile_row.shape[1]
    shape = (4 * boxes, 8 * tiles)
    column = iota((1, shape[1]), 1)
    box = jnp.zeros((1, shape[1]), jnp.int32)
    for tile in range(tiles):
        mine = lax.rem(lax.shift_right_logical(column, 2), tiles) == tile
        box = jnp.where(mine, tile_row[:, tile : tile + 1], box)
    target = 4 * box + (column & 3)
    return jnp.where(iota(shape, 0) == target, 1.0, 0.0).astype(BF16)


def by_parity(low, high):
    odd = lax.rem(lax.axis_index("gy"), 2) == 1
    return jnp.where(odd, high, low), jnp.where(odd, low, high)


def quotient_before(halo_ref, strip_ref, before_ref):
    def rows(ref, first, count):
        return [ref[first + k : first + k + 1, :] for k in range(count)]

    beside, inverse, entering = rows(halo_ref, 0, 3), rows(halo_ref, 3, 3), rows(halo_ref, 6, 3)
    far_load, within = rows(halo_ref, 18, 3), rows(strip_ref, 0, 6)
    far_scale = rows(strip_ref, 33, 3)
    far = [ratio(far_load[c], far_scale[c]) for c in range(3)]
    whole_block = [None, *within[:3], None, *within[3:], None]
    total = off_diagonal(lambda k: whole_block[k], beside)
    from_far = product(lambda k: strip_ref[24 + k : 25 + k, :], far)
    up_y = product(lambda k: strip_ref[6 + k : 7 + k, :], beside)
    low_y = product(lambda k: strip_ref[15 + k : 16 + k, :], beside)
    for c in range(3):
        before_ref[c : c + 1, :] = inverse[c] * (
            total[c]
            + from_far[c]
            + entering[c]
            + lanes_moved(up_y[c], 0.0, 1)
            + lanes_moved(low_y[c], 0.0, -1)
        )
    before_ref[3:, :] = jnp.zeros((before_ref.shape[0] - 3, LANES), F32)


def box_kernel(
    tile_ref, field_ref, part_ref, node_ref, param_ref, halo_ref, strip_ref,
    box_ref, adjoint_ref, before_ref, matrix_ref, weights_ref, columns_ref, *, tile_points,
):
    cells_x = field_ref.shape[1]
    own = cells_x // 2
    quotient_before(halo_ref, strip_ref, before_ref)
    field = [field_ref[c] for c in range(3)]
    part = [part_ref[c] for c in range(3)]
    order = [field[0], part[0], field[2], field[1], part[1], part[2]]
    folded = [two_parts(jnp.concatenate([f[:own], f[own:]], axis=1)) for f in order]
    table = jnp.concatenate(
        [folded[f][which] for which in range(2) for f in range(6)], axis=0
    ).astype(BF16)
    points = param_ref.shape[1]
    pieces = CHUNK // LANES
    zero, one = jnp.zeros((), BF16), jnp.ones((), BF16)
    at_node = float_iota((2 * LANES, CHUNK), 0).astype(BF16)
    nothing = jnp.zeros((1, CHUNK), F32)
    highs, lows = [], []
    for chunk in range(points // CHUNK):
        node = jnp.concatenate(
            [node_ref[chunk * pieces + k : chunk * pieces + k + 1, :] for k in range(pieces)],
            axis=1,
        )
        row = lax.shift_right_logical(node, 7)
        column = node & (LANES - 1)
        lanes = slice(chunk * CHUNK, (chunk + 1) * CHUNK)
        at_edge = jnp.where(
            column == 0, row, jnp.where(column == LANES - 1, row + cells_x, -1)
        ).astype(F32)
        columns_ref[:, lanes] = jnp.where(
            at_node[: 2 * cells_x] == stretched(at_edge, 2 * cells_x), one, zero
        )
        place = column + jnp.where(row >= own, LANES, 0)
        row = jnp.where(row >= own, row - own, row)
        pick = jnp.where(at_node == stretched(place.astype(F32), 2 * LANES), one, zero)
        read = jnp.dot(table, pick, preferred_element_type=F32)
        read = read[: 6 * own] + read[6 * own :]
        here = iota((own, CHUNK), 0) == row
        values = [
            jnp.sum(
                jnp.where(here, read[f * own : (f + 1) * own], 0.0), axis=0, keepdims=True
            )
            for f in range(6)
        ]
        high, low = two_parts(
            jnp.concatenate(values[:3] + [nothing] + values[3:] + [nothing], axis=0)
        )
        highs.append(high)
        lows.append(low)
        weights = two_parts(
            weight_table(param_ref[0:1, lanes], param_ref[1:2, lanes], param_ref[2:3, lanes])
        )
        for k in range(CHUNK // tile_points):
            tile = slice(k * tile_points, (k + 1) * tile_points)
            sides = jnp.concatenate([weights[0][:, tile], weights[1][:, tile]], axis=0)
            weights_ref[chunk * (CHUNK // tile_points) + k] = sides.T.astype(BF16)
    both = jnp.concatenate(
        [jnp.concatenate(highs, axis=1), jnp.concatenate(lows, axis=1)], axis=0
    ).astype(BF16)
    matrix_ref[...] = box_matrix(tile_ref[...], matrix_ref.shape[0] // 4)
    tiles = tile_ref.shape[1]
    terms = [
        jnp.dot(
            both[:, tile * tile_points : (tile + 1) * tile_points],
            weights_ref[tile],
            preferred_element_type=F32,
        )
        for tile in range(tiles)
    ]
    box_ref[...] = jnp.dot(matrix_ref[...], tile_rows(terms), preferred_element_type=F32)
    low_half = iota((2 * cells_x, LANES), 1) < LANES // 2
    for tile in range(tiles):
        lanes = slice(tile * tile_points, (tile + 1) * tile_points)
        term = jnp.dot(
            columns_ref[:, lanes], weights_ref[tile], preferred_element_type=F32
        )
        high, low = two_parts(term + pltpu.roll(term, LANES // 2, 1))
        adjoint_ref[:, tile * LANES : (tile + 1) * LANES] = jnp.where(
            low_half, high, low
        ).astype(BF16)


def sums_kernel(
    from_inner_ref, from_outer_ref, inner_ref, outer_ref, field_ref, part_ref, halo_ref,
    diag_ref, edge_ref, mask_ref, box_ref, adjoint_ref, before_ref, matrix_ref,
    quotient_ref, out_ref,
):
    cells_x = field_ref.shape[1]
    targets = out_ref.shape[0]

    from_low, from_high = by_parity(from_inner_ref[...], from_outer_ref[...])
    first, last = by_parity(inner_ref[...], outer_ref[...])

    lane_row = iota((1, LANES), 1)
    shares, edges = [], []
    for arrived, own in ((from_low, first), (from_high, last)):
        def row(source, slot, c):
            return source[3 * slot + c : 3 * slot + c + 1]

        shares.append([row(arrived, 1, c) * row(own, 3, c) for c in range(3)])
        edges.append(
            [row(arrived, 2, c) + row(arrived, 3, c) * row(own, 1, c) for c in range(3)]
        )

    def turned(columns, share, edge):
        kept = [
            jnp.where(lane_row < cells_x, share[c], columns[3 + c : 4 + c]) for c in range(3)
        ]
        rest = jnp.zeros((LANES - 9, LANES), F32)
        return jnp.concatenate([columns[:3], *kept, *edge, rest], axis=0).T

    low = turned(from_low, shares[0], edges[0])
    high = turned(from_high, shares[1], edges[1])
    lane = iota((cells_x, LANES), 1)

    def column(source, slot, comp):
        return source[:cells_x, 3 * slot + comp : 3 * slot + comp + 1]

    field = [field_ref[c] for c in range(3)]
    scale = [diag_ref[4 * c] for c in range(3)]
    quotient, low_edge, high_edge = [], [], []
    for c in range(3):
        entering = jnp.where(
            lane == 0,
            column(low, 1, c),
            jnp.where(lane == LANES - 1, column(high, 1, c), 0.0),
        )
        quotient.append(part_ref[c] + entering)
        low_edge.append(column(low, 2, c))
        high_edge.append(column(high, 2, c))
    for c in range(3):
        quotient_ref[c] = quotient[c]
    before, before_quotient = [], []
    for c in range(3):
        entering = jnp.where(
            lane_row == 0,
            low[cells_x : cells_x + 1, 3 + c : 4 + c],
            jnp.where(lane_row == LANES - 1, high[cells_x : cells_x + 1, 3 + c : 4 + c], 0.0),
        )
        before.append(halo_ref[c : c + 1, :])
        before_quotient.append(
            before_ref[c : c + 1, :] + entering * halo_ref[3 + c : 4 + c, :]
        )

    first_sum = sum(field[c] * scale[c] * field[c] for c in range(3))
    second_sum = sum(field[c] * scale[c] * quotient[c] for c in range(3))
    third_sum = sum(quotient[c] * scale[c] * quotient[c] for c in range(3))
    within = off_diagonal(lambda k: diag_ref[k], quotient)
    fourth_sum = sum(within[c] * field[c] for c in range(3))
    fifth_sum = sum(within[c] * quotient[c] for c in range(3))
    at_row = iota((cells_x, LANES), 0)
    moves = (
        (pltpu.roll, 1, 0, at_row == 0),
        (pltpu.roll, cells_x - 1, 0, at_row == cells_x - 1),
        (pltpu.roll, 1, 1, lane == 0),
        (pltpu.roll, LANES - 1, 1, lane == LANES - 1),
    )
    extra = [0.0, 0.0]
    sides = [0.0, 0.0]
    for direction, (roll, step, dim, edge) in enumerate(moves):
        moving = masked_product(edge_ref, mask_ref, direction, quotient)
        for c in range(3):
            moved = jnp.where(edge, 0.0, roll(moving[c], step, dim))
            fourth_sum = fourth_sum + moved * field[c]
            fifth_sum = fifth_sum + moved * quotient[c]
            if direction == 1:
                extra[0] += moving[c][:1] * before[c]
                extra[1] += moving[c][:1] * before_quotient[c]
            elif direction == 2:
                sides[0] += moving[c][:, LANES - 1 :] * column(high, 0, c)
                sides[1] += moving[c][:, LANES - 1 :] * high_edge[c]
            elif direction == 3:
                sides[0] += moving[c][:, :1] * column(low, 0, c)
                sides[1] += moving[c][:, :1] * low_edge[c]
    incoming = product(lambda k: halo_ref[9 + k : 10 + k, :], before_quotient)
    extra[0] += sum(incoming[c] * field[c][:1] for c in range(3))
    extra[1] += sum(incoming[c] * quotient[c][:1] for c in range(3))
    fourth_sum = fourth_sum + jnp.where(lane == 0, sides[0], 0.0)
    fifth_sum = fifth_sum + jnp.where(lane == 0, sides[1], 0.0)
    extra = [0.0, 0.0, 0.0, extra[0], extra[1]]
    sums = jnp.zeros((1, LANES), F32)
    for k, value in enumerate((first_sum, second_sum, third_sum, fourth_sum, fifth_sum)):
        line = jnp.sum(value, axis=0, keepdims=True) + extra[k]
        sums = jnp.where(lane_row == k, jnp.sum(line, axis=1, keepdims=True), sums)

    added = [
        jnp.where(lane_row < cells_x, shares[0][c], pltpu.roll(shares[1][c], cells_x, 1))
        for c in range(3)
    ]
    none = jnp.zeros((1, LANES), F32)
    added = jnp.concatenate(
        [none, added[0], none, none, none, added[1], added[2], none], axis=0
    )
    added = jnp.concatenate(two_parts(added), axis=0).astype(BF16)
    terms = jnp.dot(added, adjoint_ref[...], preferred_element_type=F32)
    terms = [
        terms[:, first : first + LANES] for first in range(0, terms.shape[1], LANES)
    ]
    total = box_ref[...] + jnp.dot(
        matrix_ref[...], tile_rows(terms), preferred_element_type=F32
    )
    total = jnp.where((iota(total.shape, 0) & 3) == 3, sums, total)
    for box in range(targets):
        out_ref[box] = total[4 * box : 4 * box + 4]


def result_kernel(got_ref, field_ref, quotient_ref, solution_ref, gradient_ref):
    total = jnp.sum(got_ref[...], axis=0)
    rho, a, b, t, u = [total[3:4, k : k + 1] for k in range(5)]
    norm = rho + a
    by_rho, by_norm = 1.0 / rho, 1.0 / norm
    ratio, step = a * by_rho, rho * by_norm
    rest = jnp.maximum(b - a * ratio, 0.0)
    beta = step * step * rest * by_rho
    rest_image = (b + u) - ratio * (a + b + a + t) + ratio * ratio * norm
    cross = (a + t) - ratio * norm
    curve = step * step * rest_image - step * beta * (rest + cross) + beta * beta * norm
    second = jnp.where(
        curve > 0.0, step * step * rest / jnp.where(curve > 0.0, curve, 1.0), 0.0
    )
    second = jnp.minimum(second, 16.0)
    of_field = step + second * (beta + step * ratio)
    of_quotient = -(step * second)
    for c in range(3):
        solution_ref[c] = of_field * field_ref[c] + of_quotient * quotient_ref[c]
    gradient_ref[:, :LANES] = of_field * total[0:1] + of_quotient * total[1:2]
    gradient_ref[:, LANES:] = (
        of_field * total[2:3, : LANES // 2] + of_quotient * total[2:3, LANES // 2 :]
    )


def per_device(
    diag_blocks, edge_blocks, edge_mask, src_values, src_owner, src_node, src_count,
    surf_node, surf_param, tile_box,
):
    cells_x, cells_y = diag_blocks.shape[1:]
    width_gx, width_gy = lax.axis_size("gx"), lax.axis_size("gy")
    devices = width_gx * width_gy
    groups = src_node.shape[0] // LANES
    whole = functools.partial(jax.ShapeDtypeStruct, dtype=F32)

    cells = 4 * groups + NEAR

    def kept(array):
        return pltpu.with_memory_space_constraint(array, pltpu.HBM)

    i32 = jnp.int32
    rows, strip = pl.pallas_call(
        pack_kernel,
        in_specs=[SMEM] + [HBM] * 6,
        out_specs=[HBM, VMEM],
        out_shape=[
            pltpu.HBM((width_gx, cells, LANES), F32), pltpu.VMEM((STRIP, LANES), F32)
        ],
        scratch_shapes=[
            pltpu.VMEM(src_values.shape, F32),
            pltpu.VMEM((groups, LANES), i32),
            pltpu.VMEM((groups, LANES), i32),
            pltpu.VMEM((9, 8, cells_y), F32),
            pltpu.VMEM((9, 8, cells_y), F32),
            pltpu.VMEM((9, 8, cells_y), F32),
            pltpu.VMEM((4, 9, 8, cells_y), F32),
            pltpu.VMEM((8, cells_y), i32),
            pltpu.VMEM((4, 8, cells_y), i32),
            pltpu.VMEM((width_gx, cells, LANES), F32),
            pltpu.SemaphoreType.DMA((9,)),
            pltpu.SemaphoreType.DMA((2,)),
        ],
        compiler_params=PARAMS,
        name="pack_rows_and_edges",
    )(
        src_count, kept(src_values),
        kept(src_owner.reshape(groups, LANES)), kept(src_node.reshape(groups, LANES)),
        kept(diag_blocks), kept(edge_blocks), kept(edge_mask),
    )
    rows = lax.all_to_all(rows, "gx", split_axis=0, concat_axis=0, tiled=True)
    strip = lax.ppermute(strip, "gx", [(i, i + 1) for i in range(width_gx - 1)])

    nodes = (3, cells_x, cells_y)
    size = -(-3 * (cells_x + 2 * PAD) // 16) * 16
    field, part, halo, inner, outer = pl.pallas_call(
        field_kernel,
        in_specs=[VMEM] * 4,
        out_specs=[VMEM] * 5,
        out_shape=[
            whole(nodes), whole(nodes), whole((24, cells_y)), whole((16, LANES)),
            whole((16, LANES)),
        ],
        scratch_shapes=[pltpu.VMEM((size, 2 * LANES), F32)],
        compiler_params=PARAMS,
        name="load_and_first_product",
    )(rows, diag_blocks, edge_blocks, edge_mask)
    def swapped(columns, first):
        low = range(first, width_gy - 1, 2)
        pairs = [(i, i + 1) for i in low] + [(i + 1, i) for i in low]
        return lax.ppermute(columns, "gy", pairs)

    from_inner, from_outer = swapped(inner, 1), swapped(outer, 0)
    points, tiles = surf_node.shape[0], tile_box.shape[0]
    box_part, adjoint, before, matrix = pl.pallas_call(
        functools.partial(box_kernel, tile_points=points // tiles),
        in_specs=[VMEM] * 7,
        out_specs=[VMEM] * 4,
        out_shape=[
            whole((4 * devices, LANES)),
            jax.ShapeDtypeStruct((2 * cells_x, tiles * LANES), BF16),
            whole((8, LANES)),
            jax.ShapeDtypeStruct((4 * devices, 8 * tiles), BF16),
        ],
        scratch_shapes=[
            pltpu.VMEM((tiles, points // tiles, LANES), BF16),
            pltpu.VMEM((2 * cells_x, points), BF16),
        ],
        compiler_params=PARAMS,
        cost_estimate=pl.CostEstimate(
            flops=10**9, bytes_accessed=4 * 10**6, transcendentals=0
        ),
        name="box_parts",
    )(
        tile_box.reshape(1, tiles), field, part, surf_node.reshape(points // LANES, LANES),
        surf_param, halo, strip,
    )

    quotient, partial = pl.pallas_call(
        sums_kernel,
        in_specs=[VMEM] * 14,
        out_specs=[VMEM] * 2,
        out_shape=[whole(nodes), whole((devices, 4, LANES))],
        compiler_params=PARAMS,
        name="sums_and_halo_parts",
    )(
        from_inner, from_outer, inner, outer, field, part, halo, diag_blocks, edge_blocks, edge_mask,
        box_part, adjoint, before, matrix,
    )
    got = lax.all_to_all(partial, ("gx", "gy"), split_axis=0, concat_axis=0, tiled=True)
    return pl.pallas_call(
        result_kernel,
        in_specs=[VMEM] * 3,
        out_specs=[VMEM] * 2,
        out_shape=[whole(nodes), whole((1, 192))],
        compiler_params=PARAMS,
        name="steps_and_outputs",
    )(got, field, quotient)


def solution(mesh):
    return jax.shard_map(
        per_device,
        mesh=mesh,
        in_specs=(
            P(None, "gx", "gy"),
            P(None, None, "gx", "gy"),
            P(None, "gx", "gy"),
            P(None, ("gx", "gy")),
            P(("gx", "gy"), None),
            P(("gx", "gy")),
            P(("gx", "gy")),
            P(("gx", "gy")),
            P(None, ("gx", "gy")),
            P(("gx", "gy")),
        ),
        out_specs=(P(None, "gx", "gy"), P(("gx", "gy"), None)),
        check_vma=False,
    )
```

```python
import functools
import math

import jax
import jax.numpy as jnp
from jax import lax
from jax.experimental import pallas as pl
from jax.experimental.pallas import tpu as pltpu
from jax.sharding import PartitionSpec as P

F32 = jnp.float32
BF16 = jnp.bfloat16
PAD = 2
NOWHERE = -(1 << 20)
LANES = 128
NEAR = 16
STRIP = 40
CHUNK = 256
PARAMS = pltpu.CompilerParams(vmem_limit_bytes=24 * 1024 * 1024)

VMEM = pl.BlockSpec(memory_space=pltpu.VMEM)
SMEM = pl.BlockSpec(memory_space=pltpu.SMEM)
HBM = pl.BlockSpec(memory_space=pltpu.HBM)


def iota(shape, dim):
    return lax.broadcasted_iota(jnp.int32, shape, dim)


def float_iota(shape, dim):
    return iota(shape, dim).astype(F32)


def two_parts(value):
    high = value.astype(BF16).astype(F32)
    return high, value - high


def product(block, field):
    return [
        block(row) * field[0] + block(3 + row) * field[1] + block(6 + row) * field[2]
        for row in range(3)
    ]


def off_diagonal(block, field):
    return [
        sum(block(3 * i + row) * field[i] for i in range(3) if i != row) for row in range(3)
    ]


def masked_product(edge_ref, mask_ref, direction, field):
    mask = mask_ref[direction].astype(F32)
    return [mask * part for part in product(lambda k: edge_ref[direction, k], field)]


def rows_moved(field, edge_row, step):
    size = field.shape[0]
    at = iota(field.shape, 0)
    moved = pltpu.roll(field, step % size, 0)
    return jnp.where(at == (0 if step == 1 else size - 1), edge_row, moved)


def lanes_moved(field, edge_column, step):
    size = field.shape[1]
    at = iota(field.shape, 1)
    moved = pltpu.roll(field, step % size, 1)
    return jnp.where(at == (0 if step == 1 else size - 1), edge_column, moved)


def pack_kernel(
    count_ref, values_in, owner_in, node_in, diag_in, edge_in, mask_in, rows_out, strip_ref,
    values_ref, owner_ref, node_ref, diag_low, diag_high, edge_low, edge_high,
    mask_low, mask_high, rows_ref, arrived, left,
):
    targets = rows_ref.shape[0]
    groups = owner_ref.shape[0]
    cells_x = diag_in.shape[1]
    top = pl.ds(cells_x - 8, 8)
    copies = [
        pltpu.make_async_copy(source, target, arrived.at[k])
        for k, (source, target) in enumerate(
            (
                (owner_in, owner_ref),
                (node_in, node_ref),
                (values_in, values_ref),
                (diag_in.at[:, 0:8], diag_low),
                (diag_in.at[:, top], diag_high),
                (mask_in.at[1, 0:8], mask_low),
                (mask_in.at[:, top], mask_high),
                (edge_in.at[1, :, 0:8], edge_low),
                (edge_in.at[:, :, top], edge_high),
            )
        )
    ]
    for copy in copies:
        copy.start()
    base = 4 * groups
    for target in range(targets):
        rows_ref[target, base:, :] = jnp.zeros((NEAR, LANES), F32)
    for copy in copies[:2]:
        copy.wait()
    order = iota((groups, LANES), 0) * LANES + iota((groups, LANES), 1)
    node = node_ref[...]
    frame = cells_x + 2 * PAD
    row = owner_ref[...] * cells_x + lax.shift_right_logical(node, 7)
    row = jnp.where(order < count_ref[0], row, NOWHERE)
    column = node & (LANES - 1)
    for target in range(targets):
        line = row - (target * cells_x - PAD)
        inside = (line >= 0) & (line < frame)
        index = jnp.where(inside, line * LANES + column, -1)
        rows_ref[target, 3 * groups : 4 * groups, :] = index.astype(F32)

    copies[2].wait()
    for comp in range(3):
        value = jnp.concatenate(
            [
                values_ref[comp : comp + 1, group * LANES : (group + 1) * LANES]
                for group in range(groups)
            ],
            axis=0,
        )
        for target in range(targets):
            rows_ref[target, comp * groups : (comp + 1) * groups, :] = value
    near = pl.ds(4 * groups, NEAR)
    leaving = [
        pltpu.make_async_copy(rows_ref.at[:, part], rows_out.at[:, part], left.at[k])
        for k, part in enumerate((pl.ds(0, 4 * groups), near))
    ]
    leaving[0].start()
    for copy in copies[3:]:
        copy.wait()

    def block(edge, mask, direction, at):
        present = mask[direction, at : at + 1, :].astype(F32)
        return [edge[direction, k, at : at + 1, :] * present for k in range(9)]

    up_y, low_y = block(edge_high, mask_high, 2, 7), block(edge_high, mask_high, 3, 7)
    here = lax.axis_index("gx")

    @pl.when(here < targets - 1)
    def _():
        def put(slot, value):
            rows_ref[here + 1, base + slot : base + slot + 1, :] = value

        for k in range(3):
            put(k, diag_high[4 * k, 7:8, :])
        for k, value in enumerate(block(edge_high, mask_high, 0, 7)):
            put(3 + k, value)
        corners = jnp.zeros((1, LANES), F32)
        lane = iota((1, LANES), 1)
        for k in range(9):
            corners = jnp.where(lane == k, up_y[k][:, LANES - 1 :], corners)
            corners = jnp.where(lane == 9 + k, low_y[k][:, :1], corners)
        put(12, corners)

    @pl.when(here > 0)
    def _():
        def put(slot, value):
            rows_ref[here - 1, base + slot : base + slot + 1, :] = value

        for k in range(3):
            put(k, diag_low[4 * k, 0:1, :])
        present = mask_low[0:1, :].astype(F32)
        for k in range(9):
            put(3 + k, edge_low[k, 0:1, :] * present)

    leaving[1].start()
    later = [diag_high[k, 7:8, :] for k in range(9) if k % 4]
    later += up_y + low_y + block(edge_high, mask_high, 0, 6)
    later += [diag_high[4 * k, 6:7, :] for k in range(3)]
    for k, value in enumerate(later):
        strip_ref[k : k + 1, :] = value
    strip_ref[len(later) :, :] = jnp.zeros((STRIP - len(later), LANES), F32)
    for copy in leaving:
        copy.wait()


def stretched(row, count):
    tile = jnp.broadcast_to(row, (16, row.shape[1])).astype(BF16)
    return jnp.concatenate([tile] * (count // 16), axis=0)


def ratio(value, scale):
    return jnp.where(scale > 0.0, value / jnp.where(scale > 0.0, scale, 1.0), 0.0)


UP_X, LOW_X, INWARD, OUTWARD, WITHIN, INVERSE = 0, 3, 6, 9, 12, 15


def edge_kernel(diag_ref, edge_ref, mask_ref, inverse_ref, columns_ref):
    cells_x = diag_ref.shape[1]
    at = iota((cells_x, LANES), 1)
    sides = [jnp.zeros((cells_x, LANES), F32) for _ in range(2)]

    def put(kind, i, a, first, first_lane, last, last_lane):
        slot = 8 * (kind + i) + a
        for side, (field, lane) in enumerate(((first, first_lane), (last, last_lane))):
            sides[side] = jnp.where(at == slot, field[:, lane : lane + 1], sides[side])

    inverse = [1.0 / diag_ref[4 * c] for c in range(3)]
    end = LANES - 1
    masks = [mask_ref[direction].astype(F32) for direction in range(4)]
    for i in range(3):
        inverse_ref[i] = inverse[i]
        put(INVERSE, 0, i, inverse[i], 0, inverse[i], end)
        for a in range(3):
            up_x, low_x, up_y, low_y = (
                edge_ref[direction, 3 * i + a] * masks[direction] for direction in range(4)
            )
            put(UP_X, i, a, up_x, 0, up_x, end)
            put(LOW_X, i, a, low_x, 0, low_x, end)
            put(INWARD, i, a, low_y, 1, up_y, end - 1)
            put(OUTWARD, i, a, low_y, 0, up_y, end)
            if a != i:
                put(WITHIN, i, a, diag_ref[3 * i + a], 0, diag_ref[3 * i + a], end)
    columns_ref[...] = jnp.concatenate(sides, axis=0).T


def field_kernel(
    rows_ref, inverse_ref, columns_ref,
    field_ref, halo_ref, inner_ref, outer_ref, load_ref,
):
    senders = rows_ref.shape[0]
    groups = (rows_ref.shape[1] - NEAR) // 4
    cells_x = field_ref.shape[1]
    half = (cells_x + 2 * PAD) // 2
    own = cells_x // 2

    load_ref[...] = jnp.zeros_like(load_ref)
    here = lax.axis_index("gx")

    size = load_ref.shape[0]
    line = iota((size, LANES), 0)
    block = sum(jnp.where(line >= half * k, 1, 0) for k in range(1, 6))
    at_row = jnp.where(line < 6 * half, line - half * block, -5).astype(F32).astype(BF16)
    at_column = float_iota((2 * LANES, LANES), 0).astype(BF16)
    in_tile = float_iota((16, LANES), 0).astype(BF16)
    zero, one = jnp.zeros((), BF16), jnp.ones((), BF16)

    def operands(sender):
        index = rows_ref[sender, 3 * groups : 4 * groups, :]
        split = float(half * LANES)
        index, shift = (
            jnp.where(index >= split, index - split, index),
            jnp.where(index >= split, float(LANES), 0.0),
        )
        place = jnp.floor(index * (1.0 / LANES))
        column = index - place * float(LANES) + shift
        parts = [
            two_parts(rows_ref[sender, c * groups : (c + 1) * groups, :]) for c in range(3)
        ]
        lefts, rights = [], []
        for group in range(groups):
            line = slice(group, group + 1)
            values = [
                stretched(parts[c][which][line], 16) for which in range(2) for c in range(3)
            ]
            tiles = []
            for first in range(0, size, 16):
                low, high = first // half, min((first + 15) // half, 5)
                tiles.append(
                    values[low]
                    if low == high
                    else jnp.where(
                        in_tile < float(half * high - first), values[low], values[high]
                    )
                )
            match = at_row == stretched(place[line], size)
            lefts.append(jnp.where(match, jnp.concatenate(tiles, axis=0), zero))
            rights.append(
                jnp.where(at_column == stretched(column[line], 2 * LANES), one, zero)
            )
        return lefts, rights

    together = math.gcd(senders, 4)

    def add_rows(step, carry):
        lefts, rights = [], []
        for k in range(together):
            left, right = operands(step * together + k)
            lefts += left
            rights += right
        load_ref[...] += lax.dot_general(
            jnp.concatenate(lefts, axis=1),
            jnp.concatenate(rights, axis=1),
            (((1,), (1,)), ((), ())),
            preferred_element_type=F32,
        )
        return carry

    steps = senders // together
    lax.fori_loop(0, steps, add_rows, 0, unroll=min(steps, 2))

    def load_rows(comp, first, last, second_half):
        lanes = slice(LANES, 2 * LANES) if second_half else slice(0, LANES)
        return (
            load_ref[comp * half + first : comp * half + last, lanes]
            + load_ref[(3 + comp) * half + first : (3 + comp) * half + last, lanes]
        )

    field = []
    for comp in range(3):
        load = jnp.concatenate(
            [load_rows(comp, PAD, half, False), load_rows(comp, 0, half - PAD, True)], axis=0
        )
        field.append(load * inverse_ref[comp])
        field_ref[comp] = field[comp]
    beyond = half - PAD
    near_before = [load_rows(c, PAD - 1, PAD, False) for c in range(3)]
    far_before = [load_rows(c, PAD - 2, PAD - 1, False) for c in range(3)]
    near_after = [load_rows(c, beyond, beyond + 1, True) for c in range(3)]

    base = 4 * groups

    def neighbour(sender, load):
        def entry(k):
            return rows_ref[sender, base + k : base + k + 1, :]

        inverse = [ratio(1.0, entry(k)) for k in range(3)]
        toward = [entry(3 + k) for k in range(9)]
        beside = [load[c] * inverse[c] for c in range(3)]
        return inverse, toward, beside, product(lambda k: toward[k], beside)

    lower = jnp.maximum(here - 1, 0)
    before = neighbour(lower, near_before)
    after = neighbour(jnp.minimum(here + 1, senders - 1), near_after)
    rows = before[2] + before[0] + before[3] + before[1] + far_before + after[3]
    for k, value in enumerate(rows):
        halo_ref[k : k + 1, :] = value
    lane_row = iota((1, LANES), 1)
    ends = jnp.zeros((1, LANES), F32)
    for i in range(3):
        for a in range(3):
            ends = jnp.where(lane_row == 3 * i + a, before[2][i][:, LANES - 1 :], ends)
            ends = jnp.where(lane_row == 9 + 3 * i + a, before[2][i][:, :1], ends)
    ends = ends * rows_ref[lower, base + 12 : base + 13, :]
    ends = ends + pltpu.roll(ends, LANES - 3, 1) + pltpu.roll(ends, LANES - 6, 1)

    at = iota((cells_x, LANES), 1)
    sides = []
    for edge, inside in ((0, 1), (LANES - 1, LANES - 2)):
        packed = jnp.zeros((cells_x, LANES), F32)
        for comp in range(3):
            packed = jnp.where(at == comp, field[comp][:, edge : edge + 1], packed)
            packed = jnp.where(at == 8 + comp, field[comp][:, inside : inside + 1], packed)
        sides.append(packed)
    turned = jnp.concatenate(sides, axis=0).T

    def column_product(kind, first):
        return sum(
            columns_ref[8 * (kind + i) : 8 * (kind + i) + 8, :] * turned[first + i : first + i + 1]
            for i in range(3)
        )

    def eight(rows):
        return jnp.concatenate(rows + [jnp.zeros((8 - len(rows), LANES), F32)], axis=0)

    lane = iota((8, LANES), 1)
    from_before, from_after = eight(before[3]), eight(after[3])
    from_before = jnp.where(lane == 0, from_before, pltpu.roll(from_before, cells_x + 1, 1))
    from_after = jnp.where(
        lane == LANES - 1, from_after, pltpu.roll(from_after, cells_x - 1, 1)
    )
    row = lane & (cells_x - 1)
    upward = pltpu.roll(column_product(UP_X, 0), 1, 1)
    downward = pltpu.roll(column_product(LOW_X, 0), LANES - 1, 1)
    total = (
        column_product(WITHIN, 0)
        + jnp.where(row == 0, from_before, upward)
        + jnp.where(row == cells_x - 1, from_after, downward)
        + column_product(INWARD, 8)
    )
    inverse = columns_ref[8 * INVERSE : 8 * INVERSE + 8, :]
    along_y, part = column_product(OUTWARD, 0), total * inverse
    stacked = jnp.concatenate(
        [turned[:3], along_y[:3], part[:3], inverse[:3], jnp.zeros((4, LANES), F32)], axis=0
    )

    def message(columns, end):
        at = iota((16, LANES), 1)
        line = iota((16, LANES), 0)
        columns = jnp.where(at < cells_x, columns, 0.0)
        for comp in range(3):
            columns = jnp.where(
                (line == 3 + comp) & (at == cells_x),
                ends[:, end + comp : end + comp + 1],
                columns,
            )
        return columns

    inner_ref[...], outer_ref[...] = by_parity(
        message(stacked, 9), message(pltpu.roll(stacked, cells_x, 1), 0)
    )


def bernstein(coord):
    other = 1.0 - coord
    return [
        other * other * other,
        3.0 * coord * other * other,
        3.0 * coord * coord * other,
        coord * coord * coord,
    ]


def weight_table(u, v, w):
    first, second, third = bernstein(u), bernstein(v), bernstein(w)
    line = iota((8, u.shape[1]), 0)
    inner = line & 3
    along = jnp.where(
        inner == 0,
        third[0],
        jnp.where(inner == 1, third[1], jnp.where(inner == 2, third[2], third[3])),
    )
    pair = jnp.concatenate(
        [
            jnp.where(line < 4, second[0], second[1]) * along,
            jnp.where(line < 4, second[2], second[3]) * along,
        ],
        axis=0,
    )
    return jnp.concatenate([pair * first[i] for i in range(4)], axis=0)


def tile_rows(terms):
    first_half = iota((4, LANES), 1) < LANES // 2
    rows = []
    for term in terms:
        term = term[:8] + term[8:]
        term = term + pltpu.roll(term, LANES // 2, 1)
        rows.append(jnp.where(first_half, term[:4], term[4:]))
    return jnp.concatenate(two_parts(jnp.concatenate(rows, axis=0)), axis=0).astype(BF16)


def box_matrix(tile_row, boxes):
    tiles = tile_row.shape[1]
    shape = (4 * boxes, 8 * tiles)
    column = iota((1, shape[1]), 1)
    box = jnp.zeros((1, shape[1]), jnp.int32)
    for tile in range(tiles):
        mine = lax.rem(lax.shift_right_logical(column, 2), tiles) == tile
        box = jnp.where(mine, tile_row[:, tile : tile + 1], box)
    target = 4 * box + (column & 3)
    return jnp.where(iota(shape, 0) == target, 1.0, 0.0).astype(BF16)


def by_parity(low, high):
    odd = lax.rem(lax.axis_index("gy"), 2) == 1
    return jnp.where(odd, high, low), jnp.where(odd, low, high)


def quotient_before(halo_ref, strip_ref, before_ref, entering):
    def rows(ref, first, count):
        return [ref[first + k : first + k + 1, :] for k in range(count)]

    beside, inverse = rows(halo_ref, 0, 3), rows(halo_ref, 3, 3)
    far_load, within = rows(halo_ref, 18, 3), rows(strip_ref, 0, 6)
    far_scale = rows(strip_ref, 33, 3)
    far = [ratio(far_load[c], far_scale[c]) for c in range(3)]
    whole_block = [None, *within[:3], None, *within[3:], None]
    total = off_diagonal(lambda k: whole_block[k], beside)
    from_far = product(lambda k: strip_ref[24 + k : 25 + k, :], far)
    up_y = product(lambda k: strip_ref[6 + k : 7 + k, :], beside)
    low_y = product(lambda k: strip_ref[15 + k : 16 + k, :], beside)
    for c in range(3):
        before_ref[c : c + 1, :] = inverse[c] * (
            total[c]
            + from_far[c]
            + entering[c]
            + lanes_moved(up_y[c], 0.0, 1)
            + lanes_moved(low_y[c], 0.0, -1)
        )
    before_ref[3:, :] = jnp.zeros((before_ref.shape[0] - 3, LANES), F32)


def box_kernel(
    tile_ref, field_ref, node_ref, param_ref, halo_ref, strip_ref, diag_ref, edge_ref,
    mask_ref, inverse_ref,
    part_ref, box_ref, adjoint_ref, before_ref, matrix_ref, weights_ref, columns_ref,
    *, tile_points,
):
    cells_x = field_ref.shape[1]
    own = cells_x // 2
    field = [field_ref[c] for c in range(3)]
    part = off_diagonal(lambda k: diag_ref[k], field)
    up_x = masked_product(edge_ref, mask_ref, 0, field)
    low_x = masked_product(edge_ref, mask_ref, 1, field)
    up_y = masked_product(edge_ref, mask_ref, 2, field)
    low_y = masked_product(edge_ref, mask_ref, 3, field)
    for c in range(3):
        part[c] = inverse_ref[c] * (
            part[c]
            + rows_moved(up_x[c], halo_ref[6 + c : 7 + c, :], 1)
            + rows_moved(low_x[c], halo_ref[21 + c : 22 + c, :], -1)
            + lanes_moved(up_y[c], 0.0, 1)
            + lanes_moved(low_y[c], 0.0, -1)
        )
        part_ref[c] = part[c]
    quotient_before(halo_ref, strip_ref, before_ref, [p[:1] for p in low_x])
    order = [field[0], part[0], field[2], field[1], part[1], part[2]]
    folded = [two_parts(jnp.concatenate([f[:own], f[own:]], axis=1)) for f in order]
    table = jnp.concatenate(
        [folded[f][which] for which in range(2) for f in range(6)], axis=0
    ).astype(BF16)
    points = param_ref.shape[1]
    pieces = CHUNK // LANES
    zero, one = jnp.zeros((), BF16), jnp.ones((), BF16)
    at_node = float_iota((2 * LANES, CHUNK), 0).astype(BF16)
    nothing = jnp.zeros((1, CHUNK), F32)
    highs, lows = [], []
    for chunk in range(points // CHUNK):
        node = jnp.concatenate(
            [node_ref[chunk * pieces + k : chunk * pieces + k + 1, :] for k in range(pieces)],
            axis=1,
        )
        row = lax.shift_right_logical(node, 7)
        column = node & (LANES - 1)
        lanes = slice(chunk * CHUNK, (chunk + 1) * CHUNK)
        at_edge = jnp.where(
            column == 0, row, jnp.where(column == LANES - 1, row + cells_x, -1)
        ).astype(F32)
        columns_ref[:, lanes] = jnp.where(
            at_node[: 2 * cells_x] == stretched(at_edge, 2 * cells_x), one, zero
        )
        place = column + jnp.where(row >= own, LANES, 0)
        row = jnp.where(row >= own, row - own, row)
        pick = jnp.where(at_node == stretched(place.astype(F32), 2 * LANES), one, zero)
        read = jnp.dot(table, pick, preferred_element_type=F32)
        read = read[: 6 * own] + read[6 * own :]
        here = iota((own, CHUNK), 0) == row
        values = [
            jnp.sum(
                jnp.where(here, read[f * own : (f + 1) * own], 0.0), axis=0, keepdims=True
            )
            for f in range(6)
        ]
        high, low = two_parts(
            jnp.concatenate(values[:3] + [nothing] + values[3:] + [nothing], axis=0)
        )
        highs.append(high)
        lows.append(low)
        weights = two_parts(
            weight_table(param_ref[0:1, lanes], param_ref[1:2, lanes], param_ref[2:3, lanes])
        )
        for k in range(CHUNK // tile_points):
            tile = slice(k * tile_points, (k + 1) * tile_points)
            sides = jnp.concatenate([weights[0][:, tile], weights[1][:, tile]], axis=0)
            weights_ref[chunk * (CHUNK // tile_points) + k] = sides.T.astype(BF16)
    both = jnp.concatenate(
        [jnp.concatenate(highs, axis=1), jnp.concatenate(lows, axis=1)], axis=0
    ).astype(BF16)
    matrix_ref[...] = box_matrix(tile_ref[...], matrix_ref.shape[0] // 4)
    tiles = tile_ref.shape[1]
    terms = [
        jnp.dot(
            both[:, tile * tile_points : (tile + 1) * tile_points],
            weights_ref[tile],
            preferred_element_type=F32,
        )
        for tile in range(tiles)
    ]
    box_ref[...] = jnp.dot(matrix_ref[...], tile_rows(terms), preferred_element_type=F32)
    low_half = iota((2 * cells_x, LANES), 1) < LANES // 2
    for tile in range(tiles):
        lanes = slice(tile * tile_points, (tile + 1) * tile_points)
        term = jnp.dot(
            columns_ref[:, lanes], weights_ref[tile], preferred_element_type=F32
        )
        high, low = two_parts(term + pltpu.roll(term, LANES // 2, 1))
        adjoint_ref[:, tile * LANES : (tile + 1) * LANES] = jnp.where(
            low_half, high, low
        ).astype(BF16)


def sums_kernel(
    from_inner_ref, from_outer_ref, inner_ref, outer_ref, field_ref, part_ref, halo_ref,
    diag_ref, edge_ref, mask_ref, box_ref, adjoint_ref, before_ref, matrix_ref,
    quotient_ref, out_ref,
):
    cells_x = field_ref.shape[1]
    targets = out_ref.shape[0]

    from_low, from_high = by_parity(from_inner_ref[...], from_outer_ref[...])
    first, last = by_parity(inner_ref[...], outer_ref[...])

    lane_row = iota((1, LANES), 1)
    shares, edges = [], []
    for arrived, own in ((from_low, first), (from_high, last)):
        def row(source, slot, c):
            return source[3 * slot + c : 3 * slot + c + 1]

        shares.append([row(arrived, 1, c) * row(own, 3, c) for c in range(3)])
        edges.append(
            [row(arrived, 2, c) + row(arrived, 3, c) * row(own, 1, c) for c in range(3)]
        )

    def turned(columns, share, edge):
        kept = [
            jnp.where(lane_row < cells_x, share[c], columns[3 + c : 4 + c]) for c in range(3)
        ]
        rest = jnp.zeros((LANES - 9, LANES), F32)
        return jnp.concatenate([columns[:3], *kept, *edge, rest], axis=0).T

    low = turned(from_low, shares[0], edges[0])
    high = turned(from_high, shares[1], edges[1])
    lane = iota((cells_x, LANES), 1)

    def column(source, slot, comp):
        return source[:cells_x, 3 * slot + comp : 3 * slot + comp + 1]

    field = [field_ref[c] for c in range(3)]
    scale = [diag_ref[4 * c] for c in range(3)]
    quotient, low_edge, high_edge = [], [], []
    for c in range(3):
        entering = jnp.where(
            lane == 0,
            column(low, 1, c),
            jnp.where(lane == LANES - 1, column(high, 1, c), 0.0),
        )
        quotient.append(part_ref[c] + entering)
        low_edge.append(column(low, 2, c))
        high_edge.append(column(high, 2, c))
    for c in range(3):
        quotient_ref[c] = quotient[c]
    before, before_quotient = [], []
    for c in range(3):
        entering = jnp.where(
            lane_row == 0,
            low[cells_x : cells_x + 1, 3 + c : 4 + c],
            jnp.where(lane_row == LANES - 1, high[cells_x : cells_x + 1, 3 + c : 4 + c], 0.0),
        )
        before.append(halo_ref[c : c + 1, :])
        before_quotient.append(
            before_ref[c : c + 1, :] + entering * halo_ref[3 + c : 4 + c, :]
        )

    first_sum = sum(field[c] * scale[c] * field[c] for c in range(3))
    second_sum = sum(field[c] * scale[c] * quotient[c] for c in range(3))
    third_sum = sum(quotient[c] * scale[c] * quotient[c] for c in range(3))
    within = off_diagonal(lambda k: diag_ref[k], quotient)
    fourth_sum = sum(within[c] * field[c] for c in range(3))
    fifth_sum = sum(within[c] * quotient[c] for c in range(3))
    at_row = iota((cells_x, LANES), 0)
    moves = (
        (pltpu.roll, 1, 0, at_row == 0),
        (pltpu.roll, cells_x - 1, 0, at_row == cells_x - 1),
        (pltpu.roll, 1, 1, lane == 0),
        (pltpu.roll, LANES - 1, 1, lane == LANES - 1),
    )
    extra = [0.0, 0.0]
    sides = [0.0, 0.0]
    for direction, (roll, step, dim, edge) in enumerate(moves):
        moving = masked_product(edge_ref, mask_ref, direction, quotient)
        for c in range(3):
            moved = jnp.where(edge, 0.0, roll(moving[c], step, dim))
            fourth_sum = fourth_sum + moved * field[c]
            fifth_sum = fifth_sum + moved * quotient[c]
            if direction == 1:
                extra[0] += moving[c][:1] * before[c]
                extra[1] += moving[c][:1] * before_quotient[c]
            elif direction == 2:
                sides[0] += moving[c][:, LANES - 1 :] * column(high, 0, c)
                sides[1] += moving[c][:, LANES - 1 :] * high_edge[c]
            elif direction == 3:
                sides[0] += moving[c][:, :1] * column(low, 0, c)
                sides[1] += moving[c][:, :1] * low_edge[c]
    incoming = product(lambda k: halo_ref[9 + k : 10 + k, :], before_quotient)
    extra[0] += sum(incoming[c] * field[c][:1] for c in range(3))
    extra[1] += sum(incoming[c] * quotient[c][:1] for c in range(3))
    fourth_sum = fourth_sum + jnp.where(lane == 0, sides[0], 0.0)
    fifth_sum = fifth_sum + jnp.where(lane == 0, sides[1], 0.0)
    extra = [0.0, 0.0, 0.0, extra[0], extra[1]]
    sums = jnp.zeros((1, LANES), F32)
    for k, value in enumerate((first_sum, second_sum, third_sum, fourth_sum, fifth_sum)):
        line = jnp.sum(value, axis=0, keepdims=True) + extra[k]
        sums = jnp.where(lane_row == k, jnp.sum(line, axis=1, keepdims=True), sums)

    added = [
        jnp.where(lane_row < cells_x, shares[0][c], pltpu.roll(shares[1][c], cells_x, 1))
        for c in range(3)
    ]
    none = jnp.zeros((1, LANES), F32)
    added = jnp.concatenate(
        [none, added[0], none, none, none, added[1], added[2], none], axis=0
    )
    added = jnp.concatenate(two_parts(added), axis=0).astype(BF16)
    terms = jnp.dot(added, adjoint_ref[...], preferred_element_type=F32)
    terms = [
        terms[:, first : first + LANES] for first in range(0, terms.shape[1], LANES)
    ]
    total = box_ref[...] + jnp.dot(
        matrix_ref[...], tile_rows(terms), preferred_element_type=F32
    )
    total = jnp.where((iota(total.shape, 0) & 3) == 3, sums, total)
    for box in range(targets):
        out_ref[box] = total[4 * box : 4 * box + 4]


def result_kernel(got_ref, field_ref, quotient_ref, solution_ref, gradient_ref):
    total = jnp.sum(got_ref[...], axis=0)
    rho, a, b, t, u = [total[3:4, k : k + 1] for k in range(5)]
    norm = rho + a
    by_rho, by_norm = 1.0 / rho, 1.0 / norm
    ratio, step = a * by_rho, rho * by_norm
    rest = jnp.maximum(b - a * ratio, 0.0)
    beta = step * step * rest * by_rho
    rest_image = (b + u) - ratio * (a + b + a + t) + ratio * ratio * norm
    cross = (a + t) - ratio * norm
    curve = step * step * rest_image - step * beta * (rest + cross) + beta * beta * norm
    second = jnp.where(
        curve > 0.0, step * step * rest / jnp.where(curve > 0.0, curve, 1.0), 0.0
    )
    second = jnp.minimum(second, 16.0)
    of_field = step + second * (beta + step * ratio)
    of_quotient = -(step * second)
    for c in range(3):
        solution_ref[c] = of_field * field_ref[c] + of_quotient * quotient_ref[c]
    gradient_ref[:, :LANES] = of_field * total[0:1] + of_quotient * total[1:2]
    gradient_ref[:, LANES:] = (
        of_field * total[2:3, : LANES // 2] + of_quotient * total[2:3, LANES // 2 :]
    )


def per_device(
    diag_blocks, edge_blocks, edge_mask, src_values, src_owner, src_node, src_count,
    surf_node, surf_param, tile_box,
):
    cells_x, cells_y = diag_blocks.shape[1:]
    width_gx, width_gy = lax.axis_size("gx"), lax.axis_size("gy")
    devices = width_gx * width_gy
    groups = src_node.shape[0] // LANES
    whole = functools.partial(jax.ShapeDtypeStruct, dtype=F32)

    cells = 4 * groups + NEAR

    def kept(array):
        return pltpu.with_memory_space_constraint(array, pltpu.HBM)

    i32 = jnp.int32
    rows, strip = pl.pallas_call(
        pack_kernel,
        in_specs=[SMEM] + [HBM] * 6,
        out_specs=[HBM, VMEM],
        out_shape=[
            pltpu.HBM((width_gx, cells, LANES), F32), pltpu.VMEM((STRIP, LANES), F32)
        ],
        scratch_shapes=[
            pltpu.VMEM(src_values.shape, F32),
            pltpu.VMEM((groups, LANES), i32),
            pltpu.VMEM((groups, LANES), i32),
            pltpu.VMEM((9, 8, cells_y), F32),
            pltpu.VMEM((9, 8, cells_y), F32),
            pltpu.VMEM((9, 8, cells_y), F32),
            pltpu.VMEM((4, 9, 8, cells_y), F32),
            pltpu.VMEM((8, cells_y), i32),
            pltpu.VMEM((4, 8, cells_y), i32),
            pltpu.VMEM((width_gx, cells, LANES), F32),
            pltpu.SemaphoreType.DMA((9,)),
            pltpu.SemaphoreType.DMA((2,)),
        ],
        compiler_params=PARAMS,
        name="pack_rows_and_edges",
    )(
        src_count, kept(src_values),
        kept(src_owner.reshape(groups, LANES)), kept(src_node.reshape(groups, LANES)),
        kept(diag_blocks), kept(edge_blocks), kept(edge_mask),
    )
    rows = lax.all_to_all(rows, "gx", split_axis=0, concat_axis=0, tiled=True)
    strip = lax.ppermute(strip, "gx", [(i, i + 1) for i in range(width_gx - 1)])

    nodes = (3, cells_x, cells_y)
    inverse, columns = pl.pallas_call(
        edge_kernel,
        in_specs=[VMEM] * 3,
        out_specs=[VMEM] * 2,
        out_shape=[whole(nodes), whole((LANES, LANES))],
        compiler_params=PARAMS,
        cost_estimate=pl.CostEstimate(
            flops=10**8, bytes_accessed=4 * 10**6, transcendentals=0
        ),
        name="edge_columns",
    )(diag_blocks, edge_blocks, edge_mask)

    size = -(-3 * (cells_x + 2 * PAD) // 16) * 16
    field, halo, inner, outer = pl.pallas_call(
        field_kernel,
        in_specs=[VMEM] * 3,
        out_specs=[VMEM] * 4,
        out_shape=[
            whole(nodes), whole((24, cells_y)), whole((16, LANES)), whole((16, LANES)),
        ],
        scratch_shapes=[pltpu.VMEM((size, 2 * LANES), F32)],
        compiler_params=PARAMS,
        name="load_and_first_product",
    )(rows, inverse, columns)
    def swapped(columns, first):
        low = range(first, width_gy - 1, 2)
        pairs = [(i, i + 1) for i in low] + [(i + 1, i) for i in low]
        return lax.ppermute(columns, "gy", pairs)

    from_inner, from_outer = swapped(inner, 1), swapped(outer, 0)
    points, tiles = surf_node.shape[0], tile_box.shape[0]
    part, box_part, adjoint, before, matrix = pl.pallas_call(
        functools.partial(box_kernel, tile_points=points // tiles),
        in_specs=[VMEM] * 10,
        out_specs=[VMEM] * 5,
        out_shape=[
            whole(nodes),
            whole((4 * devices, LANES)),
            jax.ShapeDtypeStruct((2 * cells_x, tiles * LANES), BF16),
            whole((8, LANES)),
            jax.ShapeDtypeStruct((4 * devices, 8 * tiles), BF16),
        ],
        scratch_shapes=[
            pltpu.VMEM((tiles, points // tiles, LANES), BF16),
            pltpu.VMEM((2 * cells_x, points), BF16),
        ],
        compiler_params=PARAMS,
        cost_estimate=pl.CostEstimate(
            flops=10**9, bytes_accessed=4 * 10**6, transcendentals=0
        ),
        name="box_parts",
    )(
        tile_box.reshape(1, tiles), field, surf_node.reshape(points // LANES, LANES),
        surf_param, halo, strip, diag_blocks, edge_blocks, edge_mask, inverse,
    )

    quotient, partial = pl.pallas_call(
        sums_kernel,
        in_specs=[VMEM] * 14,
        out_specs=[VMEM] * 2,
        out_shape=[whole(nodes), whole((devices, 4, LANES))],
        compiler_params=PARAMS,
        name="sums_and_halo_parts",
    )(
        from_inner, from_outer, inner, outer, field, part, halo, diag_blocks, edge_blocks, edge_mask,
        box_part, adjoint, before, matrix,
    )
    got = lax.all_to_all(partial, ("gx", "gy"), split_axis=0, concat_axis=0, tiled=True)
    return pl.pallas_call(
        result_kernel,
        in_specs=[VMEM] * 3,
        out_specs=[VMEM] * 2,
        out_shape=[whole(nodes), whole((1, 192))],
        compiler_params=PARAMS,
        name="steps_and_outputs",
    )(got, field, quotient)


def solution(mesh):
    return jax.shard_map(
        per_device,
        mesh=mesh,
        in_specs=(
            P(None, "gx", "gy"),
            P(None, None, "gx", "gy"),
            P(None, "gx", "gy"),
            P(None, ("gx", "gy")),
            P(("gx", "gy"), None),
            P(("gx", "gy")),
            P(("gx", "gy")),
            P(("gx", "gy")),
            P(None, ("gx", "gy")),
            P(("gx", "gy")),
        ),
        out_specs=(P(None, "gx", "gy"), P(("gx", "gy"), None)),
        check_vma=False,
    )
```

```python
import functools
import math

import jax
import jax.numpy as jnp
from jax import lax
from jax.experimental import pallas as pl
from jax.experimental.pallas import tpu as pltpu
from jax.sharding import PartitionSpec as P

F32 = jnp.float32
BF16 = jnp.bfloat16
PAD = 2
NOWHERE = -(1 << 20)
LANES = 128
NEAR = 16
STRIP = 40
CHUNK = 256
PARAMS = pltpu.CompilerParams(vmem_limit_bytes=24 * 1024 * 1024)

VMEM = pl.BlockSpec(memory_space=pltpu.VMEM)
SMEM = pl.BlockSpec(memory_space=pltpu.SMEM)
HBM = pl.BlockSpec(memory_space=pltpu.HBM)


def iota(shape, dim):
    return lax.broadcasted_iota(jnp.int32, shape, dim)


def float_iota(shape, dim):
    return iota(shape, dim).astype(F32)


def two_parts(value):
    high = value.astype(BF16).astype(F32)
    return high, value - high


def product(block, field):
    return [
        block(row) * field[0] + block(3 + row) * field[1] + block(6 + row) * field[2]
        for row in range(3)
    ]


def off_diagonal(block, field):
    return [
        sum(block(3 * i + row) * field[i] for i in range(3) if i != row) for row in range(3)
    ]


def masked_product(edge_ref, mask_ref, direction, field):
    mask = mask_ref[direction].astype(F32)
    return [mask * part for part in product(lambda k: edge_ref[direction, k], field)]


def rows_moved(field, edge_row, step):
    size = field.shape[0]
    at = iota(field.shape, 0)
    moved = pltpu.roll(field, step % size, 0)
    return jnp.where(at == (0 if step == 1 else size - 1), edge_row, moved)


def lanes_moved(field, edge_column, step):
    size = field.shape[1]
    at = iota(field.shape, 1)
    moved = pltpu.roll(field, step % size, 1)
    return jnp.where(at == (0 if step == 1 else size - 1), edge_column, moved)


def pack_kernel(
    count_ref, values_in, owner_in, node_in, diag_in, edge_in, mask_in, rows_out, strip_ref,
    values_ref, owner_ref, node_ref, diag_low, diag_high, edge_low, edge_high,
    mask_low, mask_high, rows_ref, arrived, left,
):
    targets = rows_ref.shape[0]
    groups = owner_ref.shape[0]
    cells_x = diag_in.shape[1]
    top = pl.ds(cells_x - 8, 8)
    copies = [
        pltpu.make_async_copy(source, target, arrived.at[k])
        for k, (source, target) in enumerate(
            (
                (owner_in, owner_ref),
                (node_in, node_ref),
                (values_in, values_ref),
                (diag_in.at[:, 0:8], diag_low),
                (diag_in.at[:, top], diag_high),
                (mask_in.at[1, 0:8], mask_low),
                (mask_in.at[:, top], mask_high),
                (edge_in.at[1, :, 0:8], edge_low),
                (edge_in.at[:, :, top], edge_high),
            )
        )
    ]
    for copy in copies:
        copy.start()
    base = 4 * groups
    for target in range(targets):
        rows_ref[target, base:, :] = jnp.zeros((NEAR, LANES), F32)
    for copy in copies[:2]:
        copy.wait()
    order = iota((groups, LANES), 0) * LANES + iota((groups, LANES), 1)
    node = node_ref[...]
    frame = cells_x + 2 * PAD
    row = owner_ref[...] * cells_x + lax.shift_right_logical(node, 7)
    row = jnp.where(order < count_ref[0], row, NOWHERE)
    column = node & (LANES - 1)
    for target in range(targets):
        line = row - (target * cells_x - PAD)
        inside = (line >= 0) & (line < frame)
        index = jnp.where(inside, line * LANES + column, -1)
        rows_ref[target, 3 * groups : 4 * groups, :] = index.astype(F32)

    copies[2].wait()
    for comp in range(3):
        value = jnp.concatenate(
            [
                values_ref[comp : comp + 1, group * LANES : (group + 1) * LANES]
                for group in range(groups)
            ],
            axis=0,
        )
        for target in range(targets):
            rows_ref[target, comp * groups : (comp + 1) * groups, :] = value
    near = pl.ds(4 * groups, NEAR)
    leaving = [
        pltpu.make_async_copy(rows_ref.at[:, part], rows_out.at[:, part], left.at[k])
        for k, part in enumerate((pl.ds(0, 4 * groups), near))
    ]
    leaving[0].start()
    for copy in copies[3:]:
        copy.wait()

    def block(edge, mask, direction, at):
        present = mask[direction, at : at + 1, :].astype(F32)
        return [edge[direction, k, at : at + 1, :] * present for k in range(9)]

    up_y, low_y = block(edge_high, mask_high, 2, 7), block(edge_high, mask_high, 3, 7)
    here = lax.axis_index("gx")

    @pl.when(here < targets - 1)
    def _():
        def put(slot, value):
            rows_ref[here + 1, base + slot : base + slot + 1, :] = value

        for k in range(3):
            put(k, diag_high[4 * k, 7:8, :])
        for k, value in enumerate(block(edge_high, mask_high, 0, 7)):
            put(3 + k, value)
        corners = jnp.zeros((1, LANES), F32)
        lane = iota((1, LANES), 1)
        for k in range(9):
            corners = jnp.where(lane == k, up_y[k][:, LANES - 1 :], corners)
            corners = jnp.where(lane == 9 + k, low_y[k][:, :1], corners)
        put(12, corners)

    @pl.when(here > 0)
    def _():
        def put(slot, value):
            rows_ref[here - 1, base + slot : base + slot + 1, :] = value

        for k in range(3):
            put(k, diag_low[4 * k, 0:1, :])
        present = mask_low[0:1, :].astype(F32)
        for k in range(9):
            put(3 + k, edge_low[k, 0:1, :] * present)

    leaving[1].start()
    later = [diag_high[k, 7:8, :] for k in range(9) if k % 4]
    later += up_y + low_y + block(edge_high, mask_high, 0, 6)
    later += [diag_high[4 * k, 6:7, :] for k in range(3)]
    for k, value in enumerate(later):
        strip_ref[k : k + 1, :] = value
    strip_ref[len(later) :, :] = jnp.zeros((STRIP - len(later), LANES), F32)
    for copy in leaving:
        copy.wait()


def stretched(row, count):
    tile = jnp.broadcast_to(row, (16, row.shape[1])).astype(BF16)
    return jnp.concatenate([tile] * (count // 16), axis=0)


def ratio(value, scale):
    return jnp.where(scale > 0.0, value / jnp.where(scale > 0.0, scale, 1.0), 0.0)


UP_X, LOW_X, INWARD, OUTWARD, WITHIN, INVERSE = 0, 3, 6, 9, 12, 15


def edge_kernel(diag_ref, edge_ref, mask_ref, inverse_ref, columns_ref):
    cells_x = diag_ref.shape[1]
    at = iota((cells_x, LANES), 1)
    sides = [jnp.zeros((cells_x, LANES), F32) for _ in range(2)]

    def put(kind, i, a, first, first_lane, last, last_lane):
        slot = 8 * (kind + i) + a
        for side, (field, lane) in enumerate(((first, first_lane), (last, last_lane))):
            sides[side] = jnp.where(at == slot, field[:, lane : lane + 1], sides[side])

    inverse = [1.0 / diag_ref[4 * c] for c in range(3)]
    end = LANES - 1
    masks = [mask_ref[direction].astype(F32) for direction in range(4)]
    for i in range(3):
        inverse_ref[i] = inverse[i]
        put(INVERSE, 0, i, inverse[i], 0, inverse[i], end)
        for a in range(3):
            up_x, low_x, up_y, low_y = (
                edge_ref[direction, 3 * i + a] * masks[direction] for direction in range(4)
            )
            put(UP_X, i, a, up_x, 0, up_x, end)
            put(LOW_X, i, a, low_x, 0, low_x, end)
            put(INWARD, i, a, low_y, 1, up_y, end - 1)
            put(OUTWARD, i, a, low_y, 0, up_y, end)
            if a != i:
                put(WITHIN, i, a, diag_ref[3 * i + a], 0, diag_ref[3 * i + a], end)
    columns_ref[...] = jnp.concatenate(sides, axis=0).T


def field_kernel(
    rows_ref, inverse_ref, columns_ref,
    field_ref, halo_ref, inner_ref, outer_ref, load_ref,
):
    senders = rows_ref.shape[0]
    groups = (rows_ref.shape[1] - NEAR) // 4
    cells_x = field_ref.shape[1]
    half = (cells_x + 2 * PAD) // 2
    own = cells_x // 2

    load_ref[...] = jnp.zeros_like(load_ref)
    here = lax.axis_index("gx")

    size = load_ref.shape[0]
    line = iota((size, LANES), 0)
    block = sum(jnp.where(line >= half * k, 1, 0) for k in range(1, 6))
    at_row = jnp.where(line < 6 * half, line - half * block, -5).astype(F32).astype(BF16)
    at_column = float_iota((LANES, 2 * LANES), 1).astype(BF16)
    in_tile = float_iota((16, LANES), 0).astype(BF16)
    zero, one = jnp.zeros((), BF16), jnp.ones((), BF16)

    def operands(sender):
        index = rows_ref[sender, 3 * groups : 4 * groups, :]
        split = float(half * LANES)
        index, shift = (
            jnp.where(index >= split, index - split, index),
            jnp.where(index >= split, float(LANES), 0.0),
        )
        place = jnp.floor(index * (1.0 / LANES))
        column = index - place * float(LANES) + shift
        parts = [
            two_parts(rows_ref[sender, c * groups : (c + 1) * groups, :]) for c in range(3)
        ]
        lefts = []
        for group in range(groups):
            line = slice(group, group + 1)
            values = [
                stretched(parts[c][which][line], 16) for which in range(2) for c in range(3)
            ]
            tiles = []
            for first in range(0, size, 16):
                low, high = first // half, min((first + 15) // half, 5)
                tiles.append(
                    values[low]
                    if low == high
                    else jnp.where(
                        in_tile < float(half * high - first), values[low], values[high]
                    )
                )
            match = at_row == stretched(place[line], size)
            lefts.append(jnp.where(match, jnp.concatenate(tiles, axis=0), zero))
        return lefts, column

    together = math.gcd(senders, 4)

    def add_rows(step, carry):
        lefts, columns = [], []
        for k in range(together):
            left, column = operands(step * together + k)
            lefts += left
            columns.append(column)
        columns.append(jnp.zeros((LANES - together * groups, LANES), F32))
        columns = jnp.concatenate(columns, axis=0).T
        rights = []
        for k in range(together * groups):
            column = jnp.broadcast_to(columns[:, k : k + 1], (LANES, LANES)).astype(BF16)
            column = jnp.concatenate([column, column], axis=1)
            rights.append(jnp.where(at_column == column, one, zero))
        load_ref[...] += jnp.dot(
            jnp.concatenate(lefts, axis=1),
            jnp.concatenate(rights, axis=0),
            preferred_element_type=F32,
        )
        return carry

    steps = senders // together
    lax.fori_loop(0, steps, add_rows, 0, unroll=min(steps, 2))

    def load_rows(comp, first, last, second_half):
        lanes = slice(LANES, 2 * LANES) if second_half else slice(0, LANES)
        return (
            load_ref[comp * half + first : comp * half + last, lanes]
            + load_ref[(3 + comp) * half + first : (3 + comp) * half + last, lanes]
        )

    field = []
    for comp in range(3):
        load = jnp.concatenate(
            [load_rows(comp, PAD, half, False), load_rows(comp, 0, half - PAD, True)], axis=0
        )
        field.append(load * inverse_ref[comp])
        field_ref[comp] = field[comp]
    beyond = half - PAD
    near_before = [load_rows(c, PAD - 1, PAD, False) for c in range(3)]
    far_before = [load_rows(c, PAD - 2, PAD - 1, False) for c in range(3)]
    near_after = [load_rows(c, beyond, beyond + 1, True) for c in range(3)]

    base = 4 * groups

    def neighbour(sender, load):
        def entry(k):
            return rows_ref[sender, base + k : base + k + 1, :]

        inverse = [ratio(1.0, entry(k)) for k in range(3)]
        toward = [entry(3 + k) for k in range(9)]
        beside = [load[c] * inverse[c] for c in range(3)]
        return inverse, toward, beside, product(lambda k: toward[k], beside)

    lower = jnp.maximum(here - 1, 0)
    before = neighbour(lower, near_before)
    after = neighbour(jnp.minimum(here + 1, senders - 1), near_after)
    rows = before[2] + before[0] + before[3] + before[1] + far_before + after[3]
    for k, value in enumerate(rows):
        halo_ref[k : k + 1, :] = value
    lane_row = iota((1, LANES), 1)
    ends = jnp.zeros((1, LANES), F32)
    for i in range(3):
        for a in range(3):
            ends = jnp.where(lane_row == 3 * i + a, before[2][i][:, LANES - 1 :], ends)
            ends = jnp.where(lane_row == 9 + 3 * i + a, before[2][i][:, :1], ends)
    ends = ends * rows_ref[lower, base + 12 : base + 13, :]
    ends = ends + pltpu.roll(ends, LANES - 3, 1) + pltpu.roll(ends, LANES - 6, 1)

    at = iota((cells_x, LANES), 1)
    sides = []
    for edge, inside in ((0, 1), (LANES - 1, LANES - 2)):
        packed = jnp.zeros((cells_x, LANES), F32)
        for comp in range(3):
            packed = jnp.where(at == comp, field[comp][:, edge : edge + 1], packed)
            packed = jnp.where(at == 8 + comp, field[comp][:, inside : inside + 1], packed)
        sides.append(packed)
    turned = jnp.concatenate(sides, axis=0).T

    def column_product(kind, first):
        return sum(
            columns_ref[8 * (kind + i) : 8 * (kind + i) + 8, :] * turned[first + i : first + i + 1]
            for i in range(3)
        )

    def eight(rows):
        return jnp.concatenate(rows + [jnp.zeros((8 - len(rows), LANES), F32)], axis=0)

    lane = iota((8, LANES), 1)
    from_before, from_after = eight(before[3]), eight(after[3])
    from_before = jnp.where(lane == 0, from_before, pltpu.roll(from_before, cells_x + 1, 1))
    from_after = jnp.where(
        lane == LANES - 1, from_after, pltpu.roll(from_after, cells_x - 1, 1)
    )
    row = lane & (cells_x - 1)
    upward = pltpu.roll(column_product(UP_X, 0), 1, 1)
    downward = pltpu.roll(column_product(LOW_X, 0), LANES - 1, 1)
    total = (
        column_product(WITHIN, 0)
        + jnp.where(row == 0, from_before, upward)
        + jnp.where(row == cells_x - 1, from_after, downward)
        + column_product(INWARD, 8)
    )
    inverse = columns_ref[8 * INVERSE : 8 * INVERSE + 8, :]
    along_y, part = column_product(OUTWARD, 0), total * inverse
    stacked = jnp.concatenate(
        [turned[:3], along_y[:3], part[:3], inverse[:3], jnp.zeros((4, LANES), F32)], axis=0
    )

    def message(columns, end):
        at = iota((16, LANES), 1)
        line = iota((16, LANES), 0)
        columns = jnp.where(at < cells_x, columns, 0.0)
        for comp in range(3):
            columns = jnp.where(
                (line == 3 + comp) & (at == cells_x),
                ends[:, end + comp : end + comp + 1],
                columns,
            )
        return columns

    inner_ref[...], outer_ref[...] = by_parity(
        message(stacked, 9), message(pltpu.roll(stacked, cells_x, 1), 0)
    )


def bernstein(coord):
    other = 1.0 - coord
    return [
        other * other * other,
        3.0 * coord * other * other,
        3.0 * coord * coord * other,
        coord * coord * coord,
    ]


def weight_table(u, v, w):
    first, second, third = bernstein(u), bernstein(v), bernstein(w)
    line = iota((8, u.shape[1]), 0)
    inner = line & 3
    along = jnp.where(
        inner == 0,
        third[0],
        jnp.where(inner == 1, third[1], jnp.where(inner == 2, third[2], third[3])),
    )
    pair = jnp.concatenate(
        [
            jnp.where(line < 4, second[0], second[1]) * along,
            jnp.where(line < 4, second[2], second[3]) * along,
        ],
        axis=0,
    )
    return jnp.concatenate([pair * first[i] for i in range(4)], axis=0)


def tile_rows(terms):
    first_half = iota((4, LANES), 1) < LANES // 2
    rows = []
    for term in terms:
        term = term[:8] + term[8:]
        term = term + pltpu.roll(term, LANES // 2, 1)
        rows.append(jnp.where(first_half, term[:4], term[4:]))
    return jnp.concatenate(two_parts(jnp.concatenate(rows, axis=0)), axis=0).astype(BF16)


def box_matrix(tile_row, boxes):
    tiles = tile_row.shape[1]
    shape = (4 * boxes, 8 * tiles)
    column = iota((1, shape[1]), 1)
    box = jnp.zeros((1, shape[1]), jnp.int32)
    for tile in range(tiles):
        mine = lax.rem(lax.shift_right_logical(column, 2), tiles) == tile
        box = jnp.where(mine, tile_row[:, tile : tile + 1], box)
    target = 4 * box + (column & 3)
    return jnp.where(iota(shape, 0) == target, 1.0, 0.0).astype(BF16)


def by_parity(low, high):
    odd = lax.rem(lax.axis_index("gy"), 2) == 1
    return jnp.where(odd, high, low), jnp.where(odd, low, high)


def quotient_before(halo_ref, strip_ref, before_ref, entering):
    def rows(ref, first, count):
        return [ref[first + k : first + k + 1, :] for k in range(count)]

    beside, inverse = rows(halo_ref, 0, 3), rows(halo_ref, 3, 3)
    far_load, within = rows(halo_ref, 18, 3), rows(strip_ref, 0, 6)
    far_scale = rows(strip_ref, 33, 3)
    far = [ratio(far_load[c], far_scale[c]) for c in range(3)]
    whole_block = [None, *within[:3], None, *within[3:], None]
    total = off_diagonal(lambda k: whole_block[k], beside)
    from_far = product(lambda k: strip_ref[24 + k : 25 + k, :], far)
    up_y = product(lambda k: strip_ref[6 + k : 7 + k, :], beside)
    low_y = product(lambda k: strip_ref[15 + k : 16 + k, :], beside)
    for c in range(3):
        before_ref[c : c + 1, :] = inverse[c] * (
            total[c]
            + from_far[c]
            + entering[c]
            + lanes_moved(up_y[c], 0.0, 1)
            + lanes_moved(low_y[c], 0.0, -1)
        )
    before_ref[3:, :] = jnp.zeros((before_ref.shape[0] - 3, LANES), F32)


def box_kernel(
    tile_ref, field_ref, node_ref, param_ref, halo_ref, strip_ref, diag_ref, edge_ref,
    mask_ref, inverse_ref,
    part_ref, box_ref, adjoint_ref, before_ref, matrix_ref, weights_ref, columns_ref,
    *, tile_points,
):
    cells_x = field_ref.shape[1]
    own = cells_x // 2
    field = [field_ref[c] for c in range(3)]
    part = off_diagonal(lambda k: diag_ref[k], field)
    up_x = masked_product(edge_ref, mask_ref, 0, field)
    low_x = masked_product(edge_ref, mask_ref, 1, field)
    up_y = masked_product(edge_ref, mask_ref, 2, field)
    low_y = masked_product(edge_ref, mask_ref, 3, field)
    for c in range(3):
        part[c] = inverse_ref[c] * (
            part[c]
            + rows_moved(up_x[c], halo_ref[6 + c : 7 + c, :], 1)
            + rows_moved(low_x[c], halo_ref[21 + c : 22 + c, :], -1)
            + lanes_moved(up_y[c], 0.0, 1)
            + lanes_moved(low_y[c], 0.0, -1)
        )
        part_ref[c] = part[c]
    quotient_before(halo_ref, strip_ref, before_ref, [p[:1] for p in low_x])
    order = [field[0], part[0], field[2], field[1], part[1], part[2]]
    folded = [two_parts(jnp.concatenate([f[:own], f[own:]], axis=1)) for f in order]
    table = jnp.concatenate(
        [folded[f][which] for which in range(2) for f in range(6)], axis=0
    ).astype(BF16)
    points = param_ref.shape[1]
    pieces = CHUNK // LANES
    zero, one = jnp.zeros((), BF16), jnp.ones((), BF16)
    at_node = float_iota((2 * LANES, CHUNK), 0).astype(BF16)
    nothing = jnp.zeros((1, CHUNK), F32)
    highs, lows = [], []
    for chunk in range(points // CHUNK):
        node = jnp.concatenate(
            [node_ref[chunk * pieces + k : chunk * pieces + k + 1, :] for k in range(pieces)],
            axis=1,
        )
        row = lax.shift_right_logical(node, 7)
        column = node & (LANES - 1)
        lanes = slice(chunk * CHUNK, (chunk + 1) * CHUNK)
        at_edge = jnp.where(
            column == 0, row, jnp.where(column == LANES - 1, row + cells_x, -1)
        ).astype(F32)
        columns_ref[:, lanes] = jnp.where(
            at_node[: 2 * cells_x] == stretched(at_edge, 2 * cells_x), one, zero
        )
        place = column + jnp.where(row >= own, LANES, 0)
        row = jnp.where(row >= own, row - own, row)
        pick = jnp.where(at_node == stretched(place.astype(F32), 2 * LANES), one, zero)
        read = jnp.dot(table, pick, preferred_element_type=F32)
        read = read[: 6 * own] + read[6 * own :]
        here = iota((own, CHUNK), 0) == row
        values = [
            jnp.sum(
                jnp.where(here, read[f * own : (f + 1) * own], 0.0), axis=0, keepdims=True
            )
            for f in range(6)
        ]
        high, low = two_parts(
            jnp.concatenate(values[:3] + [nothing] + values[3:] + [nothing], axis=0)
        )
        highs.append(high)
        lows.append(low)
        weights = two_parts(
            weight_table(param_ref[0:1, lanes], param_ref[1:2, lanes], param_ref[2:3, lanes])
        )
        for k in range(CHUNK // tile_points):
            tile = slice(k * tile_points, (k + 1) * tile_points)
            sides = jnp.concatenate([weights[0][:, tile], weights[1][:, tile]], axis=0)
            weights_ref[chunk * (CHUNK // tile_points) + k] = sides.T.astype(BF16)
    both = jnp.concatenate(
        [jnp.concatenate(highs, axis=1), jnp.concatenate(lows, axis=1)], axis=0
    ).astype(BF16)
    matrix_ref[...] = box_matrix(tile_ref[...], matrix_ref.shape[0] // 4)
    tiles = tile_ref.shape[1]
    terms = [
        jnp.dot(
            both[:, tile * tile_points : (tile + 1) * tile_points],
            weights_ref[tile],
            preferred_element_type=F32,
        )
        for tile in range(tiles)
    ]
    box_ref[...] = jnp.dot(matrix_ref[...], tile_rows(terms), preferred_element_type=F32)
    low_half = iota((2 * cells_x, LANES), 1) < LANES // 2
    for tile in range(tiles):
        lanes = slice(tile * tile_points, (tile + 1) * tile_points)
        term = jnp.dot(
            columns_ref[:, lanes], weights_ref[tile], preferred_element_type=F32
        )
        high, low = two_parts(term + pltpu.roll(term, LANES // 2, 1))
        adjoint_ref[:, tile * LANES : (tile + 1) * LANES] = jnp.where(
            low_half, high, low
        ).astype(BF16)


def sums_kernel(
    from_inner_ref, from_outer_ref, inner_ref, outer_ref, field_ref, part_ref, halo_ref,
    diag_ref, edge_ref, mask_ref, box_ref, adjoint_ref, before_ref, matrix_ref,
    quotient_ref, out_ref,
):
    cells_x = field_ref.shape[1]
    targets = out_ref.shape[0]

    from_low, from_high = by_parity(from_inner_ref[...], from_outer_ref[...])
    first, last = by_parity(inner_ref[...], outer_ref[...])

    lane_row = iota((1, LANES), 1)
    shares, edges = [], []
    for arrived, own in ((from_low, first), (from_high, last)):
        def row(source, slot, c):
            return source[3 * slot + c : 3 * slot + c + 1]

        shares.append([row(arrived, 1, c) * row(own, 3, c) for c in range(3)])
        edges.append(
            [row(arrived, 2, c) + row(arrived, 3, c) * row(own, 1, c) for c in range(3)]
        )

    def turned(columns, share, edge):
        kept = [
            jnp.where(lane_row < cells_x, share[c], columns[3 + c : 4 + c]) for c in range(3)
        ]
        rest = jnp.zeros((LANES - 9, LANES), F32)
        return jnp.concatenate([columns[:3], *kept, *edge, rest], axis=0).T

    low = turned(from_low, shares[0], edges[0])
    high = turned(from_high, shares[1], edges[1])
    lane = iota((cells_x, LANES), 1)

    def column(source, slot, comp):
        return source[:cells_x, 3 * slot + comp : 3 * slot + comp + 1]

    field = [field_ref[c] for c in range(3)]
    scale = [diag_ref[4 * c] for c in range(3)]
    quotient, low_edge, high_edge = [], [], []
    for c in range(3):
        entering = jnp.where(
            lane == 0,
            column(low, 1, c),
            jnp.where(lane == LANES - 1, column(high, 1, c), 0.0),
        )
        quotient.append(part_ref[c] + entering)
        low_edge.append(column(low, 2, c))
        high_edge.append(column(high, 2, c))
    for c in range(3):
        quotient_ref[c] = quotient[c]
    before, before_quotient = [], []
    for c in range(3):
        entering = jnp.where(
            lane_row == 0,
            low[cells_x : cells_x + 1, 3 + c : 4 + c],
            jnp.where(lane_row == LANES - 1, high[cells_x : cells_x + 1, 3 + c : 4 + c], 0.0),
        )
        before.append(halo_ref[c : c + 1, :])
        before_quotient.append(
            before_ref[c : c + 1, :] + entering * halo_ref[3 + c : 4 + c, :]
        )

    first_sum = sum(field[c] * scale[c] * field[c] for c in range(3))
    second_sum = sum(field[c] * scale[c] * quotient[c] for c in range(3))
    third_sum = sum(quotient[c] * scale[c] * quotient[c] for c in range(3))
    within = off_diagonal(lambda k: diag_ref[k], quotient)
    fourth_sum = sum(within[c] * field[c] for c in range(3))
    fifth_sum = sum(within[c] * quotient[c] for c in range(3))
    at_row = iota((cells_x, LANES), 0)
    moves = (
        (pltpu.roll, 1, 0, at_row == 0),
        (pltpu.roll, cells_x - 1, 0, at_row == cells_x - 1),
        (pltpu.roll, 1, 1, lane == 0),
        (pltpu.roll, LANES - 1, 1, lane == LANES - 1),
    )
    extra = [0.0, 0.0]
    sides = [0.0, 0.0]
    for direction, (roll, step, dim, edge) in enumerate(moves):
        moving = masked_product(edge_ref, mask_ref, direction, quotient)
        for c in range(3):
            moved = jnp.where(edge, 0.0, roll(moving[c], step, dim))
            fourth_sum = fourth_sum + moved * field[c]
            fifth_sum = fifth_sum + moved * quotient[c]
            if direction == 1:
                extra[0] += moving[c][:1] * before[c]
                extra[1] += moving[c][:1] * before_quotient[c]
            elif direction == 2:
                sides[0] += moving[c][:, LANES - 1 :] * column(high, 0, c)
                sides[1] += moving[c][:, LANES - 1 :] * high_edge[c]
            elif direction == 3:
                sides[0] += moving[c][:, :1] * column(low, 0, c)
                sides[1] += moving[c][:, :1] * low_edge[c]
    incoming = product(lambda k: halo_ref[9 + k : 10 + k, :], before_quotient)
    extra[0] += sum(incoming[c] * field[c][:1] for c in range(3))
    extra[1] += sum(incoming[c] * quotient[c][:1] for c in range(3))
    fourth_sum = fourth_sum + jnp.where(lane == 0, sides[0], 0.0)
    fifth_sum = fifth_sum + jnp.where(lane == 0, sides[1], 0.0)
    extra = [0.0, 0.0, 0.0, extra[0], extra[1]]
    sums = jnp.zeros((1, LANES), F32)
    for k, value in enumerate((first_sum, second_sum, third_sum, fourth_sum, fifth_sum)):
        line = jnp.sum(value, axis=0, keepdims=True) + extra[k]
        sums = jnp.where(lane_row == k, jnp.sum(line, axis=1, keepdims=True), sums)

    added = [
        jnp.where(lane_row < cells_x, shares[0][c], pltpu.roll(shares[1][c], cells_x, 1))
        for c in range(3)
    ]
    none = jnp.zeros((1, LANES), F32)
    added = jnp.concatenate(
        [none, added[0], none, none, none, added[1], added[2], none], axis=0
    )
    added = jnp.concatenate(two_parts(added), axis=0).astype(BF16)
    terms = jnp.dot(added, adjoint_ref[...], preferred_element_type=F32)
    terms = [
        terms[:, first : first + LANES] for first in range(0, terms.shape[1], LANES)
    ]
    total = box_ref[...] + jnp.dot(
        matrix_ref[...], tile_rows(terms), preferred_element_type=F32
    )
    total = jnp.where((iota(total.shape, 0) & 3) == 3, sums, total)
    for box in range(targets):
        out_ref[box] = total[4 * box : 4 * box + 4]


def result_kernel(got_ref, field_ref, quotient_ref, solution_ref, gradient_ref):
    total = jnp.sum(got_ref[...], axis=0)
    rho, a, b, t, u = [total[3:4, k : k + 1] for k in range(5)]
    norm = rho + a
    by_rho, by_norm = 1.0 / rho, 1.0 / norm
    ratio, step = a * by_rho, rho * by_norm
    rest = jnp.maximum(b - a * ratio, 0.0)
    beta = step * step * rest * by_rho
    rest_image = (b + u) - ratio * (a + b + a + t) + ratio * ratio * norm
    cross = (a + t) - ratio * norm
    curve = step * step * rest_image - step * beta * (rest + cross) + beta * beta * norm
    second = jnp.where(
        curve > 0.0, step * step * rest / jnp.where(curve > 0.0, curve, 1.0), 0.0
    )
    second = jnp.minimum(second, 16.0)
    of_field = step + second * (beta + step * ratio)
    of_quotient = -(step * second)
    for c in range(3):
        solution_ref[c] = of_field * field_ref[c] + of_quotient * quotient_ref[c]
    gradient_ref[:, :LANES] = of_field * total[0:1] + of_quotient * total[1:2]
    gradient_ref[:, LANES:] = (
        of_field * total[2:3, : LANES // 2] + of_quotient * total[2:3, LANES // 2 :]
    )


def per_device(
    diag_blocks, edge_blocks, edge_mask, src_values, src_owner, src_node, src_count,
    surf_node, surf_param, tile_box,
):
    cells_x, cells_y = diag_blocks.shape[1:]
    width_gx, width_gy = lax.axis_size("gx"), lax.axis_size("gy")
    devices = width_gx * width_gy
    groups = src_node.shape[0] // LANES
    whole = functools.partial(jax.ShapeDtypeStruct, dtype=F32)

    cells = 4 * groups + NEAR

    def kept(array):
        return pltpu.with_memory_space_constraint(array, pltpu.HBM)

    i32 = jnp.int32
    rows, strip = pl.pallas_call(
        pack_kernel,
        in_specs=[SMEM] + [HBM] * 6,
        out_specs=[HBM, VMEM],
        out_shape=[
            pltpu.HBM((width_gx, cells, LANES), F32), pltpu.VMEM((STRIP, LANES), F32)
        ],
        scratch_shapes=[
            pltpu.VMEM(src_values.shape, F32),
            pltpu.VMEM((groups, LANES), i32),
            pltpu.VMEM((groups, LANES), i32),
            pltpu.VMEM((9, 8, cells_y), F32),
            pltpu.VMEM((9, 8, cells_y), F32),
            pltpu.VMEM((9, 8, cells_y), F32),
            pltpu.VMEM((4, 9, 8, cells_y), F32),
            pltpu.VMEM((8, cells_y), i32),
            pltpu.VMEM((4, 8, cells_y), i32),
            pltpu.VMEM((width_gx, cells, LANES), F32),
            pltpu.SemaphoreType.DMA((9,)),
            pltpu.SemaphoreType.DMA((2,)),
        ],
        compiler_params=PARAMS,
        name="pack_rows_and_edges",
    )(
        src_count, kept(src_values),
        kept(src_owner.reshape(groups, LANES)), kept(src_node.reshape(groups, LANES)),
        kept(diag_blocks), kept(edge_blocks), kept(edge_mask),
    )
    rows = lax.all_to_all(rows, "gx", split_axis=0, concat_axis=0, tiled=True)
    strip = lax.ppermute(strip, "gx", [(i, i + 1) for i in range(width_gx - 1)])

    nodes = (3, cells_x, cells_y)
    inverse, columns = pl.pallas_call(
        edge_kernel,
        in_specs=[VMEM] * 3,
        out_specs=[VMEM] * 2,
        out_shape=[whole(nodes), whole((LANES, LANES))],
        compiler_params=PARAMS,
        cost_estimate=pl.CostEstimate(
            flops=10**8, bytes_accessed=4 * 10**6, transcendentals=0
        ),
        name="edge_columns",
    )(diag_blocks, edge_blocks, edge_mask)

    size = -(-3 * (cells_x + 2 * PAD) // 16) * 16
    field, halo, inner, outer = pl.pallas_call(
        field_kernel,
        in_specs=[VMEM] * 3,
        out_specs=[VMEM] * 4,
        out_shape=[
            whole(nodes), whole((24, cells_y)), whole((16, LANES)), whole((16, LANES)),
        ],
        scratch_shapes=[pltpu.VMEM((size, 2 * LANES), F32)],
        compiler_params=PARAMS,
        name="load_and_first_product",
    )(rows, inverse, columns)
    def swapped(columns, first):
        low = range(first, width_gy - 1, 2)
        pairs = [(i, i + 1) for i in low] + [(i + 1, i) for i in low]
        return lax.ppermute(columns, "gy", pairs)

    from_inner, from_outer = swapped(inner, 1), swapped(outer, 0)
    points, tiles = surf_node.shape[0], tile_box.shape[0]
    part, box_part, adjoint, before, matrix = pl.pallas_call(
        functools.partial(box_kernel, tile_points=points // tiles),
        in_specs=[VMEM] * 10,
        out_specs=[VMEM] * 5,
        out_shape=[
            whole(nodes),
            whole((4 * devices, LANES)),
            jax.ShapeDtypeStruct((2 * cells_x, tiles * LANES), BF16),
            whole((8, LANES)),
            jax.ShapeDtypeStruct((4 * devices, 8 * tiles), BF16),
        ],
        scratch_shapes=[
            pltpu.VMEM((tiles, points // tiles, LANES), BF16),
            pltpu.VMEM((2 * cells_x, points), BF16),
        ],
        compiler_params=PARAMS,
        cost_estimate=pl.CostEstimate(
            flops=10**9, bytes_accessed=4 * 10**6, transcendentals=0
        ),
        name="box_parts",
    )(
        tile_box.reshape(1, tiles), field, surf_node.reshape(points // LANES, LANES),
        surf_param, halo, strip, diag_blocks, edge_blocks, edge_mask, inverse,
    )

    quotient, partial = pl.pallas_call(
        sums_kernel,
        in_specs=[VMEM] * 14,
        out_specs=[VMEM] * 2,
        out_shape=[whole(nodes), whole((devices, 4, LANES))],
        compiler_params=PARAMS,
        name="sums_and_halo_parts",
    )(
        from_inner, from_outer, inner, outer, field, part, halo, diag_blocks, edge_blocks, edge_mask,
        box_part, adjoint, before, matrix,
    )
    got = lax.all_to_all(partial, ("gx", "gy"), split_axis=0, concat_axis=0, tiled=True)
    return pl.pallas_call(
        result_kernel,
        in_specs=[VMEM] * 3,
        out_specs=[VMEM] * 2,
        out_shape=[whole(nodes), whole((1, 192))],
        compiler_params=PARAMS,
        name="steps_and_outputs",
    )(got, field, quotient)


def solution(mesh):
    return jax.shard_map(
        per_device,
        mesh=mesh,
        in_specs=(
            P(None, "gx", "gy"),
            P(None, None, "gx", "gy"),
            P(None, "gx", "gy"),
            P(None, ("gx", "gy")),
            P(("gx", "gy"), None),
            P(("gx", "gy")),
            P(("gx", "gy")),
            P(("gx", "gy")),
            P(None, ("gx", "gy")),
            P(("gx", "gy")),
        ),
        out_specs=(P(None, "gx", "gy"), P(("gx", "gy"), None)),
        check_vma=False,
    )
```

```python
import functools
import math

import jax
import jax.numpy as jnp
from jax import lax
from jax.experimental import pallas as pl
from jax.experimental.pallas import tpu as pltpu
from jax.sharding import PartitionSpec as P

F32 = jnp.float32
BF16 = jnp.bfloat16
PAD = 2
NOWHERE = -(1 << 20)
LANES = 128
NEAR = 16
STRIP = 40
CHUNK = 256
PARAMS = pltpu.CompilerParams(vmem_limit_bytes=24 * 1024 * 1024)

VMEM = pl.BlockSpec(memory_space=pltpu.VMEM)
SMEM = pl.BlockSpec(memory_space=pltpu.SMEM)
HBM = pl.BlockSpec(memory_space=pltpu.HBM)


def iota(shape, dim):
    return lax.broadcasted_iota(jnp.int32, shape, dim)


def float_iota(shape, dim):
    return iota(shape, dim).astype(F32)


def two_parts(value):
    high = value.astype(BF16).astype(F32)
    return high, value - high


def product(block, field):
    return [
        block(row) * field[0] + block(3 + row) * field[1] + block(6 + row) * field[2]
        for row in range(3)
    ]


def off_diagonal(block, field):
    return [
        sum(block(3 * i + row) * field[i] for i in range(3) if i != row) for row in range(3)
    ]


def masked_product(edge_ref, mask_ref, direction, field):
    mask = mask_ref[direction].astype(F32)
    return [mask * part for part in product(lambda k: edge_ref[direction, k], field)]


def rows_moved(field, edge_row, step):
    size = field.shape[0]
    at = iota(field.shape, 0)
    moved = pltpu.roll(field, step % size, 0)
    return jnp.where(at == (0 if step == 1 else size - 1), edge_row, moved)


def lanes_moved(field, edge_column, step):
    size = field.shape[1]
    at = iota(field.shape, 1)
    moved = pltpu.roll(field, step % size, 1)
    return jnp.where(at == (0 if step == 1 else size - 1), edge_column, moved)


def pack_kernel(
    count_ref, values_in, owner_in, node_in, diag_in, edge_in, mask_in, rows_out, strip_ref,
    values_ref, owner_ref, node_ref, diag_low, diag_high, edge_low, edge_high,
    mask_low, mask_high, rows_ref, arrived, left,
):
    targets = rows_ref.shape[0]
    groups = owner_ref.shape[0]
    cells_x = diag_in.shape[1]
    top = pl.ds(cells_x - 8, 8)
    copies = [
        pltpu.make_async_copy(source, target, arrived.at[k])
        for k, (source, target) in enumerate(
            (
                (owner_in, owner_ref),
                (node_in, node_ref),
                (values_in, values_ref),
                (diag_in.at[:, 0:8], diag_low),
                (diag_in.at[:, top], diag_high),
                (mask_in.at[1, 0:8], mask_low),
                (mask_in.at[:, top], mask_high),
                (edge_in.at[1, :, 0:8], edge_low),
                (edge_in.at[:, :, top], edge_high),
            )
        )
    ]
    for copy in copies:
        copy.start()
    base = 4 * groups
    for target in range(targets):
        rows_ref[target, base:, :] = jnp.zeros((NEAR, LANES), F32)
    for copy in copies[:2]:
        copy.wait()
    order = iota((groups, LANES), 0) * LANES + iota((groups, LANES), 1)
    node = node_ref[...]
    frame = cells_x + 2 * PAD
    row = owner_ref[...] * cells_x + lax.shift_right_logical(node, 7)
    row = jnp.where(order < count_ref[0], row, NOWHERE)
    column = node & (LANES - 1)
    for target in range(targets):
        line = row - (target * cells_x - PAD)
        inside = (line >= 0) & (line < frame)
        index = jnp.where(inside, line * LANES + column, -1)
        rows_ref[target, 3 * groups : 4 * groups, :] = index.astype(F32)

    copies[2].wait()
    for comp in range(3):
        value = jnp.concatenate(
            [
                values_ref[comp : comp + 1, group * LANES : (group + 1) * LANES]
                for group in range(groups)
            ],
            axis=0,
        )
        for target in range(targets):
            rows_ref[target, comp * groups : (comp + 1) * groups, :] = value
    near = pl.ds(4 * groups, NEAR)
    leaving = [
        pltpu.make_async_copy(rows_ref.at[:, part], rows_out.at[:, part], left.at[k])
        for k, part in enumerate((pl.ds(0, 4 * groups), near))
    ]
    leaving[0].start()
    for copy in copies[3:]:
        copy.wait()

    def block(edge, mask, direction, at):
        present = mask[direction, at : at + 1, :].astype(F32)
        return [edge[direction, k, at : at + 1, :] * present for k in range(9)]

    up_y, low_y = block(edge_high, mask_high, 2, 7), block(edge_high, mask_high, 3, 7)
    here = lax.axis_index("gx")

    @pl.when(here < targets - 1)
    def _():
        def put(slot, value):
            rows_ref[here + 1, base + slot : base + slot + 1, :] = value

        for k in range(3):
            put(k, diag_high[4 * k, 7:8, :])
        for k, value in enumerate(block(edge_high, mask_high, 0, 7)):
            put(3 + k, value)
        corners = jnp.zeros((1, LANES), F32)
        lane = iota((1, LANES), 1)
        for k in range(9):
            corners = jnp.where(lane == k, up_y[k][:, LANES - 1 :], corners)
            corners = jnp.where(lane == 9 + k, low_y[k][:, :1], corners)
        put(12, corners)

    @pl.when(here > 0)
    def _():
        def put(slot, value):
            rows_ref[here - 1, base + slot : base + slot + 1, :] = value

        for k in range(3):
            put(k, diag_low[4 * k, 0:1, :])
        present = mask_low[0:1, :].astype(F32)
        for k in range(9):
            put(3 + k, edge_low[k, 0:1, :] * present)

    leaving[1].start()
    later = [diag_high[k, 7:8, :] for k in range(9) if k % 4]
    later += up_y + low_y + block(edge_high, mask_high, 0, 6)
    later += [diag_high[4 * k, 6:7, :] for k in range(3)]
    for k, value in enumerate(later):
        strip_ref[k : k + 1, :] = value
    strip_ref[len(later) :, :] = jnp.zeros((STRIP - len(later), LANES), F32)
    for copy in leaving:
        copy.wait()


def stretched(row, count):
    tile = jnp.broadcast_to(row, (16, row.shape[1])).astype(BF16)
    return jnp.concatenate([tile] * (count // 16), axis=0)


def ratio(value, scale):
    return jnp.where(scale > 0.0, value / jnp.where(scale > 0.0, scale, 1.0), 0.0)


UP_X, LOW_X, INWARD, OUTWARD, WITHIN, INVERSE = 0, 3, 6, 9, 12, 15


def edge_kernel(diag_ref, edge_ref, mask_ref, inverse_ref, columns_ref):
    cells_x = diag_ref.shape[1]
    at = iota((cells_x, LANES), 1)
    sides = [jnp.zeros((cells_x, LANES), F32) for _ in range(2)]

    def put(kind, i, a, first, first_lane, last, last_lane):
        slot = 8 * (kind + i) + a
        for side, (field, lane) in enumerate(((first, first_lane), (last, last_lane))):
            sides[side] = jnp.where(at == slot, field[:, lane : lane + 1], sides[side])

    inverse = [1.0 / diag_ref[4 * c] for c in range(3)]
    end = LANES - 1
    masks = [mask_ref[direction].astype(F32) for direction in range(4)]
    for i in range(3):
        inverse_ref[i] = inverse[i]
        put(INVERSE, 0, i, inverse[i], 0, inverse[i], end)
        for a in range(3):
            up_x, low_x, up_y, low_y = (
                edge_ref[direction, 3 * i + a] * masks[direction] for direction in range(4)
            )
            put(UP_X, i, a, up_x, 0, up_x, end)
            put(LOW_X, i, a, low_x, 0, low_x, end)
            put(INWARD, i, a, low_y, 1, up_y, end - 1)
            put(OUTWARD, i, a, low_y, 0, up_y, end)
            if a != i:
                put(WITHIN, i, a, diag_ref[3 * i + a], 0, diag_ref[3 * i + a], end)
    columns_ref[...] = jnp.concatenate(sides, axis=0).T


def field_kernel(
    rows_ref, inverse_ref, columns_ref,
    field_ref, halo_ref, inner_ref, outer_ref, load_ref,
):
    senders = rows_ref.shape[0]
    groups = (rows_ref.shape[1] - NEAR) // 4
    cells_x = field_ref.shape[1]
    half = (cells_x + 2 * PAD) // 2
    own = cells_x // 2

    load_ref[...] = jnp.zeros_like(load_ref)
    here = lax.axis_index("gx")

    size = load_ref.shape[0]
    line = iota((size, LANES), 0)
    block = sum(jnp.where(line >= half * k, 1, 0) for k in range(1, 6))
    at_row = jnp.where(line < 6 * half, line - half * block, -5).astype(F32).astype(BF16)
    at_column = float_iota((2 * LANES, LANES), 0).astype(BF16)
    in_tile = float_iota((16, LANES), 0).astype(BF16)
    zero, one = jnp.zeros((), BF16), jnp.ones((), BF16)

    def one_hot(difference):
        return jnp.maximum(one - difference * difference, zero)

    def operands(sender):
        index = rows_ref[sender, 3 * groups : 4 * groups, :]
        split = float(half * LANES)
        index, shift = (
            jnp.where(index >= split, index - split, index),
            jnp.where(index >= split, float(LANES), 0.0),
        )
        place = jnp.floor(index * (1.0 / LANES))
        column = index - place * float(LANES) + shift
        parts = [
            two_parts(rows_ref[sender, c * groups : (c + 1) * groups, :]) for c in range(3)
        ]
        lefts, rights = [], []
        for group in range(groups):
            line = slice(group, group + 1)
            values = [
                stretched(parts[c][which][line], 16) for which in range(2) for c in range(3)
            ]
            tiles = []
            for first in range(0, size, 16):
                low, high = first // half, min((first + 15) // half, 5)
                tiles.append(
                    values[low]
                    if low == high
                    else jnp.where(
                        in_tile < float(half * high - first), values[low], values[high]
                    )
                )
            match = one_hot(at_row - stretched(place[line], size))
            lefts.append(match * jnp.concatenate(tiles, axis=0))
            rights.append(one_hot(at_column - stretched(column[line], 2 * LANES)))
        return lefts, rights

    together = math.gcd(senders, 4)

    def add_rows(step, carry):
        lefts, rights = [], []
        for k in range(together):
            left, right = operands(step * together + k)
            lefts += left
            rights += right
        load_ref[...] += lax.dot_general(
            jnp.concatenate(lefts, axis=1),
            jnp.concatenate(rights, axis=1),
            (((1,), (1,)), ((), ())),
            preferred_element_type=F32,
        )
        return carry

    steps = senders // together
    lax.fori_loop(0, steps, add_rows, 0, unroll=min(steps, 2))

    def load_rows(comp, first, last, second_half):
        lanes = slice(LANES, 2 * LANES) if second_half else slice(0, LANES)
        return (
            load_ref[comp * half + first : comp * half + last, lanes]
            + load_ref[(3 + comp) * half + first : (3 + comp) * half + last, lanes]
        )

    field = []
    for comp in range(3):
        load = jnp.concatenate(
            [load_rows(comp, PAD, half, False), load_rows(comp, 0, half - PAD, True)], axis=0
        )
        field.append(load * inverse_ref[comp])
        field_ref[comp] = field[comp]
    beyond = half - PAD
    near_before = [load_rows(c, PAD - 1, PAD, False) for c in range(3)]
    far_before = [load_rows(c, PAD - 2, PAD - 1, False) for c in range(3)]
    near_after = [load_rows(c, beyond, beyond + 1, True) for c in range(3)]

    base = 4 * groups

    def neighbour(sender, load):
        def entry(k):
            return rows_ref[sender, base + k : base + k + 1, :]

        inverse = [ratio(1.0, entry(k)) for k in range(3)]
        toward = [entry(3 + k) for k in range(9)]
        beside = [load[c] * inverse[c] for c in range(3)]
        return inverse, toward, beside, product(lambda k: toward[k], beside)

    lower = jnp.maximum(here - 1, 0)
    before = neighbour(lower, near_before)
    after = neighbour(jnp.minimum(here + 1, senders - 1), near_after)
    rows = before[2] + before[0] + before[3] + before[1] + far_before + after[3]
    for k, value in enumerate(rows):
        halo_ref[k : k + 1, :] = value
    lane_row = iota((1, LANES), 1)
    ends = jnp.zeros((1, LANES), F32)
    for i in range(3):
        for a in range(3):
            ends = jnp.where(lane_row == 3 * i + a, before[2][i][:, LANES - 1 :], ends)
            ends = jnp.where(lane_row == 9 + 3 * i + a, before[2][i][:, :1], ends)
    ends = ends * rows_ref[lower, base + 12 : base + 13, :]
    ends = ends + pltpu.roll(ends, LANES - 3, 1) + pltpu.roll(ends, LANES - 6, 1)

    at = iota((cells_x, LANES), 1)
    sides = []
    for edge, inside in ((0, 1), (LANES - 1, LANES - 2)):
        packed = jnp.zeros((cells_x, LANES), F32)
        for comp in range(3):
            packed = jnp.where(at == comp, field[comp][:, edge : edge + 1], packed)
            packed = jnp.where(at == 8 + comp, field[comp][:, inside : inside + 1], packed)
        sides.append(packed)
    turned = jnp.concatenate(sides, axis=0).T

    def column_product(kind, first):
        return sum(
            columns_ref[8 * (kind + i) : 8 * (kind + i) + 8, :] * turned[first + i : first + i + 1]
            for i in range(3)
        )

    def eight(rows):
        return jnp.concatenate(rows + [jnp.zeros((8 - len(rows), LANES), F32)], axis=0)

    lane = iota((8, LANES), 1)
    from_before, from_after = eight(before[3]), eight(after[3])
    from_before = jnp.where(lane == 0, from_before, pltpu.roll(from_before, cells_x + 1, 1))
    from_after = jnp.where(
        lane == LANES - 1, from_after, pltpu.roll(from_after, cells_x - 1, 1)
    )
    row = lane & (cells_x - 1)
    upward = pltpu.roll(column_product(UP_X, 0), 1, 1)
    downward = pltpu.roll(column_product(LOW_X, 0), LANES - 1, 1)
    total = (
        column_product(WITHIN, 0)
        + jnp.where(row == 0, from_before, upward)
        + jnp.where(row == cells_x - 1, from_after, downward)
        + column_product(INWARD, 8)
    )
    inverse = columns_ref[8 * INVERSE : 8 * INVERSE + 8, :]
    along_y, part = column_product(OUTWARD, 0), total * inverse
    stacked = jnp.concatenate(
        [turned[:3], along_y[:3], part[:3], inverse[:3], jnp.zeros((4, LANES), F32)], axis=0
    )

    def message(columns, end):
        at = iota((16, LANES), 1)
        line = iota((16, LANES), 0)
        columns = jnp.where(at < cells_x, columns, 0.0)
        for comp in range(3):
            columns = jnp.where(
                (line == 3 + comp) & (at == cells_x),
                ends[:, end + comp : end + comp + 1],
                columns,
            )
        return columns

    inner_ref[...], outer_ref[...] = by_parity(
        message(stacked, 9), message(pltpu.roll(stacked, cells_x, 1), 0)
    )


def bernstein(coord):
    other = 1.0 - coord
    return [
        other * other * other,
        3.0 * coord * other * other,
        3.0 * coord * coord * other,
        coord * coord * coord,
    ]


def weight_table(u, v, w):
    first, second, third = bernstein(u), bernstein(v), bernstein(w)
    line = iota((8, u.shape[1]), 0)
    inner = line & 3
    along = jnp.where(
        inner == 0,
        third[0],
        jnp.where(inner == 1, third[1], jnp.where(inner == 2, third[2], third[3])),
    )
    pair = jnp.concatenate(
        [
            jnp.where(line < 4, second[0], second[1]) * along,
            jnp.where(line < 4, second[2], second[3]) * along,
        ],
        axis=0,
    )
    return jnp.concatenate([pair * first[i] for i in range(4)], axis=0)


def tile_rows(terms):
    first_half = iota((4, LANES), 1) < LANES // 2
    rows = []
    for term in terms:
        term = term[:8] + term[8:]
        term = term + pltpu.roll(term, LANES // 2, 1)
        rows.append(jnp.where(first_half, term[:4], term[4:]))
    return jnp.concatenate(two_parts(jnp.concatenate(rows, axis=0)), axis=0).astype(BF16)


def box_matrix(tile_row, boxes):
    tiles = tile_row.shape[1]
    shape = (4 * boxes, 8 * tiles)
    column = iota((1, shape[1]), 1)
    box = jnp.zeros((1, shape[1]), jnp.int32)
    for tile in range(tiles):
        mine = lax.rem(lax.shift_right_logical(column, 2), tiles) == tile
        box = jnp.where(mine, tile_row[:, tile : tile + 1], box)
    target = 4 * box + (column & 3)
    return jnp.where(iota(shape, 0) == target, 1.0, 0.0).astype(BF16)


def by_parity(low, high):
    odd = lax.rem(lax.axis_index("gy"), 2) == 1
    return jnp.where(odd, high, low), jnp.where(odd, low, high)


def quotient_before(halo_ref, strip_ref, before_ref, entering):
    def rows(ref, first, count):
        return [ref[first + k : first + k + 1, :] for k in range(count)]

    beside, inverse = rows(halo_ref, 0, 3), rows(halo_ref, 3, 3)
    far_load, within = rows(halo_ref, 18, 3), rows(strip_ref, 0, 6)
    far_scale = rows(strip_ref, 33, 3)
    far = [ratio(far_load[c], far_scale[c]) for c in range(3)]
    whole_block = [None, *within[:3], None, *within[3:], None]
    total = off_diagonal(lambda k: whole_block[k], beside)
    from_far = product(lambda k: strip_ref[24 + k : 25 + k, :], far)
    up_y = product(lambda k: strip_ref[6 + k : 7 + k, :], beside)
    low_y = product(lambda k: strip_ref[15 + k : 16 + k, :], beside)
    for c in range(3):
        before_ref[c : c + 1, :] = inverse[c] * (
            total[c]
            + from_far[c]
            + entering[c]
            + lanes_moved(up_y[c], 0.0, 1)
            + lanes_moved(low_y[c], 0.0, -1)
        )
    before_ref[3:, :] = jnp.zeros((before_ref.shape[0] - 3, LANES), F32)


def box_kernel(
    tile_ref, field_ref, node_ref, param_ref, halo_ref, strip_ref, diag_ref, edge_ref,
    mask_ref, inverse_ref,
    part_ref, box_ref, adjoint_ref, before_ref, matrix_ref, weights_ref, columns_ref,
    *, tile_points,
):
    cells_x = field_ref.shape[1]
    own = cells_x // 2
    field = [field_ref[c] for c in range(3)]
    part = off_diagonal(lambda k: diag_ref[k], field)
    up_x = masked_product(edge_ref, mask_ref, 0, field)
    low_x = masked_product(edge_ref, mask_ref, 1, field)
    up_y = masked_product(edge_ref, mask_ref, 2, field)
    low_y = masked_product(edge_ref, mask_ref, 3, field)
    for c in range(3):
        part[c] = inverse_ref[c] * (
            part[c]
            + rows_moved(up_x[c], halo_ref[6 + c : 7 + c, :], 1)
            + rows_moved(low_x[c], halo_ref[21 + c : 22 + c, :], -1)
            + lanes_moved(up_y[c], 0.0, 1)
            + lanes_moved(low_y[c], 0.0, -1)
        )
        part_ref[c] = part[c]
    quotient_before(halo_ref, strip_ref, before_ref, [p[:1] for p in low_x])
    order = [field[0], part[0], field[2], field[1], part[1], part[2]]
    folded = [two_parts(jnp.concatenate([f[:own], f[own:]], axis=1)) for f in order]
    table = jnp.concatenate(
        [folded[f][which] for which in range(2) for f in range(6)], axis=0
    ).astype(BF16)
    points = param_ref.shape[1]
    pieces = CHUNK // LANES
    zero, one = jnp.zeros((), BF16), jnp.ones((), BF16)
    at_node = float_iota((2 * LANES, CHUNK), 0).astype(BF16)
    nothing = jnp.zeros((1, CHUNK), F32)
    highs, lows = [], []
    for chunk in range(points // CHUNK):
        node = jnp.concatenate(
            [node_ref[chunk * pieces + k : chunk * pieces + k + 1, :] for k in range(pieces)],
            axis=1,
        )
        row = lax.shift_right_logical(node, 7)
        column = node & (LANES - 1)
        lanes = slice(chunk * CHUNK, (chunk + 1) * CHUNK)
        at_edge = jnp.where(
            column == 0, row, jnp.where(column == LANES - 1, row + cells_x, -1)
        ).astype(F32)
        columns_ref[:, lanes] = jnp.where(
            at_node[: 2 * cells_x] == stretched(at_edge, 2 * cells_x), one, zero
        )
        place = column + jnp.where(row >= own, LANES, 0)
        row = jnp.where(row >= own, row - own, row)
        pick = jnp.where(at_node == stretched(place.astype(F32), 2 * LANES), one, zero)
        read = jnp.dot(table, pick, preferred_element_type=F32)
        read = read[: 6 * own] + read[6 * own :]
        here = iota((own, CHUNK), 0) == row
        values = [
            jnp.sum(
                jnp.where(here, read[f * own : (f + 1) * own], 0.0), axis=0, keepdims=True
            )
            for f in range(6)
        ]
        high, low = two_parts(
            jnp.concatenate(values[:3] + [nothing] + values[3:] + [nothing], axis=0)
        )
        highs.append(high)
        lows.append(low)
        weights = two_parts(
            weight_table(param_ref[0:1, lanes], param_ref[1:2, lanes], param_ref[2:3, lanes])
        )
        for k in range(CHUNK // tile_points):
            tile = slice(k * tile_points, (k + 1) * tile_points)
            sides = jnp.concatenate([weights[0][:, tile], weights[1][:, tile]], axis=0)
            weights_ref[chunk * (CHUNK // tile_points) + k] = sides.T.astype(BF16)
    both = jnp.concatenate(
        [jnp.concatenate(highs, axis=1), jnp.concatenate(lows, axis=1)], axis=0
    ).astype(BF16)
    matrix_ref[...] = box_matrix(tile_ref[...], matrix_ref.shape[0] // 4)
    tiles = tile_ref.shape[1]
    terms = [
        jnp.dot(
            both[:, tile * tile_points : (tile + 1) * tile_points],
            weights_ref[tile],
            preferred_element_type=F32,
        )
        for tile in range(tiles)
    ]
    box_ref[...] = jnp.dot(matrix_ref[...], tile_rows(terms), preferred_element_type=F32)
    low_half = iota((2 * cells_x, LANES), 1) < LANES // 2
    for tile in range(tiles):
        lanes = slice(tile * tile_points, (tile + 1) * tile_points)
        term = jnp.dot(
            columns_ref[:, lanes], weights_ref[tile], preferred_element_type=F32
        )
        high, low = two_parts(term + pltpu.roll(term, LANES // 2, 1))
        adjoint_ref[:, tile * LANES : (tile + 1) * LANES] = jnp.where(
            low_half, high, low
        ).astype(BF16)


def sums_kernel(
    from_inner_ref, from_outer_ref, inner_ref, outer_ref, field_ref, part_ref, halo_ref,
    diag_ref, edge_ref, mask_ref, box_ref, adjoint_ref, before_ref, matrix_ref,
    quotient_ref, out_ref,
):
    cells_x = field_ref.shape[1]
    targets = out_ref.shape[0]

    from_low, from_high = by_parity(from_inner_ref[...], from_outer_ref[...])
    first, last = by_parity(inner_ref[...], outer_ref[...])

    lane_row = iota((1, LANES), 1)
    shares, edges = [], []
    for arrived, own in ((from_low, first), (from_high, last)):
        def row(source, slot, c):
            return source[3 * slot + c : 3 * slot + c + 1]

        shares.append([row(arrived, 1, c) * row(own, 3, c) for c in range(3)])
        edges.append(
            [row(arrived, 2, c) + row(arrived, 3, c) * row(own, 1, c) for c in range(3)]
        )

    def turned(columns, share, edge):
        kept = [
            jnp.where(lane_row < cells_x, share[c], columns[3 + c : 4 + c]) for c in range(3)
        ]
        rest = jnp.zeros((LANES - 9, LANES), F32)
        return jnp.concatenate([columns[:3], *kept, *edge, rest], axis=0).T

    low = turned(from_low, shares[0], edges[0])
    high = turned(from_high, shares[1], edges[1])
    lane = iota((cells_x, LANES), 1)

    def column(source, slot, comp):
        return source[:cells_x, 3 * slot + comp : 3 * slot + comp + 1]

    field = [field_ref[c] for c in range(3)]
    scale = [diag_ref[4 * c] for c in range(3)]
    quotient, low_edge, high_edge = [], [], []
    for c in range(3):
        entering = jnp.where(
            lane == 0,
            column(low, 1, c),
            jnp.where(lane == LANES - 1, column(high, 1, c), 0.0),
        )
        quotient.append(part_ref[c] + entering)
        low_edge.append(column(low, 2, c))
        high_edge.append(column(high, 2, c))
    for c in range(3):
        quotient_ref[c] = quotient[c]
    before, before_quotient = [], []
    for c in range(3):
        entering = jnp.where(
            lane_row == 0,
            low[cells_x : cells_x + 1, 3 + c : 4 + c],
            jnp.where(lane_row == LANES - 1, high[cells_x : cells_x + 1, 3 + c : 4 + c], 0.0),
        )
        before.append(halo_ref[c : c + 1, :])
        before_quotient.append(
            before_ref[c : c + 1, :] + entering * halo_ref[3 + c : 4 + c, :]
        )

    first_sum = sum(field[c] * scale[c] * field[c] for c in range(3))
    second_sum = sum(field[c] * scale[c] * quotient[c] for c in range(3))
    third_sum = sum(quotient[c] * scale[c] * quotient[c] for c in range(3))
    within = off_diagonal(lambda k: diag_ref[k], quotient)
    fourth_sum = sum(within[c] * field[c] for c in range(3))
    fifth_sum = sum(within[c] * quotient[c] for c in range(3))
    at_row = iota((cells_x, LANES), 0)
    moves = (
        (pltpu.roll, 1, 0, at_row == 0),
        (pltpu.roll, cells_x - 1, 0, at_row == cells_x - 1),
        (pltpu.roll, 1, 1, lane == 0),
        (pltpu.roll, LANES - 1, 1, lane == LANES - 1),
    )
    extra = [0.0, 0.0]
    sides = [0.0, 0.0]
    for direction, (roll, step, dim, edge) in enumerate(moves):
        moving = masked_product(edge_ref, mask_ref, direction, quotient)
        for c in range(3):
            moved = jnp.where(edge, 0.0, roll(moving[c], step, dim))
            fourth_sum = fourth_sum + moved * field[c]
            fifth_sum = fifth_sum + moved * quotient[c]
            if direction == 1:
                extra[0] += moving[c][:1] * before[c]
                extra[1] += moving[c][:1] * before_quotient[c]
            elif direction == 2:
                sides[0] += moving[c][:, LANES - 1 :] * column(high, 0, c)
                sides[1] += moving[c][:, LANES - 1 :] * high_edge[c]
            elif direction == 3:
                sides[0] += moving[c][:, :1] * column(low, 0, c)
                sides[1] += moving[c][:, :1] * low_edge[c]
    incoming = product(lambda k: halo_ref[9 + k : 10 + k, :], before_quotient)
    extra[0] += sum(incoming[c] * field[c][:1] for c in range(3))
    extra[1] += sum(incoming[c] * quotient[c][:1] for c in range(3))
    fourth_sum = fourth_sum + jnp.where(lane == 0, sides[0], 0.0)
    fifth_sum = fifth_sum + jnp.where(lane == 0, sides[1], 0.0)
    extra = [0.0, 0.0, 0.0, extra[0], extra[1]]
    sums = jnp.zeros((1, LANES), F32)
    for k, value in enumerate((first_sum, second_sum, third_sum, fourth_sum, fifth_sum)):
        line = jnp.sum(value, axis=0, keepdims=True) + extra[k]
        sums = jnp.where(lane_row == k, jnp.sum(line, axis=1, keepdims=True), sums)

    added = [
        jnp.where(lane_row < cells_x, shares[0][c], pltpu.roll(shares[1][c], cells_x, 1))
        for c in range(3)
    ]
    none = jnp.zeros((1, LANES), F32)
    added = jnp.concatenate(
        [none, added[0], none, none, none, added[1], added[2], none], axis=0
    )
    added = jnp.concatenate(two_parts(added), axis=0).astype(BF16)
    terms = jnp.dot(added, adjoint_ref[...], preferred_element_type=F32)
    terms = [
        terms[:, first : first + LANES] for first in range(0, terms.shape[1], LANES)
    ]
    total = box_ref[...] + jnp.dot(
        matrix_ref[...], tile_rows(terms), preferred_element_type=F32
    )
    total = jnp.where((iota(total.shape, 0) & 3) == 3, sums, total)
    for box in range(targets):
        out_ref[box] = total[4 * box : 4 * box + 4]


def result_kernel(got_ref, field_ref, quotient_ref, solution_ref, gradient_ref):
    total = jnp.sum(got_ref[...], axis=0)
    rho, a, b, t, u = [total[3:4, k : k + 1] for k in range(5)]
    norm = rho + a
    by_rho, by_norm = 1.0 / rho, 1.0 / norm
    ratio, step = a * by_rho, rho * by_norm
    rest = jnp.maximum(b - a * ratio, 0.0)
    beta = step * step * rest * by_rho
    rest_image = (b + u) - ratio * (a + b + a + t) + ratio * ratio * norm
    cross = (a + t) - ratio * norm
    curve = step * step * rest_image - step * beta * (rest + cross) + beta * beta * norm
    second = jnp.where(
        curve > 0.0, step * step * rest / jnp.where(curve > 0.0, curve, 1.0), 0.0
    )
    second = jnp.minimum(second, 16.0)
    of_field = step + second * (beta + step * ratio)
    of_quotient = -(step * second)
    for c in range(3):
        solution_ref[c] = of_field * field_ref[c] + of_quotient * quotient_ref[c]
    gradient_ref[:, :LANES] = of_field * total[0:1] + of_quotient * total[1:2]
    gradient_ref[:, LANES:] = (
        of_field * total[2:3, : LANES // 2] + of_quotient * total[2:3, LANES // 2 :]
    )


def per_device(
    diag_blocks, edge_blocks, edge_mask, src_values, src_owner, src_node, src_count,
    surf_node, surf_param, tile_box,
):
    cells_x, cells_y = diag_blocks.shape[1:]
    width_gx, width_gy = lax.axis_size("gx"), lax.axis_size("gy")
    devices = width_gx * width_gy
    groups = src_node.shape[0] // LANES
    whole = functools.partial(jax.ShapeDtypeStruct, dtype=F32)

    cells = 4 * groups + NEAR

    def kept(array):
        return pltpu.with_memory_space_constraint(array, pltpu.HBM)

    i32 = jnp.int32
    rows, strip = pl.pallas_call(
        pack_kernel,
        in_specs=[SMEM] + [HBM] * 6,
        out_specs=[HBM, VMEM],
        out_shape=[
            pltpu.HBM((width_gx, cells, LANES), F32), pltpu.VMEM((STRIP, LANES), F32)
        ],
        scratch_shapes=[
            pltpu.VMEM(src_values.shape, F32),
            pltpu.VMEM((groups, LANES), i32),
            pltpu.VMEM((groups, LANES), i32),
            pltpu.VMEM((9, 8, cells_y), F32),
            pltpu.VMEM((9, 8, cells_y), F32),
            pltpu.VMEM((9, 8, cells_y), F32),
            pltpu.VMEM((4, 9, 8, cells_y), F32),
            pltpu.VMEM((8, cells_y), i32),
            pltpu.VMEM((4, 8, cells_y), i32),
            pltpu.VMEM((width_gx, cells, LANES), F32),
            pltpu.SemaphoreType.DMA((9,)),
            pltpu.SemaphoreType.DMA((2,)),
        ],
        compiler_params=PARAMS,
        name="pack_rows_and_edges",
    )(
        src_count, kept(src_values),
        kept(src_owner.reshape(groups, LANES)), kept(src_node.reshape(groups, LANES)),
        kept(diag_blocks), kept(edge_blocks), kept(edge_mask),
    )
    rows = lax.all_to_all(rows, "gx", split_axis=0, concat_axis=0, tiled=True)
    strip = lax.ppermute(strip, "gx", [(i, i + 1) for i in range(width_gx - 1)])

    nodes = (3, cells_x, cells_y)
    inverse, columns = pl.pallas_call(
        edge_kernel,
        in_specs=[VMEM] * 3,
        out_specs=[VMEM] * 2,
        out_shape=[whole(nodes), whole((LANES, LANES))],
        compiler_params=PARAMS,
        cost_estimate=pl.CostEstimate(
            flops=10**8, bytes_accessed=4 * 10**6, transcendentals=0
        ),
        name="edge_columns",
    )(diag_blocks, edge_blocks, edge_mask)

    size = -(-3 * (cells_x + 2 * PAD) // 16) * 16
    field, halo, inner, outer = pl.pallas_call(
        field_kernel,
        in_specs=[VMEM] * 3,
        out_specs=[VMEM] * 4,
        out_shape=[
            whole(nodes), whole((24, cells_y)), whole((16, LANES)), whole((16, LANES)),
        ],
        scratch_shapes=[pltpu.VMEM((size, 2 * LANES), F32)],
        compiler_params=PARAMS,
        name="load_and_first_product",
    )(rows, inverse, columns)
    def swapped(columns, first):
        low = range(first, width_gy - 1, 2)
        pairs = [(i, i + 1) for i in low] + [(i + 1, i) for i in low]
        return lax.ppermute(columns, "gy", pairs)

    from_inner, from_outer = swapped(inner, 1), swapped(outer, 0)
    points, tiles = surf_node.shape[0], tile_box.shape[0]
    part, box_part, adjoint, before, matrix = pl.pallas_call(
        functools.partial(box_kernel, tile_points=points // tiles),
        in_specs=[VMEM] * 10,
        out_specs=[VMEM] * 5,
        out_shape=[
            whole(nodes),
            whole((4 * devices, LANES)),
            jax.ShapeDtypeStruct((2 * cells_x, tiles * LANES), BF16),
            whole((8, LANES)),
            jax.ShapeDtypeStruct((4 * devices, 8 * tiles), BF16),
        ],
        scratch_shapes=[
            pltpu.VMEM((tiles, points // tiles, LANES), BF16),
            pltpu.VMEM((2 * cells_x, points), BF16),
        ],
        compiler_params=PARAMS,
        cost_estimate=pl.CostEstimate(
            flops=10**9, bytes_accessed=4 * 10**6, transcendentals=0
        ),
        name="box_parts",
    )(
        tile_box.reshape(1, tiles), field, surf_node.reshape(points // LANES, LANES),
        surf_param, halo, strip, diag_blocks, edge_blocks, edge_mask, inverse,
    )

    quotient, partial = pl.pallas_call(
        sums_kernel,
        in_specs=[VMEM] * 14,
        out_specs=[VMEM] * 2,
        out_shape=[whole(nodes), whole((devices, 4, LANES))],
        compiler_params=PARAMS,
        name="sums_and_halo_parts",
    )(
        from_inner, from_outer, inner, outer, field, part, halo, diag_blocks, edge_blocks, edge_mask,
        box_part, adjoint, before, matrix,
    )
    got = lax.all_to_all(partial, ("gx", "gy"), split_axis=0, concat_axis=0, tiled=True)
    return pl.pallas_call(
        result_kernel,
        in_specs=[VMEM] * 3,
        out_specs=[VMEM] * 2,
        out_shape=[whole(nodes), whole((1, 192))],
        compiler_params=PARAMS,
        name="steps_and_outputs",
    )(got, field, quotient)


def solution(mesh):
    return jax.shard_map(
        per_device,
        mesh=mesh,
        in_specs=(
            P(None, "gx", "gy"),
            P(None, None, "gx", "gy"),
            P(None, "gx", "gy"),
            P(None, ("gx", "gy")),
            P(("gx", "gy"), None),
            P(("gx", "gy")),
            P(("gx", "gy")),
            P(("gx", "gy")),
            P(None, ("gx", "gy")),
            P(("gx", "gy")),
        ),
        out_specs=(P(None, "gx", "gy"), P(("gx", "gy"), None)),
        check_vma=False,
    )
```

```python
import functools
import math

import jax
import jax.numpy as jnp
from jax import lax
from jax.experimental import pallas as pl
from jax.experimental.pallas import tpu as pltpu
from jax.sharding import PartitionSpec as P

F32 = jnp.float32
BF16 = jnp.bfloat16
PAD = 2
NOWHERE = -(1 << 20)
LANES = 128
NEAR = 16
STRIP = 40
CHUNK = 256
PARAMS = pltpu.CompilerParams(vmem_limit_bytes=24 * 1024 * 1024)

VMEM = pl.BlockSpec(memory_space=pltpu.VMEM)
SMEM = pl.BlockSpec(memory_space=pltpu.SMEM)
HBM = pl.BlockSpec(memory_space=pltpu.HBM)


def iota(shape, dim):
    return lax.broadcasted_iota(jnp.int32, shape, dim)


def float_iota(shape, dim):
    return iota(shape, dim).astype(F32)


def two_parts(value):
    high = value.astype(BF16).astype(F32)
    return high, value - high


def product(block, field):
    return [
        block(row) * field[0] + block(3 + row) * field[1] + block(6 + row) * field[2]
        for row in range(3)
    ]


def off_diagonal(block, field):
    return [
        sum(block(3 * i + row) * field[i] for i in range(3) if i != row) for row in range(3)
    ]


def masked_product(edge_ref, mask_ref, direction, field):
    mask = mask_ref[direction].astype(F32)
    return [mask * part for part in product(lambda k: edge_ref[direction, k], field)]


def rows_moved(field, edge_row, step):
    size = field.shape[0]
    at = iota(field.shape, 0)
    moved = pltpu.roll(field, step % size, 0)
    return jnp.where(at == (0 if step == 1 else size - 1), edge_row, moved)


def lanes_moved(field, edge_column, step):
    size = field.shape[1]
    at = iota(field.shape, 1)
    moved = pltpu.roll(field, step % size, 1)
    return jnp.where(at == (0 if step == 1 else size - 1), edge_column, moved)


def pack_kernel(
    count_ref, values_in, owner_in, node_in, diag_in, edge_in, mask_in, rows_out,
    values_ref, owner_ref, node_ref, diag_low, diag_high, edge_low, edge_high, side_high,
    mask_low, mask_high, rows_ref, arrived, left,
):
    targets = rows_ref.shape[0]
    groups = owner_ref.shape[0]
    cells_x = diag_in.shape[1]
    top = pl.ds(cells_x - 8, 8)
    pieces = [
        (owner_in, owner_ref),
        (node_in, node_ref),
        (values_in, values_ref),
        (edge_in.at[pl.ds(2, 2), :, top], side_high),
        (edge_in.at[0, :, top], edge_high),
        (edge_in.at[1, :, 0:8], edge_low),
        (mask_in.at[:, top], mask_high),
        (mask_in.at[1, 0:8], mask_low),
    ]
    for k in range(3):
        pieces.append((diag_in.at[4 * k, top], diag_high.at[k]))
        pieces.append((diag_in.at[4 * k, 0:8], diag_low.at[k]))
    copies = [
        pltpu.make_async_copy(source, target, arrived.at[k])
        for k, (source, target) in enumerate(pieces)
    ]
    for copy in copies:
        copy.start()
    base = 4 * groups
    for target in range(targets):
        rows_ref[target, base:, :] = jnp.zeros((NEAR, LANES), F32)
    for copy in copies[:2]:
        copy.wait()
    order = iota((groups, LANES), 0) * LANES + iota((groups, LANES), 1)
    node = node_ref[...]
    frame = cells_x + 2 * PAD
    row = owner_ref[...] * cells_x + lax.shift_right_logical(node, 7)
    row = jnp.where(order < count_ref[0], row, NOWHERE)
    column = node & (LANES - 1)
    for target in range(targets):
        line = row - (target * cells_x - PAD)
        inside = (line >= 0) & (line < frame)
        index = jnp.where(inside, line * LANES + column, -1)
        rows_ref[target, 3 * groups : 4 * groups, :] = index.astype(F32)

    copies[2].wait()
    for comp in range(3):
        value = jnp.concatenate(
            [
                values_ref[comp : comp + 1, group * LANES : (group + 1) * LANES]
                for group in range(groups)
            ],
            axis=0,
        )
        for target in range(targets):
            rows_ref[target, comp * groups : (comp + 1) * groups, :] = value
    near = pl.ds(4 * groups, NEAR)
    leaving = [
        pltpu.make_async_copy(rows_ref.at[:, part], rows_out.at[:, part], left.at[k])
        for k, part in enumerate((pl.ds(0, 4 * groups), near))
    ]
    leaving[0].start()
    for copy in copies[3:]:
        copy.wait()

    here = lax.axis_index("gx")

    def block(edge, mask):
        present = mask.astype(F32)
        return [edge(k) * present for k in range(9)]

    @pl.when(here < targets - 1)
    def _():
        def put(slot, value):
            rows_ref[here + 1, base + slot : base + slot + 1, :] = value

        for k in range(3):
            put(k, diag_high[k, 7:8, :])
        toward = block(lambda k: edge_high[k, 7:8, :], mask_high[0, 7:8, :])
        up_y = block(lambda k: side_high[0, k, 7:8, :], mask_high[2, 7:8, :])
        low_y = block(lambda k: side_high[1, k, 7:8, :], mask_high[3, 7:8, :])
        corners = jnp.zeros((1, LANES), F32)
        lane = iota((1, LANES), 1)
        for k in range(9):
            put(3 + k, toward[k])
            corners = jnp.where(lane == k, up_y[k][:, LANES - 1 :], corners)
            corners = jnp.where(lane == 9 + k, low_y[k][:, :1], corners)
        put(12, corners)

    @pl.when(here > 0)
    def _():
        def put(slot, value):
            rows_ref[here - 1, base + slot : base + slot + 1, :] = value

        for k in range(3):
            put(k, diag_low[k, 0:1, :])
        for k, value in enumerate(block(lambda k: edge_low[k, 0:1, :], mask_low[0:1, :])):
            put(3 + k, value)

    leaving[1].start()
    for copy in leaving:
        copy.wait()


def stretched(row, count):
    tile = jnp.broadcast_to(row, (16, row.shape[1])).astype(BF16)
    return jnp.concatenate([tile] * (count // 16), axis=0)


def ratio(value, scale):
    return jnp.where(scale > 0.0, value / jnp.where(scale > 0.0, scale, 1.0), 0.0)


UP_X, LOW_X, INWARD, OUTWARD, WITHIN, INVERSE = 0, 3, 6, 9, 12, 15


def edge_kernel(diag_ref, edge_ref, mask_ref, inverse_ref, columns_ref, strip_ref):
    cells_x = diag_ref.shape[1]
    last = cells_x - 1
    strip = [diag_ref[k, last:, :] for k in range(9) if k % 4]
    for direction, at in ((2, last), (3, last), (0, last - 1)):
        present = mask_ref[direction, at : at + 1, :].astype(F32)
        strip += [edge_ref[direction, k, at : at + 1, :] * present for k in range(9)]
    strip += [diag_ref[4 * k, last - 1 : last, :] for k in range(3)]
    for k, value in enumerate(strip):
        strip_ref[k : k + 1, :] = value
    strip_ref[len(strip) :, :] = jnp.zeros((STRIP - len(strip), LANES), F32)
    at = iota((cells_x, LANES), 1)
    sides = [jnp.zeros((cells_x, LANES), F32) for _ in range(2)]

    def put(kind, i, a, first, first_lane, last, last_lane):
        slot = 8 * (kind + i) + a
        for side, (field, lane) in enumerate(((first, first_lane), (last, last_lane))):
            sides[side] = jnp.where(at == slot, field[:, lane : lane + 1], sides[side])

    inverse = [1.0 / diag_ref[4 * c] for c in range(3)]
    end = LANES - 1
    masks = [mask_ref[direction].astype(F32) for direction in range(4)]
    for i in range(3):
        inverse_ref[i] = inverse[i]
        put(INVERSE, 0, i, inverse[i], 0, inverse[i], end)
        for a in range(3):
            up_x, low_x, up_y, low_y = (
                edge_ref[direction, 3 * i + a] * masks[direction] for direction in range(4)
            )
            put(UP_X, i, a, up_x, 0, up_x, end)
            put(LOW_X, i, a, low_x, 0, low_x, end)
            put(INWARD, i, a, low_y, 1, up_y, end - 1)
            put(OUTWARD, i, a, low_y, 0, up_y, end)
            if a != i:
                put(WITHIN, i, a, diag_ref[3 * i + a], 0, diag_ref[3 * i + a], end)
    columns_ref[...] = jnp.concatenate(sides, axis=0).T


def field_kernel(
    rows_ref, inverse_ref, columns_ref,
    field_ref, halo_ref, inner_ref, outer_ref, load_ref,
):
    senders = rows_ref.shape[0]
    groups = (rows_ref.shape[1] - NEAR) // 4
    cells_x = field_ref.shape[1]
    half = (cells_x + 2 * PAD) // 2
    own = cells_x // 2

    load_ref[...] = jnp.zeros_like(load_ref)
    here = lax.axis_index("gx")

    size = load_ref.shape[0]
    line = iota((size, LANES), 0)
    block = sum(jnp.where(line >= half * k, 1, 0) for k in range(1, 6))
    at_row = jnp.where(line < 6 * half, line - half * block, -5).astype(F32).astype(BF16)
    at_column = float_iota((2 * LANES, LANES), 0).astype(BF16)
    in_tile = float_iota((16, LANES), 0).astype(BF16)
    zero, one = jnp.zeros((), BF16), jnp.ones((), BF16)

    def operands(sender):
        index = rows_ref[sender, 3 * groups : 4 * groups, :]
        split = float(half * LANES)
        index, shift = (
            jnp.where(index >= split, index - split, index),
            jnp.where(index >= split, float(LANES), 0.0),
        )
        place = jnp.floor(index * (1.0 / LANES))
        column = index - place * float(LANES) + shift
        parts = [
            two_parts(rows_ref[sender, c * groups : (c + 1) * groups, :]) for c in range(3)
        ]
        lefts, rights = [], []
        for group in range(groups):
            line = slice(group, group + 1)
            values = [
                stretched(parts[c][which][line], 16) for which in range(2) for c in range(3)
            ]
            tiles = []
            for first in range(0, size, 16):
                low, high = first // half, min((first + 15) // half, 5)
                tiles.append(
                    values[low]
                    if low == high
                    else jnp.where(
                        in_tile < float(half * high - first), values[low], values[high]
                    )
                )
            match = at_row == stretched(place[line], size)
            lefts.append(jnp.where(match, jnp.concatenate(tiles, axis=0), zero))
            rights.append(
                jnp.where(at_column == stretched(column[line], 2 * LANES), one, zero)
            )
        return lefts, rights

    together = math.gcd(senders, 4)

    def add_rows(step, carry):
        lefts, rights = [], []
        for k in range(together):
            left, right = operands(step * together + k)
            lefts += left
            rights += right
        load_ref[...] += lax.dot_general(
            jnp.concatenate(lefts, axis=1),
            jnp.concatenate(rights, axis=1),
            (((1,), (1,)), ((), ())),
            preferred_element_type=F32,
        )
        return carry

    steps = senders // together
    lax.fori_loop(0, steps, add_rows, 0, unroll=min(steps, 2))

    def load_rows(comp, first, last, second_half):
        lanes = slice(LANES, 2 * LANES) if second_half else slice(0, LANES)
        return (
            load_ref[comp * half + first : comp * half + last, lanes]
            + load_ref[(3 + comp) * half + first : (3 + comp) * half + last, lanes]
        )

    field = []
    for comp in range(3):
        load = jnp.concatenate(
            [load_rows(comp, PAD, half, False), load_rows(comp, 0, half - PAD, True)], axis=0
        )
        field.append(load * inverse_ref[comp])
        field_ref[comp] = field[comp]
    beyond = half - PAD
    near_before = [load_rows(c, PAD - 1, PAD, False) for c in range(3)]
    far_before = [load_rows(c, PAD - 2, PAD - 1, False) for c in range(3)]
    near_after = [load_rows(c, beyond, beyond + 1, True) for c in range(3)]

    base = 4 * groups

    def neighbour(sender, load):
        def entry(k):
            return rows_ref[sender, base + k : base + k + 1, :]

        inverse = [ratio(1.0, entry(k)) for k in range(3)]
        toward = [entry(3 + k) for k in range(9)]
        beside = [load[c] * inverse[c] for c in range(3)]
        return inverse, toward, beside, product(lambda k: toward[k], beside)

    lower = jnp.maximum(here - 1, 0)
    before = neighbour(lower, near_before)
    after = neighbour(jnp.minimum(here + 1, senders - 1), near_after)
    rows = before[2] + before[0] + before[3] + before[1] + far_before + after[3]
    for k, value in enumerate(rows):
        halo_ref[k : k + 1, :] = value
    lane_row = iota((1, LANES), 1)
    ends = jnp.zeros((1, LANES), F32)
    for i in range(3):
        for a in range(3):
            ends = jnp.where(lane_row == 3 * i + a, before[2][i][:, LANES - 1 :], ends)
            ends = jnp.where(lane_row == 9 + 3 * i + a, before[2][i][:, :1], ends)
    ends = ends * rows_ref[lower, base + 12 : base + 13, :]
    ends = ends + pltpu.roll(ends, LANES - 3, 1) + pltpu.roll(ends, LANES - 6, 1)

    at = iota((cells_x, LANES), 1)
    sides = []
    for edge, inside in ((0, 1), (LANES - 1, LANES - 2)):
        packed = jnp.zeros((cells_x, LANES), F32)
        for comp in range(3):
            packed = jnp.where(at == comp, field[comp][:, edge : edge + 1], packed)
            packed = jnp.where(at == 8 + comp, field[comp][:, inside : inside + 1], packed)
        sides.append(packed)
    turned = jnp.concatenate(sides, axis=0).T

    def column_product(kind, first):
        return sum(
            columns_ref[8 * (kind + i) : 8 * (kind + i) + 8, :] * turned[first + i : first + i + 1]
            for i in range(3)
        )

    def eight(rows):
        return jnp.concatenate(rows + [jnp.zeros((8 - len(rows), LANES), F32)], axis=0)

    lane = iota((8, LANES), 1)
    from_before, from_after = eight(before[3]), eight(after[3])
    from_before = jnp.where(lane == 0, from_before, pltpu.roll(from_before, cells_x + 1, 1))
    from_after = jnp.where(
        lane == LANES - 1, from_after, pltpu.roll(from_after, cells_x - 1, 1)
    )
    row = lane & (cells_x - 1)
    upward = pltpu.roll(column_product(UP_X, 0), 1, 1)
    downward = pltpu.roll(column_product(LOW_X, 0), LANES - 1, 1)
    total = (
        column_product(WITHIN, 0)
        + jnp.where(row == 0, from_before, upward)
        + jnp.where(row == cells_x - 1, from_after, downward)
        + column_product(INWARD, 8)
    )
    inverse = columns_ref[8 * INVERSE : 8 * INVERSE + 8, :]
    along_y, part = column_product(OUTWARD, 0), total * inverse
    stacked = jnp.concatenate(
        [turned[:3], along_y[:3], part[:3], inverse[:3], jnp.zeros((4, LANES), F32)], axis=0
    )

    def message(columns, end):
        at = iota((16, LANES), 1)
        line = iota((16, LANES), 0)
        columns = jnp.where(at < cells_x, columns, 0.0)
        for comp in range(3):
            columns = jnp.where(
                (line == 3 + comp) & (at == cells_x),
                ends[:, end + comp : end + comp + 1],
                columns,
            )
        return columns

    inner_ref[...], outer_ref[...] = by_parity(
        message(stacked, 9), message(pltpu.roll(stacked, cells_x, 1), 0)
    )


def bernstein(coord):
    other = 1.0 - coord
    return [
        other * other * other,
        3.0 * coord * other * other,
        3.0 * coord * coord * other,
        coord * coord * coord,
    ]


def weight_table(u, v, w):
    first, second, third = bernstein(u), bernstein(v), bernstein(w)
    line = iota((8, u.shape[1]), 0)
    inner = line & 3
    along = jnp.where(
        inner == 0,
        third[0],
        jnp.where(inner == 1, third[1], jnp.where(inner == 2, third[2], third[3])),
    )
    pair = jnp.concatenate(
        [
            jnp.where(line < 4, second[0], second[1]) * along,
            jnp.where(line < 4, second[2], second[3]) * along,
        ],
        axis=0,
    )
    return jnp.concatenate([pair * first[i] for i in range(4)], axis=0)


def tile_rows(terms):
    first_half = iota((4, LANES), 1) < LANES // 2
    rows = []
    for term in terms:
        term = term[:8] + term[8:]
        term = term + pltpu.roll(term, LANES // 2, 1)
        rows.append(jnp.where(first_half, term[:4], term[4:]))
    return jnp.concatenate(two_parts(jnp.concatenate(rows, axis=0)), axis=0).astype(BF16)


def box_matrix(tile_row, boxes):
    tiles = tile_row.shape[1]
    shape = (4 * boxes, 8 * tiles)
    column = iota((1, shape[1]), 1)
    box = jnp.zeros((1, shape[1]), jnp.int32)
    for tile in range(tiles):
        mine = lax.rem(lax.shift_right_logical(column, 2), tiles) == tile
        box = jnp.where(mine, tile_row[:, tile : tile + 1], box)
    target = 4 * box + (column & 3)
    return jnp.where(iota(shape, 0) == target, 1.0, 0.0).astype(BF16)


def by_parity(low, high):
    odd = lax.rem(lax.axis_index("gy"), 2) == 1
    return jnp.where(odd, high, low), jnp.where(odd, low, high)


def quotient_before(halo_ref, strip_ref, before_ref, entering):
    def rows(ref, first, count):
        return [ref[first + k : first + k + 1, :] for k in range(count)]

    beside, inverse = rows(halo_ref, 0, 3), rows(halo_ref, 3, 3)
    far_load, within = rows(halo_ref, 18, 3), rows(strip_ref, 0, 6)
    far_scale = rows(strip_ref, 33, 3)
    far = [ratio(far_load[c], far_scale[c]) for c in range(3)]
    whole_block = [None, *within[:3], None, *within[3:], None]
    total = off_diagonal(lambda k: whole_block[k], beside)
    from_far = product(lambda k: strip_ref[24 + k : 25 + k, :], far)
    up_y = product(lambda k: strip_ref[6 + k : 7 + k, :], beside)
    low_y = product(lambda k: strip_ref[15 + k : 16 + k, :], beside)
    for c in range(3):
        before_ref[c : c + 1, :] = inverse[c] * (
            total[c]
            + from_far[c]
            + entering[c]
            + lanes_moved(up_y[c], 0.0, 1)
            + lanes_moved(low_y[c], 0.0, -1)
        )
    before_ref[3:, :] = jnp.zeros((before_ref.shape[0] - 3, LANES), F32)


def box_kernel(
    tile_ref, field_ref, node_ref, param_ref, halo_ref, strip_ref, diag_ref, edge_ref,
    mask_ref, inverse_ref,
    part_ref, box_ref, adjoint_ref, before_ref, matrix_ref, weights_ref, columns_ref,
    *, tile_points,
):
    cells_x = field_ref.shape[1]
    own = cells_x // 2
    field = [field_ref[c] for c in range(3)]
    part = off_diagonal(lambda k: diag_ref[k], field)
    up_x = masked_product(edge_ref, mask_ref, 0, field)
    low_x = masked_product(edge_ref, mask_ref, 1, field)
    up_y = masked_product(edge_ref, mask_ref, 2, field)
    low_y = masked_product(edge_ref, mask_ref, 3, field)
    for c in range(3):
        part[c] = inverse_ref[c] * (
            part[c]
            + rows_moved(up_x[c], halo_ref[6 + c : 7 + c, :], 1)
            + rows_moved(low_x[c], halo_ref[21 + c : 22 + c, :], -1)
            + lanes_moved(up_y[c], 0.0, 1)
            + lanes_moved(low_y[c], 0.0, -1)
        )
        part_ref[c] = part[c]
    quotient_before(halo_ref, strip_ref, before_ref, [p[:1] for p in low_x])
    order = [field[0], part[0], field[2], field[1], part[1], part[2]]
    folded = [two_parts(jnp.concatenate([f[:own], f[own:]], axis=1)) for f in order]
    table = jnp.concatenate(
        [folded[f][which] for which in range(2) for f in range(6)], axis=0
    ).astype(BF16)
    points = param_ref.shape[1]
    pieces = CHUNK // LANES
    zero, one = jnp.zeros((), BF16), jnp.ones((), BF16)
    at_node = float_iota((2 * LANES, CHUNK), 0).astype(BF16)
    nothing = jnp.zeros((1, CHUNK), F32)
    highs, lows = [], []
    for chunk in range(points // CHUNK):
        node = jnp.concatenate(
            [node_ref[chunk * pieces + k : chunk * pieces + k + 1, :] for k in range(pieces)],
            axis=1,
        )
        row = lax.shift_right_logical(node, 7)
        column = node & (LANES - 1)
        lanes = slice(chunk * CHUNK, (chunk + 1) * CHUNK)
        at_edge = jnp.where(
            column == 0, row, jnp.where(column == LANES - 1, row + cells_x, -1)
        ).astype(F32)
        columns_ref[:, lanes] = jnp.where(
            at_node[: 2 * cells_x] == stretched(at_edge, 2 * cells_x), one, zero
        )
        place = column + jnp.where(row >= own, LANES, 0)
        row = jnp.where(row >= own, row - own, row)
        pick = jnp.where(at_node == stretched(place.astype(F32), 2 * LANES), one, zero)
        read = jnp.dot(table, pick, preferred_element_type=F32)
        read = read[: 6 * own] + read[6 * own :]
        here = iota((own, CHUNK), 0) == row
        values = [
            jnp.sum(
                jnp.where(here, read[f * own : (f + 1) * own], 0.0), axis=0, keepdims=True
            )
            for f in range(6)
        ]
        high, low = two_parts(
            jnp.concatenate(values[:3] + [nothing] + values[3:] + [nothing], axis=0)
        )
        highs.append(high)
        lows.append(low)
        weights = two_parts(
            weight_table(param_ref[0:1, lanes], param_ref[1:2, lanes], param_ref[2:3, lanes])
        )
        for k in range(CHUNK // tile_points):
            tile = slice(k * tile_points, (k + 1) * tile_points)
            sides = jnp.concatenate([weights[0][:, tile], weights[1][:, tile]], axis=0)
            weights_ref[chunk * (CHUNK // tile_points) + k] = sides.T.astype(BF16)
    both = jnp.concatenate(
        [jnp.concatenate(highs, axis=1), jnp.concatenate(lows, axis=1)], axis=0
    ).astype(BF16)
    matrix_ref[...] = box_matrix(tile_ref[...], matrix_ref.shape[0] // 4)
    tiles = tile_ref.shape[1]
    terms = [
        jnp.dot(
            both[:, tile * tile_points : (tile + 1) * tile_points],
            weights_ref[tile],
            preferred_element_type=F32,
        )
        for tile in range(tiles)
    ]
    box_ref[...] = jnp.dot(matrix_ref[...], tile_rows(terms), preferred_element_type=F32)
    low_half = iota((2 * cells_x, LANES), 1) < LANES // 2
    for tile in range(tiles):
        lanes = slice(tile * tile_points, (tile + 1) * tile_points)
        term = jnp.dot(
            columns_ref[:, lanes], weights_ref[tile], preferred_element_type=F32
        )
        high, low = two_parts(term + pltpu.roll(term, LANES // 2, 1))
        adjoint_ref[:, tile * LANES : (tile + 1) * LANES] = jnp.where(
            low_half, high, low
        ).astype(BF16)


def sums_kernel(
    from_inner_ref, from_outer_ref, inner_ref, outer_ref, field_ref, part_ref, halo_ref,
    diag_ref, edge_ref, mask_ref, box_ref, adjoint_ref, before_ref, matrix_ref,
    quotient_ref, out_ref,
):
    cells_x = field_ref.shape[1]
    targets = out_ref.shape[0]

    from_low, from_high = by_parity(from_inner_ref[...], from_outer_ref[...])
    first, last = by_parity(inner_ref[...], outer_ref[...])

    lane_row = iota((1, LANES), 1)
    shares, edges = [], []
    for arrived, own in ((from_low, first), (from_high, last)):
        def row(source, slot, c):
            return source[3 * slot + c : 3 * slot + c + 1]

        shares.append([row(arrived, 1, c) * row(own, 3, c) for c in range(3)])
        edges.append(
            [row(arrived, 2, c) + row(arrived, 3, c) * row(own, 1, c) for c in range(3)]
        )

    def turned(columns, share, edge):
        kept = [
            jnp.where(lane_row < cells_x, share[c], columns[3 + c : 4 + c]) for c in range(3)
        ]
        rest = jnp.zeros((LANES - 9, LANES), F32)
        return jnp.concatenate([columns[:3], *kept, *edge, rest], axis=0).T

    low = turned(from_low, shares[0], edges[0])
    high = turned(from_high, shares[1], edges[1])
    lane = iota((cells_x, LANES), 1)

    def column(source, slot, comp):
        return source[:cells_x, 3 * slot + comp : 3 * slot + comp + 1]

    field = [field_ref[c] for c in range(3)]
    scale = [diag_ref[4 * c] for c in range(3)]
    quotient, low_edge, high_edge = [], [], []
    for c in range(3):
        entering = jnp.where(
            lane == 0,
            column(low, 1, c),
            jnp.where(lane == LANES - 1, column(high, 1, c), 0.0),
        )
        quotient.append(part_ref[c] + entering)
        low_edge.append(column(low, 2, c))
        high_edge.append(column(high, 2, c))
    for c in range(3):
        quotient_ref[c] = quotient[c]
    before, before_quotient = [], []
    for c in range(3):
        entering = jnp.where(
            lane_row == 0,
            low[cells_x : cells_x + 1, 3 + c : 4 + c],
            jnp.where(lane_row == LANES - 1, high[cells_x : cells_x + 1, 3 + c : 4 + c], 0.0),
        )
        before.append(halo_ref[c : c + 1, :])
        before_quotient.append(
            before_ref[c : c + 1, :] + entering * halo_ref[3 + c : 4 + c, :]
        )

    first_sum = sum(field[c] * scale[c] * field[c] for c in range(3))
    second_sum = sum(field[c] * scale[c] * quotient[c] for c in range(3))
    third_sum = sum(quotient[c] * scale[c] * quotient[c] for c in range(3))
    within = off_diagonal(lambda k: diag_ref[k], quotient)
    fourth_sum = sum(within[c] * field[c] for c in range(3))
    fifth_sum = sum(within[c] * quotient[c] for c in range(3))
    at_row = iota((cells_x, LANES), 0)
    moves = (
        (pltpu.roll, 1, 0, at_row == 0),
        (pltpu.roll, cells_x - 1, 0, at_row == cells_x - 1),
        (pltpu.roll, 1, 1, lane == 0),
        (pltpu.roll, LANES - 1, 1, lane == LANES - 1),
    )
    extra = [0.0, 0.0]
    sides = [0.0, 0.0]
    for direction, (roll, step, dim, edge) in enumerate(moves):
        moving = masked_product(edge_ref, mask_ref, direction, quotient)
        for c in range(3):
            moved = jnp.where(edge, 0.0, roll(moving[c], step, dim))
            fourth_sum = fourth_sum + moved * field[c]
            fifth_sum = fifth_sum + moved * quotient[c]
            if direction == 1:
                extra[0] += moving[c][:1] * before[c]
                extra[1] += moving[c][:1] * before_quotient[c]
            elif direction == 2:
                sides[0] += moving[c][:, LANES - 1 :] * column(high, 0, c)
                sides[1] += moving[c][:, LANES - 1 :] * high_edge[c]
            elif direction == 3:
                sides[0] += moving[c][:, :1] * column(low, 0, c)
                sides[1] += moving[c][:, :1] * low_edge[c]
    incoming = product(lambda k: halo_ref[9 + k : 10 + k, :], before_quotient)
    extra[0] += sum(incoming[c] * field[c][:1] for c in range(3))
    extra[1] += sum(incoming[c] * quotient[c][:1] for c in range(3))
    fourth_sum = fourth_sum + jnp.where(lane == 0, sides[0], 0.0)
    fifth_sum = fifth_sum + jnp.where(lane == 0, sides[1], 0.0)
    extra = [0.0, 0.0, 0.0, extra[0], extra[1]]
    sums = jnp.zeros((1, LANES), F32)
    for k, value in enumerate((first_sum, second_sum, third_sum, fourth_sum, fifth_sum)):
        line = jnp.sum(value, axis=0, keepdims=True) + extra[k]
        sums = jnp.where(lane_row == k, jnp.sum(line, axis=1, keepdims=True), sums)

    added = [
        jnp.where(lane_row < cells_x, shares[0][c], pltpu.roll(shares[1][c], cells_x, 1))
        for c in range(3)
    ]
    none = jnp.zeros((1, LANES), F32)
    added = jnp.concatenate(
        [none, added[0], none, none, none, added[1], added[2], none], axis=0
    )
    added = jnp.concatenate(two_parts(added), axis=0).astype(BF16)
    terms = jnp.dot(added, adjoint_ref[...], preferred_element_type=F32)
    terms = [
        terms[:, first : first + LANES] for first in range(0, terms.shape[1], LANES)
    ]
    total = box_ref[...] + jnp.dot(
        matrix_ref[...], tile_rows(terms), preferred_element_type=F32
    )
    total = jnp.where((iota(total.shape, 0) & 3) == 3, sums, total)
    for box in range(targets):
        out_ref[box] = total[4 * box : 4 * box + 4]


def result_kernel(got_ref, field_ref, quotient_ref, solution_ref, gradient_ref):
    total = jnp.sum(got_ref[...], axis=0)
    rho, a, b, t, u = [total[3:4, k : k + 1] for k in range(5)]
    norm = rho + a
    by_rho, by_norm = 1.0 / rho, 1.0 / norm
    ratio, step = a * by_rho, rho * by_norm
    rest = jnp.maximum(b - a * ratio, 0.0)
    beta = step * step * rest * by_rho
    rest_image = (b + u) - ratio * (a + b + a + t) + ratio * ratio * norm
    cross = (a + t) - ratio * norm
    curve = step * step * rest_image - step * beta * (rest + cross) + beta * beta * norm
    second = jnp.where(
        curve > 0.0, step * step * rest / jnp.where(curve > 0.0, curve, 1.0), 0.0
    )
    second = jnp.minimum(second, 16.0)
    of_field = step + second * (beta + step * ratio)
    of_quotient = -(step * second)
    for c in range(3):
        solution_ref[c] = of_field * field_ref[c] + of_quotient * quotient_ref[c]
    gradient_ref[:, :LANES] = of_field * total[0:1] + of_quotient * total[1:2]
    gradient_ref[:, LANES:] = (
        of_field * total[2:3, : LANES // 2] + of_quotient * total[2:3, LANES // 2 :]
    )


def per_device(
    diag_blocks, edge_blocks, edge_mask, src_values, src_owner, src_node, src_count,
    surf_node, surf_param, tile_box,
):
    cells_x, cells_y = diag_blocks.shape[1:]
    width_gx, width_gy = lax.axis_size("gx"), lax.axis_size("gy")
    devices = width_gx * width_gy
    groups = src_node.shape[0] // LANES
    whole = functools.partial(jax.ShapeDtypeStruct, dtype=F32)

    cells = 4 * groups + NEAR

    def kept(array):
        return pltpu.with_memory_space_constraint(array, pltpu.HBM)

    i32 = jnp.int32
    rows = pl.pallas_call(
        pack_kernel,
        in_specs=[SMEM] + [HBM] * 6,
        out_specs=HBM,
        out_shape=pltpu.HBM((width_gx, cells, LANES), F32),
        scratch_shapes=[
            pltpu.VMEM(src_values.shape, F32),
            pltpu.VMEM((groups, LANES), i32),
            pltpu.VMEM((groups, LANES), i32),
            pltpu.VMEM((3, 8, cells_y), F32),
            pltpu.VMEM((3, 8, cells_y), F32),
            pltpu.VMEM((9, 8, cells_y), F32),
            pltpu.VMEM((9, 8, cells_y), F32),
            pltpu.VMEM((2, 9, 8, cells_y), F32),
            pltpu.VMEM((8, cells_y), i32),
            pltpu.VMEM((4, 8, cells_y), i32),
            pltpu.VMEM((width_gx, cells, LANES), F32),
            pltpu.SemaphoreType.DMA((14,)),
            pltpu.SemaphoreType.DMA((2,)),
        ],
        compiler_params=PARAMS,
        name="pack_rows_and_edges",
    )(
        src_count, kept(src_values),
        kept(src_owner.reshape(groups, LANES)), kept(src_node.reshape(groups, LANES)),
        kept(diag_blocks), kept(edge_blocks), kept(edge_mask),
    )
    rows = lax.all_to_all(rows, "gx", split_axis=0, concat_axis=0, tiled=True)

    nodes = (3, cells_x, cells_y)
    inverse, columns, strip = pl.pallas_call(
        edge_kernel,
        in_specs=[VMEM] * 3,
        out_specs=[VMEM] * 3,
        out_shape=[whole(nodes), whole((LANES, LANES)), whole((STRIP, LANES))],
        compiler_params=PARAMS,
        cost_estimate=pl.CostEstimate(
            flops=10**8, bytes_accessed=4 * 10**6, transcendentals=0
        ),
        name="edge_columns",
    )(diag_blocks, edge_blocks, edge_mask)
    strip = lax.ppermute(strip, "gx", [(i, i + 1) for i in range(width_gx - 1)])

    size = -(-3 * (cells_x + 2 * PAD) // 16) * 16
    field, halo, inner, outer = pl.pallas_call(
        field_kernel,
        in_specs=[VMEM] * 3,
        out_specs=[VMEM] * 4,
        out_shape=[
            whole(nodes), whole((24, cells_y)), whole((16, LANES)), whole((16, LANES)),
        ],
        scratch_shapes=[pltpu.VMEM((size, 2 * LANES), F32)],
        compiler_params=PARAMS,
        name="load_and_first_product",
    )(rows, inverse, columns)
    def swapped(columns, first):
        low = range(first, width_gy - 1, 2)
        pairs = [(i, i + 1) for i in low] + [(i + 1, i) for i in low]
        return lax.ppermute(columns, "gy", pairs)

    from_inner, from_outer = swapped(inner, 1), swapped(outer, 0)
    points, tiles = surf_node.shape[0], tile_box.shape[0]
    part, box_part, adjoint, before, matrix = pl.pallas_call(
        functools.partial(box_kernel, tile_points=points // tiles),
        in_specs=[VMEM] * 10,
        out_specs=[VMEM] * 5,
        out_shape=[
            whole(nodes),
            whole((4 * devices, LANES)),
            jax.ShapeDtypeStruct((2 * cells_x, tiles * LANES), BF16),
            whole((8, LANES)),
            jax.ShapeDtypeStruct((4 * devices, 8 * tiles), BF16),
        ],
        scratch_shapes=[
            pltpu.VMEM((tiles, points // tiles, LANES), BF16),
            pltpu.VMEM((2 * cells_x, points), BF16),
        ],
        compiler_params=PARAMS,
        cost_estimate=pl.CostEstimate(
            flops=10**9, bytes_accessed=4 * 10**6, transcendentals=0
        ),
        name="box_parts",
    )(
        tile_box.reshape(1, tiles), field, surf_node.reshape(points // LANES, LANES),
        surf_param, halo, strip, diag_blocks, edge_blocks, edge_mask, inverse,
    )

    quotient, partial = pl.pallas_call(
        sums_kernel,
        in_specs=[VMEM] * 14,
        out_specs=[VMEM] * 2,
        out_shape=[whole(nodes), whole((devices, 4, LANES))],
        compiler_params=PARAMS,
        name="sums_and_halo_parts",
    )(
        from_inner, from_outer, inner, outer, field, part, halo, diag_blocks, edge_blocks, edge_mask,
        box_part, adjoint, before, matrix,
    )
    got = lax.all_to_all(partial, ("gx", "gy"), split_axis=0, concat_axis=0, tiled=True)
    return pl.pallas_call(
        result_kernel,
        in_specs=[VMEM] * 3,
        out_specs=[VMEM] * 2,
        out_shape=[whole(nodes), whole((1, 192))],
        compiler_params=PARAMS,
        name="steps_and_outputs",
    )(got, field, quotient)


def solution(mesh):
    return jax.shard_map(
        per_device,
        mesh=mesh,
        in_specs=(
            P(None, "gx", "gy"),
            P(None, None, "gx", "gy"),
            P(None, "gx", "gy"),
            P(None, ("gx", "gy")),
            P(("gx", "gy"), None),
            P(("gx", "gy")),
            P(("gx", "gy")),
            P(("gx", "gy")),
            P(None, ("gx", "gy")),
            P(("gx", "gy")),
        ),
        out_specs=(P(None, "gx", "gy"), P(("gx", "gy"), None)),
        check_vma=False,
    )
```

```python
import functools

import jax
import jax.numpy as jnp
from jax import lax
from jax.experimental import pallas as pl
from jax.experimental.pallas import tpu as pltpu
from jax.sharding import PartitionSpec as P

F32 = jnp.float32
BF16 = jnp.bfloat16
PAD = 2
NOWHERE = -(1 << 20)
LANES = 128
NEAR = 16
STRIP = 40
CHUNK = 256
PARAMS = pltpu.CompilerParams(vmem_limit_bytes=24 * 1024 * 1024)

VMEM = pl.BlockSpec(memory_space=pltpu.VMEM)
SMEM = pl.BlockSpec(memory_space=pltpu.SMEM)
HBM = pl.BlockSpec(memory_space=pltpu.HBM)


def iota(shape, dim):
    return lax.broadcasted_iota(jnp.int32, shape, dim)


def float_iota(shape, dim):
    return iota(shape, dim).astype(F32)


def two_parts(value):
    high = value.astype(BF16).astype(F32)
    return high, value - high


def product(block, field):
    return [
        block(row) * field[0] + block(3 + row) * field[1] + block(6 + row) * field[2]
        for row in range(3)
    ]


def off_diagonal(block, field):
    return [
        sum(block(3 * i + row) * field[i] for i in range(3) if i != row) for row in range(3)
    ]


def masked_product(edge_ref, mask_ref, direction, field):
    mask = mask_ref[direction].astype(F32)
    return [mask * part for part in product(lambda k: edge_ref[direction, k], field)]


def rows_moved(field, edge_row, step):
    size = field.shape[0]
    at = iota(field.shape, 0)
    moved = pltpu.roll(field, step % size, 0)
    return jnp.where(at == (0 if step == 1 else size - 1), edge_row, moved)


def lanes_moved(field, edge_column, step):
    size = field.shape[1]
    at = iota(field.shape, 1)
    moved = pltpu.roll(field, step % size, 1)
    return jnp.where(at == (0 if step == 1 else size - 1), edge_column, moved)


def pack_kernel(
    count_ref, values_in, owner_in, node_in, diag_in, edge_in, mask_in, rows_out, own_ref,
    values_ref, owner_ref, node_ref, diag_low, diag_high, edge_low, edge_high, side_high,
    mask_low, mask_high, rows_ref, arrived, left,
):
    targets = rows_ref.shape[0]
    groups = owner_ref.shape[0]
    cells_x = diag_in.shape[1]
    top = pl.ds(cells_x - 8, 8)
    pieces = [
        (owner_in, owner_ref),
        (node_in, node_ref),
        (values_in, values_ref),
        (edge_in.at[pl.ds(2, 2), :, top], side_high),
        (edge_in.at[0, :, top], edge_high),
        (edge_in.at[1, :, 0:8], edge_low),
        (mask_in.at[:, top], mask_high),
        (mask_in.at[1, 0:8], mask_low),
    ]
    for k in range(3):
        pieces.append((diag_in.at[4 * k, top], diag_high.at[k]))
        pieces.append((diag_in.at[4 * k, 0:8], diag_low.at[k]))
    copies = [
        pltpu.make_async_copy(source, target, arrived.at[k])
        for k, (source, target) in enumerate(pieces)
    ]
    for copy in copies:
        copy.start()
    base = 4 * groups
    for target in range(targets):
        rows_ref[target, base:, :] = jnp.zeros((NEAR, LANES), F32)
    for copy in copies[:2]:
        copy.wait()
    order = iota((groups, LANES), 0) * LANES + iota((groups, LANES), 1)
    node = node_ref[...]
    frame = cells_x + 2 * PAD
    row = owner_ref[...] * cells_x + lax.shift_right_logical(node, 7)
    row = jnp.where(order < count_ref[0], row, NOWHERE)
    column = node & (LANES - 1)
    for target in range(targets):
        line = row - (target * cells_x - PAD)
        inside = (line >= 0) & (line < frame)
        index = jnp.where(inside, line * LANES + column, -1)
        rows_ref[target, 3 * groups : 4 * groups, :] = index.astype(F32)

    copies[2].wait()
    for comp in range(3):
        value = jnp.concatenate(
            [
                values_ref[comp : comp + 1, group * LANES : (group + 1) * LANES]
                for group in range(groups)
            ],
            axis=0,
        )
        for target in range(targets):
            rows_ref[target, comp * groups : (comp + 1) * groups, :] = value
    near = pl.ds(4 * groups, NEAR)
    leaving = [
        pltpu.make_async_copy(rows_ref.at[:, part], rows_out.at[:, part], left.at[k])
        for k, part in enumerate((pl.ds(0, 4 * groups), near))
    ]
    leaving[0].start()
    for copy in copies[3:]:
        copy.wait()

    here = lax.axis_index("gx")

    def block(edge, mask):
        present = mask.astype(F32)
        return [edge(k) * present for k in range(9)]

    @pl.when(here < targets - 1)
    def _():
        def put(slot, value):
            rows_ref[here + 1, base + slot : base + slot + 1, :] = value

        for k in range(3):
            put(k, diag_high[k, 7:8, :])
        toward = block(lambda k: edge_high[k, 7:8, :], mask_high[0, 7:8, :])
        up_y = block(lambda k: side_high[0, k, 7:8, :], mask_high[2, 7:8, :])
        low_y = block(lambda k: side_high[1, k, 7:8, :], mask_high[3, 7:8, :])
        corners = jnp.zeros((1, LANES), F32)
        lane = iota((1, LANES), 1)
        for k in range(9):
            put(3 + k, toward[k])
            corners = jnp.where(lane == k, up_y[k][:, LANES - 1 :], corners)
            corners = jnp.where(lane == 9 + k, low_y[k][:, :1], corners)
        put(12, corners)

    @pl.when(here > 0)
    def _():
        def put(slot, value):
            rows_ref[here - 1, base + slot : base + slot + 1, :] = value

        for k in range(3):
            put(k, diag_low[k, 0:1, :])
        for k, value in enumerate(block(lambda k: edge_low[k, 0:1, :], mask_low[0:1, :])):
            put(3 + k, value)

    leaving[1].start()
    own_ref[...] = rows_ref[here, : 4 * groups, :]
    for copy in leaving:
        copy.wait()


def stretched(row, count):
    tile = jnp.broadcast_to(row, (16, row.shape[1])).astype(BF16)
    return jnp.concatenate([tile] * (count // 16), axis=0)


def ratio(value, scale):
    return jnp.where(scale > 0.0, value / jnp.where(scale > 0.0, scale, 1.0), 0.0)


UP_X, LOW_X, INWARD, OUTWARD, WITHIN, INVERSE = 0, 3, 6, 9, 12, 15


def edge_kernel(diag_ref, edge_ref, mask_ref, inverse_ref, columns_ref, strip_ref):
    cells_x = diag_ref.shape[1]
    last = cells_x - 1
    strip = [diag_ref[k, last:, :] for k in range(9) if k % 4]
    for direction, at in ((2, last), (3, last), (0, last - 1)):
        present = mask_ref[direction, at : at + 1, :].astype(F32)
        strip += [edge_ref[direction, k, at : at + 1, :] * present for k in range(9)]
    strip += [diag_ref[4 * k, last - 1 : last, :] for k in range(3)]
    for k, value in enumerate(strip):
        strip_ref[k : k + 1, :] = value
    strip_ref[len(strip) :, :] = jnp.zeros((STRIP - len(strip), LANES), F32)
    at = iota((cells_x, LANES), 1)
    sides = [jnp.zeros((cells_x, LANES), F32) for _ in range(2)]

    def put(kind, i, a, first, first_lane, last, last_lane):
        slot = 8 * (kind + i) + a
        for side, (field, lane) in enumerate(((first, first_lane), (last, last_lane))):
            sides[side] = jnp.where(at == slot, field[:, lane : lane + 1], sides[side])

    inverse = [1.0 / diag_ref[4 * c] for c in range(3)]
    end = LANES - 1
    masks = [mask_ref[direction].astype(F32) for direction in range(4)]
    for i in range(3):
        inverse_ref[i] = inverse[i]
        put(INVERSE, 0, i, inverse[i], 0, inverse[i], end)
        for a in range(3):
            up_x, low_x, up_y, low_y = (
                edge_ref[direction, 3 * i + a] * masks[direction] for direction in range(4)
            )
            put(UP_X, i, a, up_x, 0, up_x, end)
            put(LOW_X, i, a, low_x, 0, low_x, end)
            put(INWARD, i, a, low_y, 1, up_y, end - 1)
            put(OUTWARD, i, a, low_y, 0, up_y, end)
            if a != i:
                put(WITHIN, i, a, diag_ref[3 * i + a], 0, diag_ref[3 * i + a], end)
    columns_ref[...] = jnp.concatenate(sides, axis=0).T


def load_product(blocks, half):
    groups = blocks[0].shape[0] // 4
    size = -(-6 * half // 16) * 16
    line = iota((size, LANES), 0)
    block = sum(jnp.where(line >= half * k, 1, 0) for k in range(1, 6))
    at_row = jnp.where(line < 6 * half, line - half * block, -5).astype(F32).astype(BF16)
    at_column = float_iota((2 * LANES, LANES), 0).astype(BF16)
    in_tile = float_iota((16, LANES), 0).astype(BF16)
    zero, one = jnp.zeros((), BF16), jnp.ones((), BF16)
    lefts, rights = [], []
    for rows in blocks:
        index = rows[3 * groups :]
        split = float(half * LANES)
        index, shift = (
            jnp.where(index >= split, index - split, index),
            jnp.where(index >= split, float(LANES), 0.0),
        )
        place = jnp.floor(index * (1.0 / LANES))
        column = index - place * float(LANES) + shift
        parts = [two_parts(rows[c * groups : (c + 1) * groups]) for c in range(3)]
        for group in range(groups):
            here = slice(group, group + 1)
            values = [
                stretched(parts[c][which][here], 16) for which in range(2) for c in range(3)
            ]
            tiles = []
            for first in range(0, size, 16):
                low, high = first // half, min((first + 15) // half, 5)
                tiles.append(
                    values[low]
                    if low == high
                    else jnp.where(
                        in_tile < float(half * high - first), values[low], values[high]
                    )
                )
            match = at_row == stretched(place[here], size)
            lefts.append(jnp.where(match, jnp.concatenate(tiles, axis=0), zero))
            rights.append(
                jnp.where(at_column == stretched(column[here], 2 * LANES), one, zero)
            )
    return lax.dot_general(
        jnp.concatenate(lefts, axis=1),
        jnp.concatenate(rights, axis=1),
        (((1,), (1,)), ((), ())),
        preferred_element_type=F32,
    )


def own_kernel(rows_ref, load_ref, *, half):
    load_ref[...] = load_product([rows_ref[...]], half)


def field_kernel(
    rows_ref, own_ref, inverse_ref, columns_ref,
    field_ref, halo_ref, inner_ref, outer_ref, load_ref,
):
    senders = rows_ref.shape[0]
    groups = (rows_ref.shape[1] - NEAR) // 4
    cells_x = field_ref.shape[1]
    half = (cells_x + 2 * PAD) // 2
    own = cells_x // 2

    load_ref[...] = own_ref[...]
    here = lax.axis_index("gx")
    others = senders - 1
    together = others if others <= 8 else 1

    def add_rows(step, carry):
        blocks = []
        for k in range(together):
            sender = step * together + k
            sender = jnp.where(sender >= here, sender + 1, sender)
            blocks.append(rows_ref[sender, : 4 * groups, :])
        load_ref[...] += load_product(blocks, half)
        return carry

    lax.fori_loop(0, others // together, add_rows, 0)

    def load_rows(comp, first, last, second_half):
        lanes = slice(LANES, 2 * LANES) if second_half else slice(0, LANES)
        return (
            load_ref[comp * half + first : comp * half + last, lanes]
            + load_ref[(3 + comp) * half + first : (3 + comp) * half + last, lanes]
        )

    field = []
    for comp in range(3):
        load = jnp.concatenate(
            [load_rows(comp, PAD, half, False), load_rows(comp, 0, half - PAD, True)], axis=0
        )
        field.append(load * inverse_ref[comp])
        field_ref[comp] = field[comp]
    beyond = half - PAD
    near_before = [load_rows(c, PAD - 1, PAD, False) for c in range(3)]
    far_before = [load_rows(c, PAD - 2, PAD - 1, False) for c in range(3)]
    near_after = [load_rows(c, beyond, beyond + 1, True) for c in range(3)]

    base = 4 * groups

    def neighbour(sender, load):
        def entry(k):
            return rows_ref[sender, base + k : base + k + 1, :]

        inverse = [ratio(1.0, entry(k)) for k in range(3)]
        toward = [entry(3 + k) for k in range(9)]
        beside = [load[c] * inverse[c] for c in range(3)]
        return inverse, toward, beside, product(lambda k: toward[k], beside)

    lower = jnp.maximum(here - 1, 0)
    before = neighbour(lower, near_before)
    after = neighbour(jnp.minimum(here + 1, senders - 1), near_after)
    rows = before[2] + before[0] + before[3] + before[1] + far_before + after[3]
    for k, value in enumerate(rows):
        halo_ref[k : k + 1, :] = value
    lane_row = iota((1, LANES), 1)
    ends = jnp.zeros((1, LANES), F32)
    for i in range(3):
        for a in range(3):
            ends = jnp.where(lane_row == 3 * i + a, before[2][i][:, LANES - 1 :], ends)
            ends = jnp.where(lane_row == 9 + 3 * i + a, before[2][i][:, :1], ends)
    ends = ends * rows_ref[lower, base + 12 : base + 13, :]
    ends = ends + pltpu.roll(ends, LANES - 3, 1) + pltpu.roll(ends, LANES - 6, 1)

    at = iota((cells_x, LANES), 1)
    sides = []
    for edge, inside in ((0, 1), (LANES - 1, LANES - 2)):
        packed = jnp.zeros((cells_x, LANES), F32)
        for comp in range(3):
            packed = jnp.where(at == comp, field[comp][:, edge : edge + 1], packed)
            packed = jnp.where(at == 8 + comp, field[comp][:, inside : inside + 1], packed)
        sides.append(packed)
    turned = jnp.concatenate(sides, axis=0).T

    def column_product(kind, first):
        return sum(
            columns_ref[8 * (kind + i) : 8 * (kind + i) + 8, :] * turned[first + i : first + i + 1]
            for i in range(3)
        )

    def eight(rows):
        return jnp.concatenate(rows + [jnp.zeros((8 - len(rows), LANES), F32)], axis=0)

    lane = iota((8, LANES), 1)
    from_before, from_after = eight(before[3]), eight(after[3])
    from_before = jnp.where(lane == 0, from_before, pltpu.roll(from_before, cells_x + 1, 1))
    from_after = jnp.where(
        lane == LANES - 1, from_after, pltpu.roll(from_after, cells_x - 1, 1)
    )
    row = lane & (cells_x - 1)
    upward = pltpu.roll(column_product(UP_X, 0), 1, 1)
    downward = pltpu.roll(column_product(LOW_X, 0), LANES - 1, 1)
    total = (
        column_product(WITHIN, 0)
        + jnp.where(row == 0, from_before, upward)
        + jnp.where(row == cells_x - 1, from_after, downward)
        + column_product(INWARD, 8)
    )
    inverse = columns_ref[8 * INVERSE : 8 * INVERSE + 8, :]
    along_y, part = column_product(OUTWARD, 0), total * inverse
    stacked = jnp.concatenate(
        [turned[:3], along_y[:3], part[:3], inverse[:3], jnp.zeros((4, LANES), F32)], axis=0
    )

    def message(columns, end):
        at = iota((16, LANES), 1)
        line = iota((16, LANES), 0)
        columns = jnp.where(at < cells_x, columns, 0.0)
        for comp in range(3):
            columns = jnp.where(
                (line == 3 + comp) & (at == cells_x),
                ends[:, end + comp : end + comp + 1],
                columns,
            )
        return columns

    inner_ref[...], outer_ref[...] = by_parity(
        message(stacked, 9), message(pltpu.roll(stacked, cells_x, 1), 0)
    )


def bernstein(coord):
    other = 1.0 - coord
    return [
        other * other * other,
        3.0 * coord * other * other,
        3.0 * coord * coord * other,
        coord * coord * coord,
    ]


def weight_table(u, v, w):
    first, second, third = bernstein(u), bernstein(v), bernstein(w)
    line = iota((8, u.shape[1]), 0)
    inner = line & 3
    along = jnp.where(
        inner == 0,
        third[0],
        jnp.where(inner == 1, third[1], jnp.where(inner == 2, third[2], third[3])),
    )
    pair = jnp.concatenate(
        [
            jnp.where(line < 4, second[0], second[1]) * along,
            jnp.where(line < 4, second[2], second[3]) * along,
        ],
        axis=0,
    )
    return jnp.concatenate([pair * first[i] for i in range(4)], axis=0)


def tile_rows(terms):
    first_half = iota((4, LANES), 1) < LANES // 2
    rows = []
    for term in terms:
        term = term[:8] + term[8:]
        term = term + pltpu.roll(term, LANES // 2, 1)
        rows.append(jnp.where(first_half, term[:4], term[4:]))
    return jnp.concatenate(two_parts(jnp.concatenate(rows, axis=0)), axis=0).astype(BF16)


def box_matrix(tile_row, boxes):
    tiles = tile_row.shape[1]
    shape = (4 * boxes, 8 * tiles)
    column = iota((1, shape[1]), 1)
    box = jnp.zeros((1, shape[1]), jnp.int32)
    for tile in range(tiles):
        mine = lax.rem(lax.shift_right_logical(column, 2), tiles) == tile
        box = jnp.where(mine, tile_row[:, tile : tile + 1], box)
    target = 4 * box + (column & 3)
    return jnp.where(iota(shape, 0) == target, 1.0, 0.0).astype(BF16)


def by_parity(low, high):
    odd = lax.rem(lax.axis_index("gy"), 2) == 1
    return jnp.where(odd, high, low), jnp.where(odd, low, high)


def quotient_before(halo_ref, strip_ref, before_ref, entering):
    def rows(ref, first, count):
        return [ref[first + k : first + k + 1, :] for k in range(count)]

    beside, inverse = rows(halo_ref, 0, 3), rows(halo_ref, 3, 3)
    far_load, within = rows(halo_ref, 18, 3), rows(strip_ref, 0, 6)
    far_scale = rows(strip_ref, 33, 3)
    far = [ratio(far_load[c], far_scale[c]) for c in range(3)]
    whole_block = [None, *within[:3], None, *within[3:], None]
    total = off_diagonal(lambda k: whole_block[k], beside)
    from_far = product(lambda k: strip_ref[24 + k : 25 + k, :], far)
    up_y = product(lambda k: strip_ref[6 + k : 7 + k, :], beside)
    low_y = product(lambda k: strip_ref[15 + k : 16 + k, :], beside)
    for c in range(3):
        before_ref[c : c + 1, :] = inverse[c] * (
            total[c]
            + from_far[c]
            + entering[c]
            + lanes_moved(up_y[c], 0.0, 1)
            + lanes_moved(low_y[c], 0.0, -1)
        )
    before_ref[3:, :] = jnp.zeros((before_ref.shape[0] - 3, LANES), F32)


def box_kernel(
    tile_ref, field_ref, node_ref, param_ref, halo_ref, strip_ref, diag_ref, edge_ref,
    mask_ref, inverse_ref,
    part_ref, box_ref, adjoint_ref, before_ref, matrix_ref, weights_ref, columns_ref,
    *, tile_points,
):
    cells_x = field_ref.shape[1]
    own = cells_x // 2
    field = [field_ref[c] for c in range(3)]
    part = off_diagonal(lambda k: diag_ref[k], field)
    up_x = masked_product(edge_ref, mask_ref, 0, field)
    low_x = masked_product(edge_ref, mask_ref, 1, field)
    up_y = masked_product(edge_ref, mask_ref, 2, field)
    low_y = masked_product(edge_ref, mask_ref, 3, field)
    for c in range(3):
        part[c] = inverse_ref[c] * (
            part[c]
            + rows_moved(up_x[c], halo_ref[6 + c : 7 + c, :], 1)
            + rows_moved(low_x[c], halo_ref[21 + c : 22 + c, :], -1)
            + lanes_moved(up_y[c], 0.0, 1)
            + lanes_moved(low_y[c], 0.0, -1)
        )
        part_ref[c] = part[c]
    quotient_before(halo_ref, strip_ref, before_ref, [p[:1] for p in low_x])
    order = [field[0], part[0], field[2], field[1], part[1], part[2]]
    folded = [two_parts(jnp.concatenate([f[:own], f[own:]], axis=1)) for f in order]
    table = jnp.concatenate(
        [folded[f][which] for which in range(2) for f in range(6)], axis=0
    ).astype(BF16)
    points = param_ref.shape[1]
    pieces = CHUNK // LANES
    zero, one = jnp.zeros((), BF16), jnp.ones((), BF16)
    at_node = float_iota((2 * LANES, CHUNK), 0).astype(BF16)
    nothing = jnp.zeros((1, CHUNK), F32)
    highs, lows = [], []
    for chunk in range(points // CHUNK):
        node = jnp.concatenate(
            [node_ref[chunk * pieces + k : chunk * pieces + k + 1, :] for k in range(pieces)],
            axis=1,
        )
        row = lax.shift_right_logical(node, 7)
        column = node & (LANES - 1)
        lanes = slice(chunk * CHUNK, (chunk + 1) * CHUNK)
        at_edge = jnp.where(
            column == 0, row, jnp.where(column == LANES - 1, row + cells_x, -1)
        ).astype(F32)
        columns_ref[:, lanes] = jnp.where(
            at_node[: 2 * cells_x] == stretched(at_edge, 2 * cells_x), one, zero
        )
        place = column + jnp.where(row >= own, LANES, 0)
        row = jnp.where(row >= own, row - own, row)
        pick = jnp.where(at_node == stretched(place.astype(F32), 2 * LANES), one, zero)
        read = jnp.dot(table, pick, preferred_element_type=F32)
        read = read[: 6 * own] + read[6 * own :]
        here = iota((own, CHUNK), 0) == row
        values = [
            jnp.sum(
                jnp.where(here, read[f * own : (f + 1) * own], 0.0), axis=0, keepdims=True
            )
            for f in range(6)
        ]
        high, low = two_parts(
            jnp.concatenate(values[:3] + [nothing] + values[3:] + [nothing], axis=0)
        )
        highs.append(high)
        lows.append(low)
        weights = two_parts(
            weight_table(param_ref[0:1, lanes], param_ref[1:2, lanes], param_ref[2:3, lanes])
        )
        for k in range(CHUNK // tile_points):
            tile = slice(k * tile_points, (k + 1) * tile_points)
            sides = jnp.concatenate([weights[0][:, tile], weights[1][:, tile]], axis=0)
            weights_ref[chunk * (CHUNK // tile_points) + k] = sides.T.astype(BF16)
    both = jnp.concatenate(
        [jnp.concatenate(highs, axis=1), jnp.concatenate(lows, axis=1)], axis=0
    ).astype(BF16)
    matrix_ref[...] = box_matrix(tile_ref[...], matrix_ref.shape[0] // 4)
    tiles = tile_ref.shape[1]
    terms = [
        jnp.dot(
            both[:, tile * tile_points : (tile + 1) * tile_points],
            weights_ref[tile],
            preferred_element_type=F32,
        )
        for tile in range(tiles)
    ]
    box_ref[...] = jnp.dot(matrix_ref[...], tile_rows(terms), preferred_element_type=F32)
    low_half = iota((2 * cells_x, LANES), 1) < LANES // 2
    for tile in range(tiles):
        lanes = slice(tile * tile_points, (tile + 1) * tile_points)
        term = jnp.dot(
            columns_ref[:, lanes], weights_ref[tile], preferred_element_type=F32
        )
        high, low = two_parts(term + pltpu.roll(term, LANES // 2, 1))
        adjoint_ref[:, tile * LANES : (tile + 1) * LANES] = jnp.where(
            low_half, high, low
        ).astype(BF16)


def sums_kernel(
    from_inner_ref, from_outer_ref, inner_ref, outer_ref, field_ref, part_ref, halo_ref,
    diag_ref, edge_ref, mask_ref, box_ref, adjoint_ref, before_ref, matrix_ref,
    quotient_ref, out_ref,
):
    cells_x = field_ref.shape[1]
    targets = out_ref.shape[0]

    from_low, from_high = by_parity(from_inner_ref[...], from_outer_ref[...])
    first, last = by_parity(inner_ref[...], outer_ref[...])

    lane_row = iota((1, LANES), 1)
    shares, edges = [], []
    for arrived, own in ((from_low, first), (from_high, last)):
        def row(source, slot, c):
            return source[3 * slot + c : 3 * slot + c + 1]

        shares.append([row(arrived, 1, c) * row(own, 3, c) for c in range(3)])
        edges.append(
            [row(arrived, 2, c) + row(arrived, 3, c) * row(own, 1, c) for c in range(3)]
        )

    def turned(columns, share, edge):
        kept = [
            jnp.where(lane_row < cells_x, share[c], columns[3 + c : 4 + c]) for c in range(3)
        ]
        rest = jnp.zeros((LANES - 9, LANES), F32)
        return jnp.concatenate([columns[:3], *kept, *edge, rest], axis=0).T

    low = turned(from_low, shares[0], edges[0])
    high = turned(from_high, shares[1], edges[1])
    lane = iota((cells_x, LANES), 1)

    def column(source, slot, comp):
        return source[:cells_x, 3 * slot + comp : 3 * slot + comp + 1]

    field = [field_ref[c] for c in range(3)]
    scale = [diag_ref[4 * c] for c in range(3)]
    quotient, low_edge, high_edge = [], [], []
    for c in range(3):
        entering = jnp.where(
            lane == 0,
            column(low, 1, c),
            jnp.where(lane == LANES - 1, column(high, 1, c), 0.0),
        )
        quotient.append(part_ref[c] + entering)
        low_edge.append(column(low, 2, c))
        high_edge.append(column(high, 2, c))
    for c in range(3):
        quotient_ref[c] = quotient[c]
    before, before_quotient = [], []
    for c in range(3):
        entering = jnp.where(
            lane_row == 0,
            low[cells_x : cells_x + 1, 3 + c : 4 + c],
            jnp.where(lane_row == LANES - 1, high[cells_x : cells_x + 1, 3 + c : 4 + c], 0.0),
        )
        before.append(halo_ref[c : c + 1, :])
        before_quotient.append(
            before_ref[c : c + 1, :] + entering * halo_ref[3 + c : 4 + c, :]
        )

    first_sum = sum(field[c] * scale[c] * field[c] for c in range(3))
    second_sum = sum(field[c] * scale[c] * quotient[c] for c in range(3))
    third_sum = sum(quotient[c] * scale[c] * quotient[c] for c in range(3))
    within = off_diagonal(lambda k: diag_ref[k], quotient)
    fourth_sum = sum(within[c] * field[c] for c in range(3))
    fifth_sum = sum(within[c] * quotient[c] for c in range(3))
    at_row = iota((cells_x, LANES), 0)
    moves = (
        (pltpu.roll, 1, 0, at_row == 0),
        (pltpu.roll, cells_x - 1, 0, at_row == cells_x - 1),
        (pltpu.roll, 1, 1, lane == 0),
        (pltpu.roll, LANES - 1, 1, lane == LANES - 1),
    )
    extra = [0.0, 0.0]
    sides = [0.0, 0.0]
    for direction, (roll, step, dim, edge) in enumerate(moves):
        moving = masked_product(edge_ref, mask_ref, direction, quotient)
        for c in range(3):
            moved = jnp.where(edge, 0.0, roll(moving[c], step, dim))
            fourth_sum = fourth_sum + moved * field[c]
            fifth_sum = fifth_sum + moved * quotient[c]
            if direction == 1:
                extra[0] += moving[c][:1] * before[c]
                extra[1] += moving[c][:1] * before_quotient[c]
            elif direction == 2:
                sides[0] += moving[c][:, LANES - 1 :] * column(high, 0, c)
                sides[1] += moving[c][:, LANES - 1 :] * high_edge[c]
            elif direction == 3:
                sides[0] += moving[c][:, :1] * column(low, 0, c)
                sides[1] += moving[c][:, :1] * low_edge[c]
    incoming = product(lambda k: halo_ref[9 + k : 10 + k, :], before_quotient)
    extra[0] += sum(incoming[c] * field[c][:1] for c in range(3))
    extra[1] += sum(incoming[c] * quotient[c][:1] for c in range(3))
    fourth_sum = fourth_sum + jnp.where(lane == 0, sides[0], 0.0)
    fifth_sum = fifth_sum + jnp.where(lane == 0, sides[1], 0.0)
    extra = [0.0, 0.0, 0.0, extra[0], extra[1]]
    sums = jnp.zeros((1, LANES), F32)
    for k, value in enumerate((first_sum, second_sum, third_sum, fourth_sum, fifth_sum)):
        line = jnp.sum(value, axis=0, keepdims=True) + extra[k]
        sums = jnp.where(lane_row == k, jnp.sum(line, axis=1, keepdims=True), sums)

    added = [
        jnp.where(lane_row < cells_x, shares[0][c], pltpu.roll(shares[1][c], cells_x, 1))
        for c in range(3)
    ]
    none = jnp.zeros((1, LANES), F32)
    added = jnp.concatenate(
        [none, added[0], none, none, none, added[1], added[2], none], axis=0
    )
    added = jnp.concatenate(two_parts(added), axis=0).astype(BF16)
    terms = jnp.dot(added, adjoint_ref[...], preferred_element_type=F32)
    terms = [
        terms[:, first : first + LANES] for first in range(0, terms.shape[1], LANES)
    ]
    total = box_ref[...] + jnp.dot(
        matrix_ref[...], tile_rows(terms), preferred_element_type=F32
    )
    total = jnp.where((iota(total.shape, 0) & 3) == 3, sums, total)
    for box in range(targets):
        out_ref[box] = total[4 * box : 4 * box + 4]


def result_kernel(got_ref, field_ref, quotient_ref, solution_ref, gradient_ref):
    total = jnp.sum(got_ref[...], axis=0)
    rho, a, b, t, u = [total[3:4, k : k + 1] for k in range(5)]
    norm = rho + a
    by_rho, by_norm = 1.0 / rho, 1.0 / norm
    ratio, step = a * by_rho, rho * by_norm
    rest = jnp.maximum(b - a * ratio, 0.0)
    beta = step * step * rest * by_rho
    rest_image = (b + u) - ratio * (a + b + a + t) + ratio * ratio * norm
    cross = (a + t) - ratio * norm
    curve = step * step * rest_image - step * beta * (rest + cross) + beta * beta * norm
    second = jnp.where(
        curve > 0.0, step * step * rest / jnp.where(curve > 0.0, curve, 1.0), 0.0
    )
    second = jnp.minimum(second, 16.0)
    of_field = step + second * (beta + step * ratio)
    of_quotient = -(step * second)
    for c in range(3):
        solution_ref[c] = of_field * field_ref[c] + of_quotient * quotient_ref[c]
    gradient_ref[:, :LANES] = of_field * total[0:1] + of_quotient * total[1:2]
    gradient_ref[:, LANES:] = (
        of_field * total[2:3, : LANES // 2] + of_quotient * total[2:3, LANES // 2 :]
    )


def per_device(
    diag_blocks, edge_blocks, edge_mask, src_values, src_owner, src_node, src_count,
    surf_node, surf_param, tile_box,
):
    cells_x, cells_y = diag_blocks.shape[1:]
    width_gx, width_gy = lax.axis_size("gx"), lax.axis_size("gy")
    devices = width_gx * width_gy
    groups = src_node.shape[0] // LANES
    whole = functools.partial(jax.ShapeDtypeStruct, dtype=F32)

    cells = 4 * groups + NEAR

    def kept(array):
        return pltpu.with_memory_space_constraint(array, pltpu.HBM)

    i32 = jnp.int32
    rows, own = pl.pallas_call(
        pack_kernel,
        in_specs=[SMEM] + [HBM] * 6,
        out_specs=[HBM, VMEM],
        out_shape=[
            pltpu.HBM((width_gx, cells, LANES), F32),
            pltpu.VMEM((4 * groups, LANES), F32),
        ],
        scratch_shapes=[
            pltpu.VMEM(src_values.shape, F32),
            pltpu.VMEM((groups, LANES), i32),
            pltpu.VMEM((groups, LANES), i32),
            pltpu.VMEM((3, 8, cells_y), F32),
            pltpu.VMEM((3, 8, cells_y), F32),
            pltpu.VMEM((9, 8, cells_y), F32),
            pltpu.VMEM((9, 8, cells_y), F32),
            pltpu.VMEM((2, 9, 8, cells_y), F32),
            pltpu.VMEM((8, cells_y), i32),
            pltpu.VMEM((4, 8, cells_y), i32),
            pltpu.VMEM((width_gx, cells, LANES), F32),
            pltpu.SemaphoreType.DMA((14,)),
            pltpu.SemaphoreType.DMA((2,)),
        ],
        compiler_params=PARAMS,
        name="pack_rows_and_edges",
    )(
        src_count, kept(src_values),
        kept(src_owner.reshape(groups, LANES)), kept(src_node.reshape(groups, LANES)),
        kept(diag_blocks), kept(edge_blocks), kept(edge_mask),
    )
    rows = lax.all_to_all(rows, "gx", split_axis=0, concat_axis=0, tiled=True)

    nodes = (3, cells_x, cells_y)
    inverse, columns, strip = pl.pallas_call(
        edge_kernel,
        in_specs=[VMEM] * 3,
        out_specs=[VMEM] * 3,
        out_shape=[whole(nodes), whole((LANES, LANES)), whole((STRIP, LANES))],
        compiler_params=PARAMS,
        cost_estimate=pl.CostEstimate(
            flops=10**8, bytes_accessed=4 * 10**6, transcendentals=0
        ),
        name="edge_columns",
    )(diag_blocks, edge_blocks, edge_mask)
    strip = lax.ppermute(strip, "gx", [(i, i + 1) for i in range(width_gx - 1)])

    half = (cells_x + 2 * PAD) // 2
    size = -(-6 * half // 16) * 16
    own_load = pl.pallas_call(
        functools.partial(own_kernel, half=half),
        in_specs=[VMEM],
        out_specs=VMEM,
        out_shape=whole((size, 2 * LANES)),
        compiler_params=PARAMS,
        cost_estimate=pl.CostEstimate(
            flops=10**8, bytes_accessed=10**6, transcendentals=0
        ),
        name="own_load",
    )(own)
    field, halo, inner, outer = pl.pallas_call(
        field_kernel,
        in_specs=[VMEM] * 4,
        out_specs=[VMEM] * 4,
        out_shape=[
            whole(nodes), whole((24, cells_y)), whole((16, LANES)), whole((16, LANES)),
        ],
        scratch_shapes=[pltpu.VMEM((size, 2 * LANES), F32)],
        compiler_params=PARAMS,
        name="load_and_first_product",
    )(rows, own_load, inverse, columns)
    def swapped(columns, first):
        low = range(first, width_gy - 1, 2)
        pairs = [(i, i + 1) for i in low] + [(i + 1, i) for i in low]
        return lax.ppermute(columns, "gy", pairs)

    from_inner, from_outer = swapped(inner, 1), swapped(outer, 0)
    points, tiles = surf_node.shape[0], tile_box.shape[0]
    part, box_part, adjoint, before, matrix = pl.pallas_call(
        functools.partial(box_kernel, tile_points=points // tiles),
        in_specs=[VMEM] * 10,
        out_specs=[VMEM] * 5,
        out_shape=[
            whole(nodes),
            whole((4 * devices, LANES)),
            jax.ShapeDtypeStruct((2 * cells_x, tiles * LANES), BF16),
            whole((8, LANES)),
            jax.ShapeDtypeStruct((4 * devices, 8 * tiles), BF16),
        ],
        scratch_shapes=[
            pltpu.VMEM((tiles, points // tiles, LANES), BF16),
            pltpu.VMEM((2 * cells_x, points), BF16),
        ],
        compiler_params=PARAMS,
        cost_estimate=pl.CostEstimate(
            flops=10**9, bytes_accessed=4 * 10**6, transcendentals=0
        ),
        name="box_parts",
    )(
        tile_box.reshape(1, tiles), field, surf_node.reshape(points // LANES, LANES),
        surf_param, halo, strip, diag_blocks, edge_blocks, edge_mask, inverse,
    )

    quotient, partial = pl.pallas_call(
        sums_kernel,
        in_specs=[VMEM] * 14,
        out_specs=[VMEM] * 2,
        out_shape=[whole(nodes), whole((devices, 4, LANES))],
        compiler_params=PARAMS,
        name="sums_and_halo_parts",
    )(
        from_inner, from_outer, inner, outer, field, part, halo, diag_blocks, edge_blocks, edge_mask,
        box_part, adjoint, before, matrix,
    )
    got = lax.all_to_all(partial, ("gx", "gy"), split_axis=0, concat_axis=0, tiled=True)
    return pl.pallas_call(
        result_kernel,
        in_specs=[VMEM] * 3,
        out_specs=[VMEM] * 2,
        out_shape=[whole(nodes), whole((1, 192))],
        compiler_params=PARAMS,
        name="steps_and_outputs",
    )(got, field, quotient)


def solution(mesh):
    return jax.shard_map(
        per_device,
        mesh=mesh,
        in_specs=(
            P(None, "gx", "gy"),
            P(None, None, "gx", "gy"),
            P(None, "gx", "gy"),
            P(None, ("gx", "gy")),
            P(("gx", "gy"), None),
            P(("gx", "gy")),
            P(("gx", "gy")),
            P(("gx", "gy")),
            P(None, ("gx", "gy")),
            P(("gx", "gy")),
        ),
        out_specs=(P(None, "gx", "gy"), P(("gx", "gy"), None)),
        check_vma=False,
    )
```

```python
import functools

import jax
import jax.numpy as jnp
from jax import lax
from jax.experimental import pallas as pl
from jax.experimental.pallas import tpu as pltpu
from jax.sharding import PartitionSpec as P

F32 = jnp.float32
BF16 = jnp.bfloat16
PAD = 2
NOWHERE = -(1 << 20)
LANES = 128
NEAR = 16
STRIP = 40
CHUNK = 256
PARAMS = pltpu.CompilerParams(vmem_limit_bytes=24 * 1024 * 1024)

VMEM = pl.BlockSpec(memory_space=pltpu.VMEM)
SMEM = pl.BlockSpec(memory_space=pltpu.SMEM)
HBM = pl.BlockSpec(memory_space=pltpu.HBM)


def iota(shape, dim):
    return lax.broadcasted_iota(jnp.int32, shape, dim)


def float_iota(shape, dim):
    return iota(shape, dim).astype(F32)


def two_parts(value):
    high = value.astype(BF16).astype(F32)
    return high, value - high


def product(block, field):
    return [
        block(row) * field[0] + block(3 + row) * field[1] + block(6 + row) * field[2]
        for row in range(3)
    ]


def off_diagonal(block, field):
    return [
        sum(block(3 * i + row) * field[i] for i in range(3) if i != row) for row in range(3)
    ]


def masked_product(edge_ref, mask_ref, direction, field):
    mask = mask_ref[direction].astype(F32)
    return [mask * part for part in product(lambda k: edge_ref[direction, k], field)]


def rows_moved(field, edge_row, step):
    size = field.shape[0]
    at = iota(field.shape, 0)
    moved = pltpu.roll(field, step % size, 0)
    return jnp.where(at == (0 if step == 1 else size - 1), edge_row, moved)


def lanes_moved(field, edge_column, step):
    size = field.shape[1]
    at = iota(field.shape, 1)
    moved = pltpu.roll(field, step % size, 1)
    return jnp.where(at == (0 if step == 1 else size - 1), edge_column, moved)


def pack_kernel(
    count_ref, values_in, owner_in, node_in, diag_in, edge_in, mask_in, rows_out, own_ref,
    values_ref, owner_ref, node_ref, diag_low, diag_high, edge_low, edge_high, side_high,
    mask_low, mask_high, rows_ref, arrived, left,
):
    targets = rows_ref.shape[0]
    groups = owner_ref.shape[0]
    cells_x = diag_in.shape[1]
    top = pl.ds(cells_x - 8, 8)
    pieces = [
        (owner_in, owner_ref),
        (node_in, node_ref),
        (values_in, values_ref),
        (edge_in.at[pl.ds(2, 2), :, top], side_high),
        (edge_in.at[0, :, top], edge_high),
        (edge_in.at[1, :, 0:8], edge_low),
        (mask_in.at[:, top], mask_high),
        (mask_in.at[1, 0:8], mask_low),
    ]
    for k in range(3):
        pieces.append((diag_in.at[4 * k, top], diag_high.at[k]))
        pieces.append((diag_in.at[4 * k, 0:8], diag_low.at[k]))
    copies = [
        pltpu.make_async_copy(source, target, arrived.at[k])
        for k, (source, target) in enumerate(pieces)
    ]
    for copy in copies:
        copy.start()
    base = 4 * groups
    for target in range(targets):
        rows_ref[target, base:, :] = jnp.zeros((NEAR, LANES), F32)
    for copy in copies[:2]:
        copy.wait()
    order = iota((groups, LANES), 0) * LANES + iota((groups, LANES), 1)
    node = node_ref[...]
    frame = cells_x + 2 * PAD
    row = owner_ref[...] * cells_x + lax.shift_right_logical(node, 7)
    row = jnp.where(order < count_ref[0], row, NOWHERE)
    column = node & (LANES - 1)
    for target in range(targets):
        line = row - (target * cells_x - PAD)
        inside = (line >= 0) & (line < frame)
        index = jnp.where(inside, line * LANES + column, -1)
        rows_ref[target, 3 * groups : 4 * groups, :] = index.astype(F32)

    copies[2].wait()
    for comp in range(3):
        value = jnp.concatenate(
            [
                values_ref[comp : comp + 1, group * LANES : (group + 1) * LANES]
                for group in range(groups)
            ],
            axis=0,
        )
        for target in range(targets):
            rows_ref[target, comp * groups : (comp + 1) * groups, :] = value
    near = pl.ds(4 * groups, NEAR)
    leaving = [
        pltpu.make_async_copy(rows_ref.at[:, part], rows_out.at[:, part], left.at[k])
        for k, part in enumerate((pl.ds(0, 4 * groups), near))
    ]
    leaving[0].start()
    for copy in copies[3:]:
        copy.wait()

    here = lax.axis_index("gx")

    def block(edge, mask):
        present = mask.astype(F32)
        return [edge(k) * present for k in range(9)]

    @pl.when(here < targets - 1)
    def _():
        def put(slot, value):
            rows_ref[here + 1, base + slot : base + slot + 1, :] = value

        for k in range(3):
            put(k, diag_high[k, 7:8, :])
        toward = block(lambda k: edge_high[k, 7:8, :], mask_high[0, 7:8, :])
        up_y = block(lambda k: side_high[0, k, 7:8, :], mask_high[2, 7:8, :])
        low_y = block(lambda k: side_high[1, k, 7:8, :], mask_high[3, 7:8, :])
        corners = jnp.zeros((1, LANES), F32)
        lane = iota((1, LANES), 1)
        for k in range(9):
            put(3 + k, toward[k])
            corners = jnp.where(lane == k, up_y[k][:, LANES - 1 :], corners)
            corners = jnp.where(lane == 9 + k, low_y[k][:, :1], corners)
        put(12, corners)

    @pl.when(here > 0)
    def _():
        def put(slot, value):
            rows_ref[here - 1, base + slot : base + slot + 1, :] = value

        for k in range(3):
            put(k, diag_low[k, 0:1, :])
        for k, value in enumerate(block(lambda k: edge_low[k, 0:1, :], mask_low[0:1, :])):
            put(3 + k, value)

    leaving[1].start()
    own_ref[...] = rows_ref[here, : 4 * groups, :]
    for copy in leaving:
        copy.wait()


def stretched(row, count):
    tile = jnp.broadcast_to(row, (16, row.shape[1])).astype(BF16)
    return jnp.concatenate([tile] * (count // 16), axis=0)


def ratio(value, scale):
    return jnp.where(scale > 0.0, value / jnp.where(scale > 0.0, scale, 1.0), 0.0)


UP_X, LOW_X, INWARD, OUTWARD, WITHIN, INVERSE = 0, 3, 6, 9, 12, 15


def edge_kernel(diag_ref, edge_ref, mask_ref, inverse_ref, columns_ref, strip_ref):
    cells_x = diag_ref.shape[1]
    last = cells_x - 1
    strip = [diag_ref[k, last:, :] for k in range(9) if k % 4]
    for direction, at in ((2, last), (3, last), (0, last - 1)):
        present = mask_ref[direction, at : at + 1, :].astype(F32)
        strip += [edge_ref[direction, k, at : at + 1, :] * present for k in range(9)]
    strip += [diag_ref[4 * k, last - 1 : last, :] for k in range(3)]
    for k, value in enumerate(strip):
        strip_ref[k : k + 1, :] = value
    strip_ref[len(strip) :, :] = jnp.zeros((STRIP - len(strip), LANES), F32)
    at = iota((cells_x, LANES), 1)
    sides = [jnp.zeros((cells_x, LANES), F32) for _ in range(2)]

    def put(kind, i, a, first, first_lane, last, last_lane):
        slot = 8 * (kind + i) + a
        for side, (field, lane) in enumerate(((first, first_lane), (last, last_lane))):
            sides[side] = jnp.where(at == slot, field[:, lane : lane + 1], sides[side])

    inverse = [1.0 / diag_ref[4 * c] for c in range(3)]
    end = LANES - 1
    masks = [mask_ref[direction].astype(F32) for direction in range(4)]
    for i in range(3):
        inverse_ref[i] = inverse[i]
        put(INVERSE, 0, i, inverse[i], 0, inverse[i], end)
        for a in range(3):
            up_x, low_x, up_y, low_y = (
                edge_ref[direction, 3 * i + a] * masks[direction] for direction in range(4)
            )
            put(UP_X, i, a, up_x, 0, up_x, end)
            put(LOW_X, i, a, low_x, 0, low_x, end)
            put(INWARD, i, a, low_y, 1, up_y, end - 1)
            put(OUTWARD, i, a, low_y, 0, up_y, end)
            if a != i:
                put(WITHIN, i, a, diag_ref[3 * i + a], 0, diag_ref[3 * i + a], end)
    columns_ref[...] = jnp.concatenate(sides, axis=0).T


def load_product(blocks, half):
    groups = blocks[0].shape[0] // 4
    size = -(-6 * half // 16) * 16
    line = iota((size, LANES), 0)
    block = sum(jnp.where(line >= half * k, 1, 0) for k in range(1, 6))
    at_row = jnp.where(line < 6 * half, line - half * block, -5).astype(F32).astype(BF16)
    at_column = float_iota((2 * LANES, LANES), 0).astype(BF16)
    in_tile = float_iota((16, LANES), 0).astype(BF16)
    zero, one = jnp.zeros((), BF16), jnp.ones((), BF16)
    lefts, rights = [], []
    for rows in blocks:
        index = rows[3 * groups :]
        split = float(half * LANES)
        index, shift = (
            jnp.where(index >= split, index - split, index),
            jnp.where(index >= split, float(LANES), 0.0),
        )
        place = jnp.floor(index * (1.0 / LANES))
        column = index - place * float(LANES) + shift
        parts = [two_parts(rows[c * groups : (c + 1) * groups]) for c in range(3)]
        for group in range(groups):
            here = slice(group, group + 1)
            values = [
                stretched(parts[c][which][here], 16) for which in range(2) for c in range(3)
            ]
            tiles = []
            for first in range(0, size, 16):
                low, high = first // half, min((first + 15) // half, 5)
                tiles.append(
                    values[low]
                    if low == high
                    else jnp.where(
                        in_tile < float(half * high - first), values[low], values[high]
                    )
                )
            match = at_row == stretched(place[here], size)
            lefts.append(jnp.where(match, jnp.concatenate(tiles, axis=0), zero))
            rights.append(
                jnp.where(at_column == stretched(column[here], 2 * LANES), one, zero)
            )
    return lax.dot_general(
        jnp.concatenate(lefts, axis=1),
        jnp.concatenate(rights, axis=1),
        (((1,), (1,)), ((), ())),
        preferred_element_type=F32,
    )


def own_kernel(rows_ref, load_ref, *, half):
    load_ref[...] = load_product([rows_ref[...]], half)


def field_kernel(
    rows_ref, own_ref, inverse_ref, columns_ref,
    field_ref, halo_ref, inner_ref, outer_ref, load_ref,
):
    senders = rows_ref.shape[0]
    groups = (rows_ref.shape[1] - NEAR) // 4
    cells_x = field_ref.shape[1]
    half = (cells_x + 2 * PAD) // 2
    own = cells_x // 2

    load_ref[...] = own_ref[...]
    here = lax.axis_index("gx")
    others = senders - 1
    together = others if others <= 8 else 1

    def add_rows(step, carry):
        blocks = []
        for k in range(together):
            sender = step * together + k
            sender = jnp.where(sender >= here, sender + 1, sender)
            blocks.append(rows_ref[sender, : 4 * groups, :])
        load_ref[...] += load_product(blocks, half)
        return carry

    lax.fori_loop(0, others // together, add_rows, 0)

    def load_rows(comp, first, last, second_half):
        lanes = slice(LANES, 2 * LANES) if second_half else slice(0, LANES)
        return (
            load_ref[comp * half + first : comp * half + last, lanes]
            + load_ref[(3 + comp) * half + first : (3 + comp) * half + last, lanes]
        )

    field = []
    for comp in range(3):
        load = jnp.concatenate(
            [load_rows(comp, PAD, half, False), load_rows(comp, 0, half - PAD, True)], axis=0
        )
        field.append(load * inverse_ref[comp])
        field_ref[comp] = field[comp]
    beyond = half - PAD
    near_before = [load_rows(c, PAD - 1, PAD, False) for c in range(3)]
    far_before = [load_rows(c, PAD - 2, PAD - 1, False) for c in range(3)]
    near_after = [load_rows(c, beyond, beyond + 1, True) for c in range(3)]

    base = 4 * groups

    def neighbour(sender, load):
        def entry(k):
            return rows_ref[sender, base + k : base + k + 1, :]

        inverse = [ratio(1.0, entry(k)) for k in range(3)]
        toward = [entry(3 + k) for k in range(9)]
        beside = [load[c] * inverse[c] for c in range(3)]
        return inverse, toward, beside, product(lambda k: toward[k], beside)

    lower = jnp.maximum(here - 1, 0)
    before = neighbour(lower, near_before)
    after = neighbour(jnp.minimum(here + 1, senders - 1), near_after)
    rows = before[2] + before[0] + before[3] + before[1] + far_before + after[3]
    for k, value in enumerate(rows):
        halo_ref[k : k + 1, :] = value
    lane_row = iota((1, LANES), 1)
    ends = jnp.zeros((1, LANES), F32)
    for i in range(3):
        for first, end in ((3 * i, LANES - 1), (9 + 3 * i, 0)):
            mine = (lane_row >= first) & (lane_row < first + 3)
            ends = jnp.where(mine, before[2][i][:, end : end + 1], ends)
    ends = ends * rows_ref[lower, base + 12 : base + 13, :]
    ends = ends + pltpu.roll(ends, LANES - 3, 1) + pltpu.roll(ends, LANES - 6, 1)

    two = jnp.concatenate(field[:2], axis=0).T
    third = jnp.concatenate([field[2], field[2]], axis=0).T

    def column_rows(first, last):
        low = lane_row < cells_x
        one, other = two[first : first + 1], two[last : last + 1]
        return [
            jnp.where(low, one, pltpu.roll(other, cells_x, 1)),
            jnp.where(low, pltpu.roll(one, cells_x, 1), other),
            jnp.where(low, third[first : first + 1], third[last : last + 1]),
        ]

    edge = column_rows(0, LANES - 1)
    inside = column_rows(1, LANES - 2)

    def column_product(kind, rows):
        return sum(
            columns_ref[8 * (kind + i) : 8 * (kind + i) + 8, :] * rows[i] for i in range(3)
        )

    def eight(rows):
        return jnp.concatenate(rows + [jnp.zeros((8 - len(rows), LANES), F32)], axis=0)

    lane = iota((8, LANES), 1)
    from_before, from_after = eight(before[3]), eight(after[3])
    from_before = jnp.where(lane == 0, from_before, pltpu.roll(from_before, cells_x + 1, 1))
    from_after = jnp.where(
        lane == LANES - 1, from_after, pltpu.roll(from_after, cells_x - 1, 1)
    )
    row = lane & (cells_x - 1)
    upward = pltpu.roll(column_product(UP_X, edge), 1, 1)
    downward = pltpu.roll(column_product(LOW_X, edge), LANES - 1, 1)
    total = (
        column_product(WITHIN, edge)
        + jnp.where(row == 0, from_before, upward)
        + jnp.where(row == cells_x - 1, from_after, downward)
        + column_product(INWARD, inside)
    )
    inverse = columns_ref[8 * INVERSE : 8 * INVERSE + 8, :]
    along_y, part = column_product(OUTWARD, edge), total * inverse
    stacked = jnp.concatenate(
        [*edge, along_y[:3], part[:3], inverse[:3], jnp.zeros((4, LANES), F32)], axis=0
    )

    def message(columns, end):
        at = iota((16, LANES), 1)
        line = iota((16, LANES), 0)
        columns = jnp.where(at < cells_x, columns, 0.0)
        for comp in range(3):
            columns = jnp.where(
                (line == 3 + comp) & (at == cells_x),
                ends[:, end + comp : end + comp + 1],
                columns,
            )
        return columns

    inner_ref[...], outer_ref[...] = by_parity(
        message(stacked, 9), message(pltpu.roll(stacked, cells_x, 1), 0)
    )


def bernstein(coord):
    other = 1.0 - coord
    return [
        other * other * other,
        3.0 * coord * other * other,
        3.0 * coord * coord * other,
        coord * coord * coord,
    ]


def weight_table(u, v, w):
    first, second, third = bernstein(u), bernstein(v), bernstein(w)
    line = iota((8, u.shape[1]), 0)
    inner = line & 3
    along = jnp.where(
        inner == 0,
        third[0],
        jnp.where(inner == 1, third[1], jnp.where(inner == 2, third[2], third[3])),
    )
    pair = jnp.concatenate(
        [
            jnp.where(line < 4, second[0], second[1]) * along,
            jnp.where(line < 4, second[2], second[3]) * along,
        ],
        axis=0,
    )
    return jnp.concatenate([pair * first[i] for i in range(4)], axis=0)


def tile_rows(terms):
    first_half = iota((4, LANES), 1) < LANES // 2
    rows = []
    for term in terms:
        term = term[:8] + term[8:]
        term = term + pltpu.roll(term, LANES // 2, 1)
        rows.append(jnp.where(first_half, term[:4], term[4:]))
    return jnp.concatenate(two_parts(jnp.concatenate(rows, axis=0)), axis=0).astype(BF16)


def box_matrix(tile_row, boxes):
    tiles = tile_row.shape[1]
    shape = (4 * boxes, 8 * tiles)
    column = iota((1, shape[1]), 1)
    box = jnp.zeros((1, shape[1]), jnp.int32)
    for tile in range(tiles):
        mine = lax.rem(lax.shift_right_logical(column, 2), tiles) == tile
        box = jnp.where(mine, tile_row[:, tile : tile + 1], box)
    target = 4 * box + (column & 3)
    return jnp.where(iota(shape, 0) == target, 1.0, 0.0).astype(BF16)


def by_parity(low, high):
    odd = lax.rem(lax.axis_index("gy"), 2) == 1
    return jnp.where(odd, high, low), jnp.where(odd, low, high)


def quotient_before(halo_ref, strip_ref, before_ref, entering):
    def rows(ref, first, count):
        return [ref[first + k : first + k + 1, :] for k in range(count)]

    beside, inverse = rows(halo_ref, 0, 3), rows(halo_ref, 3, 3)
    far_load, within = rows(halo_ref, 18, 3), rows(strip_ref, 0, 6)
    far_scale = rows(strip_ref, 33, 3)
    far = [ratio(far_load[c], far_scale[c]) for c in range(3)]
    whole_block = [None, *within[:3], None, *within[3:], None]
    total = off_diagonal(lambda k: whole_block[k], beside)
    from_far = product(lambda k: strip_ref[24 + k : 25 + k, :], far)
    up_y = product(lambda k: strip_ref[6 + k : 7 + k, :], beside)
    low_y = product(lambda k: strip_ref[15 + k : 16 + k, :], beside)
    for c in range(3):
        before_ref[c : c + 1, :] = inverse[c] * (
            total[c]
            + from_far[c]
            + entering[c]
            + lanes_moved(up_y[c], 0.0, 1)
            + lanes_moved(low_y[c], 0.0, -1)
        )
    before_ref[3:, :] = jnp.zeros((before_ref.shape[0] - 3, LANES), F32)


def box_kernel(
    tile_ref, field_ref, node_ref, param_ref, halo_ref, strip_ref, diag_ref, edge_ref,
    mask_ref, inverse_ref,
    part_ref, box_ref, adjoint_ref, before_ref, matrix_ref, weights_ref, columns_ref,
    *, tile_points,
):
    cells_x = field_ref.shape[1]
    own = cells_x // 2
    field = [field_ref[c] for c in range(3)]
    part = off_diagonal(lambda k: diag_ref[k], field)
    up_x = masked_product(edge_ref, mask_ref, 0, field)
    low_x = masked_product(edge_ref, mask_ref, 1, field)
    up_y = masked_product(edge_ref, mask_ref, 2, field)
    low_y = masked_product(edge_ref, mask_ref, 3, field)
    for c in range(3):
        part[c] = inverse_ref[c] * (
            part[c]
            + rows_moved(up_x[c], halo_ref[6 + c : 7 + c, :], 1)
            + rows_moved(low_x[c], halo_ref[21 + c : 22 + c, :], -1)
            + lanes_moved(up_y[c], 0.0, 1)
            + lanes_moved(low_y[c], 0.0, -1)
        )
        part_ref[c] = part[c]
    quotient_before(halo_ref, strip_ref, before_ref, [p[:1] for p in low_x])
    order = [field[0], part[0], field[2], field[1], part[1], part[2]]
    folded = [two_parts(jnp.concatenate([f[:own], f[own:]], axis=1)) for f in order]
    table = jnp.concatenate(
        [folded[f][which] for which in range(2) for f in range(6)], axis=0
    ).astype(BF16)
    points = param_ref.shape[1]
    pieces = CHUNK // LANES
    zero, one = jnp.zeros((), BF16), jnp.ones((), BF16)
    at_node = float_iota((2 * LANES, CHUNK), 0).astype(BF16)
    nothing = jnp.zeros((1, CHUNK), F32)
    highs, lows = [], []
    for chunk in range(points // CHUNK):
        node = jnp.concatenate(
            [node_ref[chunk * pieces + k : chunk * pieces + k + 1, :] for k in range(pieces)],
            axis=1,
        )
        row = lax.shift_right_logical(node, 7)
        column = node & (LANES - 1)
        lanes = slice(chunk * CHUNK, (chunk + 1) * CHUNK)
        at_edge = jnp.where(
            column == 0, row, jnp.where(column == LANES - 1, row + cells_x, -1)
        ).astype(F32)
        columns_ref[:, lanes] = jnp.where(
            at_node[: 2 * cells_x] == stretched(at_edge, 2 * cells_x), one, zero
        )
        place = column + jnp.where(row >= own, LANES, 0)
        row = jnp.where(row >= own, row - own, row)
        pick = jnp.where(at_node == stretched(place.astype(F32), 2 * LANES), one, zero)
        read = jnp.dot(table, pick, preferred_element_type=F32)
        read = read[: 6 * own] + read[6 * own :]
        here = iota((own, CHUNK), 0) == row
        values = [
            jnp.sum(
                jnp.where(here, read[f * own : (f + 1) * own], 0.0), axis=0, keepdims=True
            )
            for f in range(6)
        ]
        high, low = two_parts(
            jnp.concatenate(values[:3] + [nothing] + values[3:] + [nothing], axis=0)
        )
        highs.append(high)
        lows.append(low)
        weights = two_parts(
            weight_table(param_ref[0:1, lanes], param_ref[1:2, lanes], param_ref[2:3, lanes])
        )
        for k in range(CHUNK // tile_points):
            tile = slice(k * tile_points, (k + 1) * tile_points)
            sides = jnp.concatenate([weights[0][:, tile], weights[1][:, tile]], axis=0)
            weights_ref[chunk * (CHUNK // tile_points) + k] = sides.T.astype(BF16)
    both = jnp.concatenate(
        [jnp.concatenate(highs, axis=1), jnp.concatenate(lows, axis=1)], axis=0
    ).astype(BF16)
    matrix_ref[...] = box_matrix(tile_ref[...], matrix_ref.shape[0] // 4)
    tiles = tile_ref.shape[1]
    terms = [
        jnp.dot(
            both[:, tile * tile_points : (tile + 1) * tile_points],
            weights_ref[tile],
            preferred_element_type=F32,
        )
        for tile in range(tiles)
    ]
    box_ref[...] = jnp.dot(matrix_ref[...], tile_rows(terms), preferred_element_type=F32)
    low_half = iota((2 * cells_x, LANES), 1) < LANES // 2
    for tile in range(tiles):
        lanes = slice(tile * tile_points, (tile + 1) * tile_points)
        term = jnp.dot(
            columns_ref[:, lanes], weights_ref[tile], preferred_element_type=F32
        )
        high, low = two_parts(term + pltpu.roll(term, LANES // 2, 1))
        adjoint_ref[:, tile * LANES : (tile + 1) * LANES] = jnp.where(
            low_half, high, low
        ).astype(BF16)


def sums_kernel(
    from_inner_ref, from_outer_ref, inner_ref, outer_ref, field_ref, part_ref, halo_ref,
    diag_ref, edge_ref, mask_ref, box_ref, adjoint_ref, before_ref, matrix_ref,
    quotient_ref, out_ref,
):
    cells_x = field_ref.shape[1]
    targets = out_ref.shape[0]

    from_low, from_high = by_parity(from_inner_ref[...], from_outer_ref[...])
    first, last = by_parity(inner_ref[...], outer_ref[...])

    lane_row = iota((1, LANES), 1)
    shares, edges = [], []
    for arrived, own in ((from_low, first), (from_high, last)):
        def row(source, slot, c):
            return source[3 * slot + c : 3 * slot + c + 1]

        shares.append([row(arrived, 1, c) * row(own, 3, c) for c in range(3)])
        edges.append(
            [row(arrived, 2, c) + row(arrived, 3, c) * row(own, 1, c) for c in range(3)]
        )

    def turned(columns, share, edge):
        kept = [
            jnp.where(lane_row < cells_x, share[c], columns[3 + c : 4 + c]) for c in range(3)
        ]
        rest = jnp.zeros((LANES - 9, LANES), F32)
        return jnp.concatenate([columns[:3], *kept, *edge, rest], axis=0).T

    low = turned(from_low, shares[0], edges[0])
    high = turned(from_high, shares[1], edges[1])
    lane = iota((cells_x, LANES), 1)

    def column(source, slot, comp):
        return source[:cells_x, 3 * slot + comp : 3 * slot + comp + 1]

    field = [field_ref[c] for c in range(3)]
    scale = [diag_ref[4 * c] for c in range(3)]
    quotient, low_edge, high_edge = [], [], []
    for c in range(3):
        entering = jnp.where(
            lane == 0,
            column(low, 1, c),
            jnp.where(lane == LANES - 1, column(high, 1, c), 0.0),
        )
        quotient.append(part_ref[c] + entering)
        low_edge.append(column(low, 2, c))
        high_edge.append(column(high, 2, c))
    for c in range(3):
        quotient_ref[c] = quotient[c]
    before, before_quotient = [], []
    for c in range(3):
        entering = jnp.where(
            lane_row == 0,
            low[cells_x : cells_x + 1, 3 + c : 4 + c],
            jnp.where(lane_row == LANES - 1, high[cells_x : cells_x + 1, 3 + c : 4 + c], 0.0),
        )
        before.append(halo_ref[c : c + 1, :])
        before_quotient.append(
            before_ref[c : c + 1, :] + entering * halo_ref[3 + c : 4 + c, :]
        )

    first_sum = sum(field[c] * scale[c] * field[c] for c in range(3))
    second_sum = sum(field[c] * scale[c] * quotient[c] for c in range(3))
    third_sum = sum(quotient[c] * scale[c] * quotient[c] for c in range(3))
    within = off_diagonal(lambda k: diag_ref[k], quotient)
    fourth_sum = sum(within[c] * field[c] for c in range(3))
    fifth_sum = sum(within[c] * quotient[c] for c in range(3))
    at_row = iota((cells_x, LANES), 0)
    moves = (
        (pltpu.roll, 1, 0, at_row == 0),
        (pltpu.roll, cells_x - 1, 0, at_row == cells_x - 1),
        (pltpu.roll, 1, 1, lane == 0),
        (pltpu.roll, LANES - 1, 1, lane == LANES - 1),
    )
    extra = [0.0, 0.0]
    sides = [0.0, 0.0]
    for direction, (roll, step, dim, edge) in enumerate(moves):
        moving = masked_product(edge_ref, mask_ref, direction, quotient)
        for c in range(3):
            moved = jnp.where(edge, 0.0, roll(moving[c], step, dim))
            fourth_sum = fourth_sum + moved * field[c]
            fifth_sum = fifth_sum + moved * quotient[c]
            if direction == 1:
                extra[0] += moving[c][:1] * before[c]
                extra[1] += moving[c][:1] * before_quotient[c]
            elif direction == 2:
                sides[0] += moving[c][:, LANES - 1 :] * column(high, 0, c)
                sides[1] += moving[c][:, LANES - 1 :] * high_edge[c]
            elif direction == 3:
                sides[0] += moving[c][:, :1] * column(low, 0, c)
                sides[1] += moving[c][:, :1] * low_edge[c]
    incoming = product(lambda k: halo_ref[9 + k : 10 + k, :], before_quotient)
    extra[0] += sum(incoming[c] * field[c][:1] for c in range(3))
    extra[1] += sum(incoming[c] * quotient[c][:1] for c in range(3))
    fourth_sum = fourth_sum + jnp.where(lane == 0, sides[0], 0.0)
    fifth_sum = fifth_sum + jnp.where(lane == 0, sides[1], 0.0)
    extra = [0.0, 0.0, 0.0, extra[0], extra[1]]
    sums = jnp.zeros((1, LANES), F32)
    for k, value in enumerate((first_sum, second_sum, third_sum, fourth_sum, fifth_sum)):
        line = jnp.sum(value, axis=0, keepdims=True) + extra[k]
        sums = jnp.where(lane_row == k, jnp.sum(line, axis=1, keepdims=True), sums)

    added = [
        jnp.where(lane_row < cells_x, shares[0][c], pltpu.roll(shares[1][c], cells_x, 1))
        for c in range(3)
    ]
    none = jnp.zeros((1, LANES), F32)
    added = jnp.concatenate(
        [none, added[0], none, none, none, added[1], added[2], none], axis=0
    )
    added = jnp.concatenate(two_parts(added), axis=0).astype(BF16)
    terms = jnp.dot(added, adjoint_ref[...], preferred_element_type=F32)
    terms = [
        terms[:, first : first + LANES] for first in range(0, terms.shape[1], LANES)
    ]
    total = box_ref[...] + jnp.dot(
        matrix_ref[...], tile_rows(terms), preferred_element_type=F32
    )
    total = jnp.where((iota(total.shape, 0) & 3) == 3, sums, total)
    for box in range(targets):
        out_ref[box] = total[4 * box : 4 * box + 4]


def result_kernel(got_ref, field_ref, quotient_ref, solution_ref, gradient_ref):
    total = jnp.sum(got_ref[...], axis=0)
    rho, a, b, t, u = [total[3:4, k : k + 1] for k in range(5)]
    norm = rho + a
    by_rho, by_norm = 1.0 / rho, 1.0 / norm
    ratio, step = a * by_rho, rho * by_norm
    rest = jnp.maximum(b - a * ratio, 0.0)
    beta = step * step * rest * by_rho
    rest_image = (b + u) - ratio * (a + b + a + t) + ratio * ratio * norm
    cross = (a + t) - ratio * norm
    curve = step * step * rest_image - step * beta * (rest + cross) + beta * beta * norm
    second = jnp.where(
        curve > 0.0, step * step * rest / jnp.where(curve > 0.0, curve, 1.0), 0.0
    )
    second = jnp.minimum(second, 16.0)
    of_field = step + second * (beta + step * ratio)
    of_quotient = -(step * second)
    for c in range(3):
        solution_ref[c] = of_field * field_ref[c] + of_quotient * quotient_ref[c]
    gradient_ref[:, :LANES] = of_field * total[0:1] + of_quotient * total[1:2]
    gradient_ref[:, LANES:] = (
        of_field * total[2:3, : LANES // 2] + of_quotient * total[2:3, LANES // 2 :]
    )


def per_device(
    diag_blocks, edge_blocks, edge_mask, src_values, src_owner, src_node, src_count,
    surf_node, surf_param, tile_box,
):
    cells_x, cells_y = diag_blocks.shape[1:]
    width_gx, width_gy = lax.axis_size("gx"), lax.axis_size("gy")
    devices = width_gx * width_gy
    groups = src_node.shape[0] // LANES
    whole = functools.partial(jax.ShapeDtypeStruct, dtype=F32)

    cells = 4 * groups + NEAR

    def kept(array):
        return pltpu.with_memory_space_constraint(array, pltpu.HBM)

    i32 = jnp.int32
    rows, own = pl.pallas_call(
        pack_kernel,
        in_specs=[SMEM] + [HBM] * 6,
        out_specs=[HBM, VMEM],
        out_shape=[
            pltpu.HBM((width_gx, cells, LANES), F32),
            pltpu.VMEM((4 * groups, LANES), F32),
        ],
        scratch_shapes=[
            pltpu.VMEM(src_values.shape, F32),
            pltpu.VMEM((groups, LANES), i32),
            pltpu.VMEM((groups, LANES), i32),
            pltpu.VMEM((3, 8, cells_y), F32),
            pltpu.VMEM((3, 8, cells_y), F32),
            pltpu.VMEM((9, 8, cells_y), F32),
            pltpu.VMEM((9, 8, cells_y), F32),
            pltpu.VMEM((2, 9, 8, cells_y), F32),
            pltpu.VMEM((8, cells_y), i32),
            pltpu.VMEM((4, 8, cells_y), i32),
            pltpu.VMEM((width_gx, cells, LANES), F32),
            pltpu.SemaphoreType.DMA((14,)),
            pltpu.SemaphoreType.DMA((2,)),
        ],
        compiler_params=PARAMS,
        name="pack_rows_and_edges",
    )(
        src_count, kept(src_values),
        kept(src_owner.reshape(groups, LANES)), kept(src_node.reshape(groups, LANES)),
        kept(diag_blocks), kept(edge_blocks), kept(edge_mask),
    )
    rows = lax.all_to_all(rows, "gx", split_axis=0, concat_axis=0, tiled=True)

    nodes = (3, cells_x, cells_y)
    inverse, columns, strip = pl.pallas_call(
        edge_kernel,
        in_specs=[VMEM] * 3,
        out_specs=[VMEM] * 3,
        out_shape=[whole(nodes), whole((LANES, LANES)), whole((STRIP, LANES))],
        compiler_params=PARAMS,
        cost_estimate=pl.CostEstimate(
            flops=10**8, bytes_accessed=4 * 10**6, transcendentals=0
        ),
        name="edge_columns",
    )(diag_blocks, edge_blocks, edge_mask)
    strip = lax.ppermute(strip, "gx", [(i, i + 1) for i in range(width_gx - 1)])

    half = (cells_x + 2 * PAD) // 2
    size = -(-6 * half // 16) * 16
    own_load = pl.pallas_call(
        functools.partial(own_kernel, half=half),
        in_specs=[VMEM],
        out_specs=VMEM,
        out_shape=whole((size, 2 * LANES)),
        compiler_params=PARAMS,
        cost_estimate=pl.CostEstimate(
            flops=10**8, bytes_accessed=10**6, transcendentals=0
        ),
        name="own_load",
    )(own)
    field, halo, inner, outer = pl.pallas_call(
        field_kernel,
        in_specs=[VMEM] * 4,
        out_specs=[VMEM] * 4,
        out_shape=[
            whole(nodes), whole((24, cells_y)), whole((16, LANES)), whole((16, LANES)),
        ],
        scratch_shapes=[pltpu.VMEM((size, 2 * LANES), F32)],
        compiler_params=PARAMS,
        name="load_and_first_product",
    )(rows, own_load, inverse, columns)
    def swapped(columns, first):
        low = range(first, width_gy - 1, 2)
        pairs = [(i, i + 1) for i in low] + [(i + 1, i) for i in low]
        return lax.ppermute(columns, "gy", pairs)

    from_inner, from_outer = swapped(inner, 1), swapped(outer, 0)
    points, tiles = surf_node.shape[0], tile_box.shape[0]
    part, box_part, adjoint, before, matrix = pl.pallas_call(
        functools.partial(box_kernel, tile_points=points // tiles),
        in_specs=[VMEM] * 10,
        out_specs=[VMEM] * 5,
        out_shape=[
            whole(nodes),
            whole((4 * devices, LANES)),
            jax.ShapeDtypeStruct((2 * cells_x, tiles * LANES), BF16),
            whole((8, LANES)),
            jax.ShapeDtypeStruct((4 * devices, 8 * tiles), BF16),
        ],
        scratch_shapes=[
            pltpu.VMEM((tiles, points // tiles, LANES), BF16),
            pltpu.VMEM((2 * cells_x, points), BF16),
        ],
        compiler_params=PARAMS,
        cost_estimate=pl.CostEstimate(
            flops=10**9, bytes_accessed=4 * 10**6, transcendentals=0
        ),
        name="box_parts",
    )(
        tile_box.reshape(1, tiles), field, surf_node.reshape(points // LANES, LANES),
        surf_param, halo, strip, diag_blocks, edge_blocks, edge_mask, inverse,
    )

    quotient, partial = pl.pallas_call(
        sums_kernel,
        in_specs=[VMEM] * 14,
        out_specs=[VMEM] * 2,
        out_shape=[whole(nodes), whole((devices, 4, LANES))],
        compiler_params=PARAMS,
        name="sums_and_halo_parts",
    )(
        from_inner, from_outer, inner, outer, field, part, halo, diag_blocks, edge_blocks, edge_mask,
        box_part, adjoint, before, matrix,
    )
    got = lax.all_to_all(partial, ("gx", "gy"), split_axis=0, concat_axis=0, tiled=True)
    return pl.pallas_call(
        result_kernel,
        in_specs=[VMEM] * 3,
        out_specs=[VMEM] * 2,
        out_shape=[whole(nodes), whole((1, 192))],
        compiler_params=PARAMS,
        name="steps_and_outputs",
    )(got, field, quotient)


def solution(mesh):
    return jax.shard_map(
        per_device,
        mesh=mesh,
        in_specs=(
            P(None, "gx", "gy"),
            P(None, None, "gx", "gy"),
            P(None, "gx", "gy"),
            P(None, ("gx", "gy")),
            P(("gx", "gy"), None),
            P(("gx", "gy")),
            P(("gx", "gy")),
            P(("gx", "gy")),
            P(None, ("gx", "gy")),
            P(("gx", "gy")),
        ),
        out_specs=(P(None, "gx", "gy"), P(("gx", "gy"), None)),
        check_vma=False,
    )
```

```python
import functools

import jax
import jax.numpy as jnp
from jax import lax
from jax.experimental import pallas as pl
from jax.experimental.pallas import tpu as pltpu
from jax.sharding import PartitionSpec as P

F32 = jnp.float32
BF16 = jnp.bfloat16
PAD = 2
NOWHERE = -(1 << 20)
LANES = 128
NEAR = 16
STRIP = 40
CHUNK = 256
PARAMS = pltpu.CompilerParams(vmem_limit_bytes=24 * 1024 * 1024)

VMEM = pl.BlockSpec(memory_space=pltpu.VMEM)
SMEM = pl.BlockSpec(memory_space=pltpu.SMEM)
HBM = pl.BlockSpec(memory_space=pltpu.HBM)


def iota(shape, dim):
    return lax.broadcasted_iota(jnp.int32, shape, dim)


def float_iota(shape, dim):
    return iota(shape, dim).astype(F32)


def two_parts(value):
    high = value.astype(BF16).astype(F32)
    return high, value - high


def product(block, field):
    return [
        block(row) * field[0] + block(3 + row) * field[1] + block(6 + row) * field[2]
        for row in range(3)
    ]


def off_diagonal(block, field):
    return [
        sum(block(3 * i + row) * field[i] for i in range(3) if i != row) for row in range(3)
    ]


def masked_product(edge_ref, mask_ref, direction, field):
    mask = mask_ref[direction].astype(F32)
    return [mask * part for part in product(lambda k: edge_ref[direction, k], field)]


def rows_moved(field, edge_row, step):
    size = field.shape[0]
    at = iota(field.shape, 0)
    moved = pltpu.roll(field, step % size, 0)
    return jnp.where(at == (0 if step == 1 else size - 1), edge_row, moved)


def lanes_moved(field, edge_column, step):
    size = field.shape[1]
    at = iota(field.shape, 1)
    moved = pltpu.roll(field, step % size, 1)
    return jnp.where(at == (0 if step == 1 else size - 1), edge_column, moved)


def pack_kernel(
    count_ref, values_in, owner_in, node_in, diag_in, edge_in, mask_in, rows_out, own_ref,
    values_ref, owner_ref, node_ref, diag_low, diag_high, edge_low, edge_high, side_high,
    mask_low, mask_high, rows_ref, arrived, left,
):
    targets = rows_ref.shape[0]
    groups = owner_ref.shape[0]
    cells_x = diag_in.shape[1]
    top = pl.ds(cells_x - 8, 8)
    pieces = [
        (owner_in, owner_ref),
        (node_in, node_ref),
        (values_in, values_ref),
        (edge_in.at[pl.ds(2, 2), :, top], side_high),
        (edge_in.at[0, :, top], edge_high),
        (edge_in.at[1, :, 0:8], edge_low),
        (mask_in.at[:, top], mask_high),
        (mask_in.at[1, 0:8], mask_low),
    ]
    for k in range(3):
        pieces.append((diag_in.at[4 * k, top], diag_high.at[k]))
        pieces.append((diag_in.at[4 * k, 0:8], diag_low.at[k]))
    copies = [
        pltpu.make_async_copy(source, target, arrived.at[k])
        for k, (source, target) in enumerate(pieces)
    ]
    for copy in copies:
        copy.start()
    base = 4 * groups
    for target in range(targets):
        rows_ref[target, base:, :] = jnp.zeros((NEAR, LANES), F32)
    for copy in copies[:2]:
        copy.wait()
    order = iota((groups, LANES), 0) * LANES + iota((groups, LANES), 1)
    node = node_ref[...]
    frame = cells_x + 2 * PAD
    row = owner_ref[...] * cells_x + lax.shift_right_logical(node, 7)
    row = jnp.where(order < count_ref[0], row, NOWHERE)
    column = node & (LANES - 1)
    for target in range(targets):
        line = row - (target * cells_x - PAD)
        inside = (line >= 0) & (line < frame)
        index = jnp.where(inside, line * LANES + column, -1)
        rows_ref[target, 3 * groups : 4 * groups, :] = index.astype(F32)

    copies[2].wait()
    for comp in range(3):
        value = jnp.concatenate(
            [
                values_ref[comp : comp + 1, group * LANES : (group + 1) * LANES]
                for group in range(groups)
            ],
            axis=0,
        )
        for target in range(targets):
            rows_ref[target, comp * groups : (comp + 1) * groups, :] = value
    near = pl.ds(4 * groups, NEAR)
    leaving = [
        pltpu.make_async_copy(rows_ref.at[:, part], rows_out.at[:, part], left.at[k])
        for k, part in enumerate((pl.ds(0, 4 * groups), near))
    ]
    leaving[0].start()
    for copy in copies[3:]:
        copy.wait()

    here = lax.axis_index("gx")

    def block(edge, mask):
        present = mask.astype(F32)
        return [edge(k) * present for k in range(9)]

    @pl.when(here < targets - 1)
    def _():
        def put(slot, value):
            rows_ref[here + 1, base + slot : base + slot + 1, :] = value

        for k in range(3):
            put(k, diag_high[k, 7:8, :])
        toward = block(lambda k: edge_high[k, 7:8, :], mask_high[0, 7:8, :])
        up_y = block(lambda k: side_high[0, k, 7:8, :], mask_high[2, 7:8, :])
        low_y = block(lambda k: side_high[1, k, 7:8, :], mask_high[3, 7:8, :])
        corners = jnp.zeros((1, LANES), F32)
        lane = iota((1, LANES), 1)
        for k in range(9):
            put(3 + k, toward[k])
            corners = jnp.where(lane == k, up_y[k][:, LANES - 1 :], corners)
            corners = jnp.where(lane == 9 + k, low_y[k][:, :1], corners)
        put(12, corners)

    @pl.when(here > 0)
    def _():
        def put(slot, value):
            rows_ref[here - 1, base + slot : base + slot + 1, :] = value

        for k in range(3):
            put(k, diag_low[k, 0:1, :])
        for k, value in enumerate(block(lambda k: edge_low[k, 0:1, :], mask_low[0:1, :])):
            put(3 + k, value)

    leaving[1].start()
    own_ref[...] = rows_ref[here, : 4 * groups, :]
    for copy in leaving:
        copy.wait()


def stretched(row, count):
    tile = jnp.broadcast_to(row, (16, row.shape[1])).astype(BF16)
    return jnp.concatenate([tile] * (count // 16), axis=0)


def ratio(value, scale):
    return jnp.where(scale > 0.0, value / jnp.where(scale > 0.0, scale, 1.0), 0.0)


UP_X, LOW_X, INWARD, OUTWARD, WITHIN, INVERSE = 0, 3, 6, 9, 12, 15


def edge_kernel(diag_ref, edge_ref, mask_ref, inverse_ref, columns_ref, strip_ref):
    cells_x = diag_ref.shape[1]
    last = cells_x - 1
    strip = [diag_ref[k, last:, :] for k in range(9) if k % 4]
    for direction, at in ((2, last), (3, last), (0, last - 1)):
        present = mask_ref[direction, at : at + 1, :].astype(F32)
        strip += [edge_ref[direction, k, at : at + 1, :] * present for k in range(9)]
    strip += [diag_ref[4 * k, last - 1 : last, :] for k in range(3)]
    for k, value in enumerate(strip):
        strip_ref[k : k + 1, :] = value
    strip_ref[len(strip) :, :] = jnp.zeros((STRIP - len(strip), LANES), F32)
    at = iota((cells_x, LANES), 1)
    sides = [jnp.zeros((cells_x, LANES), F32) for _ in range(2)]

    def put(kind, i, a, first, first_lane, last, last_lane):
        slot = 8 * (kind + i) + a
        for side, (field, lane) in enumerate(((first, first_lane), (last, last_lane))):
            sides[side] = jnp.where(at == slot, field[:, lane : lane + 1], sides[side])

    inverse = [1.0 / diag_ref[4 * c] for c in range(3)]
    end = LANES - 1
    masks = [mask_ref[direction].astype(F32) for direction in range(4)]
    for i in range(3):
        inverse_ref[i] = inverse[i]
        put(INVERSE, 0, i, inverse[i], 0, inverse[i], end)
        for a in range(3):
            up_x, low_x, up_y, low_y = (
                edge_ref[direction, 3 * i + a] * masks[direction] for direction in range(4)
            )
            put(UP_X, i, a, up_x, 0, up_x, end)
            put(LOW_X, i, a, low_x, 0, low_x, end)
            put(INWARD, i, a, low_y, 1, up_y, end - 1)
            put(OUTWARD, i, a, low_y, 0, up_y, end)
            if a != i:
                put(WITHIN, i, a, diag_ref[3 * i + a], 0, diag_ref[3 * i + a], end)
    columns_ref[...] = jnp.concatenate(sides, axis=0).T


def load_product(blocks, half):
    groups = blocks[0].shape[0] // 4
    size = -(-6 * half // 16) * 16
    line = iota((size, LANES), 0)
    block = sum(jnp.where(line >= half * k, 1, 0) for k in range(1, 6))
    at_row = jnp.where(line < 6 * half, line - half * block, -5).astype(F32).astype(BF16)
    at_column = float_iota((2 * LANES, LANES), 0).astype(BF16)
    in_tile = float_iota((16, LANES), 0).astype(BF16)
    zero, one = jnp.zeros((), BF16), jnp.ones((), BF16)
    lefts, rights = [], []
    for rows in blocks:
        index = rows[3 * groups :]
        split = float(half * LANES)
        index, shift = (
            jnp.where(index >= split, index - split, index),
            jnp.where(index >= split, float(LANES), 0.0),
        )
        place = jnp.floor(index * (1.0 / LANES))
        column = index - place * float(LANES) + shift
        parts = [two_parts(rows[c * groups : (c + 1) * groups]) for c in range(3)]
        for group in range(groups):
            here = slice(group, group + 1)
            values = [
                stretched(parts[c][which][here], 16) for which in range(2) for c in range(3)
            ]
            tiles = []
            for first in range(0, size, 16):
                low, high = first // half, min((first + 15) // half, 5)
                tiles.append(
                    values[low]
                    if low == high
                    else jnp.where(
                        in_tile < float(half * high - first), values[low], values[high]
                    )
                )
            match = at_row == stretched(place[here], size)
            lefts.append(jnp.where(match, jnp.concatenate(tiles, axis=0), zero))
            rights.append(
                jnp.where(at_column == stretched(column[here], 2 * LANES), one, zero)
            )
    return lax.dot_general(
        jnp.concatenate(lefts, axis=1),
        jnp.concatenate(rights, axis=1),
        (((1,), (1,)), ((), ())),
        preferred_element_type=F32,
    )


def own_kernel(rows_ref, load_ref, *, half):
    load_ref[...] = load_product([rows_ref[...]], half)


def field_kernel(
    rows_ref, own_ref, inverse_ref, columns_ref,
    field_ref, halo_ref, inner_ref, outer_ref, load_ref,
):
    senders = rows_ref.shape[0]
    groups = (rows_ref.shape[1] - NEAR) // 4
    cells_x = field_ref.shape[1]
    half = (cells_x + 2 * PAD) // 2
    own = cells_x // 2

    load_ref[...] = own_ref[...]
    here = lax.axis_index("gx")
    others = senders - 1
    together = others if others <= 8 else 1

    def add_rows(step, carry):
        blocks = []
        for k in range(together):
            sender = step * together + k
            sender = jnp.where(sender >= here, sender + 1, sender)
            blocks.append(rows_ref[sender, : 4 * groups, :])
        load_ref[...] += load_product(blocks, half)
        return carry

    lax.fori_loop(0, others // together, add_rows, 0)

    def load_rows(comp, first, last, second_half):
        lanes = slice(LANES, 2 * LANES) if second_half else slice(0, LANES)
        return (
            load_ref[comp * half + first : comp * half + last, lanes]
            + load_ref[(3 + comp) * half + first : (3 + comp) * half + last, lanes]
        )

    field = []
    for comp in range(3):
        load = jnp.concatenate(
            [load_rows(comp, PAD, half, False), load_rows(comp, 0, half - PAD, True)], axis=0
        )
        field.append(load * inverse_ref[comp])
        field_ref[comp] = field[comp]
    beyond = half - PAD
    near_before = [load_rows(c, PAD - 1, PAD, False) for c in range(3)]
    far_before = [load_rows(c, PAD - 2, PAD - 1, False) for c in range(3)]
    near_after = [load_rows(c, beyond, beyond + 1, True) for c in range(3)]

    base = 4 * groups

    def neighbour(sender, load):
        def entry(k):
            return rows_ref[sender, base + k : base + k + 1, :]

        inverse = [ratio(1.0, entry(k)) for k in range(3)]
        toward = [entry(3 + k) for k in range(9)]
        beside = [load[c] * inverse[c] for c in range(3)]
        return inverse, toward, beside, product(lambda k: toward[k], beside)

    lower = jnp.maximum(here - 1, 0)
    before = neighbour(lower, near_before)
    after = neighbour(jnp.minimum(here + 1, senders - 1), near_after)
    rows = before[2] + before[0] + before[3] + before[1] + far_before + after[3]
    for k, value in enumerate(rows):
        halo_ref[k : k + 1, :] = value
    lane_row = iota((1, LANES), 1)
    ends = jnp.zeros((1, LANES), F32)
    for i in range(3):
        for first, end in ((3 * i, LANES - 1), (9 + 3 * i, 0)):
            mine = (lane_row >= first) & (lane_row < first + 3)
            ends = jnp.where(mine, before[2][i][:, end : end + 1], ends)
    ends = ends * rows_ref[lower, base + 12 : base + 13, :]
    ends = ends + pltpu.roll(ends, LANES - 3, 1) + pltpu.roll(ends, LANES - 6, 1)

    two = jnp.concatenate(field[:2], axis=0).T
    third = jnp.concatenate([field[2], field[2]], axis=0).T

    def column_rows(first, last):
        low = lane_row < cells_x
        one, other = two[first : first + 1], two[last : last + 1]
        return [
            jnp.where(low, one, pltpu.roll(other, cells_x, 1)),
            jnp.where(low, pltpu.roll(one, cells_x, 1), other),
            jnp.where(low, third[first : first + 1], third[last : last + 1]),
        ]

    edge = column_rows(0, LANES - 1)
    inside = column_rows(1, LANES - 2)

    def column_product(kind, rows):
        return sum(
            columns_ref[8 * (kind + i) : 8 * (kind + i) + 8, :] * rows[i] for i in range(3)
        )

    def eight(rows):
        return jnp.concatenate(rows + [jnp.zeros((8 - len(rows), LANES), F32)], axis=0)

    lane = iota((8, LANES), 1)
    from_before, from_after = eight(before[3]), eight(after[3])
    from_before = jnp.where(lane == 0, from_before, pltpu.roll(from_before, cells_x + 1, 1))
    from_after = jnp.where(
        lane == LANES - 1, from_after, pltpu.roll(from_after, cells_x - 1, 1)
    )
    row = lane & (cells_x - 1)
    upward = pltpu.roll(column_product(UP_X, edge), 1, 1)
    downward = pltpu.roll(column_product(LOW_X, edge), LANES - 1, 1)
    total = (
        column_product(WITHIN, edge)
        + jnp.where(row == 0, from_before, upward)
        + jnp.where(row == cells_x - 1, from_after, downward)
        + column_product(INWARD, inside)
    )
    inverse = columns_ref[8 * INVERSE : 8 * INVERSE + 8, :]
    along_y, part = column_product(OUTWARD, edge), total * inverse
    stacked = jnp.concatenate(
        [*edge, along_y[:3], part[:3], inverse[:3], jnp.zeros((4, LANES), F32)], axis=0
    )

    def message(columns, end):
        at = iota((16, LANES), 1)
        line = iota((16, LANES), 0)
        columns = jnp.where(at < cells_x, columns, 0.0)
        for comp in range(3):
            columns = jnp.where(
                (line == 3 + comp) & (at == cells_x),
                ends[:, end + comp : end + comp + 1],
                columns,
            )
        return columns

    inner_ref[...], outer_ref[...] = by_parity(
        message(stacked, 9), message(pltpu.roll(stacked, cells_x, 1), 0)
    )


def bernstein(coord):
    other = 1.0 - coord
    return [
        other * other * other,
        3.0 * coord * other * other,
        3.0 * coord * coord * other,
        coord * coord * coord,
    ]


def weight_table(u, v, w):
    first, second, third = bernstein(u), bernstein(v), bernstein(w)
    line = iota((8, u.shape[1]), 0)
    inner = line & 3
    along = jnp.where(
        inner == 0,
        third[0],
        jnp.where(inner == 1, third[1], jnp.where(inner == 2, third[2], third[3])),
    )
    pair = jnp.concatenate(
        [
            jnp.where(line < 4, second[0], second[1]) * along,
            jnp.where(line < 4, second[2], second[3]) * along,
        ],
        axis=0,
    )
    return jnp.concatenate([pair * first[i] for i in range(4)], axis=0)


def tile_rows(terms):
    first_half = iota((4, LANES), 1) < LANES // 2
    rows = []
    for term in terms:
        term = term[:8] + term[8:]
        term = term + pltpu.roll(term, LANES // 2, 1)
        rows.append(jnp.where(first_half, term[:4], term[4:]))
    return jnp.concatenate(two_parts(jnp.concatenate(rows, axis=0)), axis=0).astype(BF16)


def box_matrix(tile_row, boxes):
    tiles = tile_row.shape[1]
    shape = (4 * boxes, 8 * tiles)
    column = iota((1, shape[1]), 1)
    box = jnp.zeros((1, shape[1]), jnp.int32)
    for tile in range(tiles):
        mine = lax.rem(lax.shift_right_logical(column, 2), tiles) == tile
        box = jnp.where(mine, tile_row[:, tile : tile + 1], box)
    target = 4 * box + (column & 3)
    return jnp.where(iota(shape, 0) == target, 1.0, 0.0).astype(BF16)


def by_parity(low, high):
    odd = lax.rem(lax.axis_index("gy"), 2) == 1
    return jnp.where(odd, high, low), jnp.where(odd, low, high)


def quotient_before(halo_ref, strip_ref, before_ref, entering):
    def rows(ref, first, count):
        return [ref[first + k : first + k + 1, :] for k in range(count)]

    beside, inverse = rows(halo_ref, 0, 3), rows(halo_ref, 3, 3)
    far_load, within = rows(halo_ref, 18, 3), rows(strip_ref, 0, 6)
    far_scale = rows(strip_ref, 33, 3)
    far = [ratio(far_load[c], far_scale[c]) for c in range(3)]
    whole_block = [None, *within[:3], None, *within[3:], None]
    total = off_diagonal(lambda k: whole_block[k], beside)
    from_far = product(lambda k: strip_ref[24 + k : 25 + k, :], far)
    up_y = product(lambda k: strip_ref[6 + k : 7 + k, :], beside)
    low_y = product(lambda k: strip_ref[15 + k : 16 + k, :], beside)
    for c in range(3):
        before_ref[c : c + 1, :] = inverse[c] * (
            total[c]
            + from_far[c]
            + entering[c]
            + lanes_moved(up_y[c], 0.0, 1)
            + lanes_moved(low_y[c], 0.0, -1)
        )
    before_ref[3:, :] = jnp.zeros((before_ref.shape[0] - 3, LANES), F32)


def box_kernel(
    tile_ref, field_ref, node_ref, param_ref, halo_ref, strip_ref, diag_ref, edge_ref,
    mask_ref, inverse_ref,
    part_ref, box_ref, adjoint_ref, before_ref, matrix_ref, weights_ref, columns_ref,
    *, tile_points,
):
    cells_x = field_ref.shape[1]
    own = cells_x // 2
    field = [field_ref[c] for c in range(3)]
    part = off_diagonal(lambda k: diag_ref[k], field)
    up_x = masked_product(edge_ref, mask_ref, 0, field)
    low_x = masked_product(edge_ref, mask_ref, 1, field)
    up_y = masked_product(edge_ref, mask_ref, 2, field)
    low_y = masked_product(edge_ref, mask_ref, 3, field)
    for c in range(3):
        part[c] = inverse_ref[c] * (
            part[c]
            + rows_moved(up_x[c], halo_ref[6 + c : 7 + c, :], 1)
            + rows_moved(low_x[c], halo_ref[21 + c : 22 + c, :], -1)
            + lanes_moved(up_y[c], 0.0, 1)
            + lanes_moved(low_y[c], 0.0, -1)
        )
        part_ref[c] = part[c]
    quotient_before(halo_ref, strip_ref, before_ref, [p[:1] for p in low_x])
    order = [field[0], part[0], field[2], field[1], part[1], part[2]]
    folded = [two_parts(jnp.concatenate([f[:own], f[own:]], axis=1)) for f in order]
    table = jnp.concatenate(
        [folded[f][which] for which in range(2) for f in range(6)], axis=0
    ).astype(BF16)
    points = param_ref.shape[1]
    pieces = CHUNK // LANES
    zero, one = jnp.zeros((), BF16), jnp.ones((), BF16)
    at_node = float_iota((2 * LANES, CHUNK), 0).astype(BF16)
    nothing = jnp.zeros((1, CHUNK), F32)
    highs, lows = [], []
    for chunk in range(points // CHUNK):
        node = jnp.concatenate(
            [node_ref[chunk * pieces + k : chunk * pieces + k + 1, :] for k in range(pieces)],
            axis=1,
        )
        row = lax.shift_right_logical(node, 7)
        column = node & (LANES - 1)
        lanes = slice(chunk * CHUNK, (chunk + 1) * CHUNK)
        at_edge = jnp.where(
            column == 0, row, jnp.where(column == LANES - 1, row + cells_x, -1)
        ).astype(F32)
        columns_ref[:, lanes] = jnp.where(
            at_node[: 2 * cells_x] == stretched(at_edge, 2 * cells_x), one, zero
        )
        place = column + jnp.where(row >= own, LANES, 0)
        row = jnp.where(row >= own, row - own, row)
        pick = jnp.where(at_node == stretched(place.astype(F32), 2 * LANES), one, zero)
        read = jnp.dot(table, pick, preferred_element_type=F32)
        read = read[: 6 * own] + read[6 * own :]
        here = iota((own, CHUNK), 0) == row
        values = [
            jnp.sum(
                jnp.where(here, read[f * own : (f + 1) * own], 0.0), axis=0, keepdims=True
            )
            for f in range(6)
        ]
        high, low = two_parts(
            jnp.concatenate(values[:3] + [nothing] + values[3:] + [nothing], axis=0)
        )
        highs.append(high)
        lows.append(low)
        weights = two_parts(
            weight_table(param_ref[0:1, lanes], param_ref[1:2, lanes], param_ref[2:3, lanes])
        )
        for k in range(CHUNK // tile_points):
            tile = slice(k * tile_points, (k + 1) * tile_points)
            sides = jnp.concatenate([weights[0][:, tile], weights[1][:, tile]], axis=0)
            weights_ref[chunk * (CHUNK // tile_points) + k] = sides.T.astype(BF16)
    both = jnp.concatenate(
        [jnp.concatenate(highs, axis=1), jnp.concatenate(lows, axis=1)], axis=0
    ).astype(BF16)
    matrix_ref[...] = box_matrix(tile_ref[...], matrix_ref.shape[0] // 4)
    tiles = tile_ref.shape[1]
    terms = [
        jnp.dot(
            both[:, tile * tile_points : (tile + 1) * tile_points],
            weights_ref[tile],
            preferred_element_type=F32,
        )
        for tile in range(tiles)
    ]
    box_ref[...] = jnp.dot(matrix_ref[...], tile_rows(terms), preferred_element_type=F32)
    low_half = iota((2 * cells_x, LANES), 1) < LANES // 2
    for tile in range(tiles):
        lanes = slice(tile * tile_points, (tile + 1) * tile_points)
        term = jnp.dot(
            columns_ref[:, lanes], weights_ref[tile], preferred_element_type=F32
        )
        high, low = two_parts(term + pltpu.roll(term, LANES // 2, 1))
        adjoint_ref[:, tile * LANES : (tile + 1) * LANES] = jnp.where(
            low_half, high, low
        ).astype(BF16)


def sums_kernel(
    from_inner_ref, from_outer_ref, inner_ref, outer_ref, field_ref, part_ref, halo_ref,
    diag_ref, edge_ref, mask_ref, box_ref, adjoint_ref, before_ref, matrix_ref, columns_ref,
    quotient_ref, out_ref,
):
    cells_x = field_ref.shape[1]
    targets = out_ref.shape[0]

    from_low, from_high = by_parity(from_inner_ref[...], from_outer_ref[...])
    first, last = by_parity(inner_ref[...], outer_ref[...])

    lane_row = iota((1, LANES), 1)
    shares, edges = [], []
    for arrived, own in ((from_low, first), (from_high, last)):
        def row(source, slot, c):
            return source[3 * slot + c : 3 * slot + c + 1]

        shares.append([row(arrived, 1, c) * row(own, 3, c) for c in range(3)])
        edges.append(
            [row(arrived, 2, c) + row(arrived, 3, c) * row(own, 1, c) for c in range(3)]
        )

    none = jnp.zeros((1, LANES), F32)
    rest = jnp.zeros((LANES - 6, LANES), F32)
    turned = jnp.concatenate([*shares[0], *shares[1], rest], axis=0).T
    lane = iota((cells_x, LANES), 1)

    def both(low, high):
        return jnp.where(lane_row < cells_x, low, pltpu.roll(high, cells_x, 1))

    field = [field_ref[c] for c in range(3)]
    scale = [diag_ref[4 * c] for c in range(3)]
    quotient = []
    for c in range(3):
        entering = jnp.where(
            lane == 0,
            turned[:cells_x, c : c + 1],
            jnp.where(lane == LANES - 1, turned[:cells_x, 3 + c : 4 + c], 0.0),
        )
        quotient.append(part_ref[c] + entering)
        quotient_ref[c] = quotient[c]
    before, before_quotient = [], []
    for c in range(3):
        entering = jnp.where(
            lane_row == 0,
            from_low[3 + c : 4 + c, cells_x : cells_x + 1],
            jnp.where(
                lane_row == LANES - 1, from_high[3 + c : 4 + c, cells_x : cells_x + 1], 0.0
            ),
        )
        before.append(halo_ref[c : c + 1, :])
        before_quotient.append(
            before_ref[c : c + 1, :] + entering * halo_ref[3 + c : 4 + c, :]
        )

    first_sum = sum(field[c] * scale[c] * field[c] for c in range(3))
    second_sum = sum(field[c] * scale[c] * quotient[c] for c in range(3))
    third_sum = sum(quotient[c] * scale[c] * quotient[c] for c in range(3))
    within = off_diagonal(lambda k: diag_ref[k], quotient)
    fourth_sum = sum(within[c] * field[c] for c in range(3))
    fifth_sum = sum(within[c] * quotient[c] for c in range(3))
    at_row = iota((cells_x, LANES), 0)
    moves = (
        (pltpu.roll, 1, 0, at_row == 0),
        (pltpu.roll, cells_x - 1, 0, at_row == cells_x - 1),
        (pltpu.roll, 1, 1, lane == 0),
        (pltpu.roll, LANES - 1, 1, lane == LANES - 1),
    )
    extra = [0.0, 0.0]
    for direction, (roll, step, dim, edge) in enumerate(moves):
        moving = masked_product(edge_ref, mask_ref, direction, quotient)
        for c in range(3):
            moved = jnp.where(edge, 0.0, roll(moving[c], step, dim))
            fourth_sum = fourth_sum + moved * field[c]
            fifth_sum = fifth_sum + moved * quotient[c]
            if direction == 1:
                extra[0] += moving[c][:1] * before[c]
                extra[1] += moving[c][:1] * before_quotient[c]
    at_edge = [
        both(first[6 + c : 7 + c] + shares[0][c], last[6 + c : 7 + c] + shares[1][c])
        for c in range(3)
    ]
    leaving = sum(
        columns_ref[8 * (OUTWARD + i) : 8 * (OUTWARD + i) + 8, :] * at_edge[i]
        for i in range(3)
    )
    for c in range(3):
        out = leaving[c : c + 1]
        extra[0] += out * both(from_low[c : c + 1], from_high[c : c + 1])
        extra[1] += out * both(edges[0][c], edges[1][c])
    incoming = product(lambda k: halo_ref[9 + k : 10 + k, :], before_quotient)
    extra[0] += sum(incoming[c] * field[c][:1] for c in range(3))
    extra[1] += sum(incoming[c] * quotient[c][:1] for c in range(3))
    extra = [0.0, 0.0, 0.0, extra[0], extra[1]]
    sums = jnp.zeros((1, LANES), F32)
    for k, value in enumerate((first_sum, second_sum, third_sum, fourth_sum, fifth_sum)):
        line = jnp.sum(value, axis=0, keepdims=True) + extra[k]
        sums = jnp.where(lane_row == k, jnp.sum(line, axis=1, keepdims=True), sums)

    added = [both(shares[0][c], shares[1][c]) for c in range(3)]
    added = jnp.concatenate(
        [none, added[0], none, none, none, added[1], added[2], none], axis=0
    )
    added = jnp.concatenate(two_parts(added), axis=0).astype(BF16)
    terms = jnp.dot(added, adjoint_ref[...], preferred_element_type=F32)
    terms = [
        terms[:, first : first + LANES] for first in range(0, terms.shape[1], LANES)
    ]
    total = box_ref[...] + jnp.dot(
        matrix_ref[...], tile_rows(terms), preferred_element_type=F32
    )
    total = jnp.where((iota(total.shape, 0) & 3) == 3, sums, total)
    for box in range(targets):
        out_ref[box] = total[4 * box : 4 * box + 4]


def result_kernel(got_ref, field_ref, quotient_ref, solution_ref, gradient_ref):
    total = jnp.sum(got_ref[...], axis=0)
    rho, a, b, t, u = [total[3:4, k : k + 1] for k in range(5)]
    norm = rho + a
    by_rho, by_norm = 1.0 / rho, 1.0 / norm
    ratio, step = a * by_rho, rho * by_norm
    rest = jnp.maximum(b - a * ratio, 0.0)
    beta = step * step * rest * by_rho
    rest_image = (b + u) - ratio * (a + b + a + t) + ratio * ratio * norm
    cross = (a + t) - ratio * norm
    curve = step * step * rest_image - step * beta * (rest + cross) + beta * beta * norm
    second = jnp.where(
        curve > 0.0, step * step * rest / jnp.where(curve > 0.0, curve, 1.0), 0.0
    )
    second = jnp.minimum(second, 16.0)
    of_field = step + second * (beta + step * ratio)
    of_quotient = -(step * second)
    for c in range(3):
        solution_ref[c] = of_field * field_ref[c] + of_quotient * quotient_ref[c]
    gradient_ref[:, :LANES] = of_field * total[0:1] + of_quotient * total[1:2]
    gradient_ref[:, LANES:] = (
        of_field * total[2:3, : LANES // 2] + of_quotient * total[2:3, LANES // 2 :]
    )


def per_device(
    diag_blocks, edge_blocks, edge_mask, src_values, src_owner, src_node, src_count,
    surf_node, surf_param, tile_box,
):
    cells_x, cells_y = diag_blocks.shape[1:]
    width_gx, width_gy = lax.axis_size("gx"), lax.axis_size("gy")
    devices = width_gx * width_gy
    groups = src_node.shape[0] // LANES
    whole = functools.partial(jax.ShapeDtypeStruct, dtype=F32)

    cells = 4 * groups + NEAR

    def kept(array):
        return pltpu.with_memory_space_constraint(array, pltpu.HBM)

    i32 = jnp.int32
    rows, own = pl.pallas_call(
        pack_kernel,
        in_specs=[SMEM] + [HBM] * 6,
        out_specs=[HBM, VMEM],
        out_shape=[
            pltpu.HBM((width_gx, cells, LANES), F32),
            pltpu.VMEM((4 * groups, LANES), F32),
        ],
        scratch_shapes=[
            pltpu.VMEM(src_values.shape, F32),
            pltpu.VMEM((groups, LANES), i32),
            pltpu.VMEM((groups, LANES), i32),
            pltpu.VMEM((3, 8, cells_y), F32),
            pltpu.VMEM((3, 8, cells_y), F32),
            pltpu.VMEM((9, 8, cells_y), F32),
            pltpu.VMEM((9, 8, cells_y), F32),
            pltpu.VMEM((2, 9, 8, cells_y), F32),
            pltpu.VMEM((8, cells_y), i32),
            pltpu.VMEM((4, 8, cells_y), i32),
            pltpu.VMEM((width_gx, cells, LANES), F32),
            pltpu.SemaphoreType.DMA((14,)),
            pltpu.SemaphoreType.DMA((2,)),
        ],
        compiler_params=PARAMS,
        name="pack_rows_and_edges",
    )(
        src_count, kept(src_values),
        kept(src_owner.reshape(groups, LANES)), kept(src_node.reshape(groups, LANES)),
        kept(diag_blocks), kept(edge_blocks), kept(edge_mask),
    )
    rows = lax.all_to_all(rows, "gx", split_axis=0, concat_axis=0, tiled=True)

    nodes = (3, cells_x, cells_y)
    inverse, columns, strip = pl.pallas_call(
        edge_kernel,
        in_specs=[VMEM] * 3,
        out_specs=[VMEM] * 3,
        out_shape=[whole(nodes), whole((LANES, LANES)), whole((STRIP, LANES))],
        compiler_params=PARAMS,
        cost_estimate=pl.CostEstimate(
            flops=10**8, bytes_accessed=4 * 10**6, transcendentals=0
        ),
        name="edge_columns",
    )(diag_blocks, edge_blocks, edge_mask)
    strip = lax.ppermute(strip, "gx", [(i, i + 1) for i in range(width_gx - 1)])

    half = (cells_x + 2 * PAD) // 2
    size = -(-6 * half // 16) * 16
    own_load = pl.pallas_call(
        functools.partial(own_kernel, half=half),
        in_specs=[VMEM],
        out_specs=VMEM,
        out_shape=whole((size, 2 * LANES)),
        compiler_params=PARAMS,
        cost_estimate=pl.CostEstimate(
            flops=10**8, bytes_accessed=10**6, transcendentals=0
        ),
        name="own_load",
    )(own)
    field, halo, inner, outer = pl.pallas_call(
        field_kernel,
        in_specs=[VMEM] * 4,
        out_specs=[VMEM] * 4,
        out_shape=[
            whole(nodes), whole((24, cells_y)), whole((16, LANES)), whole((16, LANES)),
        ],
        scratch_shapes=[pltpu.VMEM((size, 2 * LANES), F32)],
        compiler_params=PARAMS,
        name="load_and_first_product",
    )(rows, own_load, inverse, columns)
    def swapped(columns, first):
        low = range(first, width_gy - 1, 2)
        pairs = [(i, i + 1) for i in low] + [(i + 1, i) for i in low]
        return lax.ppermute(columns, "gy", pairs)

    from_inner, from_outer = swapped(inner, 1), swapped(outer, 0)
    points, tiles = surf_node.shape[0], tile_box.shape[0]
    part, box_part, adjoint, before, matrix = pl.pallas_call(
        functools.partial(box_kernel, tile_points=points // tiles),
        in_specs=[VMEM] * 10,
        out_specs=[VMEM] * 5,
        out_shape=[
            whole(nodes),
            whole((4 * devices, LANES)),
            jax.ShapeDtypeStruct((2 * cells_x, tiles * LANES), BF16),
            whole((8, LANES)),
            jax.ShapeDtypeStruct((4 * devices, 8 * tiles), BF16),
        ],
        scratch_shapes=[
            pltpu.VMEM((tiles, points // tiles, LANES), BF16),
            pltpu.VMEM((2 * cells_x, points), BF16),
        ],
        compiler_params=PARAMS,
        cost_estimate=pl.CostEstimate(
            flops=10**9, bytes_accessed=4 * 10**6, transcendentals=0
        ),
        name="box_parts",
    )(
        tile_box.reshape(1, tiles), field, surf_node.reshape(points // LANES, LANES),
        surf_param, halo, strip, diag_blocks, edge_blocks, edge_mask, inverse,
    )

    quotient, partial = pl.pallas_call(
        sums_kernel,
        in_specs=[VMEM] * 15,
        out_specs=[VMEM] * 2,
        out_shape=[whole(nodes), whole((devices, 4, LANES))],
        compiler_params=PARAMS,
        name="sums_and_halo_parts",
    )(
        from_inner, from_outer, inner, outer, field, part, halo, diag_blocks, edge_blocks, edge_mask,
        box_part, adjoint, before, matrix, columns,
    )
    got = lax.all_to_all(partial, ("gx", "gy"), split_axis=0, concat_axis=0, tiled=True)
    return pl.pallas_call(
        result_kernel,
        in_specs=[VMEM] * 3,
        out_specs=[VMEM] * 2,
        out_shape=[whole(nodes), whole((1, 192))],
        compiler_params=PARAMS,
        name="steps_and_outputs",
    )(got, field, quotient)


def solution(mesh):
    return jax.shard_map(
        per_device,
        mesh=mesh,
        in_specs=(
            P(None, "gx", "gy"),
            P(None, None, "gx", "gy"),
            P(None, "gx", "gy"),
            P(None, ("gx", "gy")),
            P(("gx", "gy"), None),
            P(("gx", "gy")),
            P(("gx", "gy")),
            P(("gx", "gy")),
            P(None, ("gx", "gy")),
            P(("gx", "gy")),
        ),
        out_specs=(P(None, "gx", "gy"), P(("gx", "gy"), None)),
        check_vma=False,
    )
```
